32 devices in a mesh: fsdp: 4 (over y, x), ctx: 4 (over z), tp: 2 (over core).
Axes of the slice: x: 2, y: 2, z: 4, core: 2. Of those that a mesh axis runs over, the one named last changes fastest.
Arguments:
- hidden_in: bfloat16 [4096, 2048], P(('fsdp', 'ctx')), may hold values from -6 to 6
- out_cotangent: bfloat16 [4096, 2048], P(('fsdp', 'ctx')), may hold values from -6 to 6
- norm1_gain: bfloat16 [2048], P('fsdp'), may hold values from 0.25 to 1.75
- q_weight: bfloat16 [2048, 2048], P('fsdp', 'tp'), may hold values from -0.125 to 0.125
- key_projection_weight: bfloat16 [2048, 512], P('fsdp', 'tp'), may hold values from -0.125 to 0.125
- value_projection_weight: bfloat16 [2048, 512], P('fsdp', 'tp'), may hold values from -0.125 to 0.125
- o_weight: bfloat16 [2048, 2048], P('fsdp', 'tp'), may hold values from -1 to 1
- norm2_gain: bfloat16 [2048], P('fsdp'), may hold values from 0.25 to 1.75
- gate_weight: bfloat16 [2048, 8192], P('fsdp', 'tp'), may hold values from -0.125 to 0.125
- up_weight: bfloat16 [2048, 8192], P('fsdp', 'tp'), may hold values from -0.125 to 0.125
- down_weight: bfloat16 [2048, 8192], P('fsdp', 'tp'), may hold values from -0.0625 to 0.0625
- seq_lengths: int32 [4, 4], P('fsdp'), may hold values from 1 to 768, as said below
- span_order: int32 [4, 4], P('fsdp'), may hold values from 0 to 3, each once within a row
Outputs:
- out_hidden: bfloat16 [4096, 2048], P(('fsdp', 'ctx'))
- in_grad: bfloat16 [4096, 2048], P(('fsdp', 'ctx'))
- norm1_grad: float32 [2048], P('fsdp')
- q_grad: float32 [2048, 2048], P('fsdp', 'tp')
- k_grad: float32 [2048, 512], P('fsdp', 'tp')
- v_grad: float32 [2048, 512], P('fsdp', 'tp')
- o_grad: float32 [2048, 2048], P('fsdp', 'tp')
- norm2_grad: float32 [2048], P('fsdp')
- gate_grad: float32 [2048, 8192], P('fsdp', 'tp')
- up_grad: float32 [2048, 8192], P('fsdp', 'tp')
- down_grad: float32 [2048, 8192], P('fsdp', 'tp')
The draws below stay inside these ranges and needn't reach their ends.
Inputs may be any that keep to these rules, and one draw needn't show every extreme that they name: `seq_lengths`: each row holds 4 positive lengths that sum to 1024; exactly one of them is 768. `span_order`: each row is a permutation.
All inputs are finite; a program needn't handle non-finite values.
Results may differ from the reference program's by a relative error of at most 0.02.
Values may be sent and summed in bfloat16 or wider, within the bound.
No kernel may reach another device: no remote copies, remote signals or barrier semaphores. Data moves between devices by JAX's collectives and lax.ppermute only.
A program may use at most 320 MiB of HBM per device.

```python
import math
import jax
import jax.numpy as jnp
from jax import lax

MODEL_WIDTH = 2048
QUERY_HEADS = 32
KEY_VALUE_HEADS = 8
HEAD_SIZE = 64
FF = 8192
TOK_DEV = 256
NSEQ = 4
PACK_TOKENS = 1024
TOTAL_TOKENS = 4096
N_FSDP = 4
N_CTX = 4


def draw_seq_lengths(key, part):
    key = jax.random.fold_in(key, 7)
    longest_len = 3 * PACK_TOKENS // 4
    remainder = PACK_TOKENS - longest_len

    def one_row(row_key):
        cut_key, side_key = jax.random.split(row_key)
        cut_points = jnp.sort(jax.random.choice(cut_key, remainder - 1, (NSEQ - 2,), replace=False) + 1).astype(jnp.int32)
        bounds = jnp.concatenate([jnp.zeros((1,), jnp.int32), cut_points, jnp.full((1,), remainder, jnp.int32)])
        short_ones = bounds[1:] - bounds[:-1]
        longest = jnp.full((1,), longest_len, jnp.int32)
        placed_last = jax.random.randint(side_key, (), 0, 2)
        return jnp.where(placed_last == 0, jnp.concatenate([longest, short_ones]), jnp.concatenate([short_ones, longest]))
    return jax.vmap(one_row)(jax.random.split(key, N_FSDP))


def level_of(own_key, dims, cuts, smallest, largest):
    def one(position, parts):
        heights = jax.random.uniform(jax.random.fold_in(jax.random.fold_in(own_key, 6), position), (parts,), jnp.float32, smallest / len(cuts), largest / len(cuts))
        return jnp.repeat(jnp.exp(heights), dims[position] // parts).reshape((-1,) + (1,) * (len(dims) - position - 1))

    factor_of = one(*cuts[0])
    for cut in cuts[1:]:
        factor_of = factor_of * one(*cut)
    return factor_of


def bell_draw(stream_key, shape, deviation, bound, cuts=(), kind=jnp.bfloat16):
    array = deviation * jax.random.normal(stream_key, shape, jnp.float32)
    if cuts:
        array = array * level_of(stream_key, shape, cuts, -0.22, 0.18)
    return jnp.clip(array, -bound, bound).astype(kind)


def setup_inputs(seed: int = 0) -> dict:
    keys = jax.random.split(jax.random.key(seed), 14)
    hidden_in = bell_draw(keys[0], (TOTAL_TOKENS, MODEL_WIDTH), 1.0, 6.0, ((0, 16),))
    out_cotangent = bell_draw(keys[1], (TOTAL_TOKENS, MODEL_WIDTH), 1.0, 6.0, ((0, 16),))
    norm1_gain = jnp.clip(1.0 + 0.15 * jax.random.normal(keys[2], (MODEL_WIDTH,), jnp.float32), 0.25, 1.75).astype(jnp.bfloat16)
    q_weight = bell_draw(keys[3], (MODEL_WIDTH, QUERY_HEADS * HEAD_SIZE), MODEL_WIDTH ** -0.5, 0.125, ((0, 4), (1, 2)))
    key_projection_weight = bell_draw(keys[4], (MODEL_WIDTH, KEY_VALUE_HEADS * HEAD_SIZE), MODEL_WIDTH ** -0.5, 0.125, ((0, 4), (1, 2)))
    value_projection_weight = bell_draw(keys[5], (MODEL_WIDTH, KEY_VALUE_HEADS * HEAD_SIZE), MODEL_WIDTH ** -0.5, 0.125, ((0, 4), (1, 2)))
    o_weight = bell_draw(keys[6], (MODEL_WIDTH, QUERY_HEADS * HEAD_SIZE), (QUERY_HEADS * HEAD_SIZE // 64) ** -0.5, 1.0, ((0, 4), (1, 2)))
    norm2_gain = jnp.clip(1.0 + 0.15 * jax.random.normal(keys[7], (MODEL_WIDTH,), jnp.float32), 0.25, 1.75).astype(jnp.bfloat16)
    gate_weight = bell_draw(keys[8], (MODEL_WIDTH, FF), MODEL_WIDTH ** -0.5, 0.125, ((0, 4), (1, 2)))
    up_weight = bell_draw(keys[9], (MODEL_WIDTH, FF), MODEL_WIDTH ** -0.5, 0.125, ((0, 4), (1, 2)))
    down_weight = bell_draw(keys[10], (MODEL_WIDTH, FF), FF ** -0.5, 0.0625, ((0, 4), (1, 2)))
    seq_lengths = draw_seq_lengths(jax.random.fold_in(keys[13], 71), 0)
    span_order = jax.vmap(lambda own: jax.random.permutation(own, N_CTX))(jax.random.split(keys[12], N_FSDP)).reshape((N_FSDP, N_CTX)).astype(jnp.int32)
    return {"hidden_in": hidden_in, "out_cotangent": out_cotangent, "norm1_gain": norm1_gain, "q_weight": q_weight, "key_projection_weight": key_projection_weight, "value_projection_weight": value_projection_weight, "o_weight": o_weight, "norm2_gain": norm2_gain, "gate_weight": gate_weight, "up_weight": up_weight, "down_weight": down_weight, "seq_lengths": seq_lengths, "span_order": span_order}


@jax.custom_vjp
def reduced_precision(v):
    return lax.optimization_barrier(v.astype(jnp.bfloat16)).astype(jnp.float32)

@jax.custom_vjp
def reduced_precision_back(v):
    return v

def low_keep(v):
    return (reduced_precision(v), None)

def low_pass(kept, grad):
    return (grad,)

def back_keep(v):
    return (v, None)

def back_low(kept, grad):
    return (reduced_precision(grad),)
reduced_precision.defvjp(low_keep, low_pass)
reduced_precision_back.defvjp(back_keep, back_low)

def stream_place(row_ids, order_row, length_row, tok_dev):
    cycle_size = order_row.shape[0]
    half_len = tok_dev // 2
    cycle_rank = row_ids // tok_dev
    within = row_ids % tok_dev
    first_section = lax.optimization_barrier(jnp.sum(jnp.where(cycle_rank[:, None] == jnp.arange(cycle_size, dtype=jnp.int32)[None, :], order_row[None, :], 0), axis=1, dtype=jnp.int32))
    section = jnp.where(within >= half_len, 2 * cycle_size - 1 - first_section, first_section)
    places = (section * half_len + within % half_len).astype(jnp.int32)
    seq_ends = jnp.cumsum(length_row, dtype=jnp.int32)
    passed = places[:, None] >= seq_ends[None, :]
    segment = lax.optimization_barrier(jnp.sum(passed.astype(jnp.int32), axis=1, dtype=jnp.int32))
    offset = places - lax.optimization_barrier(jnp.sum(jnp.where(passed, length_row[None, :], 0), axis=1, dtype=jnp.int32))
    return (places, segment, offset.astype(jnp.int32))

def rotary_embedding(values, positions):
    half_len = values.shape[-1] // 2
    frequency = jnp.exp(-math.log(500000.0) * jnp.arange(half_len, dtype=jnp.float32) * 2.0 / values.shape[-1])
    angles = positions.astype(jnp.float32)[:, None] * frequency[None, :]
    cosine = jnp.cos(angles)[:, None, :]
    sine = jnp.sin(angles)[:, None, :]
    lower_half = values[..., :half_len]
    upper_half = values[..., half_len:]
    return jnp.concatenate([lower_half * cosine - upper_half * sine, upper_half * cosine + lower_half * sine], axis=-1)

def normalize(values, gain_vec):
    return values * lax.rsqrt(lax.optimization_barrier(jnp.mean(values * values, axis=-1, keepdims=True)) + 1e-05) * gain_vec

def matrix_product(left, right):
    return jnp.dot(left, right, precision=lax.Precision.HIGHEST, preferred_element_type=jnp.float32)

def reference(hidden_in, out_cotangent, norm1_gain, q_weight, key_projection_weight, value_projection_weight, o_weight, norm2_gain, gate_weight, up_weight, down_weight, seq_lengths, span_order):
    query_groups = QUERY_HEADS // KEY_VALUE_HEADS
    score_scale = 1.0 / math.sqrt(HEAD_SIZE)
    row_ids = jnp.arange(PACK_TOKENS, dtype=jnp.int32)
    places, segments, offsets = jax.vmap(lambda order_row, length_row: stream_place(row_ids, order_row, length_row, TOK_DEV))(span_order, seq_lengths)
    key_total_width = math.gcd(PACK_TOKENS, 512)

    def pack_attention(pack_in):
        query_rows, key_row_block, value_row_block, pack_positions, pack_segment_ids = pack_in

        def block_fn(query_block, query_places, query_segments):
            scores = reduced_precision_back(jnp.einsum('qkgd,skd->kgqs', query_block, key_row_block, precision=lax.Precision.HIGHEST) * score_scale)
            visible = (query_places[:, None] >= pack_positions[None, :]) & (query_segments[:, None] == pack_segment_ids[None, :])
            scores = jnp.where(visible[None, None], scores, -1e+30)
            prob_rows = jax.nn.softmax(scores, axis=-1)
            mixed_out = jnp.einsum('kgqs,skd->qkgd', reduced_precision(prob_rows), value_row_block, precision=lax.Precision.HIGHEST)
            return reduced_precision_back(reduced_precision(mixed_out))
        checked = jax.checkpoint(block_fn)
        incoming_blocks = (query_rows.reshape(PACK_TOKENS // key_total_width, key_total_width, KEY_VALUE_HEADS, query_groups, HEAD_SIZE), pack_positions.reshape(-1, key_total_width), pack_segment_ids.reshape(-1, key_total_width))
        outputs = lax.map(lambda block_in: checked(*block_in), incoming_blocks)
        return outputs.reshape(PACK_TOKENS, QUERY_HEADS * HEAD_SIZE)

    def forward(hidden, gain_one, q_full, key_full_matrix, value_full_matrix, o_full, gain_two, gate_full, up_full, down_full):
        first_normalized = reduced_precision(normalize(hidden, gain_one))
        query_linear_rows = reduced_precision_back(matrix_product(first_normalized, q_full)).reshape(TOTAL_TOKENS, QUERY_HEADS, HEAD_SIZE)
        key_linear_rows = reduced_precision_back(matrix_product(first_normalized, key_full_matrix)).reshape(TOTAL_TOKENS, KEY_VALUE_HEADS, HEAD_SIZE)
        value_row_block = reduced_precision_back(reduced_precision(matrix_product(first_normalized, value_full_matrix))).reshape(N_FSDP, PACK_TOKENS, KEY_VALUE_HEADS, HEAD_SIZE)
        flattened_offsets = offsets.reshape(TOTAL_TOKENS)
        query_rows = reduced_precision(rotary_embedding(query_linear_rows, flattened_offsets)).reshape(N_FSDP, PACK_TOKENS, KEY_VALUE_HEADS, query_groups, HEAD_SIZE)
        key_row_block = reduced_precision(rotary_embedding(key_linear_rows, flattened_offsets)).reshape(N_FSDP, PACK_TOKENS, KEY_VALUE_HEADS, HEAD_SIZE)
        attended = lax.map(pack_attention, (query_rows, key_row_block, value_row_block, places, segments)).reshape(TOTAL_TOKENS, QUERY_HEADS * HEAD_SIZE)
        middle = hidden + reduced_precision_back(matrix_product(attended, o_full.T))
        normed_two = reduced_precision(normalize(middle, gain_two))
        gate_val = reduced_precision_back(matrix_product(normed_two, gate_full))
        up_val = reduced_precision_back(matrix_product(normed_two, up_full))
        hidden_act = reduced_precision(jax.nn.silu(gate_val) * up_val)
        return middle + reduced_precision_back(matrix_product(hidden_act, down_full.T))
    params = [item.astype(jnp.float32) for item in (hidden_in, norm1_gain, q_weight, key_projection_weight, value_projection_weight, o_weight, norm2_gain, gate_weight, up_weight, down_weight)]
    result, back_fn = jax.vjp(forward, *params)
    grads = back_fn(out_cotangent.astype(jnp.float32))
    return (result.astype(jnp.bfloat16), grads[0].astype(jnp.bfloat16), grads[1], grads[2], grads[3], grads[4], grads[5], grads[6], grads[7], grads[8], grads[9])
```

```python
import math

import jax
import jax.numpy as jnp
from jax import lax
from jax.sharding import PartitionSpec as P

QUERY_HEADS = 32
KEY_VALUE_HEADS = 8
HEAD_SIZE = 64


def stream_place(row_ids, order_row, length_row, tok_dev):
    cycle_size = order_row.shape[0]
    half_len = tok_dev // 2
    cycle_rank = row_ids // tok_dev
    within = row_ids % tok_dev
    first_section = jnp.sum(
        jnp.where(
            cycle_rank[:, None] == jnp.arange(cycle_size, dtype=jnp.int32)[None, :],
            order_row[None, :],
            0,
        ),
        axis=1,
        dtype=jnp.int32,
    )
    section = jnp.where(within >= half_len, 2 * cycle_size - 1 - first_section, first_section)
    places = section * half_len + within % half_len
    seq_ends = jnp.cumsum(length_row, dtype=jnp.int32)
    passed = places[:, None] >= seq_ends[None, :]
    segment = jnp.sum(passed.astype(jnp.int32), axis=1, dtype=jnp.int32)
    offset = places - jnp.sum(jnp.where(passed, length_row[None, :], 0), axis=1, dtype=jnp.int32)
    return (places, segment, offset)


def rotary_embedding(values, positions):
    half_len = values.shape[-1] // 2
    frequency = jnp.exp(
        -math.log(500000.0) * jnp.arange(half_len, dtype=jnp.float32) * 2.0 / values.shape[-1]
    )
    angles = positions.astype(jnp.float32)[:, None] * frequency[None, :]
    cosine = jnp.cos(angles)[:, None, :]
    sine = jnp.sin(angles)[:, None, :]
    lower_half = values[..., :half_len]
    upper_half = values[..., half_len:]
    return jnp.concatenate(
        [lower_half * cosine - upper_half * sine, upper_half * cosine + lower_half * sine], axis=-1
    )


def normalize(values, gain_vec):
    return values * lax.rsqrt(jnp.mean(values * values, axis=-1, keepdims=True) + 1e-05) * gain_vec


def swiglu(gate_val, up_val):
    return jax.nn.silu(gate_val) * up_val


def contract_last(left, right):
    return lax.dot_general(
        left, right, (((1,), (1,)), ((), ())), preferred_element_type=jnp.float32
    )


def contract_first(left, right):
    return lax.dot_general(
        left, right, (((0,), (0,)), ((), ())), preferred_element_type=jnp.float32
    )


def swap(array, axis, distance):
    size = lax.axis_size(axis)
    return lax.ppermute(array, axis, [(i, i ^ distance) for i in range(size)])


def line_sum(part, axis):
    size = lax.axis_size(axis)
    index = lax.axis_index(axis)
    middle = size // 2
    total = part
    for step in range(middle - 1):
        came = lax.ppermute(total, axis, [(step, step + 1), (size - 1 - step, size - 2 - step)])
        total = add_low(total, came)
    if size > 1:
        came = lax.ppermute(total, axis, [(middle - 1, middle), (middle, middle - 1)])
        total = add_low(total, came)
    for step in range(middle - 2, -1, -1):
        came = lax.ppermute(total, axis, [(step + 1, step), (size - 2 - step, size - 1 - step)])
        receives = (index == step) | (index == size - 1 - step)
        total = jnp.where(receives, came, total)
    return total


def add_low(left, right):
    return (left.astype(jnp.float32) + right.astype(jnp.float32)).astype(jnp.bfloat16)


def gather_tokens(own):
    blocks = []
    for k in range(lax.axis_size("fsdp")):
        block = swap(own, "fsdp", k) if k else own
        blocks += [block, swap(block, "tp", 1)]
    return jnp.concatenate(blocks, axis=0)


def scatter_tokens(partial):
    count = lax.axis_size("fsdp")
    blocks = partial.reshape(count, 2, -1, partial.shape[-1])
    mine = [add_low(blocks[k, 0], swap(blocks[k, 1], "tp", 1)) for k in range(count)]
    total = mine[0].astype(jnp.float32)
    for k in range(1, count):
        total = total + swap(mine[k], "fsdp", k).astype(jnp.float32)
    return total


def send_columns(weight, width):
    count = lax.axis_size("fsdp")
    index = lax.axis_index("fsdp")
    rows = weight.shape[0]
    whole = jnp.zeros((rows * count, width), weight.dtype)
    for k in range(count):
        piece = lax.dynamic_slice_in_dim(weight, (index ^ k) * width, width, 1)
        if k:
            piece = swap(piece, "fsdp", k)
        whole = lax.dynamic_update_slice_in_dim(whole, piece, (index ^ k) * rows, 0)
    return whole


def return_rows(grad, out, column_of):
    count = lax.axis_size("fsdp")
    index = lax.axis_index("fsdp")
    rows = grad.shape[0] // count
    pieces = []
    for k in range(count):
        piece = lax.dynamic_slice_in_dim(grad, (index ^ k) * rows, rows, 0)
        if k:
            piece = swap(piece, "fsdp", k)
        pieces.append(line_sum(piece, "ctx"))
    return pieces


def fill_columns(pieces, first, width):
    count = len(pieces)
    index = lax.axis_index("fsdp")
    out = jnp.zeros((pieces[0].shape[0], count * width), jnp.float32)
    for k in range(count):
        part = pieces[k][:, first : first + width].astype(jnp.float32)
        out = lax.dynamic_update_slice_in_dim(out, part, (index ^ k) * width, 1)
    return out


def sum_all(vector):
    count = lax.axis_size("fsdp")
    index = lax.axis_index("fsdp")
    width = vector.shape[0] // count
    both = vector + swap(vector, "tp", 1)
    total = lax.dynamic_slice_in_dim(both, index * width, width, 0)
    for k in range(1, count):
        total = total + swap(lax.dynamic_slice_in_dim(both, (index ^ k) * width, width, 0), "fsdp", k)
    distance = 1
    while distance < lax.axis_size("ctx"):
        total = total + swap(total, "ctx", distance)
        distance *= 2
    return total


def gather_gain(gain):
    count = lax.axis_size("fsdp")
    index = lax.axis_index("fsdp")
    width = gain.shape[0]
    whole = jnp.zeros((count * width,), gain.dtype)
    for k in range(count):
        piece = swap(gain, "fsdp", k) if k else gain
        whole = lax.dynamic_update_slice_in_dim(whole, piece, (index ^ k) * width, 0)
    return whole.astype(jnp.float32)


def split_heads(
    hidden_in,
    out_cotangent,
    norm1_gain,
    q_weight,
    key_projection_weight,
    value_projection_weight,
    o_weight,
    norm2_gain,
    gate_weight,
    up_weight,
    down_weight,
    seq_lengths,
    span_order,
):
    packs = lax.axis_size("fsdp")
    cycle = lax.axis_size("ctx")
    core = lax.axis_index("tp")
    here = lax.axis_index("ctx")
    rows = hidden_in.shape[0]
    half = rows // 2
    q_width = q_weight.shape[1] // packs
    k_width = key_projection_weight.shape[1] // packs
    ff_width = gate_weight.shape[1] // packs
    groups = q_width // k_width
    kv_heads = k_width // HEAD_SIZE
    score_scale = 1.0 / math.sqrt(HEAD_SIZE)

    own_in = lax.dynamic_slice_in_dim(hidden_in, core * half, half, 0)
    own_cot = lax.dynamic_slice_in_dim(out_cotangent, core * half, half, 0)
    all_in = gather_tokens(own_in)
    gain_one = gather_gain(norm1_gain)
    gain_two = gather_gain(norm2_gain)
    wqkv = send_columns_joined((q_weight, key_projection_weight, value_projection_weight))
    wo = send_columns(o_weight, q_width)
    wg = send_columns(gate_weight, ff_width)
    wu = send_columns(up_weight, ff_width)
    wd = send_columns(down_weight, ff_width)
    all_cot = gather_tokens(own_cot)

    order_len = span_order.shape[1]
    meta = jnp.concatenate([span_order[0], seq_lengths[0]])
    places, segments, offsets = [], [], []
    within = jnp.arange(half, dtype=jnp.int32)
    for k in range(packs):
        meta_k = swap(meta, "fsdp", k) if k else meta
        order_row = meta_k[:order_len]
        length_row = meta_k[order_len:]
        ends = jnp.cumsum(length_row, dtype=jnp.int32)
        for j in range(cycle):
            first = lax.dynamic_index_in_dim(order_row, here ^ j, 0, keepdims=False)
            for h in range(2):
                section = jnp.where((core ^ h) == 0, first, 2 * cycle - 1 - first)
                place = section * half + within
                passed = place[:, None] >= ends[None, :]
                places.append(place)
                segments.append(jnp.sum(passed.astype(jnp.int32), axis=1, dtype=jnp.int32))
                offsets.append(
                    place
                    - jnp.sum(jnp.where(passed, length_row[None, :], 0), axis=1, dtype=jnp.int32)
                )
    places = jnp.stack(places).reshape(packs, cycle * rows)
    segments = jnp.stack(segments).reshape(packs, cycle * rows)
    offsets = jnp.stack(offsets).reshape(packs, cycle * rows)[:, :rows].reshape(-1)
    visible = (
        (places[:, :rows, None] >= places[:, None, :])
        & (segments[:, :rows, None] == segments[:, None, :])
    )[:, None, None]

    tokens = packs * rows
    normed_low = normalize(all_in.astype(jnp.float32), gain_one).astype(jnp.bfloat16)
    qkv = jnp.dot(normed_low, wqkv, preferred_element_type=jnp.float32)
    rope = lambda lin: rotary_embedding(lin.reshape(tokens, -1, HEAD_SIZE), offsets)
    q_rot = (
        rope(qkv[:, :q_width])
        .astype(jnp.bfloat16)
        .reshape(packs, rows, kv_heads, groups, HEAD_SIZE)
    )
    k_rot = rope(qkv[:, q_width : q_width + k_width]).astype(jnp.bfloat16).reshape(tokens, k_width)
    v_low = qkv[:, q_width + k_width :].astype(jnp.bfloat16)
    kv_own = jnp.concatenate([k_rot, v_low], axis=1)
    kv_all = jnp.stack([swap(kv_own, "ctx", j) if j else kv_own for j in range(cycle)])
    kv_all = kv_all.reshape(cycle, packs, rows, 2, kv_heads, HEAD_SIZE)
    kv_all = jnp.transpose(kv_all, (3, 1, 0, 2, 4, 5)).reshape(
        2, packs, cycle * rows, kv_heads, HEAD_SIZE
    )
    k_all, v_all = kv_all[0], kv_all[1]
    scores = (
        jnp.einsum("pqkgd,pskd->pkgqs", q_rot, k_all, preferred_element_type=jnp.float32)
        * score_scale
    )
    scores = jnp.where(visible, scores, -1e30)
    row_max = jnp.max(scores, axis=-1, keepdims=True)
    weights = jnp.where(visible, jnp.exp(scores - row_max), 0.0)
    totals = jnp.sum(weights, axis=-1, keepdims=True)
    probs = weights / totals
    probs_low = probs.astype(jnp.bfloat16)
    mixed = jnp.einsum("pkgqs,pskd->pqkgd", probs_low, v_all, preferred_element_type=jnp.float32)
    attn_low = mixed.reshape(tokens, q_width).astype(jnp.bfloat16)
    branch = scatter_tokens(contract_last(attn_low, wo).astype(jnp.bfloat16))
    middle = own_in.astype(jnp.float32) + branch

    normed_two = normalize(middle, gain_two)
    normed_two_low = gather_tokens(normed_two.astype(jnp.bfloat16))
    gate_val = jnp.dot(normed_two_low, wg, preferred_element_type=jnp.float32)
    up_val = jnp.dot(normed_two_low, wu, preferred_element_type=jnp.float32)
    hidden = swiglu(gate_val, up_val).astype(jnp.bfloat16)
    down_pieces = return_rows(contract_first(all_cot, hidden).astype(jnp.bfloat16), None, None)
    d_hidden = jnp.dot(all_cot, wd, preferred_element_type=jnp.float32)
    _, swiglu_back = jax.vjp(swiglu, gate_val, up_val)
    d_gate, d_up = swiglu_back(d_hidden)
    d_gate_low = d_gate.astype(jnp.bfloat16)
    d_up_low = d_up.astype(jnp.bfloat16)
    gate_pieces = return_rows(
        contract_first(normed_two_low, d_gate_low).astype(jnp.bfloat16), None, None
    )
    up_pieces = return_rows(
        contract_first(normed_two_low, d_up_low).astype(jnp.bfloat16), None, None
    )
    ffn_out = scatter_tokens(contract_last(hidden, wd).astype(jnp.bfloat16))
    result = (middle + ffn_out).astype(jnp.bfloat16)
    d_normed_two = scatter_tokens(
        (contract_last(d_gate_low, wg) + contract_last(d_up_low, wu)).astype(jnp.bfloat16)
    )
    _, norm_two_back = jax.vjp(normalize, middle, gain_two)
    d_middle_norm, d_gain_two = norm_two_back(d_normed_two)
    d_middle = own_cot.astype(jnp.float32) + d_middle_norm

    d_branch = gather_tokens(d_middle.astype(jnp.bfloat16))
    d_wo = contract_first(d_branch, attn_low).astype(jnp.bfloat16)
    d_attn = (
        jnp.dot(d_branch, wo, preferred_element_type=jnp.float32)
        .astype(jnp.bfloat16)
        .reshape(packs, rows, kv_heads, groups, HEAD_SIZE)
    )
    row_delta = jnp.einsum("pqkgd,pqkgd->pkgq", d_attn.astype(jnp.float32), mixed)
    d_values = jnp.einsum("pkgqs,pqkgd->pskd", probs_low, d_attn, preferred_element_type=jnp.float32)
    d_probs = jnp.einsum("pqkgd,pskd->pkgqs", d_attn, v_all, preferred_element_type=jnp.float32)
    d_scores = (probs * (d_probs - row_delta[..., None])).astype(jnp.bfloat16)
    d_q_rot = (
        jnp.einsum("pkgqs,pskd->pqkgd", d_scores, k_all, preferred_element_type=jnp.float32)
        * score_scale
    )
    d_keys = (
        jnp.einsum("pkgqs,pqkgd->pskd", d_scores, q_rot, preferred_element_type=jnp.float32)
        * score_scale
    )
    d_kv = jnp.stack([d_keys, d_values]).astype(jnp.bfloat16)
    d_kv = d_kv.reshape(2, packs, cycle, rows, k_width)
    d_kv_own = d_kv[:, :, 0].astype(jnp.float32)
    for j in range(1, cycle):
        d_kv_own = d_kv_own + swap(d_kv[:, :, j], "ctx", j).astype(jnp.float32)
    d_k_rot = d_kv_own[0].reshape(tokens, kv_heads, HEAD_SIZE)
    d_v_low = d_kv_own[1].reshape(tokens, k_width).astype(jnp.bfloat16)
    turn = lambda grad: rotary_embedding(grad, -offsets)
    d_q_low = turn(d_q_rot.reshape(tokens, -1, HEAD_SIZE)).reshape(tokens, q_width)
    d_k_low = turn(d_k_rot).reshape(tokens, k_width)
    d_qkv = jnp.concatenate(
        [d_q_low.astype(jnp.bfloat16), d_k_low.astype(jnp.bfloat16), d_v_low], axis=1
    )
    d_wqkv = contract_first(normed_low, d_qkv).astype(jnp.bfloat16)
    qkvo_pieces = return_rows(jnp.concatenate([d_wo, d_wqkv], axis=1), None, None)
    d_normed_one = scatter_tokens(contract_last(d_qkv, wqkv).astype(jnp.bfloat16))
    _, norm_one_back = jax.vjp(normalize, own_in.astype(jnp.float32), gain_one)
    d_inputs_norm, d_gain_one = norm_one_back(d_normed_one)
    in_grad = (d_middle + d_inputs_norm).astype(jnp.bfloat16)

    return (
        both_halves(result),
        both_halves(in_grad),
        sum_all(d_gain_one),
        fill_columns(qkvo_pieces, q_width, q_width),
        fill_columns(qkvo_pieces, 2 * q_width, k_width),
        fill_columns(qkvo_pieces, 2 * q_width + k_width, k_width),
        fill_columns(qkvo_pieces, 0, q_width),
        sum_all(d_gain_two),
        fill_columns(gate_pieces, 0, ff_width),
        fill_columns(up_pieces, 0, ff_width),
        fill_columns(down_pieces, 0, ff_width),
    )


def both_halves(own):
    core = lax.axis_index("tp")
    other = swap(own, "tp", 1)
    first = jnp.where(core == 0, own, other)
    second = jnp.where(core == 0, other, own)
    return jnp.concatenate([first, second], axis=0)


def send_columns_joined(weights):
    count = lax.axis_size("fsdp")
    index = lax.axis_index("fsdp")
    rows = weights[0].shape[0]
    widths = [weight.shape[1] // count for weight in weights]
    whole = jnp.zeros((rows * count, sum(widths)), weights[0].dtype)
    for k in range(count):
        piece = jnp.concatenate(
            [
                lax.dynamic_slice_in_dim(weight, (index ^ k) * width, width, 1)
                for weight, width in zip(weights, widths)
            ],
            axis=1,
        )
        if k:
            piece = swap(piece, "fsdp", k)
        whole = lax.dynamic_update_slice_in_dim(whole, piece, (index ^ k) * rows, 0)
    return whole


def gathered_weights(
    hidden_in,
    out_cotangent,
    norm1_gain,
    q_weight,
    key_projection_weight,
    value_projection_weight,
    o_weight,
    norm2_gain,
    gate_weight,
    up_weight,
    down_weight,
    seq_lengths,
    span_order,
):
    rows_here = hidden_in.shape[0]
    order_row = span_order[0]
    length_row = seq_lengths[0]
    kv_heads = key_projection_weight.shape[1] // HEAD_SIZE
    query_groups = QUERY_HEADS // KEY_VALUE_HEADS
    score_scale = 1.0 / math.sqrt(HEAD_SIZE)
    whole_rows = rows_here * lax.axis_size("ctx")
    local_rows = lax.axis_index("ctx") * rows_here + jnp.arange(rows_here, dtype=jnp.int32)
    q_place, q_segment, q_offset = stream_place(local_rows, order_row, length_row, rows_here)
    inputs = hidden_in.astype(jnp.float32)
    gain_one, wq_full, wk_full, wv_full, wo_full = (
        lax.all_gather(norm1_gain, "fsdp", axis=0, tiled=True),
        lax.all_gather(q_weight, "fsdp", axis=0, tiled=True),
        lax.all_gather(key_projection_weight, "fsdp", axis=0, tiled=True),
        lax.all_gather(value_projection_weight, "fsdp", axis=0, tiled=True),
        lax.all_gather(o_weight, "fsdp", axis=0, tiled=True),
    )
    gain_one = gain_one.astype(jnp.float32)
    first_normalized = normalize(inputs, gain_one)
    normed_low = first_normalized.astype(jnp.bfloat16)
    q_linear = jnp.dot(normed_low, wq_full, preferred_element_type=jnp.float32).reshape(
        rows_here, kv_heads * query_groups, HEAD_SIZE
    )
    k_linear = jnp.dot(normed_low, wk_full, preferred_element_type=jnp.float32).reshape(
        rows_here, kv_heads, HEAD_SIZE
    )
    q_rotated = (
        rotary_embedding(q_linear, q_offset)
        .astype(jnp.bfloat16)
        .reshape(rows_here, kv_heads, query_groups, HEAD_SIZE)
    )
    k_rotated = (
        rotary_embedding(k_linear, q_offset)
        .astype(jnp.bfloat16)
        .reshape(rows_here, kv_heads * HEAD_SIZE)
    )
    v_low = jnp.dot(normed_low, wv_full, preferred_element_type=jnp.float32).astype(jnp.bfloat16)

    def key_blocks(shard_rows):
        row_count = shard_rows.shape[0]
        key_total_width = math.gcd(row_count, 512)
        number = row_count // key_total_width
        k_place, k_segment, _ = stream_place(
            jnp.arange(row_count, dtype=jnp.int32), order_row, length_row, rows_here
        )
        return (
            key_total_width,
            number,
            k_place.reshape(number, key_total_width),
            k_segment.reshape(number, key_total_width),
        )

    def scores_of(key_block, place_block, segment_block):
        scores = (
            jnp.einsum("qkgd,skd->kgqs", q_rotated, key_block, preferred_element_type=jnp.float32)
            * score_scale
        )
        visible = (
            (q_place[:, None] >= place_block[None, :])
            & (q_segment[:, None] == segment_block[None, :])
        )[None, None]
        return (jnp.where(visible, scores, -1e30), visible)

    start_state = (
        jnp.full((kv_heads, query_groups, rows_here), -1e30, jnp.float32),
        jnp.zeros((kv_heads, query_groups, rows_here), jnp.float32),
        jnp.zeros((kv_heads, query_groups, rows_here, HEAD_SIZE), jnp.float32),
    )
    folded = start_state
    key_row_block = lax.all_gather(k_rotated, "ctx", axis=0, tiled=True)
    value_row_block = lax.all_gather(v_low, "ctx", axis=0, tiled=True)
    key_total_width, number, k_place, k_segment = key_blocks(key_row_block)

    def one_step(carried, pieces):
        running_max, totals, accumulated = carried
        key_block, value_block, place_block, segment_block = pieces
        scores, visible = scores_of(key_block, place_block, segment_block)
        new_max = jnp.maximum(running_max, jnp.max(scores, axis=-1))
        weights = jnp.where(visible, jnp.exp(scores - new_max[..., None]), 0.0)
        factor = jnp.exp(running_max - new_max)
        totals = totals * factor + jnp.sum(weights, axis=-1)
        accumulated = accumulated * factor[..., None] + jnp.einsum(
            "kgqs,skd->kgqd",
            weights.astype(jnp.bfloat16),
            value_block,
            preferred_element_type=jnp.float32,
        )
        return ((new_max, totals, accumulated), None)

    pieces = (
        key_row_block.reshape(number, key_total_width, kv_heads, HEAD_SIZE),
        value_row_block.reshape(number, key_total_width, kv_heads, HEAD_SIZE),
        k_place,
        k_segment,
    )
    folded, _ = lax.scan(one_step, folded, pieces)
    running_max, totals, accumulated = folded
    mixed_out = jnp.transpose(accumulated / totals[..., None], (2, 0, 1, 3))
    log_sum = running_max + jnp.log(totals)
    attn_low = mixed_out.reshape(rows_here, kv_heads * query_groups * HEAD_SIZE).astype(
        jnp.bfloat16
    )
    branch = lax.psum(contract_last(attn_low, wo_full).astype(jnp.bfloat16), "tp").astype(
        jnp.float32
    )
    middle = inputs + branch
    gain_two, wg_full, wu_full, wd_full = (
        lax.all_gather(norm2_gain, "fsdp", axis=0, tiled=True),
        lax.all_gather(gate_weight, "fsdp", axis=0, tiled=True),
        lax.all_gather(up_weight, "fsdp", axis=0, tiled=True),
        lax.all_gather(down_weight, "fsdp", axis=0, tiled=True),
    )
    gain_two = gain_two.astype(jnp.float32)
    normed_two = normalize(middle, gain_two)
    normed_two_low = normed_two.astype(jnp.bfloat16)
    gate_val = jnp.dot(normed_two_low, wg_full, preferred_element_type=jnp.float32)
    up_val = jnp.dot(normed_two_low, wu_full, preferred_element_type=jnp.float32)
    hidden = swiglu(gate_val, up_val).astype(jnp.bfloat16)
    ffn_out = lax.psum(contract_last(hidden, wd_full).astype(jnp.bfloat16), "tp").astype(
        jnp.float32
    )
    result = (middle + ffn_out).astype(jnp.bfloat16)
    grad_out = out_cotangent.astype(jnp.float32)
    d_wd = contract_first(out_cotangent, hidden)
    d_hidden = jnp.dot(out_cotangent, wd_full, preferred_element_type=jnp.float32)
    _, swiglu_back = jax.vjp(swiglu, gate_val, up_val)
    d_gate, d_up = swiglu_back(d_hidden)
    d_gate_low = d_gate.astype(jnp.bfloat16)
    d_up_low = d_up.astype(jnp.bfloat16)
    d_wg = contract_first(normed_two_low, d_gate_low)
    d_wu = contract_first(normed_two_low, d_up_low)
    d_normed_two = lax.psum(
        (contract_last(d_gate_low, wg_full) + contract_last(d_up_low, wu_full)).astype(
            jnp.bfloat16
        ),
        "tp",
    ).astype(jnp.float32)
    _, norm_two_back = jax.vjp(normalize, middle, gain_two)
    d_middle_norm, d_gain_two = norm_two_back(d_normed_two)
    d_middle = grad_out + d_middle_norm
    d_branch_low = d_middle.astype(jnp.bfloat16)
    d_wo = contract_first(d_branch_low, attn_low)
    d_attn = jnp.dot(d_branch_low, wo_full, preferred_element_type=jnp.float32).astype(jnp.bfloat16)
    d_attn_heads = d_attn.reshape(rows_here, kv_heads, query_groups, HEAD_SIZE)
    row_delta = jnp.einsum("qkgd,qkgd->kgq", d_attn_heads.astype(jnp.float32), mixed_out)
    back_state = (
        jnp.zeros((rows_here, kv_heads, query_groups, HEAD_SIZE), jnp.float32),
        jnp.zeros((whole_rows, kv_heads, HEAD_SIZE), jnp.float32),
        jnp.zeros((whole_rows, kv_heads, HEAD_SIZE), jnp.float32),
    )
    folded = back_state
    key_row_block = lax.all_gather(k_rotated, "ctx", axis=0, tiled=True)
    value_row_block = lax.all_gather(v_low, "ctx", axis=0, tiled=True)
    key_total_width, number, k_place, k_segment = key_blocks(key_row_block)

    def one_step(carried, pieces):
        d_query, d_keys, d_values = carried
        key_block, value_block, place_block, segment_block, step_index = pieces
        scores, visible = scores_of(key_block, place_block, segment_block)
        prob_rows = jnp.where(visible, jnp.exp(scores - log_sum[..., None]), 0.0)
        d_values_block = jnp.einsum(
            "kgqs,qkgd->skd",
            prob_rows.astype(jnp.bfloat16),
            d_attn_heads,
            preferred_element_type=jnp.float32,
        )
        d_probs = jnp.einsum(
            "qkgd,skd->kgqs", d_attn_heads, value_block, preferred_element_type=jnp.float32
        )
        d_scores = (prob_rows * (d_probs - row_delta[..., None])).astype(jnp.bfloat16)
        d_query = (
            d_query
            + jnp.einsum("kgqs,skd->qkgd", d_scores, key_block, preferred_element_type=jnp.float32)
            * score_scale
        )
        d_keys_block = (
            jnp.einsum("kgqs,qkgd->skd", d_scores, q_rotated, preferred_element_type=jnp.float32)
            * score_scale
        )
        row_first = step_index * key_total_width
        d_keys = lax.dynamic_update_slice_in_dim(
            d_keys,
            lax.dynamic_slice_in_dim(d_keys, row_first, key_total_width, 0) + d_keys_block,
            row_first,
            0,
        )
        d_values = lax.dynamic_update_slice_in_dim(
            d_values,
            lax.dynamic_slice_in_dim(d_values, row_first, key_total_width, 0) + d_values_block,
            row_first,
            0,
        )
        return ((d_query, d_keys, d_values), None)

    pieces = (
        key_row_block.reshape(number, key_total_width, kv_heads, HEAD_SIZE),
        value_row_block.reshape(number, key_total_width, kv_heads, HEAD_SIZE),
        k_place,
        k_segment,
        jnp.arange(number, dtype=jnp.int32),
    )
    folded, _ = lax.scan(one_step, folded, pieces)
    d_query, d_keys_all, d_values_all = folded
    d_key_own, d_value_own = (
        lax.psum_scatter(
            d_keys_all.astype(jnp.bfloat16), "ctx", scatter_dimension=0, tiled=True
        ).astype(jnp.float32),
        lax.psum_scatter(
            d_values_all.astype(jnp.bfloat16), "ctx", scatter_dimension=0, tiled=True
        ).astype(jnp.float32),
    )
    _, rope_q_back = jax.vjp(lambda rotated_in: rotary_embedding(rotated_in, q_offset), q_linear)
    _, rope_k_back = jax.vjp(lambda rotated_in: rotary_embedding(rotated_in, q_offset), k_linear)
    (d_q_linear,) = rope_q_back(d_query.reshape(rows_here, kv_heads * query_groups, HEAD_SIZE))
    (d_k_linear,) = rope_k_back(d_key_own)
    d_q_low = d_q_linear.reshape(rows_here, kv_heads * query_groups * HEAD_SIZE).astype(
        jnp.bfloat16
    )
    d_k_low = d_k_linear.reshape(rows_here, kv_heads * HEAD_SIZE).astype(jnp.bfloat16)
    d_v_low = d_value_own.reshape(rows_here, kv_heads * HEAD_SIZE).astype(jnp.bfloat16)
    d_wq = contract_first(normed_low, d_q_low)
    d_wk = contract_first(normed_low, d_k_low)
    d_wv = contract_first(normed_low, d_v_low)
    d_normed_one = lax.psum(
        (
            contract_last(d_q_low, wq_full)
            + contract_last(d_k_low, wk_full)
            + contract_last(d_v_low, wv_full)
        ).astype(jnp.bfloat16),
        "tp",
    ).astype(jnp.float32)
    _, norm_one_back = jax.vjp(normalize, inputs, gain_one)
    d_inputs_norm, d_gain_one = norm_one_back(d_normed_one)
    in_grad = (d_middle + d_inputs_norm).astype(jnp.bfloat16)
    weight_grads = (d_gain_one, d_wq, d_wk, d_wv, d_wo, d_gain_two, d_wg, d_wu, d_wd)
    shares = (
        lax.psum_scatter(weight_grads[0], ("fsdp", "ctx"), scatter_dimension=0, tiled=True),
        lax.psum_scatter(weight_grads[1], ("fsdp", "ctx"), scatter_dimension=0, tiled=True),
        lax.psum_scatter(weight_grads[2], ("fsdp", "ctx"), scatter_dimension=0, tiled=True),
        lax.psum_scatter(weight_grads[3], ("fsdp", "ctx"), scatter_dimension=0, tiled=True),
        lax.psum_scatter(weight_grads[4], ("fsdp", "ctx"), scatter_dimension=0, tiled=True),
        lax.psum_scatter(weight_grads[5], ("fsdp", "ctx"), scatter_dimension=0, tiled=True),
        lax.psum_scatter(weight_grads[6], ("fsdp", "ctx"), scatter_dimension=0, tiled=True),
        lax.psum_scatter(weight_grads[7], ("fsdp", "ctx"), scatter_dimension=0, tiled=True),
        lax.psum_scatter(weight_grads[8], ("fsdp", "ctx"), scatter_dimension=0, tiled=True),
    )
    owned_grads = (
        lax.all_gather(shares[0].astype(jnp.bfloat16), "ctx", axis=0, tiled=True).astype(
            jnp.float32
        ),
        lax.all_gather(shares[1].astype(jnp.bfloat16), "ctx", axis=0, tiled=True).astype(
            jnp.float32
        ),
        lax.all_gather(shares[2].astype(jnp.bfloat16), "ctx", axis=0, tiled=True).astype(
            jnp.float32
        ),
        lax.all_gather(shares[3].astype(jnp.bfloat16), "ctx", axis=0, tiled=True).astype(
            jnp.float32
        ),
        lax.all_gather(shares[4].astype(jnp.bfloat16), "ctx", axis=0, tiled=True).astype(
            jnp.float32
        ),
        lax.all_gather(shares[5].astype(jnp.bfloat16), "ctx", axis=0, tiled=True).astype(
            jnp.float32
        ),
        lax.all_gather(shares[6].astype(jnp.bfloat16), "ctx", axis=0, tiled=True).astype(
            jnp.float32
        ),
        lax.all_gather(shares[7].astype(jnp.bfloat16), "ctx", axis=0, tiled=True).astype(
            jnp.float32
        ),
        lax.all_gather(shares[8].astype(jnp.bfloat16), "ctx", axis=0, tiled=True).astype(
            jnp.float32
        ),
    )
    return (
        result,
        in_grad,
        owned_grads[0],
        owned_grads[1],
        owned_grads[2],
        owned_grads[3],
        owned_grads[4],
        owned_grads[5],
        owned_grads[6],
        owned_grads[7],
        owned_grads[8],
    )


def solution(mesh):
    placed = (
        P(("fsdp", "ctx"), None),
        P(("fsdp", "ctx"), None),
        P("fsdp"),
        P("fsdp", "tp"),
        P("fsdp", "tp"),
        P("fsdp", "tp"),
        P("fsdp", "tp"),
        P("fsdp"),
        P("fsdp", "tp"),
        P("fsdp", "tp"),
        P("fsdp", "tp"),
        P("fsdp", None),
        P("fsdp", None),
    )
    plane = mesh.shape["fsdp"] * mesh.shape["tp"]
    splits = mesh.shape["tp"] == 2 and KEY_VALUE_HEADS % plane == 0
    return jax.shard_map(
        split_heads if splits else gathered_weights,
        mesh=mesh,
        in_specs=placed,
        out_specs=(
            P(("fsdp", "ctx"), None),
            P(("fsdp", "ctx"), None),
            P("fsdp"),
            P("fsdp", "tp"),
            P("fsdp", "tp"),
            P("fsdp", "tp"),
            P("fsdp", "tp"),
            P("fsdp"),
            P("fsdp", "tp"),
            P("fsdp", "tp"),
            P("fsdp", "tp"),
        ),
        check_vma=False,
    )
```

```python
import functools
import math

import jax
import jax.numpy as jnp
from jax import lax
from jax.experimental import pallas as pl
from jax.experimental.pallas import tpu as pltpu
from jax.sharding import PartitionSpec as P

QUERY_HEADS = 32
KEY_VALUE_HEADS = 8
HEAD_SIZE = 64


def stream_place(row_ids, order_row, length_row, tok_dev):
    cycle_size = order_row.shape[0]
    half_len = tok_dev // 2
    cycle_rank = row_ids // tok_dev
    within = row_ids % tok_dev
    first_section = jnp.sum(
        jnp.where(
            cycle_rank[:, None] == jnp.arange(cycle_size, dtype=jnp.int32)[None, :],
            order_row[None, :],
            0,
        ),
        axis=1,
        dtype=jnp.int32,
    )
    section = jnp.where(within >= half_len, 2 * cycle_size - 1 - first_section, first_section)
    places = section * half_len + within % half_len
    seq_ends = jnp.cumsum(length_row, dtype=jnp.int32)
    passed = places[:, None] >= seq_ends[None, :]
    segment = jnp.sum(passed.astype(jnp.int32), axis=1, dtype=jnp.int32)
    offset = places - jnp.sum(jnp.where(passed, length_row[None, :], 0), axis=1, dtype=jnp.int32)
    return (places, segment, offset)


def rotary_embedding(values, positions):
    half_len = values.shape[-1] // 2
    frequency = jnp.exp(
        -math.log(500000.0) * jnp.arange(half_len, dtype=jnp.float32) * 2.0 / values.shape[-1]
    )
    angles = positions.astype(jnp.float32)[:, None] * frequency[None, :]
    cosine = jnp.cos(angles)[:, None, :]
    sine = jnp.sin(angles)[:, None, :]
    lower_half = values[..., :half_len]
    upper_half = values[..., half_len:]
    return jnp.concatenate(
        [lower_half * cosine - upper_half * sine, upper_half * cosine + lower_half * sine], axis=-1
    )


def normalize(values, gain_vec):
    return values * lax.rsqrt(jnp.mean(values * values, axis=-1, keepdims=True) + 1e-05) * gain_vec


def swiglu(gate_val, up_val):
    return jax.nn.silu(gate_val) * up_val


def contract_last(left, right):
    return lax.dot_general(
        left, right, (((1,), (1,)), ((), ())), preferred_element_type=jnp.float32
    )


def contract_first(left, right):
    return lax.dot_general(
        left, right, (((0,), (0,)), ((), ())), preferred_element_type=jnp.float32
    )


VMEM_LIMIT = 48 * 1024 * 1024


def pairs_by(distance, size):
    return [(i, i ^ distance) for i in range(size)]


def swap(array, axis, distance):
    return lax.ppermute(array, axis, pairs_by(distance, lax.axis_size(axis)))


def add_low(left, right):
    return (left.astype(jnp.float32) + right.astype(jnp.float32)).astype(jnp.bfloat16)


def reorder(array, index, count):
    width = array.shape[-1] // count
    return jnp.concatenate(
        [
            lax.dynamic_slice_in_dim(array, (index ^ block) * width, width, array.ndim - 1)
            for block in range(count)
        ],
        axis=-1,
    )


def as_seen(array, distance, count):
    width = array.shape[-1] // count
    return jnp.concatenate(
        [
            array[..., (block ^ distance) * width : ((block ^ distance) + 1) * width]
            for block in range(count)
        ],
        axis=-1,
    )


class Line:
    def __init__(self, axis):
        size = lax.axis_size(axis)
        index = lax.axis_index(axis)
        middle = size // 2
        self.axis = axis
        self.size = size
        self.hops = middle
        self.outer = [(index == h) | (index == size - 1 - h) for h in range(middle)]
        self.moving = []
        self.sums = {}

    def pairs(self, hop):
        size = self.size
        if hop == self.hops - 1:
            return [(hop, hop + 1), (hop + 1, hop)]
        return [
            (hop, hop + 1),
            (hop + 1, hop),
            (size - 1 - hop, size - 2 - hop),
            (size - 2 - hop, size - 1 - hop),
        ]

    def advance(self, got, entering):
        last = self.hops - 1
        still = []
        for name, value, stage in self.moving:
            hop = stage if stage <= last else 2 * last - stage
            came = got["line", hop][:, : value.shape[1]]
            if stage <= last:
                value = add_low(value, came)
            else:
                value = jnp.where(self.outer[hop], came, value)
            if stage == 2 * last:
                self.sums[name] = value
            else:
                still.append((name, value, stage + 1))
        if entering is not None:
            if self.hops:
                still.append((entering[0], entering[1], 0))
            else:
                self.sums[entering[0]] = entering[1]
        self.moving = still
        moves = []
        for hop in range(self.hops):
            inward = [value for _, value, stage in still if stage == hop]
            outward = [value for _, value, stage in still if stage == 2 * last - hop and hop < last]
            if not inward and not outward:
                continue
            if inward and outward and inward[0].shape == outward[0].shape:
                value = jnp.where(self.outer[hop], inward[0], outward[0])
                moves.append((("line", hop), value, self.axis, self.pairs(hop)))
            elif inward and outward:
                wide = max(inward[0].shape[1], outward[0].shape[1])
                grown = [
                    jnp.pad(array, ((0, 0), (0, wide - array.shape[1])))
                    for array in (inward[0], outward[0])
                ]
                value = jnp.where(self.outer[hop], grown[0], grown[1])
                moves.append((("line", hop), value, self.axis, self.pairs(hop)))
            else:
                value = (inward or outward)[0]
                pairs = self.pairs(hop)
                if hop < last:
                    pairs = pairs[0::2] if inward else pairs[1::2]
                moves.append((("line", hop), value, self.axis, pairs))
        return moves


class Steps:
    def __init__(self, line):
        self.line = line
        self.got = {}
        self.names = []
        self.flying = []

    def step(self, moves=(), summed=None, late=None):
        moves = list(moves)
        fresh = [summed[1]] if summed is not None and summed[1] is not None else []
        if not self.flying and not moves and not fresh:
            return
        held = lax.optimization_barrier(
            tuple(self.flying) + tuple(move[1] for move in moves) + tuple(fresh)
        )
        count = len(self.flying)
        for name, value in zip(self.names, held[:count]):
            self.got[name] = value
        moves = [
            (name, value, axis, pairs)
            for (name, _, axis, pairs), value in zip(moves, held[count:])
        ]
        entering = summed
        if summed is not None:
            entering = (summed[0], held[-1] if fresh else self.take(summed[0]))
        moves = self.line.advance(self.got, entering) + moves
        moves += late() if late is not None else []
        self.names = [move[0] for move in moves]
        self.flying = [lax.ppermute(value, axis, pairs) for _, value, axis, pairs in moves]

    def take(self, name):
        return self.got.pop(name)


def turned(lin, cosine, sine):
    width = lin.shape[-1]
    quarter = HEAD_SIZE // 2
    lane = lax.broadcasted_iota(jnp.int32, lin.shape, lin.ndim - 1)
    low = lax.rem(lane, HEAD_SIZE) < quarter
    partner = jnp.where(
        low, -pltpu.roll(lin, width - quarter, lin.ndim - 1), pltpu.roll(lin, quarter, lin.ndim - 1)
    )
    return lin * cosine + partner * sine


def side_by_side(table, width):
    return jnp.concatenate([table] * (width // table.shape[-1]), axis=-1)


def of_keys(cosine, sine):
    keys = lax.broadcasted_iota(jnp.int32, cosine.shape, 1) < HEAD_SIZE
    return jnp.where(keys, cosine, 1.0), jnp.where(keys, sine, 0.0)


def qkv_kernel(x_ref, gain_ref, w_ref, cos_ref, sin_ref, normed_ref, q_ref, kv_ref):
    x = x_ref[...].astype(jnp.float32)
    mean = jnp.mean(x * x, axis=-1, keepdims=True)
    normed = (x * lax.rsqrt(mean + 1e-05) * gain_ref[...]).astype(jnp.bfloat16)
    normed_ref[...] = normed
    lin = jnp.dot(normed, w_ref[...], preferred_element_type=jnp.float32)
    cosine, sine = cos_ref[...], sin_ref[...]
    q_width = q_ref.shape[-1]
    q = turned(lin[:, :q_width], side_by_side(cosine, q_width), side_by_side(sine, q_width))
    q_ref[...] = q.astype(jnp.bfloat16)
    kv = turned(lin[:, q_width:], *of_keys(cosine, sine))
    kv_ref[...] = kv.astype(jnp.bfloat16)


def project_qkv(x, gain, weight, cosine, sine, q_width):
    tokens, depth = x.shape
    kv_width = weight.shape[1] - q_width
    block = math.gcd(tokens, 256)

    def by_rows(width):
        return pl.BlockSpec((block, width), lambda i: (i, 0))

    def whole(shape):
        return pl.BlockSpec(shape, lambda i: (0, 0))

    return pl.pallas_call(
        qkv_kernel,
        grid=(tokens // block,),
        in_specs=[
            by_rows(depth),
            whole((1, depth)),
            whole(weight.shape),
            by_rows(cosine.shape[1]),
            by_rows(cosine.shape[1]),
        ],
        out_specs=[by_rows(depth), by_rows(q_width), by_rows(kv_width)],
        out_shape=[
            jax.ShapeDtypeStruct((tokens, depth), jnp.bfloat16),
            jax.ShapeDtypeStruct((tokens, q_width), jnp.bfloat16),
            jax.ShapeDtypeStruct((tokens, kv_width), jnp.bfloat16),
        ],
        compiler_params=pltpu.CompilerParams(vmem_limit_bytes=VMEM_LIMIT),
        cost_estimate=pl.CostEstimate(
            flops=2 * tokens * depth * weight.shape[1],
            bytes_accessed=4 * tokens * depth + 2 * weight.size,
            transcendentals=0,
        ),
        name="qkv",
    )(x, gain, weight, cosine, sine)


def shares(q, k, visible):
    scores = lax.dot_general(
        q, k, (((1,), (1,)), ((), ())), preferred_element_type=jnp.float32
    ) * (1.0 / math.sqrt(HEAD_SIZE))
    scores = jnp.where(visible, scores, -1e30)
    weights = jnp.exp(scores - jnp.max(scores, axis=-1, keepdims=True))
    weights = jnp.where(visible, weights, 0.0)
    return weights, jnp.sum(weights, axis=-1, keepdims=True)


def load_attention(q_ref, place_ref, start_ref, key_place_ref, kv_refs):
    q = q_ref[...]
    q = q.reshape(q.shape[0] * q.shape[2], q.shape[3])
    kv = jnp.concatenate(
        [ref[...].reshape(q.shape[0], 2 * HEAD_SIZE) for ref in kv_refs], axis=0
    )
    key_place = key_place_ref[0]
    visible = (key_place <= place_ref[0]) & (key_place >= start_ref[0])
    return q, kv[:, :HEAD_SIZE], kv[:, HEAD_SIZE:], visible


def attend_kernel(groups, q_ref, place_ref, start_ref, key_place_ref, *refs):
    kv_refs, out_ref = refs[:-1], refs[-1]
    q, k, v, visible = load_attention(q_ref, place_ref, start_ref, key_place_ref, kv_refs)
    mixed = []
    for g in range(groups):
        weights, totals = shares(q[:, g * HEAD_SIZE : (g + 1) * HEAD_SIZE], k, visible)
        probs = (weights / totals).astype(jnp.bfloat16)
        mixed.append(jnp.dot(probs, v, preferred_element_type=jnp.float32))
    out = jnp.concatenate(mixed, axis=1).astype(jnp.bfloat16)
    out_ref[...] = out.reshape(out_ref.shape)


def attend_back_kernel(
    groups, q_ref, d_ref, cos_ref, sin_ref, place_ref, start_ref, key_place_ref, *refs
):
    kv_refs, (dq_ref, dkv_ref) = refs[:-2], refs[-2:]
    q, k, v, visible = load_attention(q_ref, place_ref, start_ref, key_place_ref, kv_refs)
    d_out = d_ref[...].reshape(q.shape)
    scale = 1.0 / math.sqrt(HEAD_SIZE)
    d_q, d_k, d_v = [], 0.0, 0.0
    for g in range(groups):
        q_head = q[:, g * HEAD_SIZE : (g + 1) * HEAD_SIZE]
        d_head = d_out[:, g * HEAD_SIZE : (g + 1) * HEAD_SIZE]
        weights, totals = shares(q_head, k, visible)
        probs = weights / totals
        d_probs = lax.dot_general(
            d_head, v, (((1,), (1,)), ((), ())), preferred_element_type=jnp.float32
        )
        row_delta = jnp.sum(probs * d_probs, axis=-1, keepdims=True)
        d_scores = (probs * (d_probs - row_delta)).astype(jnp.bfloat16)
        d_q.append(jnp.dot(d_scores, k, preferred_element_type=jnp.float32) * scale)
        d_k = d_k + contract_first(d_scores, q_head) * scale
        d_v = d_v + contract_first(probs.astype(jnp.bfloat16), d_head)
    d_q = jnp.concatenate(d_q, axis=1)
    cosine = cos_ref[...].reshape(q.shape[0], -1)
    sine = sin_ref[...].reshape(q.shape[0], -1)
    d_q = turned(d_q, side_by_side(cosine, q.shape[1]), -side_by_side(sine, q.shape[1]))
    dq_ref[...] = d_q.astype(jnp.bfloat16).reshape(dq_ref.shape)
    d_kv = jnp.concatenate([d_k, d_v], axis=1).astype(jnp.bfloat16)
    dkv_ref[...] = d_kv.reshape(dkv_ref.shape)


def attention_specs(packs, rows, cycle):
    def of_pack(width):
        return pl.BlockSpec((2, 1, rows // 2, width), lambda p: (0, p, 0, 0))

    places = [
        pl.BlockSpec((1, rows, 1), lambda p: (p, 0, 0)),
        pl.BlockSpec((1, rows, 1), lambda p: (p, 0, 0)),
        pl.BlockSpec((1, 1, cycle * rows), lambda p: (p, 0, 0)),
    ]
    return of_pack, places


def attend(q, places, kvs, groups):
    _, packs, half, width = q.shape
    rows, cycle = 2 * half, len(kvs)
    of_pack, place_specs = attention_specs(packs, rows, cycle)
    work = packs * groups * rows * cycle * rows
    return pl.pallas_call(
        functools.partial(attend_kernel, groups),
        grid=(packs,),
        in_specs=[of_pack(width)] + place_specs + [of_pack(2 * HEAD_SIZE)] * cycle,
        out_specs=of_pack(width),
        out_shape=jax.ShapeDtypeStruct(q.shape, jnp.bfloat16),
        compiler_params=pltpu.CompilerParams(vmem_limit_bytes=VMEM_LIMIT),
        cost_estimate=pl.CostEstimate(
            flops=40 * 4 * work, bytes_accessed=4 * q.size * 3, transcendentals=work
        ),
        name="attend",
    )(q, *places, *kvs)


def attend_back(q, d_out, cosine, sine, places, kvs, groups):
    _, packs, half, width = q.shape
    rows, cycle = 2 * half, len(kvs)
    of_pack, place_specs = attention_specs(packs, rows, cycle)
    work = packs * groups * rows * cycle * rows
    kv_out = (cycle, 2, packs, half, 2 * HEAD_SIZE)
    return pl.pallas_call(
        functools.partial(attend_back_kernel, groups),
        grid=(packs,),
        in_specs=[of_pack(width)] * 2
        + [of_pack(cosine.shape[-1])] * 2
        + place_specs
        + [of_pack(2 * HEAD_SIZE)] * cycle,
        out_specs=[
            of_pack(width),
            pl.BlockSpec((cycle, 2, 1, half, 2 * HEAD_SIZE), lambda p: (0, 0, p, 0, 0)),
        ],
        out_shape=[
            jax.ShapeDtypeStruct(q.shape, jnp.bfloat16),
            jax.ShapeDtypeStruct(kv_out, jnp.bfloat16),
        ],
        compiler_params=pltpu.CompilerParams(vmem_limit_bytes=VMEM_LIMIT),
        cost_estimate=pl.CostEstimate(
            flops=40 * 10 * work, bytes_accessed=4 * q.size * 4, transcendentals=work
        ),
        name="attend_back",
    )(q, d_out, cosine, sine, *places, *kvs)


def split_heads(
    hidden_in,
    out_cotangent,
    norm1_gain,
    q_weight,
    key_projection_weight,
    value_projection_weight,
    o_weight,
    norm2_gain,
    gate_weight,
    up_weight,
    down_weight,
    seq_lengths,
    span_order,
):
    packs = lax.axis_size("fsdp")
    cycle = lax.axis_size("ctx")
    pack = lax.axis_index("fsdp")
    core = lax.axis_index("tp")
    here = lax.axis_index("ctx")
    rows = hidden_in.shape[0]
    half = rows // 2
    tokens = packs * rows
    depth = q_weight.shape[0]
    width = depth * packs
    q_width = q_weight.shape[1] // packs
    k_width = key_projection_weight.shape[1] // packs
    ff_width = gate_weight.shape[1] // packs
    ff_half = ff_width // 2
    groups = q_width // k_width
    far = range(1, packs)
    steps = Steps(Line("ctx"))
    kept = {}


    def columns(weight, k, count, first=0, of=None):
        return lax.dynamic_slice_in_dim(weight, (pack ^ k) * (of or count) + first, count, 1)

    def to_pack(name, k, array):
        return ((name, k), array, "fsdp", pairs_by(k, packs))

    def spread(name, array):
        return [to_pack(name, k, as_seen(array, k, packs)) for k in far]

    def gathered(own, others):
        mine = jnp.concatenate([own] + others, axis=0)
        return jnp.concatenate([mine, swap(mine, "tp", 1)], axis=0)

    def arrived(name):
        return [steps.take((name, k)) for k in far]

    def to_rows(name, partial):
        mine = add_low(partial[: tokens // 2], swap(partial[tokens // 2 :], "tp", 1))
        blocks = mine.reshape(packs, half, width)
        return blocks[0], [to_pack(name, k, as_seen(blocks[k], k, packs)) for k in far]

    def summed_rows(name, own):
        total = own.astype(jnp.float32)
        for k in far:
            total = total + steps.take((name, k)).astype(jnp.float32)
        return total

    own_in = reorder(lax.dynamic_slice_in_dim(hidden_in, core * half, half, 0), pack, packs)
    own_cot = reorder(lax.dynamic_slice_in_dim(out_cotangent, core * half, half, 0), pack, packs)

    meta = jnp.concatenate([span_order[0], seq_lengths[0]])
    order_len, meta_len = span_order.shape[1], meta.shape[0]
    info = jnp.concatenate(
        [norm1_gain, norm2_gain, (meta // 32).astype(jnp.bfloat16), (meta % 32).astype(jnp.bfloat16)]
    )
    info = jnp.pad(info, (0, width - info.shape[0]))[None]
    info_rows = jnp.pad(info, ((0, 15), (0, 0)))

    def attention_piece(k):
        return jnp.concatenate(
            [
                columns(q_weight, k, q_width),
                columns(key_projection_weight, k, k_width),
                columns(value_projection_weight, k, k_width),
                columns(o_weight, k, q_width),
            ],
            axis=1,
        )

    steps.step(
        [
            to_pack("in", k, jnp.concatenate([as_seen(own_in, k, packs), info_rows], axis=0))
            for k in far
        ]
    )
    steps.step([to_pack("attention", k, attention_piece(k)) for k in far])
    came = arrived("in")
    all_in = gathered(own_in, [block[:half] for block in came])
    infos = jnp.concatenate([info] + [block[half : half + 1] for block in came], axis=0)
    all_gains = infos[:, : 2 * depth].astype(jnp.float32)
    gain_one = all_gains[:, :depth].reshape(-1)
    gain_two = all_gains[:, depth:].reshape(-1)
    metas = infos[:, 2 * depth : 2 * depth + 2 * meta_len].astype(jnp.int32)
    metas = metas[:, :meta_len] * 32 + metas[:, meta_len:]
    orders, lengths = metas[:, :order_len], metas[:, order_len:]

    others = jnp.stack([here ^ j for j in range(cycle)])
    first = jnp.sum(
        jnp.where(
            others[None, :, None] == jnp.arange(order_len, dtype=jnp.int32)[None, None, :],
            orders[:, None, :],
            0,
        ),
        axis=2,
    )
    halves = jnp.stack([core, core ^ 1])[None, None, :]
    section = jnp.where(halves == 0, first[:, :, None], 2 * cycle - 1 - first[:, :, None])
    places = section[..., None] * half + jnp.arange(half, dtype=jnp.int32)
    places = places.reshape(packs, cycle * rows)
    starts = jnp.zeros_like(places)
    end = jnp.zeros((packs, 1), jnp.int32)
    for j in range(lengths.shape[1]):
        end = end + lengths[:, j : j + 1]
        starts = jnp.where(places >= end, end, starts)
    place_args = (places[:, :rows, None], starts[:, :rows, None], places[:, None, :])
    offsets = (places - starts)[:, :rows].reshape(packs, 2, half).transpose(1, 0, 2)
    frequency = jnp.exp(
        -math.log(500000.0)
        * (jnp.arange(2 * HEAD_SIZE) % (HEAD_SIZE // 2)).astype(jnp.float32)
        * 2.0
        / HEAD_SIZE
    )
    angles = offsets.astype(jnp.float32).reshape(tokens, 1) * frequency[None, :]
    cosine, sine = jnp.cos(angles), jnp.sin(angles)

    side = here & 1

    def fetch(name, weight):
        return [to_pack(name, k, columns(weight, k, ff_half, side * ff_half, ff_width)) for k in far]

    steps.step(fetch("gate", gate_weight))
    w_attention = jnp.concatenate([attention_piece(0)] + arrived("attention"), axis=0)
    wqkv, wo = w_attention[:, : q_width + 2 * k_width], w_attention[:, q_width + 2 * k_width :]
    normed_low, q_rot, kv_own = project_qkv(all_in, gain_one[None], wqkv, cosine, sine, q_width)

    by_pack = (2, packs, half, -1)
    steps.step(
        [(("kv", j), kv_own, "ctx", pairs_by(j, cycle)) for j in range(1, cycle)]
        + fetch("up", up_weight)
    )

    def pass_on(k):
        kept["both", k] = jnp.concatenate([steps.take(("gate", k)), steps.take(("up", k))], axis=1)
        return to_neighbour(k)

    def to_neighbour(k):
        return [(("neighbour", k), kept["both", k], "ctx", pairs_by(1, cycle))]

    def first_of_weights():
        moves = [pass_on(k) for k in far]
        return moves[0] if moves else []

    steps.step(spread("cot", own_cot), late=first_of_weights)
    kvs = [kv_own] + [steps.take(("kv", j)) for j in range(1, cycle)]
    kvs = [kv.reshape(by_pack) for kv in kvs]
    q_rot = q_rot.reshape(by_pack)
    attn_low = attend(q_rot, place_args, kvs, groups).reshape(tokens, q_width)
    branch_own, branch_moves = to_rows("branch", contract_last(attn_low, wo).astype(jnp.bfloat16))

    steps.step(branch_moves + to_neighbour(2))
    all_cot = gathered(own_cot, arrived("cot"))

    def middle_moves():
        kept["middle"] = own_in.astype(jnp.float32) + summed_rows("branch", branch_own)
        kept["normed"] = normalize(kept["middle"], gain_two).astype(jnp.bfloat16)
        return spread("two", kept["normed"])

    steps.step(to_neighbour(3), late=middle_moves)
    middle = kept["middle"]

    def wd_moves(ks):
        return [to_pack("down", k, columns(down_weight, k, ff_width)) for k in ks]

    steps.step(wd_moves([1, 2]))
    normed_two_low = gathered(kept["normed"], arrived("two"))

    def whole_columns(weight, first):
        out = jnp.zeros((width, ff_width), weight.dtype)
        fetched = [kept["both", k][:, first : first + ff_half] for k in far]
        passed = [kept["neighbour", k][:, first : first + ff_half] for k in far]
        out = lax.dynamic_update_slice(out, columns(weight, 0, ff_width), (0, 0))
        out = lax.dynamic_update_slice(
            out, jnp.concatenate(fetched, axis=0), (depth, side * ff_half)
        )
        return lax.dynamic_update_slice(
            out, jnp.concatenate(passed, axis=0), (depth, (1 - side) * ff_half)
        )

    for k in far:
        kept["neighbour", k] = steps.take(("neighbour", k))
    wg = whole_columns(gate_weight, 0)
    wu = whole_columns(up_weight, ff_half)

    gate_val = jnp.dot(normed_two_low, wg, preferred_element_type=jnp.float32)
    up_val = jnp.dot(normed_two_low, wu, preferred_element_type=jnp.float32)
    hidden = swiglu(gate_val, up_val).astype(jnp.bfloat16)
    d_wd = contract_first(all_cot, hidden).astype(jnp.bfloat16)

    def rows_of(grad, k):
        return grad[k * depth : (k + 1) * depth]

    def back(name, grad, ks):
        return [to_pack(name, k, rows_of(grad, k)) for k in ks]

    def entry(name, k, grad=None):
        return ((name, k), rows_of(grad, 0) if k == 0 else None)

    steps.step(back("wd", d_wd, [1, 2]), summed=entry("wd", 0, d_wd))
    steps.step(wd_moves([3]), summed=entry("wd", 1))
    steps.step(back("wd", d_wd, [3]), summed=entry("wd", 2))
    wd = jnp.concatenate([columns(down_weight, 0, ff_width)] + arrived("down"), axis=0)
    d_hidden = jnp.dot(all_cot, wd, preferred_element_type=jnp.float32)
    _, swiglu_back = jax.vjp(swiglu, gate_val, up_val)
    d_gate, d_up = (grad.astype(jnp.bfloat16) for grad in swiglu_back(d_hidden))
    two_own, two_moves = to_rows(
        "d_two", (contract_last(d_gate, wg) + contract_last(d_up, wu)).astype(jnp.bfloat16)
    )
    d_wg = contract_first(normed_two_low, d_gate).astype(jnp.bfloat16)
    d_wu = contract_first(normed_two_low, d_up).astype(jnp.bfloat16)

    def branch_back():
        _, norm_two_back = jax.vjp(normalize, middle, gain_two)
        d_middle_norm, kept["d_gain_two"] = norm_two_back(summed_rows("d_two", two_own))
        kept["d_middle"] = own_cot.astype(jnp.float32) + d_middle_norm
        kept["d_branch"] = kept["d_middle"].astype(jnp.bfloat16)
        return spread("d_branch", kept["d_branch"])

    steps.step(two_moves, summed=entry("wd", 3))
    steps.step(summed=entry("wg", 0, d_wg), late=branch_back)
    steps.step(back("wg", d_wg, [1, 2]), summed=entry("wu", 0, d_wu))

    d_branch = gathered(kept["d_branch"], arrived("d_branch"))
    d_attn = jnp.dot(d_branch, wo, preferred_element_type=jnp.float32).astype(jnp.bfloat16)
    d_wo = contract_first(d_branch, attn_low).astype(jnp.bfloat16)
    d_q, d_kv = attend_back(
        q_rot,
        d_attn.reshape(by_pack),
        cosine.reshape(by_pack),
        sine.reshape(by_pack),
        place_args,
        kvs,
        groups,
    )
    d_kv = d_kv.reshape(cycle, tokens, 2 * HEAD_SIZE)
    d_kv = jnp.concatenate(
        [
            lax.dynamic_index_in_dim(d_kv, here ^ j, 0, keepdims=False)[side_rows]
            for side_rows in (slice(0, tokens // 2), slice(tokens // 2, tokens))
            for j in range(cycle)
        ],
        axis=1,
    )
    ff_own, ff_moves = to_rows("ff", contract_last(hidden, wd).astype(jnp.bfloat16))

    steps.step(back("wg", d_wg, [3]), summed=entry("wg", 1))
    steps.step(back("wu", d_wu, [1, 2]), summed=("d_kv", d_kv))
    steps.step(back("wu", d_wu, [3]), summed=entry("wg", 2))
    steps.step(ff_moves, summed=entry("wg", 3))
    steps.step(summed=entry("wu", 1))
    d_kv_sum = steps.line.sums.pop("d_kv")
    d_kv_own = jnp.concatenate(
        [
            lax.dynamic_slice_in_dim(d_kv_sum, (side * cycle + here) * 2 * HEAD_SIZE, 2 * HEAD_SIZE, 1)
            for side in range(2)
        ],
        axis=0,
    ).astype(jnp.float32)
    k_cosine, k_sine = of_keys(cosine, sine)
    low = (jnp.arange(2 * HEAD_SIZE) % HEAD_SIZE < HEAD_SIZE // 2)[None, :]
    shift = HEAD_SIZE // 2
    partner = jnp.where(low, -jnp.roll(d_kv_own, -shift, 1), jnp.roll(d_kv_own, shift, 1))
    d_kv_low = (d_kv_own * k_cosine - partner * k_sine).astype(jnp.bfloat16)
    d_qkv = jnp.concatenate([d_q.reshape(tokens, q_width), d_kv_low], axis=1)
    d_wqkvo = jnp.concatenate([contract_first(normed_low, d_qkv).astype(jnp.bfloat16), d_wo], axis=1)
    one_own, one_moves = to_rows("d_one", contract_last(d_qkv, wqkv).astype(jnp.bfloat16))
    result = (middle + summed_rows("ff", ff_own)).astype(jnp.bfloat16)

    steps.step(back("wqkvo", d_wqkvo, [1, 2]), summed=entry("wu", 2))
    steps.step(back("wqkvo", d_wqkvo, [3]), summed=entry("wu", 3))
    steps.step(one_moves, summed=entry("wqkvo", 0, d_wqkvo))

    def gains_to_packs():
        _, norm_one_back = jax.vjp(normalize, own_in.astype(jnp.float32), gain_one)
        d_inputs_norm, d_gain_one = norm_one_back(summed_rows("d_one", one_own))
        kept["in_grad"] = (kept["d_middle"] + d_inputs_norm).astype(jnp.bfloat16)
        d_gains = jnp.stack([d_gain_one, kept["d_gain_two"]])
        kept["gains"] = d_gains + swap(d_gains, "tp", 1)
        return [
            to_pack("gains", k, kept["gains"][:, k * depth : (k + 1) * depth]) for k in far
        ]

    def gains_along(distance):
        if distance == 1:
            kept["gains"] = kept["gains"][:, :depth]
            for k in far:
                kept["gains"] = kept["gains"] + steps.take(("gains", k))
        else:
            kept["gains"] = kept["gains"] + steps.take("gains")
        if distance >= cycle:
            return []
        return [("gains", kept["gains"], "ctx", pairs_by(distance, cycle))]

    tasks = [gains_to_packs]
    tasks += [functools.partial(gains_along, 1 << bit) for bit in range(cycle.bit_length())]
    for i in range(1, max(packs, len(tasks) + 1)):
        summed = entry("wqkvo", i) if i < packs else None
        steps.step(summed=summed, late=tasks[i - 1] if i <= len(tasks) else None)
    while steps.flying:
        steps.step()
    sums = steps.line.sums

    def assembled(name, count, first=0):
        out = jnp.zeros((depth, count * packs), jnp.float32)
        for k in range(packs):
            piece = sums[name, k][:, first : first + count].astype(jnp.float32)
            out = lax.dynamic_update_slice(out, piece, (0, (pack ^ k) * count))
        return out

    def both_halves(own):
        own = reorder(own, pack, packs)
        other = swap(own, "tp", 1)
        return jnp.concatenate(
            [jnp.where(core == 0, own, other), jnp.where(core == 0, other, own)], axis=0
        )

    return (
        both_halves(result),
        both_halves(kept["in_grad"]),
        kept["gains"][0],
        assembled("wqkvo", q_width),
        assembled("wqkvo", k_width, q_width),
        assembled("wqkvo", k_width, q_width + k_width),
        assembled("wqkvo", q_width, q_width + 2 * k_width),
        kept["gains"][1],
        assembled("wg", ff_width),
        assembled("wu", ff_width),
        assembled("wd", ff_width),
    )


def gathered_weights(
    hidden_in,
    out_cotangent,
    norm1_gain,
    q_weight,
    key_projection_weight,
    value_projection_weight,
    o_weight,
    norm2_gain,
    gate_weight,
    up_weight,
    down_weight,
    seq_lengths,
    span_order,
):
    rows_here = hidden_in.shape[0]
    order_row = span_order[0]
    length_row = seq_lengths[0]
    kv_heads = key_projection_weight.shape[1] // HEAD_SIZE
    query_groups = QUERY_HEADS // KEY_VALUE_HEADS
    score_scale = 1.0 / math.sqrt(HEAD_SIZE)
    whole_rows = rows_here * lax.axis_size("ctx")
    local_rows = lax.axis_index("ctx") * rows_here + jnp.arange(rows_here, dtype=jnp.int32)
    q_place, q_segment, q_offset = stream_place(local_rows, order_row, length_row, rows_here)
    inputs = hidden_in.astype(jnp.float32)
    gain_one, wq_full, wk_full, wv_full, wo_full = (
        lax.all_gather(norm1_gain, "fsdp", axis=0, tiled=True),
        lax.all_gather(q_weight, "fsdp", axis=0, tiled=True),
        lax.all_gather(key_projection_weight, "fsdp", axis=0, tiled=True),
        lax.all_gather(value_projection_weight, "fsdp", axis=0, tiled=True),
        lax.all_gather(o_weight, "fsdp", axis=0, tiled=True),
    )
    gain_one = gain_one.astype(jnp.float32)
    first_normalized = normalize(inputs, gain_one)
    normed_low = first_normalized.astype(jnp.bfloat16)
    q_linear = jnp.dot(normed_low, wq_full, preferred_element_type=jnp.float32).reshape(
        rows_here, kv_heads * query_groups, HEAD_SIZE
    )
    k_linear = jnp.dot(normed_low, wk_full, preferred_element_type=jnp.float32).reshape(
        rows_here, kv_heads, HEAD_SIZE
    )
    q_rotated = (
        rotary_embedding(q_linear, q_offset)
        .astype(jnp.bfloat16)
        .reshape(rows_here, kv_heads, query_groups, HEAD_SIZE)
    )
    k_rotated = (
        rotary_embedding(k_linear, q_offset)
        .astype(jnp.bfloat16)
        .reshape(rows_here, kv_heads * HEAD_SIZE)
    )
    v_low = jnp.dot(normed_low, wv_full, preferred_element_type=jnp.float32).astype(jnp.bfloat16)

    def key_blocks(shard_rows):
        row_count = shard_rows.shape[0]
        key_total_width = math.gcd(row_count, 512)
        number = row_count // key_total_width
        k_place, k_segment, _ = stream_place(
            jnp.arange(row_count, dtype=jnp.int32), order_row, length_row, rows_here
        )
        return (
            key_total_width,
            number,
            k_place.reshape(number, key_total_width),
            k_segment.reshape(number, key_total_width),
        )

    def scores_of(key_block, place_block, segment_block):
        scores = (
            jnp.einsum("qkgd,skd->kgqs", q_rotated, key_block, preferred_element_type=jnp.float32)
            * score_scale
        )
        visible = (
            (q_place[:, None] >= place_block[None, :])
            & (q_segment[:, None] == segment_block[None, :])
        )[None, None]
        return (jnp.where(visible, scores, -1e30), visible)

    start_state = (
        jnp.full((kv_heads, query_groups, rows_here), -1e30, jnp.float32),
        jnp.zeros((kv_heads, query_groups, rows_here), jnp.float32),
        jnp.zeros((kv_heads, query_groups, rows_here, HEAD_SIZE), jnp.float32),
    )
    folded = start_state
    key_row_block = lax.all_gather(k_rotated, "ctx", axis=0, tiled=True)
    value_row_block = lax.all_gather(v_low, "ctx", axis=0, tiled=True)
    key_total_width, number, k_place, k_segment = key_blocks(key_row_block)

    def one_step(carried, pieces):
        running_max, totals, accumulated = carried
        key_block, value_block, place_block, segment_block = pieces
        scores, visible = scores_of(key_block, place_block, segment_block)
        new_max = jnp.maximum(running_max, jnp.max(scores, axis=-1))
        weights = jnp.where(visible, jnp.exp(scores - new_max[..., None]), 0.0)
        factor = jnp.exp(running_max - new_max)
        totals = totals * factor + jnp.sum(weights, axis=-1)
        accumulated = accumulated * factor[..., None] + jnp.einsum(
            "kgqs,skd->kgqd",
            weights.astype(jnp.bfloat16),
            value_block,
            preferred_element_type=jnp.float32,
        )
        return ((new_max, totals, accumulated), None)

    pieces = (
        key_row_block.reshape(number, key_total_width, kv_heads, HEAD_SIZE),
        value_row_block.reshape(number, key_total_width, kv_heads, HEAD_SIZE),
        k_place,
        k_segment,
    )
    folded, _ = lax.scan(one_step, folded, pieces)
    running_max, totals, accumulated = folded
    mixed_out = jnp.transpose(accumulated / totals[..., None], (2, 0, 1, 3))
    log_sum = running_max + jnp.log(totals)
    attn_low = mixed_out.reshape(rows_here, kv_heads * query_groups * HEAD_SIZE).astype(
        jnp.bfloat16
    )
    branch = lax.psum(contract_last(attn_low, wo_full).astype(jnp.bfloat16), "tp").astype(
        jnp.float32
    )
    middle = inputs + branch
    gain_two, wg_full, wu_full, wd_full = (
        lax.all_gather(norm2_gain, "fsdp", axis=0, tiled=True),
        lax.all_gather(gate_weight, "fsdp", axis=0, tiled=True),
        lax.all_gather(up_weight, "fsdp", axis=0, tiled=True),
        lax.all_gather(down_weight, "fsdp", axis=0, tiled=True),
    )
    gain_two = gain_two.astype(jnp.float32)
    normed_two = normalize(middle, gain_two)
    normed_two_low = normed_two.astype(jnp.bfloat16)
    gate_val = jnp.dot(normed_two_low, wg_full, preferred_element_type=jnp.float32)
    up_val = jnp.dot(normed_two_low, wu_full, preferred_element_type=jnp.float32)
    hidden = swiglu(gate_val, up_val).astype(jnp.bfloat16)
    ffn_out = lax.psum(contract_last(hidden, wd_full).astype(jnp.bfloat16), "tp").astype(
        jnp.float32
    )
    result = (middle + ffn_out).astype(jnp.bfloat16)
    grad_out = out_cotangent.astype(jnp.float32)
    d_wd = contract_first(out_cotangent, hidden)
    d_hidden = jnp.dot(out_cotangent, wd_full, preferred_element_type=jnp.float32)
    _, swiglu_back = jax.vjp(swiglu, gate_val, up_val)
    d_gate, d_up = swiglu_back(d_hidden)
    d_gate_low = d_gate.astype(jnp.bfloat16)
    d_up_low = d_up.astype(jnp.bfloat16)
    d_wg = contract_first(normed_two_low, d_gate_low)
    d_wu = contract_first(normed_two_low, d_up_low)
    d_normed_two = lax.psum(
        (contract_last(d_gate_low, wg_full) + contract_last(d_up_low, wu_full)).astype(
            jnp.bfloat16
        ),
        "tp",
    ).astype(jnp.float32)
    _, norm_two_back = jax.vjp(normalize, middle, gain_two)
    d_middle_norm, d_gain_two = norm_two_back(d_normed_two)
    d_middle = grad_out + d_middle_norm
    d_branch_low = d_middle.astype(jnp.bfloat16)
    d_wo = contract_first(d_branch_low, attn_low)
    d_attn = jnp.dot(d_branch_low, wo_full, preferred_element_type=jnp.float32).astype(jnp.bfloat16)
    d_attn_heads = d_attn.reshape(rows_here, kv_heads, query_groups, HEAD_SIZE)
    row_delta = jnp.einsum("qkgd,qkgd->kgq", d_attn_heads.astype(jnp.float32), mixed_out)
    back_state = (
        jnp.zeros((rows_here, kv_heads, query_groups, HEAD_SIZE), jnp.float32),
        jnp.zeros((whole_rows, kv_heads, HEAD_SIZE), jnp.float32),
        jnp.zeros((whole_rows, kv_heads, HEAD_SIZE), jnp.float32),
    )
    folded = back_state
    key_row_block = lax.all_gather(k_rotated, "ctx", axis=0, tiled=True)
    value_row_block = lax.all_gather(v_low, "ctx", axis=0, tiled=True)
    key_total_width, number, k_place, k_segment = key_blocks(key_row_block)

    def one_step(carried, pieces):
        d_query, d_keys, d_values = carried
        key_block, value_block, place_block, segment_block, step_index = pieces
        scores, visible = scores_of(key_block, place_block, segment_block)
        prob_rows = jnp.where(visible, jnp.exp(scores - log_sum[..., None]), 0.0)
        d_values_block = jnp.einsum(
            "kgqs,qkgd->skd",
            prob_rows.astype(jnp.bfloat16),
            d_attn_heads,
            preferred_element_type=jnp.float32,
        )
        d_probs = jnp.einsum(
            "qkgd,skd->kgqs", d_attn_heads, value_block, preferred_element_type=jnp.float32
        )
        d_scores = (prob_rows * (d_probs - row_delta[..., None])).astype(jnp.bfloat16)
        d_query = (
            d_query
            + jnp.einsum("kgqs,skd->qkgd", d_scores, key_block, preferred_element_type=jnp.float32)
            * score_scale
        )
        d_keys_block = (
            jnp.einsum("kgqs,qkgd->skd", d_scores, q_rotated, preferred_element_type=jnp.float32)
            * score_scale
        )
        row_first = step_index * key_total_width
        d_keys = lax.dynamic_update_slice_in_dim(
            d_keys,
            lax.dynamic_slice_in_dim(d_keys, row_first, key_total_width, 0) + d_keys_block,
            row_first,
            0,
        )
        d_values = lax.dynamic_update_slice_in_dim(
            d_values,
            lax.dynamic_slice_in_dim(d_values, row_first, key_total_width, 0) + d_values_block,
            row_first,
            0,
        )
        return ((d_query, d_keys, d_values), None)

    pieces = (
        key_row_block.reshape(number, key_total_width, kv_heads, HEAD_SIZE),
        value_row_block.reshape(number, key_total_width, kv_heads, HEAD_SIZE),
        k_place,
        k_segment,
        jnp.arange(number, dtype=jnp.int32),
    )
    folded, _ = lax.scan(one_step, folded, pieces)
    d_query, d_keys_all, d_values_all = folded
    d_key_own, d_value_own = (
        lax.psum_scatter(
            d_keys_all.astype(jnp.bfloat16), "ctx", scatter_dimension=0, tiled=True
        ).astype(jnp.float32),
        lax.psum_scatter(
            d_values_all.astype(jnp.bfloat16), "ctx", scatter_dimension=0, tiled=True
        ).astype(jnp.float32),
    )
    _, rope_q_back = jax.vjp(lambda rotated_in: rotary_embedding(rotated_in, q_offset), q_linear)
    _, rope_k_back = jax.vjp(lambda rotated_in: rotary_embedding(rotated_in, q_offset), k_linear)
    (d_q_linear,) = rope_q_back(d_query.reshape(rows_here, kv_heads * query_groups, HEAD_SIZE))
    (d_k_linear,) = rope_k_back(d_key_own)
    d_q_low = d_q_linear.reshape(rows_here, kv_heads * query_groups * HEAD_SIZE).astype(
        jnp.bfloat16
    )
    d_k_low = d_k_linear.reshape(rows_here, kv_heads * HEAD_SIZE).astype(jnp.bfloat16)
    d_v_low = d_value_own.reshape(rows_here, kv_heads * HEAD_SIZE).astype(jnp.bfloat16)
    d_wq = contract_first(normed_low, d_q_low)
    d_wk = contract_first(normed_low, d_k_low)
    d_wv = contract_first(normed_low, d_v_low)
    d_normed_one = lax.psum(
        (
            contract_last(d_q_low, wq_full)
            + contract_last(d_k_low, wk_full)
            + contract_last(d_v_low, wv_full)
        ).astype(jnp.bfloat16),
        "tp",
    ).astype(jnp.float32)
    _, norm_one_back = jax.vjp(normalize, inputs, gain_one)
    d_inputs_norm, d_gain_one = norm_one_back(d_normed_one)
    in_grad = (d_middle + d_inputs_norm).astype(jnp.bfloat16)
    weight_grads = (d_gain_one, d_wq, d_wk, d_wv, d_wo, d_gain_two, d_wg, d_wu, d_wd)
    shares = (
        lax.psum_scatter(weight_grads[0], ("fsdp", "ctx"), scatter_dimension=0, tiled=True),
        lax.psum_scatter(weight_grads[1], ("fsdp", "ctx"), scatter_dimension=0, tiled=True),
        lax.psum_scatter(weight_grads[2], ("fsdp", "ctx"), scatter_dimension=0, tiled=True),
        lax.psum_scatter(weight_grads[3], ("fsdp", "ctx"), scatter_dimension=0, tiled=True),
        lax.psum_scatter(weight_grads[4], ("fsdp", "ctx"), scatter_dimension=0, tiled=True),
        lax.psum_scatter(weight_grads[5], ("fsdp", "ctx"), scatter_dimension=0, tiled=True),
        lax.psum_scatter(weight_grads[6], ("fsdp", "ctx"), scatter_dimension=0, tiled=True),
        lax.psum_scatter(weight_grads[7], ("fsdp", "ctx"), scatter_dimension=0, tiled=True),
        lax.psum_scatter(weight_grads[8], ("fsdp", "ctx"), scatter_dimension=0, tiled=True),
    )
    owned_grads = (
        lax.all_gather(shares[0].astype(jnp.bfloat16), "ctx", axis=0, tiled=True).astype(
            jnp.float32
        ),
        lax.all_gather(shares[1].astype(jnp.bfloat16), "ctx", axis=0, tiled=True).astype(
            jnp.float32
        ),
        lax.all_gather(shares[2].astype(jnp.bfloat16), "ctx", axis=0, tiled=True).astype(
            jnp.float32
        ),
        lax.all_gather(shares[3].astype(jnp.bfloat16), "ctx", axis=0, tiled=True).astype(
            jnp.float32
        ),
        lax.all_gather(shares[4].astype(jnp.bfloat16), "ctx", axis=0, tiled=True).astype(
            jnp.float32
        ),
        lax.all_gather(shares[5].astype(jnp.bfloat16), "ctx", axis=0, tiled=True).astype(
            jnp.float32
        ),
        lax.all_gather(shares[6].astype(jnp.bfloat16), "ctx", axis=0, tiled=True).astype(
            jnp.float32
        ),
        lax.all_gather(shares[7].astype(jnp.bfloat16), "ctx", axis=0, tiled=True).astype(
            jnp.float32
        ),
        lax.all_gather(shares[8].astype(jnp.bfloat16), "ctx", axis=0, tiled=True).astype(
            jnp.float32
        ),
    )
    return (
        result,
        in_grad,
        owned_grads[0],
        owned_grads[1],
        owned_grads[2],
        owned_grads[3],
        owned_grads[4],
        owned_grads[5],
        owned_grads[6],
        owned_grads[7],
        owned_grads[8],
    )


def solution(mesh):
    placed = (
        P(("fsdp", "ctx"), None),
        P(("fsdp", "ctx"), None),
        P("fsdp"),
        P("fsdp", "tp"),
        P("fsdp", "tp"),
        P("fsdp", "tp"),
        P("fsdp", "tp"),
        P("fsdp"),
        P("fsdp", "tp"),
        P("fsdp", "tp"),
        P("fsdp", "tp"),
        P("fsdp", None),
        P("fsdp", None),
    )
    plane = mesh.shape["fsdp"] * mesh.shape["tp"]
    splits = mesh.shape["tp"] == 2 and KEY_VALUE_HEADS == plane and mesh.shape["ctx"] % 2 == 0
    return jax.shard_map(
        split_heads if splits else gathered_weights,
        mesh=mesh,
        in_specs=placed,
        out_specs=(
            P(("fsdp", "ctx"), None),
            P(("fsdp", "ctx"), None),
            P("fsdp"),
            P("fsdp", "tp"),
            P("fsdp", "tp"),
            P("fsdp", "tp"),
            P("fsdp", "tp"),
            P("fsdp"),
            P("fsdp", "tp"),
            P("fsdp", "tp"),
            P("fsdp", "tp"),
        ),
        check_vma=False,
    )
```

```python
import functools
import math

import jax
import jax.numpy as jnp
from jax import lax
from jax.experimental import pallas as pl
from jax.experimental.pallas import tpu as pltpu
from jax.sharding import PartitionSpec as P

QUERY_HEADS = 32
KEY_VALUE_HEADS = 8
HEAD_SIZE = 64


def stream_place(row_ids, order_row, length_row, tok_dev):
    cycle_size = order_row.shape[0]
    half_len = tok_dev // 2
    cycle_rank = row_ids // tok_dev
    within = row_ids % tok_dev
    first_section = jnp.sum(
        jnp.where(
            cycle_rank[:, None] == jnp.arange(cycle_size, dtype=jnp.int32)[None, :],
            order_row[None, :],
            0,
        ),
        axis=1,
        dtype=jnp.int32,
    )
    section = jnp.where(within >= half_len, 2 * cycle_size - 1 - first_section, first_section)
    places = section * half_len + within % half_len
    seq_ends = jnp.cumsum(length_row, dtype=jnp.int32)
    passed = places[:, None] >= seq_ends[None, :]
    segment = jnp.sum(passed.astype(jnp.int32), axis=1, dtype=jnp.int32)
    offset = places - jnp.sum(jnp.where(passed, length_row[None, :], 0), axis=1, dtype=jnp.int32)
    return (places, segment, offset)


def rotary_embedding(values, positions):
    half_len = values.shape[-1] // 2
    frequency = jnp.exp(
        -math.log(500000.0) * jnp.arange(half_len, dtype=jnp.float32) * 2.0 / values.shape[-1]
    )
    angles = positions.astype(jnp.float32)[:, None] * frequency[None, :]
    cosine = jnp.cos(angles)[:, None, :]
    sine = jnp.sin(angles)[:, None, :]
    lower_half = values[..., :half_len]
    upper_half = values[..., half_len:]
    return jnp.concatenate(
        [lower_half * cosine - upper_half * sine, upper_half * cosine + lower_half * sine], axis=-1
    )


def normalize(values, gain_vec):
    return values * lax.rsqrt(jnp.mean(values * values, axis=-1, keepdims=True) + 1e-05) * gain_vec


def swiglu(gate_val, up_val):
    return jax.nn.silu(gate_val) * up_val


def contract_last(left, right):
    return lax.dot_general(
        left, right, (((1,), (1,)), ((), ())), preferred_element_type=jnp.float32
    )


def contract_first(left, right):
    return lax.dot_general(
        left, right, (((0,), (0,)), ((), ())), preferred_element_type=jnp.float32
    )


VMEM_LIMIT = 32 * 1024 * 1024
SMALL_LIMIT = 12 * 1024 * 1024
SMALL = pl.CostEstimate(flops=1, bytes_accessed=1, transcendentals=0)


def pairs_by(distance, size):
    return [(i, i ^ distance) for i in range(size)]


def swap(array, axis, distance):
    return lax.ppermute(array, axis, pairs_by(distance, lax.axis_size(axis)))


class Line:
    def __init__(self, axis):
        index = lax.axis_index(axis)
        size = lax.axis_size(axis)
        self.axis = axis
        self.at_end = ((index == 0) | (index == size - 1)).astype(jnp.int32)[None]
        self.entered = self.halfway = self.leaving = None
        self.sums = {}

    def advance(self, got, entering):
        if self.leaving is not None:
            name, sent = self.leaving
            self.sums[name] = (got["ends"], sent)
        moves = []
        halfway = None
        if self.entered is not None:
            name, value = self.entered
            halfway = (name, add_low(value, got["ends"]))
            moves.append(("middle", halfway[1], self.axis, [(1, 2), (2, 1)]))
        leaving = None
        inwards, outwards = [(0, 1), (3, 2)], [(1, 0), (2, 3)]
        if self.halfway is not None:
            name, value = self.halfway
            if entering is None:
                sent, pairs = add_low(value, got["middle"]), outwards
            else:
                sent = either_way(self.at_end, entering[1], value, got["middle"])
                pairs = inwards + outwards
            leaving = (name, sent)
            moves.append(("ends", sent, self.axis, pairs))
        elif entering is not None:
            moves.append(("ends", entering[1], self.axis, inwards))
        self.entered, self.halfway, self.leaving = entering, halfway, leaving
        return moves


class Steps:
    def __init__(self, line):
        self.line = line
        self.got = {}
        self.names = []
        self.flying = []

    def step(self, moves=(), summed=None, late=None, carry=()):
        moves = list(moves)
        fresh = [summed[1]] if summed is not None and summed[1] is not None else []
        held = lax.optimization_barrier(
            tuple(self.flying) + tuple(move[1] for move in moves) + tuple(fresh) + tuple(carry)
        )
        count = len(self.flying)
        for name, value in zip(self.names, held[:count]):
            self.got[name] = value
        moves = [
            (name, value, axis, pairs)
            for (name, _, axis, pairs), value in zip(moves, held[count:])
        ]
        entering = summed
        if summed is not None:
            entering = (summed[0], held[count + len(moves)] if fresh else self.take(summed[0]))
        on_line = self.line.advance(self.got, entering)
        moves = on_line + moves + (late() if late is not None else [])
        self.names = [move[0] for move in moves]
        self.flying = [lax.ppermute(value, axis, pairs) for _, value, axis, pairs in moves]
        return held[len(held) - len(carry) :]

    def take(self, name):
        return self.got.pop(name)


def in_vmem(kernel, out_shape, *args, scalars=0):
    specs = [pl.BlockSpec(memory_space=pltpu.SMEM)] * scalars
    specs += [pl.BlockSpec(memory_space=pltpu.VMEM)] * (len(args) - scalars)
    return pl.pallas_call(
        kernel,
        out_shape=out_shape,
        in_specs=specs,
        out_specs=[pl.BlockSpec(memory_space=pltpu.VMEM)] * len(out_shape),
        compiler_params=pltpu.CompilerParams(vmem_limit_bytes=SMALL_LIMIT),
        cost_estimate=SMALL,
    )(*args)


def low(*shape):
    return jax.ShapeDtypeStruct(shape, jnp.bfloat16)


def full(*shape):
    return jax.ShapeDtypeStruct(shape, jnp.float32)


def store_seen(ref, value, distance, count):
    width = value.shape[-1] // count
    for block in range(count):
        there = block ^ distance
        ref[: value.shape[0], block * width : (block + 1) * width] = value[
            :, there * width : (there + 1) * width
        ]


def prepare_kernel(count, index_ref, x_ref, *refs):
    extra_ref = refs[0] if len(refs) > count else None
    own_ref, *sends = refs[-count:]
    rows, width = own_ref.shape[0], own_ref.shape[1] // count
    first = pl.multiple_of(index_ref[1] * rows, rows)
    for block in range(count):
        column = pl.multiple_of((index_ref[0] ^ block) * width, width)
        own_ref[:, block * width : (block + 1) * width] = x_ref[
            pl.ds(first, rows), pl.ds(column, width)
        ]
    for k in range(1, count):
        store_seen(sends[k - 1], own_ref[...], k, count)
        if extra_ref is not None:
            sends[k - 1][rows:, :] = extra_ref[...]


def prepare(x, index, count, extra=()):
    rows, width = x.shape[0] // 2, x.shape[1]
    more = extra[0].shape[0] if extra else 0
    return in_vmem(
        functools.partial(prepare_kernel, count),
        [low(rows, width)] + [low(rows + more, width)] * (count - 1),
        index,
        x,
        *extra,
        scalars=1,
    )


def join_kernel(*refs):
    out_ref = refs[-1]
    rows = refs[0].shape[0]
    for i, ref in enumerate(refs[:-1]):
        out_ref[i * rows : (i + 1) * rows, :] = ref[:rows, :]


def join(own, others):
    rows, width = own.shape
    return in_vmem(join_kernel, [low(rows * (1 + len(others)), width)], own, *others)[0]


def fold_kernel(count, first_ref, came_ref, own_ref, *sends):
    rows = own_ref.shape[0]
    for k in range(count):
        here = slice(k * rows, (k + 1) * rows)
        total = first_ref[here, :].astype(jnp.float32) + came_ref[here, :].astype(jnp.float32)
        total = total.astype(jnp.bfloat16)
        if k == 0:
            own_ref[...] = total
        else:
            store_seen(sends[k - 1], total, k, count)


def fold(first, came, count):
    rows, width = first.shape[0] // count, first.shape[1]
    return in_vmem(
        functools.partial(fold_kernel, count), [low(rows, width)] * count, first, came
    )


def total_of(refs):
    total = refs[0][...].astype(jnp.float32)
    for ref in refs[1:]:
        total = total + ref[...].astype(jnp.float32)
    return total


def middle_kernel(count, in_ref, gain_ref, *refs):
    parts, (middle_ref, normed_ref, *sends) = refs[:count], refs[count:]
    middle = in_ref[...].astype(jnp.float32) + total_of(parts)
    middle_ref[...] = middle
    mean = jnp.mean(middle * middle, axis=-1, keepdims=True)
    normed = (middle * lax.rsqrt(mean + 1e-05) * gain_ref[...]).astype(jnp.bfloat16)
    normed_ref[...] = normed
    for k in range(1, count):
        store_seen(sends[k - 1], normed, k, count)


def norm_back(d_normed, x, gain):
    scale = lax.rsqrt(jnp.mean(x * x, axis=-1, keepdims=True) + 1e-05)
    unit = x * scale
    d_unit = d_normed * gain
    d_x = scale * (d_unit - unit * jnp.mean(d_unit * unit, axis=-1, keepdims=True))
    return d_x, jnp.sum(d_normed * unit, axis=0, keepdims=True)


def branch_back_kernel(count, middle_ref, gain_ref, cot_ref, *refs):
    parts, (d_middle_ref, d_gain_ref, branch_ref, *sends) = refs[:count], refs[count:]
    d_x, d_gain_ref[...] = norm_back(total_of(parts), middle_ref[...], gain_ref[...])
    d_middle = cot_ref[...].astype(jnp.float32) + d_x
    d_middle_ref[...] = d_middle
    branch = d_middle.astype(jnp.bfloat16)
    branch_ref[...] = branch
    for k in range(1, count):
        store_seen(sends[k - 1], branch, k, count)


def in_grad_kernel(count, in_ref, gain_ref, d_middle_ref, *refs):
    parts, (grad_ref, d_gain_ref) = refs[:count], refs[count:]
    x = in_ref[...].astype(jnp.float32)
    d_x, d_gain_ref[...] = norm_back(total_of(parts), x, gain_ref[...])
    grad_ref[...] = (d_middle_ref[...] + d_x).astype(jnp.bfloat16)


def gridded(kernel, steps, ins, outs, scalars=()):
    return pl.pallas_call(
        kernel,
        grid=(steps,),
        in_specs=[pl.BlockSpec(memory_space=pltpu.SMEM)] * len(scalars)
        + [pl.BlockSpec(block, index) for _, block, index in ins],
        out_specs=[pl.BlockSpec(block, index) for _, block, index in outs],
        out_shape=[shape for shape, _, _ in outs],
        compiler_params=pltpu.CompilerParams(vmem_limit_bytes=VMEM_LIMIT),
        cost_estimate=SMALL,
    )(*scalars, *[array for array, _, _ in ins])


def row_blocks(array, rows):
    return (array, (rows, array.shape[1]), lambda i: (i, 0))


def add_low(left, right):
    right = right[:, : left.shape[1]]
    return (left.astype(jnp.float32) + right.astype(jnp.float32)).astype(jnp.bfloat16)


def either_way(at_end, fresh, value, came):
    total = add_low(value, came)
    width = max(fresh.shape[1], value.shape[1])
    if fresh.shape[1] < width:
        fresh = jnp.pad(fresh, ((0, 0), (0, width - fresh.shape[1])))
    if total.shape[1] < width:
        total = jnp.pad(total, ((0, 0), (0, width - total.shape[1])))
    return jnp.where(at_end[0] == 1, fresh, total)


def settled(at_end, came_ref, sent_ref, columns):
    return jnp.where(at_end == 1, came_ref[:, columns], sent_ref[:, columns]).astype(jnp.float32)


def settle_kernel(count, at_end_ref, index_ref, *refs):
    out_ref = refs[-1]
    width = out_ref.shape[1] // count
    for k in range(count):
        column = pl.multiple_of((index_ref[0] ^ k) * width, width)
        out_ref[:, pl.ds(column, width)] = settled(
            at_end_ref[0], refs[2 * k], refs[2 * k + 1], slice(0, width)
        )


def settle(at_end, index, pairs, width):
    count = len(pairs)
    arrays = [array for pair in pairs for array in pair]
    depth = arrays[0].shape[0]
    rows = math.gcd(depth, 128)
    ins = [(array, (rows, width), lambda i: (i, 0)) for array in arrays]
    outs = [row_blocks(full(depth, width * count), rows)]
    kernel = functools.partial(settle_kernel, count)
    return gridded(kernel, depth // rows, ins, outs, scalars=(at_end, index))[0]


def settle_attention_kernel(count, q_width, kv_width, at_end_ref, index_ref, *refs):
    q_ref, k_ref, v_ref, o_ref = refs[-4:]
    o_width = o_ref.shape[1] // count
    o_first = q_width + kv_width
    kvs = []
    for k in range(count):
        came_ref, sent_ref = refs[2 * k], refs[2 * k + 1]
        column = pl.multiple_of((index_ref[0] ^ k) * q_width, q_width)
        q_ref[:, pl.ds(column, q_width)] = settled(
            at_end_ref[0], came_ref, sent_ref, slice(0, q_width)
        )
        column = pl.multiple_of((index_ref[0] ^ k) * o_width, o_width)
        o_ref[:, pl.ds(column, o_width)] = settled(
            at_end_ref[0], came_ref, sent_ref, slice(o_first, o_first + o_width)
        )
        kvs.append(settled(at_end_ref[0], came_ref, sent_ref, slice(q_width, o_first)))
    ordered = []
    for place in range(count):
        kv = kvs[0]
        for k in range(1, count):
            kv = jnp.where((index_ref[0] ^ k) == place, kvs[k], kv)
        ordered.append(kv)
    k_ref[...] = jnp.concatenate([kv[:, : kv_width // 2] for kv in ordered], axis=1)
    v_ref[...] = jnp.concatenate([kv[:, kv_width // 2 :] for kv in ordered], axis=1)


def settle_attention(at_end, index, pairs, q_width, kv_width):
    count = len(pairs)
    arrays = [array for pair in pairs for array in pair]
    depth = arrays[0].shape[0]
    width = min(array.shape[1] for array in arrays)
    o_width = width - q_width - kv_width
    rows = math.gcd(depth, 128)
    ins = [(array, (rows, width), lambda i: (i, 0)) for array in arrays]
    widths = (q_width, kv_width // 2, kv_width // 2, o_width)
    outs = [row_blocks(full(depth, each * count), rows) for each in widths]
    kernel = functools.partial(settle_attention_kernel, count, q_width, kv_width)
    return gridded(kernel, depth // rows, ins, outs, scalars=(at_end, index))


def d_qkv_kernel(at_end_ref, here_ref, came_ref, sent_ref, dq_ref, cos_ref, sin_ref, out_ref):
    lanes = 2 * HEAD_SIZE
    half, q_width = dq_ref.shape[1], dq_ref.shape[2]
    cycle = came_ref.shape[1] // lanes // 2
    for core_side in range(2):
        column = pl.multiple_of((core_side * cycle + here_ref[0]) * lanes, lanes)
        d_kv = settled(at_end_ref[0], came_ref, sent_ref, pl.ds(column, lanes))
        cosine, sine = of_keys(cos_ref[core_side], sin_ref[core_side])
        d_kv = turned(d_kv, cosine, -sine).astype(jnp.bfloat16)
        rows = slice(core_side * half, (core_side + 1) * half)
        out_ref[rows, :q_width] = dq_ref[core_side]
        out_ref[rows, q_width:] = d_kv


def rows_back_kernel(count, index_ref, own_ref, other_ref, out_ref):
    rows, width = own_ref.shape[0], own_ref.shape[1] // count
    for ref, core in ((own_ref, index_ref[1]), (other_ref, 1 - index_ref[1])):
        first = pl.multiple_of(core * rows, rows)
        for block in range(count):
            column = pl.multiple_of((index_ref[0] ^ block) * width, width)
            out_ref[pl.ds(first, rows), pl.ds(column, width)] = ref[
                :, block * width : (block + 1) * width
            ]


def result_kernel(middle_ref, *refs):
    refs[-1][...] = (middle_ref[...] + total_of(refs[:-1])).astype(jnp.bfloat16)


def still(array):
    zeros = (0,) * len(array.shape)
    return (array, array.shape, lambda i: zeros)


def dot(left, right):
    return jnp.dot(left, right, preferred_element_type=jnp.float32)


def both(mine_ref, other_ref):
    return jnp.concatenate([mine_ref[...], other_ref[...]], axis=0)


def gate_up_kernel(count, here_steps, *refs):
    x = both(refs[0], refs[1])
    refs = refs[2:]
    own, fetched, passed = refs[:2], refs[2 : 2 * count], refs[2 * count : 4 * count - 2]
    gate_ref, up_ref, hidden_ref, wg_ref, wu_ref = refs[4 * count - 2 :]
    here = pl.program_id(0) < here_steps
    lins = []
    for which, out_ref in ((0, wg_ref), (1, wu_ref)):
        pieces = [own[which][...]]
        for k in range(count - 1):
            pieces.append(
                jnp.where(here, fetched[2 * k + which][...], passed[2 * k + which][...])
            )
        weight = jnp.concatenate(pieces, axis=0)
        out_ref[...] = weight
        lins.append(dot(x, weight))
    gate, up = lins
    gate_ref[...] = gate
    up_ref[...] = up
    hidden_ref[...] = (gate * jax.nn.sigmoid(gate) * up).astype(jnp.bfloat16)


def gate_up(x, own_gate, own_up, fetched, passed):
    tokens, depth = 2 * x[0].shape[0], own_gate.shape[0]
    width, units = x[0].shape[1], own_gate.shape[1]
    count = len(fetched) + 1
    block = math.gcd(units // 2, 256)
    steps, half = units // block, units // block // 2
    ins = [still(x[0]), still(x[1])]
    ins += [(w, (depth, block), lambda i: (0, i)) for w in (own_gate, own_up)]
    for arrays in (fetched, passed):
        for array in arrays:
            ins.append((array, (depth, block), lambda i: (0, lax.rem(i, half))))
            ins.append((array, (depth, block), lambda i: (0, half + lax.rem(i, half))))
    outs = [
        (full(tokens, units), (tokens, block), lambda i: (0, i)),
        (full(tokens, units), (tokens, block), lambda i: (0, i)),
        (low(tokens, units), (tokens, block), lambda i: (0, i)),
        (low(width, units), (width, block), lambda i: (0, i)),
        (low(width, units), (width, block), lambda i: (0, i)),
    ]
    return gridded(functools.partial(gate_up_kernel, count, half), steps, ins, outs)


def units_back_kernel(count, *refs):
    d_out = both(refs[0], refs[1])
    refs = refs[2:]
    pieces, (gate_ref, up_ref, d_gate_ref, d_up_ref, wd_ref) = refs[:count], refs[count:]
    weight = jnp.concatenate([ref[...] for ref in pieces], axis=0)
    wd_ref[...] = weight
    d_hidden = dot(d_out, weight)
    gate, up = gate_ref[...], up_ref[...]
    chance = jax.nn.sigmoid(gate)
    d_up_ref[...] = (d_hidden * (gate * chance)).astype(jnp.bfloat16)
    slope = chance + gate * chance * (1.0 - chance)
    d_gate_ref[...] = (d_hidden * up * slope).astype(jnp.bfloat16)


def units_back(d_out, pieces, gate, up):
    tokens, units = gate.shape
    depth, width = pieces[0].shape[0], d_out[0].shape[1]
    block = math.gcd(units, 256)

    def by_columns(array, rows):
        return (array, (rows, block), lambda i: (0, i))

    ins = [still(d_out[0]), still(d_out[1])] + [by_columns(piece, depth) for piece in pieces]
    ins += [by_columns(gate, tokens), by_columns(up, tokens)]
    outs = [by_columns(low(tokens, units), tokens)] * 2 + [by_columns(low(width, units), width)]
    return gridded(functools.partial(units_back_kernel, len(pieces)), units // block, ins, outs)


def rows_sum_kernel(terms, *refs):
    first_ref, second_ref = refs[-2:]
    total = 0.0
    for left_ref, right_ref in zip(refs[:terms], refs[terms : 2 * terms]):
        total = total + contract_last(left_ref[...], right_ref[...])
    total = total.astype(jnp.bfloat16)
    half = first_ref.shape[0]
    first_ref[...] = total[:half]
    second_ref[...] = total[half:]


def rows_sum(lefts, rights):
    tokens, width = lefts[0].shape[0], rights[0].shape[0]
    block = math.gcd(width, 512)
    ins = [still(left) for left in lefts]
    ins += [(right, (block, right.shape[1]), lambda i: (i, 0)) for right in rights]
    outs = [(low(tokens // 2, width), (tokens // 2, block), lambda i: (0, i))] * 2
    return gridded(functools.partial(rows_sum_kernel, len(lefts)), width // block, ins, outs)


def weight_grad_kernel(count, terms, turn, *refs):
    if turn:
        side, refs = refs[0][0], refs[1:]
    outs = refs[3 * terms :]
    step = pl.program_id(0)
    first = 0
    for term in range(terms):
        mine_ref, other_ref, right_ref = refs[3 * term : 3 * term + 3]
        half = mine_ref.shape[0]
        grad = contract_first(mine_ref[...], right_ref[:half, :])
        grad = grad + contract_first(other_ref[...], right_ref[half:, :])
        grad = grad.astype(jnp.bfloat16)
        columns = grad.shape[1]
        for k in range(count):

            @pl.when(step == k)
            def _(k=k, first=first, grad=grad, columns=columns):
                if turn:
                    part = columns // 2
                    outs[k][:, pl.ds(pl.multiple_of(side * part, part), part)] = grad[:, :part]
                    outs[k][:, pl.ds(pl.multiple_of((1 - side) * part, part), part)] = grad[:, part:]
                else:
                    outs[k][:, first : first + columns] = grad

        first += columns


def weight_grad(terms, count, side=None):
    columns = sum(right.shape[1] for _, _, right in terms)
    depth = terms[0][0].shape[1] // count
    ins = []
    if side is not None:
        ins.append((side, None, None))
    for mine, other, right in terms:
        ins += [(left, (left.shape[0], depth), lambda i: (0, i)) for left in (mine, other)]
        ins.append(still(right))
    specs = [
        pl.BlockSpec(memory_space=pltpu.SMEM) if block is None else pl.BlockSpec(block, index)
        for _, block, index in ins
    ]
    return pl.pallas_call(
        functools.partial(weight_grad_kernel, count, len(terms), side is not None),
        grid=(count,),
        in_specs=specs,
        out_specs=[pl.BlockSpec((depth, columns), lambda i: (0, 0))] * count,
        out_shape=[low(depth, columns)] * count,
        compiler_params=pltpu.CompilerParams(vmem_limit_bytes=VMEM_LIMIT),
        cost_estimate=SMALL,
    )(*[array for array, _, _ in ins])


def turned(lin, cosine, sine):
    width = lin.shape[-1]
    quarter = HEAD_SIZE // 2
    lane = lax.broadcasted_iota(jnp.int32, lin.shape, lin.ndim - 1)
    first = lax.rem(lane, HEAD_SIZE) < quarter
    partner = jnp.where(
        first,
        -pltpu.roll(lin, width - quarter, lin.ndim - 1),
        pltpu.roll(lin, quarter, lin.ndim - 1),
    )
    return lin * cosine + partner * sine


def side_by_side(table, width):
    return jnp.concatenate([table] * (width // table.shape[-1]), axis=-1)


def of_keys(cosine, sine):
    keys = lax.broadcasted_iota(jnp.int32, cosine.shape, 1) < HEAD_SIZE
    return jnp.where(keys, cosine, 1.0), jnp.where(keys, sine, 0.0)


def qkv_kernel(count, q_width, kv_width, *refs):
    x_refs, (gain_ref, cos_ref, sin_ref), refs = refs[:2], refs[2:5], refs[5:]
    pieces, refs = refs[:count], refs[count:]
    normed_refs, (q_ref, kv_ref, wqkv_ref, wo_ref) = refs[:2], refs[2:]
    weight = jnp.concatenate([ref[...] for ref in pieces], axis=0)
    qkv_width = q_width + kv_width

    @pl.when(pl.program_id(0) == 0)
    def _():
        wqkv_ref[...] = weight[:, :qkv_width]
        wo_ref[...] = weight[:, qkv_width:]

    for i in range(2):
        x = x_refs[i][...].astype(jnp.float32)
        mean = jnp.mean(x * x, axis=-1, keepdims=True)
        normed = (x * lax.rsqrt(mean + 1e-05) * gain_ref[...]).astype(jnp.bfloat16)
        normed_refs[i][...] = normed
        lin = dot(normed, weight[:, :qkv_width])
        cosine, sine = cos_ref[i], sin_ref[i]
        q = turned(lin[:, :q_width], side_by_side(cosine, q_width), side_by_side(sine, q_width))
        q_ref[i] = q.astype(jnp.bfloat16)
        kv = turned(lin[:, q_width:], *of_keys(cosine, sine))
        kv_ref[i] = kv.astype(jnp.bfloat16)


def project_qkv(x, gain, cosine, sine, pieces, q_width, kv_width):
    half_rows, width = x[0].shape
    qkv_width = q_width + kv_width
    block = math.gcd(half_rows, 128)

    def rows_of(array, columns):
        return (array, (block, columns), lambda i: (i, 0))

    def of_both(array, columns):
        return (array, (2, block, columns), lambda i: (0, i, 0))

    lanes = cosine.shape[-1]
    ins = [rows_of(x[0], width), rows_of(x[1], width), still(gain)]
    ins += [of_both(cosine, lanes), of_both(sine, lanes)] + [still(piece) for piece in pieces]
    o_width = pieces[0].shape[1] - qkv_width
    outs = [rows_of(low(half_rows, width), width)] * 2
    outs += [of_both(low(2, half_rows, q_width), q_width), of_both(low(2, half_rows, kv_width), kv_width)]
    outs += [still(low(width, qkv_width)), still(low(width, o_width))]
    kernel = functools.partial(qkv_kernel, len(pieces), q_width, kv_width)
    return gridded(kernel, half_rows // block, ins, outs)


def shares(q, k, visible):
    scores = contract_last(q, k) * (1.0 / math.sqrt(HEAD_SIZE))
    scores = jnp.where(visible, scores, -1e30)
    weights = jnp.exp(scores - jnp.max(scores, axis=-1, keepdims=True))
    weights = jnp.where(visible, weights, 0.0)
    return weights, jnp.sum(weights, axis=-1, keepdims=True)


def load_attention(q_ref, place_ref, start_ref, key_place_ref, kv_refs):
    q = q_ref[...]
    q = q.reshape(q.shape[0] * q.shape[1], q.shape[2])
    kv = jnp.concatenate([ref[...].reshape(q.shape[0], 2 * HEAD_SIZE) for ref in kv_refs], axis=0)
    key_place = key_place_ref[0]
    visible = (key_place <= place_ref[0]) & (key_place >= start_ref[0])
    return q, kv[:, :HEAD_SIZE], kv[:, HEAD_SIZE:], visible


def attend_kernel(groups, q_ref, place_ref, start_ref, key_place_ref, wo_ref, *refs):
    kv_refs, (out_ref, first_ref, second_ref) = refs[:-3], refs[-3:]
    q, k, v, visible = load_attention(q_ref, place_ref, start_ref, key_place_ref, kv_refs)
    mixed = []
    for g in range(groups):
        weights, totals = shares(q[:, g * HEAD_SIZE : (g + 1) * HEAD_SIZE], k, visible)
        mixed.append(dot(weights.astype(jnp.bfloat16), v) / totals)
    out = jnp.concatenate(mixed, axis=1).astype(jnp.bfloat16)
    out_ref[...] = out.reshape(out_ref.shape)
    branch = contract_last(out, wo_ref[...]).astype(jnp.bfloat16)
    half = first_ref.shape[0]
    first_ref[...] = branch[:half]
    second_ref[...] = branch[half:]


def attend_back_kernel(
    groups,
    here_ref,
    q_ref,
    mine_ref,
    other_ref,
    cos_ref,
    sin_ref,
    place_ref,
    start_ref,
    key_place_ref,
    wo_ref,
    *refs,
):
    kv_refs, (dq_ref, dkv_ref) = refs[:-2], refs[-2:]
    q, k, v, visible = load_attention(q_ref, place_ref, start_ref, key_place_ref, kv_refs)
    d_out = dot(both(mine_ref, other_ref), wo_ref[...]).astype(jnp.bfloat16)
    scale = 1.0 / math.sqrt(HEAD_SIZE)
    d_q, d_k, d_v = [], 0.0, 0.0
    for g in range(groups):
        q_head = q[:, g * HEAD_SIZE : (g + 1) * HEAD_SIZE]
        d_head = d_out[:, g * HEAD_SIZE : (g + 1) * HEAD_SIZE]
        weights, totals = shares(q_head, k, visible)
        probs = weights / totals
        d_probs = contract_last(d_head, v)
        row_delta = jnp.sum(probs * d_probs, axis=-1, keepdims=True)
        d_scores = (probs * (d_probs - row_delta)).astype(jnp.bfloat16)
        d_q.append(dot(d_scores, k) * scale)
        d_k = d_k + contract_first(d_scores, q_head) * scale
        d_v = d_v + contract_first(probs.astype(jnp.bfloat16), d_head)
    d_q = jnp.concatenate(d_q, axis=1)
    cosine = cos_ref[...].reshape(q.shape[0], -1)
    sine = sin_ref[...].reshape(q.shape[0], -1)
    d_q = turned(d_q, side_by_side(cosine, q.shape[1]), -side_by_side(sine, q.shape[1]))
    dq_ref[...] = d_q.astype(jnp.bfloat16).reshape(dq_ref.shape)
    d_kv = jnp.concatenate([d_k, d_v], axis=1).astype(jnp.bfloat16)
    half, lanes, cycle = dkv_ref.shape[0], 2 * HEAD_SIZE, len(kv_refs)
    for j in range(cycle):
        for core_side in range(2):
            first = (2 * j + core_side) * half
            column = pl.multiple_of((core_side * cycle + (here_ref[0] ^ j)) * lanes, lanes)
            dkv_ref[:, pl.ds(column, lanes)] = d_kv[first : first + half]


def of_pack(array, half):
    return (array, (2, half, array.shape[-1]), lambda p: (0, p, 0))


def place_blocks(places):
    return [(array, (1,) + array.shape[1:], lambda p: (p, 0, 0)) for array in places]


def attend(q, places, wo, kvs, packs, groups):
    half = q.shape[1] // packs
    width = wo.shape[0]
    ins = [of_pack(q, half)] + place_blocks(places) + [still(wo)] + [of_pack(kv, half) for kv in kvs]
    outs = [of_pack(low(*q.shape), half)]
    outs += [(low(q.shape[1], width), (half, width), lambda p: (p, 0))] * 2
    return gridded(functools.partial(attend_kernel, groups), packs, ins, outs)


def attend_back(here, q, d_branch, cosine, sine, places, wo, kvs, packs, groups):
    half = q.shape[1] // packs
    cycle = len(kvs)
    ins = [of_pack(q, half)]
    ins += [(array, (half, array.shape[1]), lambda p: (p, 0)) for array in d_branch]
    ins += [of_pack(cosine, half), of_pack(sine, half)] + place_blocks(places) + [still(wo)]
    ins += [of_pack(kv, half) for kv in kvs]
    lanes = 2 * HEAD_SIZE
    outs = [of_pack(low(*q.shape), half)]
    outs.append((low(q.shape[1], 2 * cycle * lanes), (half, 2 * cycle * lanes), lambda p: (p, 0)))
    kernel = functools.partial(attend_back_kernel, groups)
    return gridded(kernel, packs, ins, outs, scalars=(here,))


def split_heads(
    hidden_in,
    out_cotangent,
    norm1_gain,
    q_weight,
    key_projection_weight,
    value_projection_weight,
    o_weight,
    norm2_gain,
    gate_weight,
    up_weight,
    down_weight,
    seq_lengths,
    span_order,
):
    packs = lax.axis_size("fsdp")
    cycle = lax.axis_size("ctx")
    pack = lax.axis_index("fsdp")
    core = lax.axis_index("tp")
    here = lax.axis_index("ctx")
    rows = hidden_in.shape[0]
    half = rows // 2
    tokens = packs * rows
    depth = q_weight.shape[0]
    width = depth * packs
    q_width = q_weight.shape[1] // packs
    k_width = key_projection_weight.shape[1] // packs
    ff_width = gate_weight.shape[1] // packs
    ff_half = ff_width // 2
    groups = q_width // k_width
    far = range(1, packs)
    steps = Steps(Line("ctx"))
    kept = {}


    def columns(weight, k, count, first=0, of=None):
        return lax.dynamic_slice_in_dim(weight, (pack ^ k) * (of or count) + first, count, 1)

    def to_pack(name, k, array):
        return ((name, k), array, "fsdp", pairs_by(k, packs))

    def send_all(name, arrays):
        return [to_pack(name, k, array) for k, array in zip(far, arrays)]

    def arrived(name):
        return [steps.take((name, k)) for k in far]

    def to_core(name, array):
        return [(name, array, "tp", pairs_by(1, 2))]

    def to_rows(name, first):
        kept[name], *others = fold(first, steps.take(name), packs)
        return send_all(name, others)

    def joined(name, own, others):
        kept[name] = join(own, others)
        return to_core(name, kept[name])

    def both_of(name):
        return kept[name], steps.take(name)

    index = jnp.stack([pack, core]).astype(jnp.int32)
    here_arg = here.astype(jnp.int32)[None]
    side_arg = here_arg & 1
    at_end = steps.line.at_end

    meta = jnp.concatenate([span_order[0], seq_lengths[0]])
    order_len, meta_len = span_order.shape[1], meta.shape[0]
    info = jnp.concatenate(
        [norm1_gain, norm2_gain, (meta // 32).astype(jnp.bfloat16), (meta % 32).astype(jnp.bfloat16)]
    )
    info = jnp.pad(info, (0, width - info.shape[0]))[None]
    own_in, *in_moves = prepare(
        hidden_in, index, packs, (jnp.pad(info, ((0, 15), (0, 0))),)
    )
    own_cot, *cot_moves = prepare(out_cotangent, index, packs)

    def attention_piece(k):
        return jnp.concatenate(
            [
                columns(q_weight, k, q_width),
                columns(key_projection_weight, k, k_width),
                columns(value_projection_weight, k, k_width),
                columns(o_weight, k, q_width),
            ],
            axis=1,
        )

    steps.step(send_all("in", in_moves))
    steps.step([to_pack("attention", k, attention_piece(k)) for k in far])
    came = arrived("in")
    all_in = join(own_in, came)
    all_in = (all_in, swap(all_in, "tp", 1))
    infos = jnp.concatenate([info] + [block[half : half + 1] for block in came], axis=0)
    all_gains = infos[:, : 2 * depth].astype(jnp.float32)
    gain_one = all_gains[:, :depth].reshape(1, -1)
    gain_two = all_gains[:, depth:].reshape(1, -1)
    metas = infos[:, 2 * depth : 2 * depth + 2 * meta_len].astype(jnp.int32)
    metas = metas[:, :meta_len] * 32 + metas[:, meta_len:]
    orders, lengths = metas[:, :order_len], metas[:, order_len:]

    others = jnp.stack([here ^ j for j in range(cycle)])
    first = jnp.sum(
        jnp.where(
            others[None, :, None] == jnp.arange(order_len, dtype=jnp.int32)[None, None, :],
            orders[:, None, :],
            0,
        ),
        axis=2,
    )
    halves = jnp.stack([core, core ^ 1])[None, None, :]
    section = jnp.where(halves == 0, first[:, :, None], 2 * cycle - 1 - first[:, :, None])
    places = section[..., None] * half + jnp.arange(half, dtype=jnp.int32)
    places = places.reshape(packs, cycle * rows)
    starts = jnp.zeros_like(places)
    end = jnp.zeros((packs, 1), jnp.int32)
    for j in range(lengths.shape[1]):
        end = end + lengths[:, j : j + 1]
        starts = jnp.where(places >= end, end, starts)
    place_args = (places[:, :rows, None], starts[:, :rows, None], places[:, None, :])
    offsets = (places - starts)[:, :rows].reshape(packs, 2, half).transpose(1, 0, 2)
    frequency = jnp.exp(
        -math.log(500000.0)
        * (jnp.arange(2 * HEAD_SIZE) % (HEAD_SIZE // 2)).astype(jnp.float32)
        * 2.0
        / HEAD_SIZE
    )
    angles = offsets.astype(jnp.float32).reshape(2, tokens // 2, 1) * frequency[None, None, :]
    cosine, sine = jnp.cos(angles), jnp.sin(angles)

    side = here & 1

    def two_halves(weight, k):
        return jnp.concatenate(
            [
                columns(weight, k, ff_half, side * ff_half, ff_width),
                columns(weight, k, ff_half, (1 - side) * ff_half, ff_width),
            ],
            axis=1,
        )

    def fetch(ks):
        return [
            to_pack(
                "gate_up",
                k,
                jnp.concatenate(
                    [
                        columns(weight, k, ff_half, side * ff_half, ff_width)
                        for weight in (gate_weight, up_weight)
                    ],
                    axis=1,
                ),
            )
            for k in ks
        ]

    def to_neighbour(k):
        return [(("neighbour", k), fetched[k], "ctx", pairs_by(1, cycle))]

    fetched = {}
    _, cosine, sine, *place_args = steps.step(
        fetch([1, 2]), carry=(all_in[1], cosine, sine, *place_args)
    )
    attention_pieces = [attention_piece(0)] + arrived("attention")
    normed_mine, normed_other, q_rot, kv_own, wqkv, wo = project_qkv(
        all_in, gain_one, cosine, sine, attention_pieces, q_width, 2 * k_width
    )
    normed_one = (normed_mine, normed_other)
    steps.step(
        [(("kv", j), kv_own, "ctx", pairs_by(j, cycle)) for j in range(1, cycle)] + fetch([3])
    )
    fetched[1], fetched[2] = steps.take(("gate_up", 1)), steps.take(("gate_up", 2))
    steps.step(send_all("cot", cot_moves) + to_neighbour(1))
    fetched[3] = steps.take(("gate_up", 3))
    kvs = [kv_own] + [steps.take(("kv", j)) for j in range(1, cycle)]
    attn, first, second = attend(q_rot, place_args, wo, kvs, packs, groups)
    attn_low = attn.reshape(tokens, q_width)
    steps.step(to_core("branch", second))
    steps.step(to_neighbour(2), late=lambda: to_rows("branch", first))
    kept["cot"] = join(own_cot, arrived("cot"))

    def middle_moves():
        kept["middle"], kept["normed"], *sends = in_vmem(
            functools.partial(middle_kernel, packs),
            [full(half, width)] + [low(half, width)] * packs,
            own_in,
            gain_two,
            kept["branch"],
            *arrived("branch"),
        )
        return send_all("two", sends)

    steps.step(to_neighbour(3) + to_core("cot", kept["cot"]), late=middle_moves)

    def wd_moves(ks):
        return [to_pack("down", k, two_halves(down_weight, k)) for k in ks]

    own_columns = [two_halves(weight, 0) for weight in (gate_weight, up_weight, down_weight)]
    own_gate, own_up, own_down = steps.step(
        wd_moves([1, 2]),
        late=lambda: joined("two", kept["normed"], arrived("two")),
        carry=own_columns,
    )
    all_cot = both_of("cot")
    neighbours = [steps.take(("neighbour", k)) for k in far]
    names = [name for name in steps.names]
    kept_two = steps.flying[names.index("two")]
    normed_two = (kept["two"], kept_two)

    gate_val, up_val, hidden, wg, wu = gate_up(
        normed_two, own_gate, own_up, [fetched[k] for k in far], neighbours
    )
    d_wd = weight_grad([(*all_cot, hidden)], packs, side_arg)

    def back(name, grad, ks):
        return [to_pack(name, k, grad[k]) for k in ks]

    def entry(name, k, grad=None):
        return ((name, k), grad[0] if k == 0 else None)

    steps.step(back("wd", d_wd, [1, 2]), summed=entry("wd", 0, d_wd))
    steps.step(wd_moves([3]), summed=entry("wd", 1))
    steps.step(back("wd", d_wd, [3]), summed=entry("wd", 2))
    d_gate, d_up, wd = units_back(all_cot, [own_down] + arrived("down"), gate_val, up_val)
    first, second = rows_sum([d_gate, d_up], [wg, wu])
    steps.step(to_core("d_two", second), summed=entry("wd", 3))
    d_wg = weight_grad([(*normed_two, d_gate)], packs, side_arg)
    steps.step(back("wg", d_wg, [1, 2]), summed=entry("wg", 0, d_wg))
    d_wu = weight_grad([(*normed_two, d_up)], packs, side_arg)
    steps.step(
        summed=entry("wu", 0, d_wu), late=functools.partial(to_rows, "d_two", first)
    )

    def branch_back():
        kept["d_middle"], kept["d_gain_two"], kept["d_branch"], *sends = in_vmem(
            functools.partial(branch_back_kernel, packs),
            [full(half, width), full(1, width)] + [low(half, width)] * packs,
            kept["middle"],
            gain_two,
            own_cot,
            kept["d_two"],
            *arrived("d_two"),
        )
        return send_all("d_branch", sends)

    first, second = rows_sum([hidden], [wd])
    steps.step(summed=entry("wg", 1), late=branch_back, carry=(first, second))
    steps.step(
        back("wg", d_wg, [3]),
        summed=entry("wg", 2),
        late=lambda: joined("all_branch", kept["d_branch"], arrived("d_branch")),
    )
    d_branch = None

    def attention_back():
        return attend_back(
            here_arg, q_rot, d_branch, cosine, sine, place_args, wo, kvs, packs, groups
        )

    sums = steps.line.sums

    def settle_all(name):
        return settle(at_end, index, [sums[name, k] for k in range(packs)], ff_width)

    steps.step(back("wu", d_wu, [1, 2]), summed=entry("wg", 3))
    d_branch = both_of("all_branch")
    d_q, d_kv = attention_back()
    steps.step(back("wu", d_wu, [3]), summed=("d_kv", d_kv))
    down_grad = settle_all("wd")
    steps.step(to_core("ff", second), summed=entry("wu", 1))
    (down_grad,) = steps.step(
        summed=entry("wu", 2),
        late=functools.partial(to_rows, "ff", first),
        carry=(down_grad,),
    )
    steps.step(summed=entry("wu", 3))
    d_qkv = in_vmem(
        d_qkv_kernel,
        [low(tokens, q_width + 2 * k_width)],
        at_end,
        here_arg,
        *sums["d_kv"],
        d_q,
        cosine,
        sine,
        scalars=2,
    )[0]
    d_wqkvo = weight_grad([(*normed_one, d_qkv), (*d_branch, attn_low)], packs)
    first, second = rows_sum([d_qkv], [wqkv])
    result = in_vmem(
        result_kernel, [low(half, width)], kept["middle"], kept["ff"], *arrived("ff")
    )[0]
    steps.step(
        back("wqkvo", d_wqkvo, [1, 2]) + to_core("d_one", second) + to_core("result", result),
        summed=entry("wqkvo", 0, d_wqkvo),
    )
    steps.step(back("wqkvo", d_wqkvo, [3]), summed=entry("wqkvo", 1))

    def both_rows(own, other):
        return in_vmem(
            functools.partial(rows_back_kernel, packs),
            [low(rows, width)],
            index,
            own,
            other,
            scalars=1,
        )[0]

    out_hidden = both_rows(result, steps.take("result"))
    gate_grad = settle_all("wg")
    out_hidden, gate_grad = steps.step(
        summed=entry("wqkvo", 2),
        late=functools.partial(to_rows, "d_one", first),
        carry=(out_hidden, gate_grad),
    )
    up_grad = settle_all("wu")

    def gains_to_core():
        kept["in_grad"], d_gain_one = in_vmem(
            functools.partial(in_grad_kernel, packs),
            [low(half, width), full(1, width)],
            own_in,
            gain_one,
            kept["d_middle"],
            kept["d_one"],
            *arrived("d_one"),
        )
        kept["gains"] = jnp.concatenate([d_gain_one, kept["d_gain_two"]], axis=0)
        return to_core("gains", kept["gains"]) + to_core("in_grad", kept["in_grad"])

    def gains_to_packs():
        kept["gains"] = kept["gains"] + steps.take("gains")
        return [to_pack("gains", k, kept["gains"][:, k * depth : (k + 1) * depth]) for k in far]

    def gains_along():
        kept["gains"] = kept["gains"][:, :depth]
        for k in far:
            kept["gains"] = kept["gains"] + steps.take(("gains", k))
        return [(("gains", j), kept["gains"], "ctx", pairs_by(j, cycle)) for j in range(1, cycle)]

    (up_grad,) = steps.step(summed=entry("wqkvo", 3), late=gains_to_core, carry=(up_grad,))
    steps.step(late=gains_to_packs)
    in_grad = both_rows(kept["in_grad"], steps.take("in_grad"))
    (in_grad,) = steps.step(late=gains_along, carry=(in_grad,))
    steps.step()
    shares_of_gains = jnp.stack(
        [kept["gains"]] + [steps.take(("gains", j)) for j in range(1, cycle)]
    )
    gains = 0.0
    for place in range(cycle):
        gains = gains + lax.dynamic_index_in_dim(shares_of_gains, here ^ place, 0, keepdims=False)
    q_grad, k_grad, v_grad, o_grad = settle_attention(
        at_end, index, [sums["wqkvo", k] for k in range(packs)], q_width, 2 * k_width
    )
    return (
        out_hidden,
        in_grad,
        gains[0],
        q_grad,
        k_grad,
        v_grad,
        o_grad,
        gains[1],
        gate_grad,
        up_grad,
        down_grad,
    )


def gathered_weights(
    hidden_in,
    out_cotangent,
    norm1_gain,
    q_weight,
    key_projection_weight,
    value_projection_weight,
    o_weight,
    norm2_gain,
    gate_weight,
    up_weight,
    down_weight,
    seq_lengths,
    span_order,
):
    rows_here = hidden_in.shape[0]
    order_row = span_order[0]
    length_row = seq_lengths[0]
    kv_heads = key_projection_weight.shape[1] // HEAD_SIZE
    query_groups = QUERY_HEADS // KEY_VALUE_HEADS
    score_scale = 1.0 / math.sqrt(HEAD_SIZE)
    whole_rows = rows_here * lax.axis_size("ctx")
    local_rows = lax.axis_index("ctx") * rows_here + jnp.arange(rows_here, dtype=jnp.int32)
    q_place, q_segment, q_offset = stream_place(local_rows, order_row, length_row, rows_here)
    inputs = hidden_in.astype(jnp.float32)
    gain_one, wq_full, wk_full, wv_full, wo_full = (
        lax.all_gather(norm1_gain, "fsdp", axis=0, tiled=True),
        lax.all_gather(q_weight, "fsdp", axis=0, tiled=True),
        lax.all_gather(key_projection_weight, "fsdp", axis=0, tiled=True),
        lax.all_gather(value_projection_weight, "fsdp", axis=0, tiled=True),
        lax.all_gather(o_weight, "fsdp", axis=0, tiled=True),
    )
    gain_one = gain_one.astype(jnp.float32)
    first_normalized = normalize(inputs, gain_one)
    normed_low = first_normalized.astype(jnp.bfloat16)
    q_linear = jnp.dot(normed_low, wq_full, preferred_element_type=jnp.float32).reshape(
        rows_here, kv_heads * query_groups, HEAD_SIZE
    )
    k_linear = jnp.dot(normed_low, wk_full, preferred_element_type=jnp.float32).reshape(
        rows_here, kv_heads, HEAD_SIZE
    )
    q_rotated = (
        rotary_embedding(q_linear, q_offset)
        .astype(jnp.bfloat16)
        .reshape(rows_here, kv_heads, query_groups, HEAD_SIZE)
    )
    k_rotated = (
        rotary_embedding(k_linear, q_offset)
        .astype(jnp.bfloat16)
        .reshape(rows_here, kv_heads * HEAD_SIZE)
    )
    v_low = jnp.dot(normed_low, wv_full, preferred_element_type=jnp.float32).astype(jnp.bfloat16)

    def key_blocks(shard_rows):
        row_count = shard_rows.shape[0]
        key_total_width = math.gcd(row_count, 512)
        number = row_count // key_total_width
        k_place, k_segment, _ = stream_place(
            jnp.arange(row_count, dtype=jnp.int32), order_row, length_row, rows_here
        )
        return (
            key_total_width,
            number,
            k_place.reshape(number, key_total_width),
            k_segment.reshape(number, key_total_width),
        )

    def scores_of(key_block, place_block, segment_block):
        scores = (
            jnp.einsum("qkgd,skd->kgqs", q_rotated, key_block, preferred_element_type=jnp.float32)
            * score_scale
        )
        visible = (
            (q_place[:, None] >= place_block[None, :])
            & (q_segment[:, None] == segment_block[None, :])
        )[None, None]
        return (jnp.where(visible, scores, -1e30), visible)

    start_state = (
        jnp.full((kv_heads, query_groups, rows_here), -1e30, jnp.float32),
        jnp.zeros((kv_heads, query_groups, rows_here), jnp.float32),
        jnp.zeros((kv_heads, query_groups, rows_here, HEAD_SIZE), jnp.float32),
    )
    folded = start_state
    key_row_block = lax.all_gather(k_rotated, "ctx", axis=0, tiled=True)
    value_row_block = lax.all_gather(v_low, "ctx", axis=0, tiled=True)
    key_total_width, number, k_place, k_segment = key_blocks(key_row_block)

    def one_step(carried, pieces):
        running_max, totals, accumulated = carried
        key_block, value_block, place_block, segment_block = pieces
        scores, visible = scores_of(key_block, place_block, segment_block)
        new_max = jnp.maximum(running_max, jnp.max(scores, axis=-1))
        weights = jnp.where(visible, jnp.exp(scores - new_max[..., None]), 0.0)
        factor = jnp.exp(running_max - new_max)
        totals = totals * factor + jnp.sum(weights, axis=-1)
        accumulated = accumulated * factor[..., None] + jnp.einsum(
            "kgqs,skd->kgqd",
            weights.astype(jnp.bfloat16),
            value_block,
            preferred_element_type=jnp.float32,
        )
        return ((new_max, totals, accumulated), None)

    pieces = (
        key_row_block.reshape(number, key_total_width, kv_heads, HEAD_SIZE),
        value_row_block.reshape(number, key_total_width, kv_heads, HEAD_SIZE),
        k_place,
        k_segment,
    )
    folded, _ = lax.scan(one_step, folded, pieces)
    running_max, totals, accumulated = folded
    mixed_out = jnp.transpose(accumulated / totals[..., None], (2, 0, 1, 3))
    log_sum = running_max + jnp.log(totals)
    attn_low = mixed_out.reshape(rows_here, kv_heads * query_groups * HEAD_SIZE).astype(
        jnp.bfloat16
    )
    branch = lax.psum(contract_last(attn_low, wo_full).astype(jnp.bfloat16), "tp").astype(
        jnp.float32
    )
    middle = inputs + branch
    gain_two, wg_full, wu_full, wd_full = (
        lax.all_gather(norm2_gain, "fsdp", axis=0, tiled=True),
        lax.all_gather(gate_weight, "fsdp", axis=0, tiled=True),
        lax.all_gather(up_weight, "fsdp", axis=0, tiled=True),
        lax.all_gather(down_weight, "fsdp", axis=0, tiled=True),
    )
    gain_two = gain_two.astype(jnp.float32)
    normed_two = normalize(middle, gain_two)
    normed_two_low = normed_two.astype(jnp.bfloat16)
    gate_val = jnp.dot(normed_two_low, wg_full, preferred_element_type=jnp.float32)
    up_val = jnp.dot(normed_two_low, wu_full, preferred_element_type=jnp.float32)
    hidden = swiglu(gate_val, up_val).astype(jnp.bfloat16)
    ffn_out = lax.psum(contract_last(hidden, wd_full).astype(jnp.bfloat16), "tp").astype(
        jnp.float32
    )
    result = (middle + ffn_out).astype(jnp.bfloat16)
    grad_out = out_cotangent.astype(jnp.float32)
    d_wd = contract_first(out_cotangent, hidden)
    d_hidden = jnp.dot(out_cotangent, wd_full, preferred_element_type=jnp.float32)
    _, swiglu_back = jax.vjp(swiglu, gate_val, up_val)
    d_gate, d_up = swiglu_back(d_hidden)
    d_gate_low = d_gate.astype(jnp.bfloat16)
    d_up_low = d_up.astype(jnp.bfloat16)
    d_wg = contract_first(normed_two_low, d_gate_low)
    d_wu = contract_first(normed_two_low, d_up_low)
    d_normed_two = lax.psum(
        (contract_last(d_gate_low, wg_full) + contract_last(d_up_low, wu_full)).astype(
            jnp.bfloat16
        ),
        "tp",
    ).astype(jnp.float32)
    _, norm_two_back = jax.vjp(normalize, middle, gain_two)
    d_middle_norm, d_gain_two = norm_two_back(d_normed_two)
    d_middle = grad_out + d_middle_norm
    d_branch_low = d_middle.astype(jnp.bfloat16)
    d_wo = contract_first(d_branch_low, attn_low)
    d_attn = jnp.dot(d_branch_low, wo_full, preferred_element_type=jnp.float32).astype(jnp.bfloat16)
    d_attn_heads = d_attn.reshape(rows_here, kv_heads, query_groups, HEAD_SIZE)
    row_delta = jnp.einsum("qkgd,qkgd->kgq", d_attn_heads.astype(jnp.float32), mixed_out)
    back_state = (
        jnp.zeros((rows_here, kv_heads, query_groups, HEAD_SIZE), jnp.float32),
        jnp.zeros((whole_rows, kv_heads, HEAD_SIZE), jnp.float32),
        jnp.zeros((whole_rows, kv_heads, HEAD_SIZE), jnp.float32),
    )
    folded = back_state
    key_row_block = lax.all_gather(k_rotated, "ctx", axis=0, tiled=True)
    value_row_block = lax.all_gather(v_low, "ctx", axis=0, tiled=True)
    key_total_width, number, k_place, k_segment = key_blocks(key_row_block)

    def one_step(carried, pieces):
        d_query, d_keys, d_values = carried
        key_block, value_block, place_block, segment_block, step_index = pieces
        scores, visible = scores_of(key_block, place_block, segment_block)
        prob_rows = jnp.where(visible, jnp.exp(scores - log_sum[..., None]), 0.0)
        d_values_block = jnp.einsum(
            "kgqs,qkgd->skd",
            prob_rows.astype(jnp.bfloat16),
            d_attn_heads,
            preferred_element_type=jnp.float32,
        )
        d_probs = jnp.einsum(
            "qkgd,skd->kgqs", d_attn_heads, value_block, preferred_element_type=jnp.float32
        )
        d_scores = (prob_rows * (d_probs - row_delta[..., None])).astype(jnp.bfloat16)
        d_query = (
            d_query
            + jnp.einsum("kgqs,skd->qkgd", d_scores, key_block, preferred_element_type=jnp.float32)
            * score_scale
        )
        d_keys_block = (
            jnp.einsum("kgqs,qkgd->skd", d_scores, q_rotated, preferred_element_type=jnp.float32)
            * score_scale
        )
        row_first = step_index * key_total_width
        d_keys = lax.dynamic_update_slice_in_dim(
            d_keys,
            lax.dynamic_slice_in_dim(d_keys, row_first, key_total_width, 0) + d_keys_block,
            row_first,
            0,
        )
        d_values = lax.dynamic_update_slice_in_dim(
            d_values,
            lax.dynamic_slice_in_dim(d_values, row_first, key_total_width, 0) + d_values_block,
            row_first,
            0,
        )
        return ((d_query, d_keys, d_values), None)

    pieces = (
        key_row_block.reshape(number, key_total_width, kv_heads, HEAD_SIZE),
        value_row_block.reshape(number, key_total_width, kv_heads, HEAD_SIZE),
        k_place,
        k_segment,
        jnp.arange(number, dtype=jnp.int32),
    )
    folded, _ = lax.scan(one_step, folded, pieces)
    d_query, d_keys_all, d_values_all = folded
    d_key_own, d_value_own = (
        lax.psum_scatter(
            d_keys_all.astype(jnp.bfloat16), "ctx", scatter_dimension=0, tiled=True
        ).astype(jnp.float32),
        lax.psum_scatter(
            d_values_all.astype(jnp.bfloat16), "ctx", scatter_dimension=0, tiled=True
        ).astype(jnp.float32),
    )
    _, rope_q_back = jax.vjp(lambda rotated_in: rotary_embedding(rotated_in, q_offset), q_linear)
    _, rope_k_back = jax.vjp(lambda rotated_in: rotary_embedding(rotated_in, q_offset), k_linear)
    (d_q_linear,) = rope_q_back(d_query.reshape(rows_here, kv_heads * query_groups, HEAD_SIZE))
    (d_k_linear,) = rope_k_back(d_key_own)
    d_q_low = d_q_linear.reshape(rows_here, kv_heads * query_groups * HEAD_SIZE).astype(
        jnp.bfloat16
    )
    d_k_low = d_k_linear.reshape(rows_here, kv_heads * HEAD_SIZE).astype(jnp.bfloat16)
    d_v_low = d_value_own.reshape(rows_here, kv_heads * HEAD_SIZE).astype(jnp.bfloat16)
    d_wq = contract_first(normed_low, d_q_low)
    d_wk = contract_first(normed_low, d_k_low)
    d_wv = contract_first(normed_low, d_v_low)
    d_normed_one = lax.psum(
        (
            contract_last(d_q_low, wq_full)
            + contract_last(d_k_low, wk_full)
            + contract_last(d_v_low, wv_full)
        ).astype(jnp.bfloat16),
        "tp",
    ).astype(jnp.float32)
    _, norm_one_back = jax.vjp(normalize, inputs, gain_one)
    d_inputs_norm, d_gain_one = norm_one_back(d_normed_one)
    in_grad = (d_middle + d_inputs_norm).astype(jnp.bfloat16)
    weight_grads = (d_gain_one, d_wq, d_wk, d_wv, d_wo, d_gain_two, d_wg, d_wu, d_wd)
    shares = (
        lax.psum_scatter(weight_grads[0], ("fsdp", "ctx"), scatter_dimension=0, tiled=True),
        lax.psum_scatter(weight_grads[1], ("fsdp", "ctx"), scatter_dimension=0, tiled=True),
        lax.psum_scatter(weight_grads[2], ("fsdp", "ctx"), scatter_dimension=0, tiled=True),
        lax.psum_scatter(weight_grads[3], ("fsdp", "ctx"), scatter_dimension=0, tiled=True),
        lax.psum_scatter(weight_grads[4], ("fsdp", "ctx"), scatter_dimension=0, tiled=True),
        lax.psum_scatter(weight_grads[5], ("fsdp", "ctx"), scatter_dimension=0, tiled=True),
        lax.psum_scatter(weight_grads[6], ("fsdp", "ctx"), scatter_dimension=0, tiled=True),
        lax.psum_scatter(weight_grads[7], ("fsdp", "ctx"), scatter_dimension=0, tiled=True),
        lax.psum_scatter(weight_grads[8], ("fsdp", "ctx"), scatter_dimension=0, tiled=True),
    )
    owned_grads = (
        lax.all_gather(shares[0].astype(jnp.bfloat16), "ctx", axis=0, tiled=True).astype(
            jnp.float32
        ),
        lax.all_gather(shares[1].astype(jnp.bfloat16), "ctx", axis=0, tiled=True).astype(
            jnp.float32
        ),
        lax.all_gather(shares[2].astype(jnp.bfloat16), "ctx", axis=0, tiled=True).astype(
            jnp.float32
        ),
        lax.all_gather(shares[3].astype(jnp.bfloat16), "ctx", axis=0, tiled=True).astype(
            jnp.float32
        ),
        lax.all_gather(shares[4].astype(jnp.bfloat16), "ctx", axis=0, tiled=True).astype(
            jnp.float32
        ),
        lax.all_gather(shares[5].astype(jnp.bfloat16), "ctx", axis=0, tiled=True).astype(
            jnp.float32
        ),
        lax.all_gather(shares[6].astype(jnp.bfloat16), "ctx", axis=0, tiled=True).astype(
            jnp.float32
        ),
        lax.all_gather(shares[7].astype(jnp.bfloat16), "ctx", axis=0, tiled=True).astype(
            jnp.float32
        ),
        lax.all_gather(shares[8].astype(jnp.bfloat16), "ctx", axis=0, tiled=True).astype(
            jnp.float32
        ),
    )
    return (
        result,
        in_grad,
        owned_grads[0],
        owned_grads[1],
        owned_grads[2],
        owned_grads[3],
        owned_grads[4],
        owned_grads[5],
        owned_grads[6],
        owned_grads[7],
        owned_grads[8],
    )


def solution(mesh):
    placed = (
        P(("fsdp", "ctx"), None),
        P(("fsdp", "ctx"), None),
        P("fsdp"),
        P("fsdp", "tp"),
        P("fsdp", "tp"),
        P("fsdp", "tp"),
        P("fsdp", "tp"),
        P("fsdp"),
        P("fsdp", "tp"),
        P("fsdp", "tp"),
        P("fsdp", "tp"),
        P("fsdp", None),
        P("fsdp", None),
    )
    plane = mesh.shape["fsdp"] * mesh.shape["tp"]
    splits = mesh.shape["tp"] == 2 and KEY_VALUE_HEADS == plane and mesh.shape["ctx"] == 4
    return jax.shard_map(
        split_heads if splits else gathered_weights,
        mesh=mesh,
        in_specs=placed,
        out_specs=(
            P(("fsdp", "ctx"), None),
            P(("fsdp", "ctx"), None),
            P("fsdp"),
            P("fsdp", "tp"),
            P("fsdp", "tp"),
            P("fsdp", "tp"),
            P("fsdp", "tp"),
            P("fsdp"),
            P("fsdp", "tp"),
            P("fsdp", "tp"),
            P("fsdp", "tp"),
        ),
        check_vma=False,
    )
```

```python
import functools
import math

import jax
import jax.numpy as jnp
from jax import lax
from jax.experimental import pallas as pl
from jax.experimental.pallas import tpu as pltpu
from jax.sharding import PartitionSpec as P

QUERY_HEADS = 32
KEY_VALUE_HEADS = 8
HEAD_SIZE = 64


def stream_place(row_ids, order_row, length_row, tok_dev):
    cycle_size = order_row.shape[0]
    half_len = tok_dev // 2
    cycle_rank = row_ids // tok_dev
    within = row_ids % tok_dev
    first_section = jnp.sum(
        jnp.where(
            cycle_rank[:, None] == jnp.arange(cycle_size, dtype=jnp.int32)[None, :],
            order_row[None, :],
            0,
        ),
        axis=1,
        dtype=jnp.int32,
    )
    section = jnp.where(within >= half_len, 2 * cycle_size - 1 - first_section, first_section)
    places = section * half_len + within % half_len
    seq_ends = jnp.cumsum(length_row, dtype=jnp.int32)
    passed = places[:, None] >= seq_ends[None, :]
    segment = jnp.sum(passed.astype(jnp.int32), axis=1, dtype=jnp.int32)
    offset = places - jnp.sum(jnp.where(passed, length_row[None, :], 0), axis=1, dtype=jnp.int32)
    return (places, segment, offset)


def rotary_embedding(values, positions):
    half_len = values.shape[-1] // 2
    frequency = jnp.exp(
        -math.log(500000.0) * jnp.arange(half_len, dtype=jnp.float32) * 2.0 / values.shape[-1]
    )
    angles = positions.astype(jnp.float32)[:, None] * frequency[None, :]
    cosine = jnp.cos(angles)[:, None, :]
    sine = jnp.sin(angles)[:, None, :]
    lower_half = values[..., :half_len]
    upper_half = values[..., half_len:]
    return jnp.concatenate(
        [lower_half * cosine - upper_half * sine, upper_half * cosine + lower_half * sine], axis=-1
    )


def normalize(values, gain_vec):
    return values * lax.rsqrt(jnp.mean(values * values, axis=-1, keepdims=True) + 1e-05) * gain_vec


def swiglu(gate_val, up_val):
    return jax.nn.silu(gate_val) * up_val


def contract_last(left, right):
    return lax.dot_general(
        left, right, (((1,), (1,)), ((), ())), preferred_element_type=jnp.float32
    )


def contract_first(left, right):
    return lax.dot_general(
        left, right, (((0,), (0,)), ((), ())), preferred_element_type=jnp.float32
    )


VMEM_LIMIT = 32 * 1024 * 1024
SMALL_LIMIT = 12 * 1024 * 1024
SMALL = pl.CostEstimate(flops=1, bytes_accessed=1, transcendentals=0)


def pairs_by(distance, size):
    return [(i, i ^ distance) for i in range(size)]


def swap(array, axis, distance):
    return lax.ppermute(array, axis, pairs_by(distance, lax.axis_size(axis)))


class Line:
    def __init__(self, axis):
        index = lax.axis_index(axis)
        size = lax.axis_size(axis)
        self.axis = axis
        self.at_end = ((index == 0) | (index == size - 1)).astype(jnp.int32)[None]
        self.entered = self.halfway = self.leaving = None
        self.sums = {}

    def advance(self, got, entering):
        if self.leaving is not None:
            name, sent = self.leaving
            self.sums[name] = (got["ends"], sent)
        moves = []
        halfway = None
        if self.entered is not None:
            name, value = self.entered
            halfway = (name, add_low(value, got["ends"]))
            moves.append(("middle", halfway[1], self.axis, [(1, 2), (2, 1)]))
        leaving = None
        inwards, outwards = [(0, 1), (3, 2)], [(1, 0), (2, 3)]
        if self.halfway is not None:
            name, value = self.halfway
            if entering is None:
                sent, pairs = add_low(value, got["middle"]), outwards
            else:
                sent = either_way(self.at_end, entering[1], value, got["middle"])
                pairs = inwards + outwards
            leaving = (name, sent)
            moves.append(("ends", sent, self.axis, pairs))
        elif entering is not None:
            moves.append(("ends", entering[1], self.axis, inwards))
        self.entered, self.halfway, self.leaving = entering, halfway, leaving
        return moves


class Steps:
    def __init__(self, line):
        self.line = line
        self.got = {}
        self.on_line = []
        self.others = []
        self.token = jnp.zeros((8, 128), jnp.float32)

    def wait(self, flying, arrays):
        count = len(flying)
        held = lax.optimization_barrier(
            (self.token,) + tuple(value for _, value in flying) + tuple(arrays)
        )
        self.token = held[0]
        for (name, _), value in zip(flying, held[1:]):
            self.got[name] = value
        return list(held[1 + count :])

    def start(self, moves):
        return [(name, lax.ppermute(value, axis, pairs)) for name, value, axis, pairs in moves]

    def step(self, moves=(), summed=None, late=None, carry=()):
        moves, carry = list(moves), list(carry)
        arrays = [move[1] for move in moves] + carry
        fresh = [summed[1]] if summed is not None and summed[1] is not None else []
        together = summed is not None and not fresh and summed[0] not in self.got
        if together or not self.on_line:
            held = self.wait(self.on_line + self.others, fresh + arrays)
            held_fresh, held = held[: len(fresh)], held[len(fresh) :]
        else:
            held_fresh = self.wait(self.on_line, fresh)
        entering = summed
        if summed is not None:
            entering = (summed[0], held_fresh[0] if fresh else self.take(summed[0]))
        along = self.line.advance(self.got, entering)
        if not together and self.on_line:
            self.on_line = self.start(along)
            held = self.wait(self.others, arrays)
        else:
            self.on_line = self.start(along)
        moves = [
            (name, value, axis, pairs) for (name, _, axis, pairs), value in zip(moves, held)
        ]
        self.others = self.start(moves + (late() if late is not None else []))
        return held[len(moves) :]

    def take(self, name):
        return self.got.pop(name)


def in_vmem(kernel, out_shape, *args, scalars=0):
    specs = [pl.BlockSpec(memory_space=pltpu.SMEM)] * scalars
    specs += [pl.BlockSpec(memory_space=pltpu.VMEM)] * (len(args) - scalars)
    return pl.pallas_call(
        kernel,
        out_shape=out_shape,
        in_specs=specs,
        out_specs=[pl.BlockSpec(memory_space=pltpu.VMEM)] * len(out_shape),
        compiler_params=pltpu.CompilerParams(vmem_limit_bytes=SMALL_LIMIT),
        cost_estimate=SMALL,
    )(*args)


def low(*shape):
    return jax.ShapeDtypeStruct(shape, jnp.bfloat16)


def full(*shape):
    return jax.ShapeDtypeStruct(shape, jnp.float32)


def store_seen(ref, value, distance, count):
    width = value.shape[-1] // count
    for block in range(count):
        there = block ^ distance
        ref[: value.shape[0], block * width : (block + 1) * width] = value[
            :, there * width : (there + 1) * width
        ]


def prepare_kernel(count, index_ref, x_ref, *refs):
    extra_ref = refs[0] if len(refs) > count else None
    own_ref, *sends = refs[-count:]
    rows, width = own_ref.shape[0], own_ref.shape[1] // count
    first = pl.multiple_of(index_ref[1] * rows, rows)
    for block in range(count):
        column = pl.multiple_of((index_ref[0] ^ block) * width, width)
        own_ref[:, block * width : (block + 1) * width] = x_ref[
            pl.ds(first, rows), pl.ds(column, width)
        ]
    for k in range(1, count):
        store_seen(sends[k - 1], own_ref[...], k, count)
        if extra_ref is not None:
            sends[k - 1][rows:, :] = extra_ref[...]


def prepare(x, index, count, extra=()):
    rows, width = x.shape[0] // 2, x.shape[1]
    more = extra[0].shape[0] if extra else 0
    return in_vmem(
        functools.partial(prepare_kernel, count),
        [low(rows, width)] + [low(rows + more, width)] * (count - 1),
        index,
        x,
        *extra,
        scalars=1,
    )


def join_kernel(*refs):
    out_ref = refs[-1]
    rows = refs[0].shape[0]
    for i, ref in enumerate(refs[:-1]):
        out_ref[i * rows : (i + 1) * rows, :] = ref[:rows, :]


def join(own, others):
    rows, width = own.shape
    return in_vmem(join_kernel, [low(rows * (1 + len(others)), width)], own, *others)[0]


def fold_kernel(count, first_ref, came_ref, own_ref, *sends):
    rows = own_ref.shape[0]
    for k in range(count):
        here = slice(k * rows, (k + 1) * rows)
        total = first_ref[here, :].astype(jnp.float32) + came_ref[here, :].astype(jnp.float32)
        total = total.astype(jnp.bfloat16)
        if k == 0:
            own_ref[...] = total
        else:
            store_seen(sends[k - 1], total, k, count)


def fold(first, came, count):
    rows, width = first.shape[0] // count, first.shape[1]
    return in_vmem(
        functools.partial(fold_kernel, count), [low(rows, width)] * count, first, came
    )


def total_of(refs):
    total = refs[0][...].astype(jnp.float32)
    for ref in refs[1:]:
        total = total + ref[...].astype(jnp.float32)
    return total


def middle_kernel(count, in_ref, gain_ref, *refs):
    parts, (middle_ref, normed_ref, *sends) = refs[:count], refs[count:]
    middle = in_ref[...].astype(jnp.float32) + total_of(parts)
    middle_ref[...] = middle
    mean = jnp.mean(middle * middle, axis=-1, keepdims=True)
    normed = (middle * lax.rsqrt(mean + 1e-05) * gain_ref[...]).astype(jnp.bfloat16)
    normed_ref[...] = normed
    for k in range(1, count):
        store_seen(sends[k - 1], normed, k, count)


def norm_back(d_normed, x, gain):
    scale = lax.rsqrt(jnp.mean(x * x, axis=-1, keepdims=True) + 1e-05)
    unit = x * scale
    d_unit = d_normed * gain
    d_x = scale * (d_unit - unit * jnp.mean(d_unit * unit, axis=-1, keepdims=True))
    return d_x, jnp.sum(d_normed * unit, axis=0, keepdims=True)


def branch_back_kernel(count, middle_ref, gain_ref, cot_ref, *refs):
    parts, (d_middle_ref, d_gain_ref, branch_ref, *sends) = refs[:count], refs[count:]
    d_x, d_gain_ref[...] = norm_back(total_of(parts), middle_ref[...], gain_ref[...])
    d_middle = cot_ref[...].astype(jnp.float32) + d_x
    d_middle_ref[...] = d_middle
    branch = d_middle.astype(jnp.bfloat16)
    branch_ref[...] = branch
    for k in range(1, count):
        store_seen(sends[k - 1], branch, k, count)


def in_grad_kernel(count, in_ref, gain_ref, d_middle_ref, *refs):
    parts, (grad_ref, d_gain_ref) = refs[:count], refs[count:]
    x = in_ref[...].astype(jnp.float32)
    d_x, d_gain_ref[...] = norm_back(total_of(parts), x, gain_ref[...])
    grad_ref[...] = (d_middle_ref[...] + d_x).astype(jnp.bfloat16)


def gridded(kernel, steps, ins, outs, scalars=()):
    return pl.pallas_call(
        kernel,
        grid=(steps,),
        in_specs=[pl.BlockSpec(memory_space=pltpu.SMEM)] * len(scalars)
        + [pl.BlockSpec(block, index) for _, block, index in ins],
        out_specs=[pl.BlockSpec(block, index) for _, block, index in outs],
        out_shape=[shape for shape, _, _ in outs],
        compiler_params=pltpu.CompilerParams(vmem_limit_bytes=VMEM_LIMIT),
        cost_estimate=SMALL,
    )(*scalars, *[array for array, _, _ in ins])


def row_blocks(array, rows):
    return (array, (rows, array.shape[1]), lambda i: (i, 0))


def add_low(left, right):
    right = right[:, : left.shape[1]]
    return (left.astype(jnp.float32) + right.astype(jnp.float32)).astype(jnp.bfloat16)


def either_way(at_end, fresh, value, came):
    total = add_low(value, came)
    width = max(fresh.shape[1], value.shape[1])
    if fresh.shape[1] < width:
        fresh = jnp.pad(fresh, ((0, 0), (0, width - fresh.shape[1])))
    if total.shape[1] < width:
        total = jnp.pad(total, ((0, 0), (0, width - total.shape[1])))
    return jnp.where(at_end[0] == 1, fresh, total)


def settled(at_end, came_ref, sent_ref, columns):
    return jnp.where(at_end == 1, came_ref[:, columns], sent_ref[:, columns]).astype(jnp.float32)


def settle_kernel(count, at_end_ref, index_ref, *refs):
    out_ref = refs[-1]
    width = out_ref.shape[1] // count
    for k in range(count):
        column = pl.multiple_of((index_ref[0] ^ k) * width, width)
        out_ref[:, pl.ds(column, width)] = settled(
            at_end_ref[0], refs[2 * k], refs[2 * k + 1], slice(0, width)
        )


def settle(at_end, index, pairs, width):
    count = len(pairs)
    arrays = [array for pair in pairs for array in pair]
    depth = arrays[0].shape[0]
    rows = math.gcd(depth, 128)
    ins = [(array, (rows, width), lambda i: (i, 0)) for array in arrays]
    outs = [row_blocks(full(depth, width * count), rows)]
    kernel = functools.partial(settle_kernel, count)
    return gridded(kernel, depth // rows, ins, outs, scalars=(at_end, index))[0]


def settle_attention_kernel(count, q_width, kv_width, at_end_ref, index_ref, *refs):
    q_ref, k_ref, v_ref, o_ref = refs[-4:]
    o_width = o_ref.shape[1] // count
    o_first = q_width + kv_width
    kvs = []
    for k in range(count):
        came_ref, sent_ref = refs[2 * k], refs[2 * k + 1]
        column = pl.multiple_of((index_ref[0] ^ k) * q_width, q_width)
        q_ref[:, pl.ds(column, q_width)] = settled(
            at_end_ref[0], came_ref, sent_ref, slice(0, q_width)
        )
        column = pl.multiple_of((index_ref[0] ^ k) * o_width, o_width)
        o_ref[:, pl.ds(column, o_width)] = settled(
            at_end_ref[0], came_ref, sent_ref, slice(o_first, o_first + o_width)
        )
        kvs.append(settled(at_end_ref[0], came_ref, sent_ref, slice(q_width, o_first)))
    ordered = []
    for place in range(count):
        kv = kvs[0]
        for k in range(1, count):
            kv = jnp.where((index_ref[0] ^ k) == place, kvs[k], kv)
        ordered.append(kv)
    k_ref[...] = jnp.concatenate([kv[:, : kv_width // 2] for kv in ordered], axis=1)
    v_ref[...] = jnp.concatenate([kv[:, kv_width // 2 :] for kv in ordered], axis=1)


def settle_attention(at_end, index, pairs, q_width, kv_width):
    count = len(pairs)
    arrays = [array for pair in pairs for array in pair]
    depth = arrays[0].shape[0]
    width = min(array.shape[1] for array in arrays)
    o_width = width - q_width - kv_width
    rows = math.gcd(depth, 128)
    ins = [(array, (rows, width), lambda i: (i, 0)) for array in arrays]
    widths = (q_width, kv_width // 2, kv_width // 2, o_width)
    outs = [row_blocks(full(depth, each * count), rows) for each in widths]
    kernel = functools.partial(settle_attention_kernel, count, q_width, kv_width)
    return gridded(kernel, depth // rows, ins, outs, scalars=(at_end, index))


def d_qkv_kernel(at_end_ref, here_ref, came_ref, sent_ref, dq_ref, cos_ref, sin_ref, out_ref):
    lanes = 2 * HEAD_SIZE
    half, q_width = dq_ref.shape[1], dq_ref.shape[2]
    cycle = came_ref.shape[1] // lanes // 2
    for core_side in range(2):
        column = pl.multiple_of((core_side * cycle + here_ref[0]) * lanes, lanes)
        d_kv = settled(at_end_ref[0], came_ref, sent_ref, pl.ds(column, lanes))
        cosine, sine = of_keys(cos_ref[core_side], sin_ref[core_side])
        d_kv = turned(d_kv, cosine, -sine).astype(jnp.bfloat16)
        rows = slice(core_side * half, (core_side + 1) * half)
        out_ref[rows, :q_width] = dq_ref[core_side]
        out_ref[rows, q_width:] = d_kv


def rows_back_kernel(count, index_ref, own_ref, other_ref, out_ref):
    rows, width = own_ref.shape[0], own_ref.shape[1] // count
    for ref, core in ((own_ref, index_ref[1]), (other_ref, 1 - index_ref[1])):
        first = pl.multiple_of(core * rows, rows)
        for block in range(count):
            column = pl.multiple_of((index_ref[0] ^ block) * width, width)
            out_ref[pl.ds(first, rows), pl.ds(column, width)] = ref[
                :, block * width : (block + 1) * width
            ]


def result_kernel(middle_ref, *refs):
    refs[-1][...] = (middle_ref[...] + total_of(refs[:-1])).astype(jnp.bfloat16)


def still(array):
    zeros = (0,) * len(array.shape)
    return (array, array.shape, lambda i: zeros)


def dot(left, right):
    return jnp.dot(left, right, preferred_element_type=jnp.float32)


def both(mine_ref, other_ref):
    return jnp.concatenate([mine_ref[...], other_ref[...]], axis=0)


def gate_up_kernel(count, here_steps, *refs):
    x = both(refs[0], refs[1])
    refs = refs[2:]
    own, fetched, passed = refs[:2], refs[2 : 2 * count], refs[2 * count : 4 * count - 2]
    gate_ref, up_ref, hidden_ref, wg_ref, wu_ref = refs[4 * count - 2 :]
    here = pl.program_id(0) < here_steps
    lins = []
    for which, out_ref in ((0, wg_ref), (1, wu_ref)):
        pieces = [own[which][...]]
        for k in range(count - 1):
            pieces.append(
                jnp.where(here, fetched[2 * k + which][...], passed[2 * k + which][...])
            )
        weight = jnp.concatenate(pieces, axis=0)
        out_ref[...] = weight
        lins.append(dot(x, weight))
    gate, up = lins
    gate_ref[...] = gate
    up_ref[...] = up
    hidden_ref[...] = (gate * jax.nn.sigmoid(gate) * up).astype(jnp.bfloat16)


def gate_up(x, own_gate, own_up, fetched, passed):
    tokens, depth = 2 * x[0].shape[0], own_gate.shape[0]
    width, units = x[0].shape[1], own_gate.shape[1]
    count = len(fetched) + 1
    block = math.gcd(units // 2, 256)
    steps, half = units // block, units // block // 2
    ins = [still(x[0]), still(x[1])]
    ins += [(w, (depth, block), lambda i: (0, i)) for w in (own_gate, own_up)]
    for arrays in (fetched, passed):
        for array in arrays:
            ins.append((array, (depth, block), lambda i: (0, lax.rem(i, half))))
            ins.append((array, (depth, block), lambda i: (0, half + lax.rem(i, half))))
    outs = [
        (full(tokens, units), (tokens, block), lambda i: (0, i)),
        (full(tokens, units), (tokens, block), lambda i: (0, i)),
        (low(tokens, units), (tokens, block), lambda i: (0, i)),
        (low(width, units), (width, block), lambda i: (0, i)),
        (low(width, units), (width, block), lambda i: (0, i)),
    ]
    return gridded(functools.partial(gate_up_kernel, count, half), steps, ins, outs)


def units_back_kernel(count, *refs):
    d_out = both(refs[0], refs[1])
    refs = refs[2:]
    pieces, (gate_ref, up_ref, d_gate_ref, d_up_ref, wd_ref) = refs[:count], refs[count:]
    weight = jnp.concatenate([ref[...] for ref in pieces], axis=0)
    wd_ref[...] = weight
    d_hidden = dot(d_out, weight)
    gate, up = gate_ref[...], up_ref[...]
    chance = jax.nn.sigmoid(gate)
    d_up_ref[...] = (d_hidden * (gate * chance)).astype(jnp.bfloat16)
    slope = chance + gate * chance * (1.0 - chance)
    d_gate_ref[...] = (d_hidden * up * slope).astype(jnp.bfloat16)


def units_back(d_out, pieces, gate, up):
    tokens, units = gate.shape
    depth, width = pieces[0].shape[0], d_out[0].shape[1]
    block = math.gcd(units, 256)

    def by_columns(array, rows):
        return (array, (rows, block), lambda i: (0, i))

    ins = [still(d_out[0]), still(d_out[1])] + [by_columns(piece, depth) for piece in pieces]
    ins += [by_columns(gate, tokens), by_columns(up, tokens)]
    outs = [by_columns(low(tokens, units), tokens)] * 2 + [by_columns(low(width, units), width)]
    return gridded(functools.partial(units_back_kernel, len(pieces)), units // block, ins, outs)


def rows_sum_kernel(terms, *refs):
    first_ref, second_ref = refs[-2:]
    total = 0.0
    for left_ref, right_ref in zip(refs[:terms], refs[terms : 2 * terms]):
        total = total + contract_last(left_ref[...], right_ref[...])
    total = total.astype(jnp.bfloat16)
    half = first_ref.shape[0]
    first_ref[...] = total[:half]
    second_ref[...] = total[half:]


def rows_sum(lefts, rights):
    tokens, width = lefts[0].shape[0], rights[0].shape[0]
    block = math.gcd(width, 512)
    ins = [still(left) for left in lefts]
    ins += [(right, (block, right.shape[1]), lambda i: (i, 0)) for right in rights]
    outs = [(low(tokens // 2, width), (tokens // 2, block), lambda i: (0, i))] * 2
    return gridded(functools.partial(rows_sum_kernel, len(lefts)), width // block, ins, outs)


def weight_grad_kernel(count, terms, turn, *refs):
    if turn:
        side, refs = refs[0][0], refs[1:]
    outs = refs[3 * terms :]
    step = pl.program_id(0)
    first = 0
    for term in range(terms):
        mine_ref, other_ref, right_ref = refs[3 * term : 3 * term + 3]
        half = mine_ref.shape[0]
        grad = contract_first(mine_ref[...], right_ref[:half, :])
        grad = grad + contract_first(other_ref[...], right_ref[half:, :])
        grad = grad.astype(jnp.bfloat16)
        columns = grad.shape[1]
        for k in range(count):

            @pl.when(step == k)
            def _(k=k, first=first, grad=grad, columns=columns):
                if turn:
                    part = columns // 2
                    outs[k][:, pl.ds(pl.multiple_of(side * part, part), part)] = grad[:, :part]
                    outs[k][:, pl.ds(pl.multiple_of((1 - side) * part, part), part)] = grad[:, part:]
                else:
                    outs[k][:, first : first + columns] = grad

        first += columns


def weight_grad(terms, count, side=None):
    columns = sum(right.shape[1] for _, _, right in terms)
    depth = terms[0][0].shape[1] // count
    ins = []
    if side is not None:
        ins.append((side, None, None))
    for mine, other, right in terms:
        ins += [(left, (left.shape[0], depth), lambda i: (0, i)) for left in (mine, other)]
        ins.append(still(right))
    specs = [
        pl.BlockSpec(memory_space=pltpu.SMEM) if block is None else pl.BlockSpec(block, index)
        for _, block, index in ins
    ]
    return pl.pallas_call(
        functools.partial(weight_grad_kernel, count, len(terms), side is not None),
        grid=(count,),
        in_specs=specs,
        out_specs=[pl.BlockSpec((depth, columns), lambda i: (0, 0))] * count,
        out_shape=[low(depth, columns)] * count,
        compiler_params=pltpu.CompilerParams(vmem_limit_bytes=VMEM_LIMIT),
        cost_estimate=SMALL,
    )(*[array for array, _, _ in ins])


def turned(lin, cosine, sine):
    width = lin.shape[-1]
    quarter = HEAD_SIZE // 2
    lane = lax.broadcasted_iota(jnp.int32, lin.shape, lin.ndim - 1)
    first = lax.rem(lane, HEAD_SIZE) < quarter
    partner = jnp.where(
        first,
        -pltpu.roll(lin, width - quarter, lin.ndim - 1),
        pltpu.roll(lin, quarter, lin.ndim - 1),
    )
    return lin * cosine + partner * sine


def side_by_side(table, width):
    return jnp.concatenate([table] * (width // table.shape[-1]), axis=-1)


def of_keys(cosine, sine):
    keys = lax.broadcasted_iota(jnp.int32, cosine.shape, 1) < HEAD_SIZE
    return jnp.where(keys, cosine, 1.0), jnp.where(keys, sine, 0.0)


def qkv_kernel(count, q_width, kv_width, *refs):
    x_refs, (gain_ref, cos_ref, sin_ref), refs = refs[:2], refs[2:5], refs[5:]
    pieces, refs = refs[:count], refs[count:]
    normed_refs, (q_ref, kv_ref, wqkv_ref, wo_ref) = refs[:2], refs[2:]
    weight = jnp.concatenate([ref[...] for ref in pieces], axis=0)
    qkv_width = q_width + kv_width

    @pl.when(pl.program_id(0) == 0)
    def _():
        wqkv_ref[...] = weight[:, :qkv_width]
        wo_ref[...] = weight[:, qkv_width:]

    for i in range(2):
        x = x_refs[i][...].astype(jnp.float32)
        mean = jnp.mean(x * x, axis=-1, keepdims=True)
        normed = (x * lax.rsqrt(mean + 1e-05) * gain_ref[...]).astype(jnp.bfloat16)
        normed_refs[i][...] = normed
        lin = dot(normed, weight[:, :qkv_width])
        cosine, sine = cos_ref[i], sin_ref[i]
        q = turned(lin[:, :q_width], side_by_side(cosine, q_width), side_by_side(sine, q_width))
        q_ref[i] = q.astype(jnp.bfloat16)
        kv = turned(lin[:, q_width:], *of_keys(cosine, sine))
        kv_ref[i] = kv.astype(jnp.bfloat16)


def project_qkv(x, gain, cosine, sine, pieces, q_width, kv_width):
    half_rows, width = x[0].shape
    qkv_width = q_width + kv_width
    block = math.gcd(half_rows, 128)

    def rows_of(array, columns):
        return (array, (block, columns), lambda i: (i, 0))

    def of_both(array, columns):
        return (array, (2, block, columns), lambda i: (0, i, 0))

    lanes = cosine.shape[-1]
    ins = [rows_of(x[0], width), rows_of(x[1], width), still(gain)]
    ins += [of_both(cosine, lanes), of_both(sine, lanes)] + [still(piece) for piece in pieces]
    o_width = pieces[0].shape[1] - qkv_width
    outs = [rows_of(low(half_rows, width), width)] * 2
    outs += [of_both(low(2, half_rows, q_width), q_width), of_both(low(2, half_rows, kv_width), kv_width)]
    outs += [still(low(width, qkv_width)), still(low(width, o_width))]
    kernel = functools.partial(qkv_kernel, len(pieces), q_width, kv_width)
    return gridded(kernel, half_rows // block, ins, outs)


def shares(q, k, visible):
    scores = contract_last(q, k) * (1.0 / math.sqrt(HEAD_SIZE))
    scores = jnp.where(visible, scores, -1e30)
    weights = jnp.exp(scores - jnp.max(scores, axis=-1, keepdims=True))
    weights = jnp.where(visible, weights, 0.0)
    return weights, jnp.sum(weights, axis=-1, keepdims=True)


def load_attention(q_ref, place_ref, start_ref, key_place_ref, kv_refs):
    q = q_ref[...]
    q = q.reshape(q.shape[0] * q.shape[1], q.shape[2])
    kv = jnp.concatenate([ref[...].reshape(q.shape[0], 2 * HEAD_SIZE) for ref in kv_refs], axis=0)
    key_place = key_place_ref[0]
    visible = (key_place <= place_ref[0]) & (key_place >= start_ref[0])
    return q, kv[:, :HEAD_SIZE], kv[:, HEAD_SIZE:], visible


def attend_kernel(groups, q_ref, place_ref, start_ref, key_place_ref, wo_ref, *refs):
    kv_refs, (out_ref, first_ref, second_ref) = refs[:-3], refs[-3:]
    q, k, v, visible = load_attention(q_ref, place_ref, start_ref, key_place_ref, kv_refs)
    mixed = []
    for g in range(groups):
        weights, totals = shares(q[:, g * HEAD_SIZE : (g + 1) * HEAD_SIZE], k, visible)
        mixed.append(dot(weights.astype(jnp.bfloat16), v) / totals)
    out = jnp.concatenate(mixed, axis=1).astype(jnp.bfloat16)
    out_ref[...] = out.reshape(out_ref.shape)
    branch = contract_last(out, wo_ref[...]).astype(jnp.bfloat16)
    half = first_ref.shape[0]
    first_ref[...] = branch[:half]
    second_ref[...] = branch[half:]


def attend_back_kernel(
    groups,
    here_ref,
    q_ref,
    mine_ref,
    other_ref,
    cos_ref,
    sin_ref,
    place_ref,
    start_ref,
    key_place_ref,
    wo_ref,
    *refs,
):
    kv_refs, (dq_ref, dkv_ref) = refs[:-2], refs[-2:]
    q, k, v, visible = load_attention(q_ref, place_ref, start_ref, key_place_ref, kv_refs)
    d_out = dot(both(mine_ref, other_ref), wo_ref[...]).astype(jnp.bfloat16)
    scale = 1.0 / math.sqrt(HEAD_SIZE)
    d_q, d_k, d_v = [], 0.0, 0.0
    for g in range(groups):
        q_head = q[:, g * HEAD_SIZE : (g + 1) * HEAD_SIZE]
        d_head = d_out[:, g * HEAD_SIZE : (g + 1) * HEAD_SIZE]
        weights, totals = shares(q_head, k, visible)
        probs = weights / totals
        d_probs = contract_last(d_head, v)
        row_delta = jnp.sum(probs * d_probs, axis=-1, keepdims=True)
        d_scores = (probs * (d_probs - row_delta)).astype(jnp.bfloat16)
        d_q.append(dot(d_scores, k) * scale)
        d_k = d_k + contract_first(d_scores, q_head) * scale
        d_v = d_v + contract_first(probs.astype(jnp.bfloat16), d_head)
    d_q = jnp.concatenate(d_q, axis=1)
    cosine = cos_ref[...].reshape(q.shape[0], -1)
    sine = sin_ref[...].reshape(q.shape[0], -1)
    d_q = turned(d_q, side_by_side(cosine, q.shape[1]), -side_by_side(sine, q.shape[1]))
    dq_ref[...] = d_q.astype(jnp.bfloat16).reshape(dq_ref.shape)
    d_kv = jnp.concatenate([d_k, d_v], axis=1).astype(jnp.bfloat16)
    half, lanes, cycle = dkv_ref.shape[0], 2 * HEAD_SIZE, len(kv_refs)
    for j in range(cycle):
        for core_side in range(2):
            first = (2 * j + core_side) * half
            column = pl.multiple_of((core_side * cycle + (here_ref[0] ^ j)) * lanes, lanes)
            dkv_ref[:, pl.ds(column, lanes)] = d_kv[first : first + half]


def of_pack(array, half):
    return (array, (2, half, array.shape[-1]), lambda p: (0, p, 0))


def place_blocks(places):
    return [(array, (1,) + array.shape[1:], lambda p: (p, 0, 0)) for array in places]


def attend(q, places, wo, kvs, packs, groups):
    half = q.shape[1] // packs
    width = wo.shape[0]
    ins = [of_pack(q, half)] + place_blocks(places) + [still(wo)] + [of_pack(kv, half) for kv in kvs]
    outs = [of_pack(low(*q.shape), half)]
    outs += [(low(q.shape[1], width), (half, width), lambda p: (p, 0))] * 2
    return gridded(functools.partial(attend_kernel, groups), packs, ins, outs)


def attend_back(here, q, d_branch, cosine, sine, places, wo, kvs, packs, groups):
    half = q.shape[1] // packs
    cycle = len(kvs)
    ins = [of_pack(q, half)]
    ins += [(array, (half, array.shape[1]), lambda p: (p, 0)) for array in d_branch]
    ins += [of_pack(cosine, half), of_pack(sine, half)] + place_blocks(places) + [still(wo)]
    ins += [of_pack(kv, half) for kv in kvs]
    lanes = 2 * HEAD_SIZE
    outs = [of_pack(low(*q.shape), half)]
    outs.append((low(q.shape[1], 2 * cycle * lanes), (half, 2 * cycle * lanes), lambda p: (p, 0)))
    kernel = functools.partial(attend_back_kernel, groups)
    return gridded(kernel, packs, ins, outs, scalars=(here,))


def split_heads(
    hidden_in,
    out_cotangent,
    norm1_gain,
    q_weight,
    key_projection_weight,
    value_projection_weight,
    o_weight,
    norm2_gain,
    gate_weight,
    up_weight,
    down_weight,
    seq_lengths,
    span_order,
):
    packs = lax.axis_size("fsdp")
    cycle = lax.axis_size("ctx")
    pack = lax.axis_index("fsdp")
    core = lax.axis_index("tp")
    here = lax.axis_index("ctx")
    rows = hidden_in.shape[0]
    half = rows // 2
    tokens = packs * rows
    depth = q_weight.shape[0]
    width = depth * packs
    q_width = q_weight.shape[1] // packs
    k_width = key_projection_weight.shape[1] // packs
    ff_width = gate_weight.shape[1] // packs
    ff_half = ff_width // 2
    groups = q_width // k_width
    far = range(1, packs)
    steps = Steps(Line("ctx"))
    kept = {}


    def columns(weight, k, count, first=0, of=None):
        return lax.dynamic_slice_in_dim(weight, (pack ^ k) * (of or count) + first, count, 1)

    def to_pack(name, k, array):
        return ((name, k), array, "fsdp", pairs_by(k, packs))

    def send_all(name, arrays):
        return [to_pack(name, k, array) for k, array in zip(far, arrays)]

    def arrived(name):
        return [steps.take((name, k)) for k in far]

    def to_core(name, array):
        return [(name, array, "tp", pairs_by(1, 2))]

    def to_rows(name, first):
        kept[name], *others = fold(first, steps.take(name), packs)
        return send_all(name, others)

    def joined(name, own, others):
        kept[name] = join(own, others)
        return to_core(name, kept[name])

    def both_of(name):
        return kept[name], steps.take(name)

    index = jnp.stack([pack, core]).astype(jnp.int32)
    here_arg = here.astype(jnp.int32)[None]
    side_arg = here_arg & 1
    at_end = steps.line.at_end

    meta = jnp.concatenate([span_order[0], seq_lengths[0]])
    order_len, meta_len = span_order.shape[1], meta.shape[0]
    info = jnp.concatenate(
        [norm1_gain, norm2_gain, (meta // 32).astype(jnp.bfloat16), (meta % 32).astype(jnp.bfloat16)]
    )
    info = jnp.pad(info, (0, width - info.shape[0]))[None]
    own_in, *in_moves = prepare(
        hidden_in, index, packs, (jnp.pad(info, ((0, 15), (0, 0))),)
    )
    own_cot, *cot_moves = prepare(out_cotangent, index, packs)

    def attention_piece(k):
        return jnp.concatenate(
            [
                columns(q_weight, k, q_width),
                columns(key_projection_weight, k, k_width),
                columns(value_projection_weight, k, k_width),
                columns(o_weight, k, q_width),
            ],
            axis=1,
        )

    steps.step(send_all("in", in_moves))
    steps.step([to_pack("attention", k, attention_piece(k)) for k in far])
    came = arrived("in")
    all_in = join(own_in, came)
    all_in = (all_in, swap(all_in, "tp", 1))
    infos = jnp.concatenate([info] + [block[half : half + 1] for block in came], axis=0)
    all_gains = infos[:, : 2 * depth].astype(jnp.float32)
    gain_one = all_gains[:, :depth].reshape(1, -1)
    gain_two = all_gains[:, depth:].reshape(1, -1)
    metas = infos[:, 2 * depth : 2 * depth + 2 * meta_len].astype(jnp.int32)
    metas = metas[:, :meta_len] * 32 + metas[:, meta_len:]
    orders, lengths = metas[:, :order_len], metas[:, order_len:]

    others = jnp.stack([here ^ j for j in range(cycle)])
    first = jnp.sum(
        jnp.where(
            others[None, :, None] == jnp.arange(order_len, dtype=jnp.int32)[None, None, :],
            orders[:, None, :],
            0,
        ),
        axis=2,
    )
    halves = jnp.stack([core, core ^ 1])[None, None, :]
    section = jnp.where(halves == 0, first[:, :, None], 2 * cycle - 1 - first[:, :, None])
    places = section[..., None] * half + jnp.arange(half, dtype=jnp.int32)
    places = places.reshape(packs, cycle * rows)
    starts = jnp.zeros_like(places)
    end = jnp.zeros((packs, 1), jnp.int32)
    for j in range(lengths.shape[1]):
        end = end + lengths[:, j : j + 1]
        starts = jnp.where(places >= end, end, starts)
    place_args = (places[:, :rows, None], starts[:, :rows, None], places[:, None, :])
    offsets = (places - starts)[:, :rows].reshape(packs, 2, half).transpose(1, 0, 2)
    frequency = jnp.exp(
        -math.log(500000.0)
        * (jnp.arange(2 * HEAD_SIZE) % (HEAD_SIZE // 2)).astype(jnp.float32)
        * 2.0
        / HEAD_SIZE
    )
    angles = offsets.astype(jnp.float32).reshape(2, tokens // 2, 1) * frequency[None, None, :]
    cosine, sine = jnp.cos(angles), jnp.sin(angles)

    side = here & 1

    def two_halves(weight, k):
        return jnp.concatenate(
            [
                columns(weight, k, ff_half, side * ff_half, ff_width),
                columns(weight, k, ff_half, (1 - side) * ff_half, ff_width),
            ],
            axis=1,
        )

    def fetch(ks):
        return [
            to_pack(
                "gate_up",
                k,
                jnp.concatenate(
                    [
                        columns(weight, k, ff_half, side * ff_half, ff_width)
                        for weight in (gate_weight, up_weight)
                    ],
                    axis=1,
                ),
            )
            for k in ks
        ]

    def to_neighbour(k):
        return [(("neighbour", k), fetched[k], "ctx", pairs_by(1, cycle))]

    fetched = {}
    _, cosine, sine, *place_args = steps.step(
        fetch([1, 2]), carry=(all_in[1], cosine, sine, *place_args)
    )
    attention_pieces = [attention_piece(0)] + arrived("attention")
    normed_mine, normed_other, q_rot, kv_own, wqkv, wo = project_qkv(
        all_in, gain_one, cosine, sine, attention_pieces, q_width, 2 * k_width
    )
    normed_one = (normed_mine, normed_other)
    steps.step(
        [(("kv", j), kv_own, "ctx", pairs_by(j, cycle)) for j in range(1, cycle)] + fetch([3])
    )
    fetched[1], fetched[2] = steps.take(("gate_up", 1)), steps.take(("gate_up", 2))
    steps.step(send_all("cot", cot_moves) + to_neighbour(1))
    fetched[3] = steps.take(("gate_up", 3))
    kvs = [kv_own] + [steps.take(("kv", j)) for j in range(1, cycle)]
    attn, first, second = attend(q_rot, place_args, wo, kvs, packs, groups)
    attn_low = attn.reshape(tokens, q_width)
    steps.step(to_core("branch", second))
    steps.step(to_neighbour(2), late=lambda: to_rows("branch", first))
    kept["cot"] = join(own_cot, arrived("cot"))

    def middle_moves():
        kept["middle"], kept["normed"], *sends = in_vmem(
            functools.partial(middle_kernel, packs),
            [full(half, width)] + [low(half, width)] * packs,
            own_in,
            gain_two,
            kept["branch"],
            *arrived("branch"),
        )
        return send_all("two", sends)

    steps.step(to_neighbour(3) + to_core("cot", kept["cot"]), late=middle_moves)

    def wd_moves(ks):
        return [to_pack("down", k, two_halves(down_weight, k)) for k in ks]

    own_columns = [two_halves(weight, 0) for weight in (gate_weight, up_weight, down_weight)]
    own_gate, own_up, own_down = steps.step(
        wd_moves([1, 2]),
        late=lambda: joined("two", kept["normed"], arrived("two")),
        carry=own_columns,
    )
    all_cot = both_of("cot")
    neighbours = [steps.take(("neighbour", k)) for k in far]
    normed_two = (kept["two"], dict(steps.others)["two"])

    gate_val, up_val, hidden, wg, wu = gate_up(
        normed_two, own_gate, own_up, [fetched[k] for k in far], neighbours
    )
    d_wd = weight_grad([(*all_cot, hidden)], packs, side_arg)

    def back(name, grad, ks):
        return [to_pack(name, k, grad[k]) for k in ks]

    def entry(name, k, grad=None):
        return ((name, k), grad[0] if k == 0 else None)

    steps.step(back("wd", d_wd, [1, 2]), summed=entry("wd", 0, d_wd))
    steps.step(wd_moves([3]), summed=entry("wd", 1))
    steps.step(back("wd", d_wd, [3]), summed=entry("wd", 2))
    d_gate, d_up, wd = units_back(all_cot, [own_down] + arrived("down"), gate_val, up_val)
    first, second = rows_sum([d_gate, d_up], [wg, wu])
    steps.step(to_core("d_two", second), summed=entry("wd", 3))
    d_wg = weight_grad([(*normed_two, d_gate)], packs, side_arg)
    steps.step(back("wg", d_wg, [1, 2]), summed=entry("wg", 0, d_wg))
    d_wu = weight_grad([(*normed_two, d_up)], packs, side_arg)
    steps.step(
        summed=entry("wu", 0, d_wu), late=functools.partial(to_rows, "d_two", first)
    )

    def branch_back():
        kept["d_middle"], kept["d_gain_two"], kept["d_branch"], *sends = in_vmem(
            functools.partial(branch_back_kernel, packs),
            [full(half, width), full(1, width)] + [low(half, width)] * packs,
            kept["middle"],
            gain_two,
            own_cot,
            kept["d_two"],
            *arrived("d_two"),
        )
        return send_all("d_branch", sends)

    first, second = rows_sum([hidden], [wd])
    steps.step(summed=entry("wg", 1), late=branch_back, carry=(first, second))
    steps.step(
        back("wg", d_wg, [3]),
        summed=entry("wg", 2),
        late=lambda: joined("all_branch", kept["d_branch"], arrived("d_branch")),
    )
    d_branch = None

    def attention_back():
        return attend_back(
            here_arg, q_rot, d_branch, cosine, sine, place_args, wo, kvs, packs, groups
        )

    sums = steps.line.sums

    def settle_all(name):
        return settle(at_end, index, [sums[name, k] for k in range(packs)], ff_width)

    steps.step(back("wu", d_wu, [1, 2]), summed=entry("wg", 3))
    d_branch = both_of("all_branch")
    d_q, d_kv = attention_back()
    steps.step(back("wu", d_wu, [3]), summed=("d_kv", d_kv))
    down_grad = settle_all("wd")
    steps.step(to_core("ff", second), summed=entry("wu", 1))
    (down_grad,) = steps.step(
        summed=entry("wu", 2),
        late=functools.partial(to_rows, "ff", first),
        carry=(down_grad,),
    )
    steps.step(summed=entry("wu", 3))
    d_qkv = in_vmem(
        d_qkv_kernel,
        [low(tokens, q_width + 2 * k_width)],
        at_end,
        here_arg,
        *sums["d_kv"],
        d_q,
        cosine,
        sine,
        scalars=2,
    )[0]
    d_wqkvo = weight_grad([(*normed_one, d_qkv), (*d_branch, attn_low)], packs)
    first, second = rows_sum([d_qkv], [wqkv])
    result = in_vmem(
        result_kernel, [low(half, width)], kept["middle"], kept["ff"], *arrived("ff")
    )[0]
    steps.step(
        back("wqkvo", d_wqkvo, [1, 2]) + to_core("d_one", second) + to_core("result", result),
        summed=entry("wqkvo", 0, d_wqkvo),
    )
    steps.step(late=functools.partial(to_rows, "d_one", first), summed=entry("wqkvo", 1))

    def both_rows(own, other):
        return in_vmem(
            functools.partial(rows_back_kernel, packs),
            [low(rows, width)],
            index,
            own,
            other,
            scalars=1,
        )[0]

    out_hidden = both_rows(result, steps.take("result"))
    gate_grad = settle_all("wg")
    def gains_to_core():
        kept["in_grad"], d_gain_one = in_vmem(
            functools.partial(in_grad_kernel, packs),
            [low(half, width), full(1, width)],
            own_in,
            gain_one,
            kept["d_middle"],
            kept["d_one"],
            *arrived("d_one"),
        )
        kept["gains"] = jnp.concatenate([d_gain_one, kept["d_gain_two"]], axis=0)
        return to_core("gains", kept["gains"]) + to_core("in_grad", kept["in_grad"])

    def gains_to_packs():
        kept["gains"] = kept["gains"] + steps.take("gains")
        return [to_pack("gains", k, kept["gains"][:, k * depth : (k + 1) * depth]) for k in far]

    def gains_along():
        kept["gains"] = kept["gains"][:, :depth]
        for k in far:
            kept["gains"] = kept["gains"] + steps.take(("gains", k))
        return [(("gains", j), kept["gains"], "ctx", pairs_by(j, cycle)) for j in range(1, cycle)]

    out_hidden, gate_grad = steps.step(
        back("wqkvo", d_wqkvo, [3]),
        summed=entry("wqkvo", 2),
        late=gains_to_core,
        carry=(out_hidden, gate_grad),
    )
    up_grad = settle_all("wu")

    (up_grad,) = steps.step(summed=entry("wqkvo", 3), late=gains_to_packs, carry=(up_grad,))
    in_grad = both_rows(kept["in_grad"], steps.take("in_grad"))
    (in_grad,) = steps.step(late=gains_along, carry=(in_grad,))
    steps.step()
    steps.step()
    shares_of_gains = jnp.stack(
        [kept["gains"]] + [steps.take(("gains", j)) for j in range(1, cycle)]
    )
    gains = steps.token[0, 0]
    for place in range(cycle):
        gains = gains + lax.dynamic_index_in_dim(shares_of_gains, here ^ place, 0, keepdims=False)
    q_grad, k_grad, v_grad, o_grad = settle_attention(
        at_end, index, [sums["wqkvo", k] for k in range(packs)], q_width, 2 * k_width
    )
    return (
        out_hidden,
        in_grad,
        gains[0],
        q_grad,
        k_grad,
        v_grad,
        o_grad,
        gains[1],
        gate_grad,
        up_grad,
        down_grad,
    )


def gathered_weights(
    hidden_in,
    out_cotangent,
    norm1_gain,
    q_weight,
    key_projection_weight,
    value_projection_weight,
    o_weight,
    norm2_gain,
    gate_weight,
    up_weight,
    down_weight,
    seq_lengths,
    span_order,
):
    rows_here = hidden_in.shape[0]
    order_row = span_order[0]
    length_row = seq_lengths[0]
    kv_heads = key_projection_weight.shape[1] // HEAD_SIZE
    query_groups = QUERY_HEADS // KEY_VALUE_HEADS
    score_scale = 1.0 / math.sqrt(HEAD_SIZE)
    whole_rows = rows_here * lax.axis_size("ctx")
    local_rows = lax.axis_index("ctx") * rows_here + jnp.arange(rows_here, dtype=jnp.int32)
    q_place, q_segment, q_offset = stream_place(local_rows, order_row, length_row, rows_here)
    inputs = hidden_in.astype(jnp.float32)
    gain_one, wq_full, wk_full, wv_full, wo_full = (
        lax.all_gather(norm1_gain, "fsdp", axis=0, tiled=True),
        lax.all_gather(q_weight, "fsdp", axis=0, tiled=True),
        lax.all_gather(key_projection_weight, "fsdp", axis=0, tiled=True),
        lax.all_gather(value_projection_weight, "fsdp", axis=0, tiled=True),
        lax.all_gather(o_weight, "fsdp", axis=0, tiled=True),
    )
    gain_one = gain_one.astype(jnp.float32)
    first_normalized = normalize(inputs, gain_one)
    normed_low = first_normalized.astype(jnp.bfloat16)
    q_linear = jnp.dot(normed_low, wq_full, preferred_element_type=jnp.float32).reshape(
        rows_here, kv_heads * query_groups, HEAD_SIZE
    )
    k_linear = jnp.dot(normed_low, wk_full, preferred_element_type=jnp.float32).reshape(
        rows_here, kv_heads, HEAD_SIZE
    )
    q_rotated = (
        rotary_embedding(q_linear, q_offset)
        .astype(jnp.bfloat16)
        .reshape(rows_here, kv_heads, query_groups, HEAD_SIZE)
    )
    k_rotated = (
        rotary_embedding(k_linear, q_offset)
        .astype(jnp.bfloat16)
        .reshape(rows_here, kv_heads * HEAD_SIZE)
    )
    v_low = jnp.dot(normed_low, wv_full, preferred_element_type=jnp.float32).astype(jnp.bfloat16)

    def key_blocks(shard_rows):
        row_count = shard_rows.shape[0]
        key_total_width = math.gcd(row_count, 512)
        number = row_count // key_total_width
        k_place, k_segment, _ = stream_place(
            jnp.arange(row_count, dtype=jnp.int32), order_row, length_row, rows_here
        )
        return (
            key_total_width,
            number,
            k_place.reshape(number, key_total_width),
            k_segment.reshape(number, key_total_width),
        )

    def scores_of(key_block, place_block, segment_block):
        scores = (
            jnp.einsum("qkgd,skd->kgqs", q_rotated, key_block, preferred_element_type=jnp.float32)
            * score_scale
        )
        visible = (
            (q_place[:, None] >= place_block[None, :])
            & (q_segment[:, None] == segment_block[None, :])
        )[None, None]
        return (jnp.where(visible, scores, -1e30), visible)

    start_state = (
        jnp.full((kv_heads, query_groups, rows_here), -1e30, jnp.float32),
        jnp.zeros((kv_heads, query_groups, rows_here), jnp.float32),
        jnp.zeros((kv_heads, query_groups, rows_here, HEAD_SIZE), jnp.float32),
    )
    folded = start_state
    key_row_block = lax.all_gather(k_rotated, "ctx", axis=0, tiled=True)
    value_row_block = lax.all_gather(v_low, "ctx", axis=0, tiled=True)
    key_total_width, number, k_place, k_segment = key_blocks(key_row_block)

    def one_step(carried, pieces):
        running_max, totals, accumulated = carried
        key_block, value_block, place_block, segment_block = pieces
        scores, visible = scores_of(key_block, place_block, segment_block)
        new_max = jnp.maximum(running_max, jnp.max(scores, axis=-1))
        weights = jnp.where(visible, jnp.exp(scores - new_max[..., None]), 0.0)
        factor = jnp.exp(running_max - new_max)
        totals = totals * factor + jnp.sum(weights, axis=-1)
        accumulated = accumulated * factor[..., None] + jnp.einsum(
            "kgqs,skd->kgqd",
            weights.astype(jnp.bfloat16),
            value_block,
            preferred_element_type=jnp.float32,
        )
        return ((new_max, totals, accumulated), None)

    pieces = (
        key_row_block.reshape(number, key_total_width, kv_heads, HEAD_SIZE),
        value_row_block.reshape(number, key_total_width, kv_heads, HEAD_SIZE),
        k_place,
        k_segment,
    )
    folded, _ = lax.scan(one_step, folded, pieces)
    running_max, totals, accumulated = folded
    mixed_out = jnp.transpose(accumulated / totals[..., None], (2, 0, 1, 3))
    log_sum = running_max + jnp.log(totals)
    attn_low = mixed_out.reshape(rows_here, kv_heads * query_groups * HEAD_SIZE).astype(
        jnp.bfloat16
    )
    branch = lax.psum(contract_last(attn_low, wo_full).astype(jnp.bfloat16), "tp").astype(
        jnp.float32
    )
    middle = inputs + branch
    gain_two, wg_full, wu_full, wd_full = (
        lax.all_gather(norm2_gain, "fsdp", axis=0, tiled=True),
        lax.all_gather(gate_weight, "fsdp", axis=0, tiled=True),
        lax.all_gather(up_weight, "fsdp", axis=0, tiled=True),
        lax.all_gather(down_weight, "fsdp", axis=0, tiled=True),
    )
    gain_two = gain_two.astype(jnp.float32)
    normed_two = normalize(middle, gain_two)
    normed_two_low = normed_two.astype(jnp.bfloat16)
    gate_val = jnp.dot(normed_two_low, wg_full, preferred_element_type=jnp.float32)
    up_val = jnp.dot(normed_two_low, wu_full, preferred_element_type=jnp.float32)
    hidden = swiglu(gate_val, up_val).astype(jnp.bfloat16)
    ffn_out = lax.psum(contract_last(hidden, wd_full).astype(jnp.bfloat16), "tp").astype(
        jnp.float32
    )
    result = (middle + ffn_out).astype(jnp.bfloat16)
    grad_out = out_cotangent.astype(jnp.float32)
    d_wd = contract_first(out_cotangent, hidden)
    d_hidden = jnp.dot(out_cotangent, wd_full, preferred_element_type=jnp.float32)
    _, swiglu_back = jax.vjp(swiglu, gate_val, up_val)
    d_gate, d_up = swiglu_back(d_hidden)
    d_gate_low = d_gate.astype(jnp.bfloat16)
    d_up_low = d_up.astype(jnp.bfloat16)
    d_wg = contract_first(normed_two_low, d_gate_low)
    d_wu = contract_first(normed_two_low, d_up_low)
    d_normed_two = lax.psum(
        (contract_last(d_gate_low, wg_full) + contract_last(d_up_low, wu_full)).astype(
            jnp.bfloat16
        ),
        "tp",
    ).astype(jnp.float32)
    _, norm_two_back = jax.vjp(normalize, middle, gain_two)
    d_middle_norm, d_gain_two = norm_two_back(d_normed_two)
    d_middle = grad_out + d_middle_norm
    d_branch_low = d_middle.astype(jnp.bfloat16)
    d_wo = contract_first(d_branch_low, attn_low)
    d_attn = jnp.dot(d_branch_low, wo_full, preferred_element_type=jnp.float32).astype(jnp.bfloat16)
    d_attn_heads = d_attn.reshape(rows_here, kv_heads, query_groups, HEAD_SIZE)
    row_delta = jnp.einsum("qkgd,qkgd->kgq", d_attn_heads.astype(jnp.float32), mixed_out)
    back_state = (
        jnp.zeros((rows_here, kv_heads, query_groups, HEAD_SIZE), jnp.float32),
        jnp.zeros((whole_rows, kv_heads, HEAD_SIZE), jnp.float32),
        jnp.zeros((whole_rows, kv_heads, HEAD_SIZE), jnp.float32),
    )
    folded = back_state
    key_row_block = lax.all_gather(k_rotated, "ctx", axis=0, tiled=True)
    value_row_block = lax.all_gather(v_low, "ctx", axis=0, tiled=True)
    key_total_width, number, k_place, k_segment = key_blocks(key_row_block)

    def one_step(carried, pieces):
        d_query, d_keys, d_values = carried
        key_block, value_block, place_block, segment_block, step_index = pieces
        scores, visible = scores_of(key_block, place_block, segment_block)
        prob_rows = jnp.where(visible, jnp.exp(scores - log_sum[..., None]), 0.0)
        d_values_block = jnp.einsum(
            "kgqs,qkgd->skd",
            prob_rows.astype(jnp.bfloat16),
            d_attn_heads,
            preferred_element_type=jnp.float32,
        )
        d_probs = jnp.einsum(
            "qkgd,skd->kgqs", d_attn_heads, value_block, preferred_element_type=jnp.float32
        )
        d_scores = (prob_rows * (d_probs - row_delta[..., None])).astype(jnp.bfloat16)
        d_query = (
            d_query
            + jnp.einsum("kgqs,skd->qkgd", d_scores, key_block, preferred_element_type=jnp.float32)
            * score_scale
        )
        d_keys_block = (
            jnp.einsum("kgqs,qkgd->skd", d_scores, q_rotated, preferred_element_type=jnp.float32)
            * score_scale
        )
        row_first = step_index * key_total_width
        d_keys = lax.dynamic_update_slice_in_dim(
            d_keys,
            lax.dynamic_slice_in_dim(d_keys, row_first, key_total_width, 0) + d_keys_block,
            row_first,
            0,
        )
        d_values = lax.dynamic_update_slice_in_dim(
            d_values,
            lax.dynamic_slice_in_dim(d_values, row_first, key_total_width, 0) + d_values_block,
            row_first,
            0,
        )
        return ((d_query, d_keys, d_values), None)

    pieces = (
        key_row_block.reshape(number, key_total_width, kv_heads, HEAD_SIZE),
        value_row_block.reshape(number, key_total_width, kv_heads, HEAD_SIZE),
        k_place,
        k_segment,
        jnp.arange(number, dtype=jnp.int32),
    )
    folded, _ = lax.scan(one_step, folded, pieces)
    d_query, d_keys_all, d_values_all = folded
    d_key_own, d_value_own = (
        lax.psum_scatter(
            d_keys_all.astype(jnp.bfloat16), "ctx", scatter_dimension=0, tiled=True
        ).astype(jnp.float32),
        lax.psum_scatter(
            d_values_all.astype(jnp.bfloat16), "ctx", scatter_dimension=0, tiled=True
        ).astype(jnp.float32),
    )
    _, rope_q_back = jax.vjp(lambda rotated_in: rotary_embedding(rotated_in, q_offset), q_linear)
    _, rope_k_back = jax.vjp(lambda rotated_in: rotary_embedding(rotated_in, q_offset), k_linear)
    (d_q_linear,) = rope_q_back(d_query.reshape(rows_here, kv_heads * query_groups, HEAD_SIZE))
    (d_k_linear,) = rope_k_back(d_key_own)
    d_q_low = d_q_linear.reshape(rows_here, kv_heads * query_groups * HEAD_SIZE).astype(
        jnp.bfloat16
    )
    d_k_low = d_k_linear.reshape(rows_here, kv_heads * HEAD_SIZE).astype(jnp.bfloat16)
    d_v_low = d_value_own.reshape(rows_here, kv_heads * HEAD_SIZE).astype(jnp.bfloat16)
    d_wq = contract_first(normed_low, d_q_low)
    d_wk = contract_first(normed_low, d_k_low)
    d_wv = contract_first(normed_low, d_v_low)
    d_normed_one = lax.psum(
        (
            contract_last(d_q_low, wq_full)
            + contract_last(d_k_low, wk_full)
            + contract_last(d_v_low, wv_full)
        ).astype(jnp.bfloat16),
        "tp",
    ).astype(jnp.float32)
    _, norm_one_back = jax.vjp(normalize, inputs, gain_one)
    d_inputs_norm, d_gain_one = norm_one_back(d_normed_one)
    in_grad = (d_middle + d_inputs_norm).astype(jnp.bfloat16)
    weight_grads = (d_gain_one, d_wq, d_wk, d_wv, d_wo, d_gain_two, d_wg, d_wu, d_wd)
    shares = (
        lax.psum_scatter(weight_grads[0], ("fsdp", "ctx"), scatter_dimension=0, tiled=True),
        lax.psum_scatter(weight_grads[1], ("fsdp", "ctx"), scatter_dimension=0, tiled=True),
        lax.psum_scatter(weight_grads[2], ("fsdp", "ctx"), scatter_dimension=0, tiled=True),
        lax.psum_scatter(weight_grads[3], ("fsdp", "ctx"), scatter_dimension=0, tiled=True),
        lax.psum_scatter(weight_grads[4], ("fsdp", "ctx"), scatter_dimension=0, tiled=True),
        lax.psum_scatter(weight_grads[5], ("fsdp", "ctx"), scatter_dimension=0, tiled=True),
        lax.psum_scatter(weight_grads[6], ("fsdp", "ctx"), scatter_dimension=0, tiled=True),
        lax.psum_scatter(weight_grads[7], ("fsdp", "ctx"), scatter_dimension=0, tiled=True),
        lax.psum_scatter(weight_grads[8], ("fsdp", "ctx"), scatter_dimension=0, tiled=True),
    )
    owned_grads = (
        lax.all_gather(shares[0].astype(jnp.bfloat16), "ctx", axis=0, tiled=True).astype(
            jnp.float32
        ),
        lax.all_gather(shares[1].astype(jnp.bfloat16), "ctx", axis=0, tiled=True).astype(
            jnp.float32
        ),
        lax.all_gather(shares[2].astype(jnp.bfloat16), "ctx", axis=0, tiled=True).astype(
            jnp.float32
        ),
        lax.all_gather(shares[3].astype(jnp.bfloat16), "ctx", axis=0, tiled=True).astype(
            jnp.float32
        ),
        lax.all_gather(shares[4].astype(jnp.bfloat16), "ctx", axis=0, tiled=True).astype(
            jnp.float32
        ),
        lax.all_gather(shares[5].astype(jnp.bfloat16), "ctx", axis=0, tiled=True).astype(
            jnp.float32
        ),
        lax.all_gather(shares[6].astype(jnp.bfloat16), "ctx", axis=0, tiled=True).astype(
            jnp.float32
        ),
        lax.all_gather(shares[7].astype(jnp.bfloat16), "ctx", axis=0, tiled=True).astype(
            jnp.float32
        ),
        lax.all_gather(shares[8].astype(jnp.bfloat16), "ctx", axis=0, tiled=True).astype(
            jnp.float32
        ),
    )
    return (
        result,
        in_grad,
        owned_grads[0],
        owned_grads[1],
        owned_grads[2],
        owned_grads[3],
        owned_grads[4],
        owned_grads[5],
        owned_grads[6],
        owned_grads[7],
        owned_grads[8],
    )


def solution(mesh):
    placed = (
        P(("fsdp", "ctx"), None),
        P(("fsdp", "ctx"), None),
        P("fsdp"),
        P("fsdp", "tp"),
        P("fsdp", "tp"),
        P("fsdp", "tp"),
        P("fsdp", "tp"),
        P("fsdp"),
        P("fsdp", "tp"),
        P("fsdp", "tp"),
        P("fsdp", "tp"),
        P("fsdp", None),
        P("fsdp", None),
    )
    plane = mesh.shape["fsdp"] * mesh.shape["tp"]
    splits = mesh.shape["tp"] == 2 and KEY_VALUE_HEADS == plane and mesh.shape["ctx"] == 4
    return jax.shard_map(
        split_heads if splits else gathered_weights,
        mesh=mesh,
        in_specs=placed,
        out_specs=(
            P(("fsdp", "ctx"), None),
            P(("fsdp", "ctx"), None),
            P("fsdp"),
            P("fsdp", "tp"),
            P("fsdp", "tp"),
            P("fsdp", "tp"),
            P("fsdp", "tp"),
            P("fsdp"),
            P("fsdp", "tp"),
            P("fsdp", "tp"),
            P("fsdp", "tp"),
        ),
        check_vma=False,
    )
```

```python
import functools
import math

import jax
import jax.numpy as jnp
from jax import lax
from jax.experimental import pallas as pl
from jax.experimental.pallas import tpu as pltpu
from jax.sharding import PartitionSpec as P

QUERY_HEADS = 32
KEY_VALUE_HEADS = 8
HEAD_SIZE = 64


def stream_place(row_ids, order_row, length_row, tok_dev):
    cycle_size = order_row.shape[0]
    half_len = tok_dev // 2
    cycle_rank = row_ids // tok_dev
    within = row_ids % tok_dev
    first_section = jnp.sum(
        jnp.where(
            cycle_rank[:, None] == jnp.arange(cycle_size, dtype=jnp.int32)[None, :],
            order_row[None, :],
            0,
        ),
        axis=1,
        dtype=jnp.int32,
    )
    section = jnp.where(within >= half_len, 2 * cycle_size - 1 - first_section, first_section)
    places = section * half_len + within % half_len
    seq_ends = jnp.cumsum(length_row, dtype=jnp.int32)
    passed = places[:, None] >= seq_ends[None, :]
    segment = jnp.sum(passed.astype(jnp.int32), axis=1, dtype=jnp.int32)
    offset = places - jnp.sum(jnp.where(passed, length_row[None, :], 0), axis=1, dtype=jnp.int32)
    return (places, segment, offset)


def rotary_embedding(values, positions):
    half_len = values.shape[-1] // 2
    frequency = jnp.exp(
        -math.log(500000.0) * jnp.arange(half_len, dtype=jnp.float32) * 2.0 / values.shape[-1]
    )
    angles = positions.astype(jnp.float32)[:, None] * frequency[None, :]
    cosine = jnp.cos(angles)[:, None, :]
    sine = jnp.sin(angles)[:, None, :]
    lower_half = values[..., :half_len]
    upper_half = values[..., half_len:]
    return jnp.concatenate(
        [lower_half * cosine - upper_half * sine, upper_half * cosine + lower_half * sine], axis=-1
    )


def normalize(values, gain_vec):
    return values * lax.rsqrt(jnp.mean(values * values, axis=-1, keepdims=True) + 1e-05) * gain_vec


def swiglu(gate_val, up_val):
    return jax.nn.silu(gate_val) * up_val


def contract_last(left, right):
    return lax.dot_general(
        left, right, (((1,), (1,)), ((), ())), preferred_element_type=jnp.float32
    )


def contract_first(left, right):
    return lax.dot_general(
        left, right, (((0,), (0,)), ((), ())), preferred_element_type=jnp.float32
    )


VMEM_LIMIT = 32 * 1024 * 1024
SMALL_LIMIT = 12 * 1024 * 1024
SMALL = pl.CostEstimate(flops=1, bytes_accessed=1, transcendentals=0)


def pairs_by(distance, size):
    return [(i, i ^ distance) for i in range(size)]


def swap(array, axis, distance):
    return lax.ppermute(array, axis, pairs_by(distance, lax.axis_size(axis)))


class Line:
    def __init__(self, axis):
        index = lax.axis_index(axis)
        size = lax.axis_size(axis)
        self.axis = axis
        self.at_end = ((index == 0) | (index == size - 1)).astype(jnp.int32)[None]
        self.entered = self.halfway = self.leaving = None
        self.sums = {}

    def advance(self, got, entering):
        if self.leaving is not None:
            name, sent = self.leaving
            self.sums[name] = (got["ends"], sent)
        moves = []
        halfway = None
        if self.entered is not None:
            name, value = self.entered
            halfway = (name, add_low(value, got["ends"]))
            moves.append(("middle", halfway[1], self.axis, [(1, 2), (2, 1)]))
        leaving = None
        inwards, outwards = [(0, 1), (3, 2)], [(1, 0), (2, 3)]
        if self.halfway is not None:
            name, value = self.halfway
            if entering is None:
                sent, pairs = add_low(value, got["middle"]), outwards
            else:
                sent = either_way(self.at_end, entering[1], value, got["middle"])
                pairs = inwards + outwards
            leaving = (name, sent)
            moves.append(("ends", sent, self.axis, pairs))
        elif entering is not None:
            moves.append(("ends", entering[1], self.axis, inwards))
        self.entered, self.halfway, self.leaving = entering, halfway, leaving
        return moves


class Steps:
    def __init__(self, line):
        self.line = line
        self.got = {}
        self.on_line = []
        self.others = []
        self.token = jnp.zeros((8, 128), jnp.float32)

    def wait(self, flying, arrays):
        count = len(flying)
        held = lax.optimization_barrier(
            (self.token,) + tuple(value for _, value in flying) + tuple(arrays)
        )
        self.token = held[0]
        for (name, _), value in zip(flying, held[1:]):
            self.got[name] = value
        return list(held[1 + count :])

    def start(self, moves):
        return [(name, lax.ppermute(value, axis, pairs)) for name, value, axis, pairs in moves]

    def step(self, moves=(), summed=None, late=None, carry=()):
        moves, carry = list(moves), list(carry)
        arrays = [move[1] for move in moves] + carry
        fresh = [summed[1]] if summed is not None and summed[1] is not None else []
        together = summed is not None and not fresh and summed[0] not in self.got
        if together or not self.on_line:
            held = self.wait(self.on_line + self.others, fresh + arrays)
            held_fresh, held = held[: len(fresh)], held[len(fresh) :]
        else:
            held_fresh = self.wait(self.on_line, fresh)
        entering = summed
        if summed is not None:
            entering = (summed[0], held_fresh[0] if fresh else self.take(summed[0]))
        along = self.line.advance(self.got, entering)
        if not together and self.on_line:
            self.on_line = self.start(along)
            held = self.wait(self.others, arrays)
        else:
            self.on_line = self.start(along)
        moves = [
            (name, value, axis, pairs) for (name, _, axis, pairs), value in zip(moves, held)
        ]
        self.others = self.start(moves + (late() if late is not None else []))
        return held[len(moves) :]

    def take(self, name):
        return self.got.pop(name)


def in_vmem(kernel, out_shape, *args, scalars=0):
    specs = [pl.BlockSpec(memory_space=pltpu.SMEM)] * scalars
    specs += [pl.BlockSpec(memory_space=pltpu.VMEM)] * (len(args) - scalars)
    return pl.pallas_call(
        kernel,
        out_shape=out_shape,
        in_specs=specs,
        out_specs=[pl.BlockSpec(memory_space=pltpu.VMEM)] * len(out_shape),
        compiler_params=pltpu.CompilerParams(vmem_limit_bytes=SMALL_LIMIT),
        cost_estimate=SMALL,
    )(*args)


def low(*shape):
    return jax.ShapeDtypeStruct(shape, jnp.bfloat16)


def full(*shape):
    return jax.ShapeDtypeStruct(shape, jnp.float32)


def store_seen(ref, value, distance, count):
    width = value.shape[-1] // count
    for block in range(count):
        there = block ^ distance
        ref[: value.shape[0], block * width : (block + 1) * width] = value[
            :, there * width : (there + 1) * width
        ]


def prepare_kernel(count, index_ref, x_ref, own_ref, *sends):
    rows, width = own_ref.shape[0], own_ref.shape[1] // count
    first = pl.multiple_of(index_ref[1] * rows, rows)
    for block in range(count):
        column = pl.multiple_of((index_ref[0] ^ block) * width, width)
        own_ref[:, block * width : (block + 1) * width] = x_ref[
            pl.ds(first, rows), pl.ds(column, width)
        ]
    for k, send in enumerate(sends, 1):
        store_seen(send, own_ref[...], k, count)


def prepare(x, index, count):
    rows, width = x.shape[0] // 2, x.shape[1]
    return in_vmem(
        functools.partial(prepare_kernel, count), [low(rows, width)] * count, index, x, scalars=1
    )


def turns_kernel(offset_ref, cos_ref, sin_ref):
    lane = lax.broadcasted_iota(jnp.int32, cos_ref.shape, 2)
    place = lax.rem(lane, HEAD_SIZE // 2).astype(jnp.float32)
    frequency = jnp.exp(-math.log(500000.0) * place * 2.0 / HEAD_SIZE)
    angle = offset_ref[...] * frequency
    cos_ref[...] = jnp.cos(angle)
    sin_ref[...] = jnp.sin(angle)


def join_kernel(*refs):
    out_ref = refs[-1]
    rows = refs[0].shape[0]
    for i, ref in enumerate(refs[:-1]):
        out_ref[i * rows : (i + 1) * rows, :] = ref[:rows, :]


def join_rows(arrays, rows):
    def kernel(*refs):
        for i, ref in enumerate(refs[:-1]):
            refs[-1][i * rows : (i + 1) * rows, :] = ref[:rows, :]

    return in_vmem(kernel, [low(rows * len(arrays), arrays[0].shape[1])], *arrays)[0]


def join(own, others):
    rows, width = own.shape
    return in_vmem(join_kernel, [low(rows * (1 + len(others)), width)], own, *others)[0]


def fold_kernel(count, first_ref, came_ref, own_ref, *sends):
    rows = own_ref.shape[0]
    for k in range(count):
        here = slice(k * rows, (k + 1) * rows)
        total = first_ref[here, :].astype(jnp.float32) + came_ref[here, :].astype(jnp.float32)
        total = total.astype(jnp.bfloat16)
        if k == 0:
            own_ref[...] = total
        else:
            store_seen(sends[k - 1], total, k, count)


def fold(first, came, count):
    rows, width = first.shape[0] // count, first.shape[1]
    return in_vmem(
        functools.partial(fold_kernel, count), [low(rows, width)] * count, first, came
    )


def total_of(refs):
    total = refs[0][...].astype(jnp.float32)
    for ref in refs[1:]:
        total = total + ref[...].astype(jnp.float32)
    return total


def middle_kernel(count, in_ref, gain_ref, *refs):
    parts, (middle_ref, normed_ref, *sends) = refs[:count], refs[count:]
    middle = in_ref[...].astype(jnp.float32) + total_of(parts)
    middle_ref[...] = middle
    mean = jnp.mean(middle * middle, axis=-1, keepdims=True)
    normed = (middle * lax.rsqrt(mean + 1e-05) * gain_ref[...]).astype(jnp.bfloat16)
    normed_ref[...] = normed
    for k in range(1, count):
        store_seen(sends[k - 1], normed, k, count)


def norm_back(d_normed, x, gain):
    scale = lax.rsqrt(jnp.mean(x * x, axis=-1, keepdims=True) + 1e-05)
    unit = x * scale
    d_unit = d_normed * gain
    d_x = scale * (d_unit - unit * jnp.mean(d_unit * unit, axis=-1, keepdims=True))
    return d_x, jnp.sum(d_normed * unit, axis=0, keepdims=True)


def branch_back_kernel(count, middle_ref, gain_ref, cot_ref, *refs):
    parts, (d_middle_ref, d_gain_ref, branch_ref, *sends) = refs[:count], refs[count:]
    d_x, d_gain_ref[...] = norm_back(total_of(parts), middle_ref[...], gain_ref[...])
    d_middle = cot_ref[...].astype(jnp.float32) + d_x
    d_middle_ref[...] = d_middle
    branch = d_middle.astype(jnp.bfloat16)
    branch_ref[...] = branch
    for k in range(1, count):
        store_seen(sends[k - 1], branch, k, count)


def in_grad_kernel(count, in_ref, gain_ref, d_middle_ref, *refs):
    parts, (grad_ref, d_gain_ref) = refs[:count], refs[count:]
    x = in_ref[...].astype(jnp.float32)
    d_x, d_gain_ref[...] = norm_back(total_of(parts), x, gain_ref[...])
    grad_ref[...] = (d_middle_ref[...] + d_x).astype(jnp.bfloat16)


def gridded(kernel, steps, ins, outs, scalars=()):
    return pl.pallas_call(
        kernel,
        grid=(steps,),
        in_specs=[pl.BlockSpec(memory_space=pltpu.SMEM)] * len(scalars)
        + [pl.BlockSpec(block, index) for _, block, index in ins],
        out_specs=[pl.BlockSpec(block, index) for _, block, index in outs],
        out_shape=[shape for shape, _, _ in outs],
        compiler_params=pltpu.CompilerParams(vmem_limit_bytes=VMEM_LIMIT),
        cost_estimate=SMALL,
    )(*scalars, *[array for array, _, _ in ins])


def row_blocks(array, rows):
    return (array, (rows, array.shape[1]), lambda i: (i, 0))


def add_low(left, right):
    right = right[:, : left.shape[1]]
    return (left.astype(jnp.float32) + right.astype(jnp.float32)).astype(jnp.bfloat16)


def either_way(at_end, fresh, value, came):
    total = add_low(value, came)
    width = max(fresh.shape[1], value.shape[1])
    if fresh.shape[1] < width:
        fresh = jnp.pad(fresh, ((0, 0), (0, width - fresh.shape[1])))
    if total.shape[1] < width:
        total = jnp.pad(total, ((0, 0), (0, width - total.shape[1])))
    return jnp.where(at_end[0] == 1, fresh, total)


def settled(at_end, came_ref, sent_ref, columns):
    return jnp.where(at_end == 1, came_ref[:, columns], sent_ref[:, columns]).astype(jnp.float32)


def settle_kernel(count, at_end_ref, index_ref, *refs):
    out_ref = refs[-1]
    width = out_ref.shape[1] // count
    for k in range(count):
        column = pl.multiple_of((index_ref[0] ^ k) * width, width)
        out_ref[:, pl.ds(column, width)] = settled(
            at_end_ref[0], refs[2 * k], refs[2 * k + 1], slice(0, width)
        )


def settle(at_end, index, pairs, width):
    count = len(pairs)
    arrays = [array for pair in pairs for array in pair]
    depth = arrays[0].shape[0]
    rows = math.gcd(depth, 128)
    ins = [(array, (rows, width), lambda i: (i, 0)) for array in arrays]
    outs = [row_blocks(full(depth, width * count), rows)]
    kernel = functools.partial(settle_kernel, count)
    return gridded(kernel, depth // rows, ins, outs, scalars=(at_end, index))[0]


def settle_attention_kernel(count, q_width, kv_width, at_end_ref, index_ref, *refs):
    q_ref, k_ref, v_ref, o_ref = refs[-4:]
    o_width = o_ref.shape[1] // count
    o_first = q_width + kv_width
    kvs = []
    for k in range(count):
        came_ref, sent_ref = refs[2 * k], refs[2 * k + 1]
        column = pl.multiple_of((index_ref[0] ^ k) * q_width, q_width)
        q_ref[:, pl.ds(column, q_width)] = settled(
            at_end_ref[0], came_ref, sent_ref, slice(0, q_width)
        )
        column = pl.multiple_of((index_ref[0] ^ k) * o_width, o_width)
        o_ref[:, pl.ds(column, o_width)] = settled(
            at_end_ref[0], came_ref, sent_ref, slice(o_first, o_first + o_width)
        )
        kvs.append(settled(at_end_ref[0], came_ref, sent_ref, slice(q_width, o_first)))
    ordered = []
    for place in range(count):
        kv = kvs[0]
        for k in range(1, count):
            kv = jnp.where((index_ref[0] ^ k) == place, kvs[k], kv)
        ordered.append(kv)
    k_ref[...] = jnp.concatenate([kv[:, : kv_width // 2] for kv in ordered], axis=1)
    v_ref[...] = jnp.concatenate([kv[:, kv_width // 2 :] for kv in ordered], axis=1)


def settle_attention(at_end, index, pairs, q_width, kv_width):
    count = len(pairs)
    arrays = [array for pair in pairs for array in pair]
    depth = arrays[0].shape[0]
    width = min(array.shape[1] for array in arrays)
    o_width = width - q_width - kv_width
    rows = math.gcd(depth, 128)
    ins = [(array, (rows, width), lambda i: (i, 0)) for array in arrays]
    widths = (q_width, kv_width // 2, kv_width // 2, o_width)
    outs = [row_blocks(full(depth, each * count), rows) for each in widths]
    kernel = functools.partial(settle_attention_kernel, count, q_width, kv_width)
    return gridded(kernel, depth // rows, ins, outs, scalars=(at_end, index))


def d_qkv_kernel(at_end_ref, here_ref, came_ref, sent_ref, dq_ref, cos_ref, sin_ref, out_ref):
    lanes = 2 * HEAD_SIZE
    half, q_width = dq_ref.shape[1], dq_ref.shape[2]
    cycle = came_ref.shape[1] // lanes // 2
    for core_side in range(2):
        column = pl.multiple_of((core_side * cycle + here_ref[0]) * lanes, lanes)
        d_kv = settled(at_end_ref[0], came_ref, sent_ref, pl.ds(column, lanes))
        cosine, sine = of_keys(cos_ref[core_side], sin_ref[core_side])
        d_kv = turned(d_kv, cosine, -sine).astype(jnp.bfloat16)
        rows = slice(core_side * half, (core_side + 1) * half)
        out_ref[rows, :q_width] = dq_ref[core_side]
        out_ref[rows, q_width:] = d_kv


def rows_back_kernel(count, index_ref, own_ref, other_ref, out_ref):
    rows, width = own_ref.shape[0], own_ref.shape[1] // count
    for ref, core in ((own_ref, index_ref[1]), (other_ref, 1 - index_ref[1])):
        first = pl.multiple_of(core * rows, rows)
        for block in range(count):
            column = pl.multiple_of((index_ref[0] ^ block) * width, width)
            out_ref[pl.ds(first, rows), pl.ds(column, width)] = ref[
                :, block * width : (block + 1) * width
            ]


def result_kernel(middle_ref, *refs):
    refs[-1][...] = (middle_ref[...] + total_of(refs[:-1])).astype(jnp.bfloat16)


def still(array):
    zeros = (0,) * len(array.shape)
    return (array, array.shape, lambda i: zeros)


def dot(left, right):
    return jnp.dot(left, right, preferred_element_type=jnp.float32)


def both(mine_ref, other_ref, weight):
    return jnp.concatenate([dot(mine_ref[...], weight), dot(other_ref[...], weight)], axis=0)


def gate_up_kernel(count, here_steps, *refs):
    x_refs, refs = refs[:2], refs[2:]
    own, fetched, passed = refs[:2], refs[2 : 2 * count], refs[2 * count : 4 * count - 2]
    gate_ref, up_ref, hidden_ref, wg_ref, wu_ref = refs[4 * count - 2 :]
    here = pl.program_id(0) < here_steps
    lins = []
    for which, out_ref in ((0, wg_ref), (1, wu_ref)):
        pieces = [own[which][...]]
        for k in range(count - 1):
            pieces.append(
                jnp.where(here, fetched[2 * k + which][...], passed[2 * k + which][...])
            )
        weight = jnp.concatenate(pieces, axis=0)
        out_ref[...] = weight
        lins.append(both(*x_refs, weight))
    gate, up = lins
    gate_ref[...] = gate
    up_ref[...] = up
    hidden_ref[...] = (gate * jax.nn.sigmoid(gate) * up).astype(jnp.bfloat16)


def gate_up(x, own_gate, own_up, fetched, passed):
    tokens, depth = 2 * x[0].shape[0], own_gate.shape[0]
    width, units = x[0].shape[1], own_gate.shape[1]
    count = len(fetched) + 1
    block = math.gcd(units // 2, 256)
    steps, half = units // block, units // block // 2
    ins = [still(x[0]), still(x[1])]
    ins += [(w, (depth, block), lambda i: (0, i)) for w in (own_gate, own_up)]
    for arrays in (fetched, passed):
        for array in arrays:
            ins.append((array, (depth, block), lambda i: (0, lax.rem(i, half))))
            ins.append((array, (depth, block), lambda i: (0, half + lax.rem(i, half))))
    outs = [
        (full(tokens, units), (tokens, block), lambda i: (0, i)),
        (full(tokens, units), (tokens, block), lambda i: (0, i)),
        (low(tokens, units), (tokens, block), lambda i: (0, i)),
        (low(width, units), (width, block), lambda i: (0, i)),
        (low(width, units), (width, block), lambda i: (0, i)),
    ]
    return gridded(functools.partial(gate_up_kernel, count, half), steps, ins, outs)


def units_back_kernel(count, *refs):
    d_refs, refs = refs[:2], refs[2:]
    pieces, (gate_ref, up_ref, d_gate_ref, d_up_ref, wd_ref) = refs[:count], refs[count:]
    weight = jnp.concatenate([ref[...] for ref in pieces], axis=0)
    wd_ref[...] = weight
    d_hidden = both(*d_refs, weight)
    gate, up = gate_ref[...], up_ref[...]
    chance = jax.nn.sigmoid(gate)
    d_up_ref[...] = (d_hidden * (gate * chance)).astype(jnp.bfloat16)
    slope = chance + gate * chance * (1.0 - chance)
    d_gate_ref[...] = (d_hidden * up * slope).astype(jnp.bfloat16)


def units_back(d_out, pieces, gate, up):
    tokens, units = gate.shape
    depth, width = pieces[0].shape[0], d_out[0].shape[1]
    block = math.gcd(units, 256)

    def by_columns(array, rows):
        return (array, (rows, block), lambda i: (0, i))

    ins = [still(d_out[0]), still(d_out[1])] + [by_columns(piece, depth) for piece in pieces]
    ins += [by_columns(gate, tokens), by_columns(up, tokens)]
    outs = [by_columns(low(tokens, units), tokens)] * 2 + [by_columns(low(width, units), width)]
    return gridded(functools.partial(units_back_kernel, len(pieces)), units // block, ins, outs)


def rows_sum_kernel(terms, *refs):
    first_ref, second_ref = refs[-2:]
    total = 0.0
    for left_ref, right_ref in zip(refs[:terms], refs[terms : 2 * terms]):
        total = total + contract_last(left_ref[...], right_ref[...])
    total = total.astype(jnp.bfloat16)
    half = first_ref.shape[0]
    first_ref[...] = total[:half]
    second_ref[...] = total[half:]


def rows_sum(lefts, rights):
    tokens, width = lefts[0].shape[0], rights[0].shape[0]
    block = math.gcd(width, 512)
    ins = [still(left) for left in lefts]
    ins += [(right, (block, right.shape[1]), lambda i: (i, 0)) for right in rights]
    outs = [(low(tokens // 2, width), (tokens // 2, block), lambda i: (0, i))] * 2
    return gridded(functools.partial(rows_sum_kernel, len(lefts)), width // block, ins, outs)


def weight_grad_kernel(count, terms, turn, *refs):
    if turn:
        side, refs = refs[0][0], refs[1:]
    outs = refs[3 * terms :]
    step = pl.program_id(0)
    first = 0
    for term in range(terms):
        mine_ref, other_ref, right_ref = refs[3 * term : 3 * term + 3]
        half = mine_ref.shape[0]
        grad = contract_first(mine_ref[...], right_ref[:half, :])
        grad = grad + contract_first(other_ref[...], right_ref[half:, :])
        grad = grad.astype(jnp.bfloat16)
        columns = grad.shape[1]
        for k in range(count):

            @pl.when(step == k)
            def _(k=k, first=first, grad=grad, columns=columns):
                if turn:
                    part = columns // 2
                    outs[k][:, pl.ds(pl.multiple_of(side * part, part), part)] = grad[:, :part]
                    outs[k][:, pl.ds(pl.multiple_of((1 - side) * part, part), part)] = grad[:, part:]
                else:
                    outs[k][:, first : first + columns] = grad

        first += columns


def weight_grad(terms, count, side=None):
    columns = sum(right.shape[1] for _, _, right in terms)
    depth = terms[0][0].shape[1] // count
    ins = []
    if side is not None:
        ins.append((side, None, None))
    for mine, other, right in terms:
        ins += [(left, (left.shape[0], depth), lambda i: (0, i)) for left in (mine, other)]
        ins.append(still(right))
    specs = [
        pl.BlockSpec(memory_space=pltpu.SMEM) if block is None else pl.BlockSpec(block, index)
        for _, block, index in ins
    ]
    return pl.pallas_call(
        functools.partial(weight_grad_kernel, count, len(terms), side is not None),
        grid=(count,),
        in_specs=specs,
        out_specs=[pl.BlockSpec((depth, columns), lambda i: (0, 0))] * count,
        out_shape=[low(depth, columns)] * count,
        compiler_params=pltpu.CompilerParams(vmem_limit_bytes=VMEM_LIMIT),
        cost_estimate=SMALL,
    )(*[array for array, _, _ in ins])


def turned(lin, cosine, sine):
    width = lin.shape[-1]
    quarter = HEAD_SIZE // 2
    lane = lax.broadcasted_iota(jnp.int32, lin.shape, lin.ndim - 1)
    first = lax.rem(lane, HEAD_SIZE) < quarter
    partner = jnp.where(
        first,
        -pltpu.roll(lin, width - quarter, lin.ndim - 1),
        pltpu.roll(lin, quarter, lin.ndim - 1),
    )
    return lin * cosine + partner * sine


def side_by_side(table, width):
    return jnp.concatenate([table] * (width // table.shape[-1]), axis=-1)


def of_keys(cosine, sine):
    keys = lax.broadcasted_iota(jnp.int32, cosine.shape, 1) < HEAD_SIZE
    return jnp.where(keys, cosine, 1.0), jnp.where(keys, sine, 0.0)


def qkv_kernel(count, q_width, kv_width, side_ref, *refs):
    x_refs, (gain_ref, cos_ref, sin_ref), refs = refs[:2], refs[2:5], refs[5:]
    own_ref, fetched, passed_ref, refs = refs[0], refs[1:count], refs[count], refs[count + 1 :]
    normed_refs, (q_ref, kv_ref, wqkv_ref, wo_ref) = refs[:2], refs[2:]
    qkv_width = q_width + kv_width
    depth = own_ref.shape[0]
    half = depth // 2

    @pl.when(pl.program_id(0) == 0)
    def _():
        wqkv_ref[:depth, :] = own_ref[:, :qkv_width]
        wo_ref[:depth, :] = own_ref[:, qkv_width:]
        for k in range(1, count):
            for which, piece in (
                (side_ref[0], fetched[k - 1][:half, :]),
                (1 - side_ref[0], passed_ref[(k - 1) * half : k * half, :]),
            ):
                first = pl.multiple_of(k * depth + which * half, half)
                wqkv_ref[pl.ds(first, half), :] = piece[:, :qkv_width]
                wo_ref[pl.ds(first, half), :] = piece[:, qkv_width:]

    for i in range(2):
        x = x_refs[i][...].astype(jnp.float32)
        mean = jnp.mean(x * x, axis=-1, keepdims=True)
        normed = (x * lax.rsqrt(mean + 1e-05) * gain_ref[...]).astype(jnp.bfloat16)
        normed_refs[i][...] = normed
        lin = dot(normed, wqkv_ref[...])
        cosine, sine = cos_ref[i], sin_ref[i]
        q = turned(lin[:, :q_width], side_by_side(cosine, q_width), side_by_side(sine, q_width))
        q_ref[i] = q.astype(jnp.bfloat16)
        kv = turned(lin[:, q_width:], *of_keys(cosine, sine))
        kv_ref[i] = kv.astype(jnp.bfloat16)


def project_qkv(side, x, gain, cosine, sine, own, fetched, passed, q_width, kv_width):
    half_rows, width = x[0].shape
    qkv_width = q_width + kv_width
    block = math.gcd(half_rows, 128)

    def rows_of(array, columns):
        return (array, (block, columns), lambda i: (i, 0))

    def of_both(array, columns):
        return (array, (2, block, columns), lambda i: (0, i, 0))

    lanes = cosine.shape[-1]
    ins = [rows_of(x[0], width), rows_of(x[1], width), still(gain)]
    ins += [of_both(cosine, lanes), of_both(sine, lanes)]
    ins += [still(array) for array in (own, *fetched, passed)]
    o_width = own.shape[1] - qkv_width
    outs = [rows_of(low(half_rows, width), width)] * 2
    outs += [of_both(low(2, half_rows, q_width), q_width), of_both(low(2, half_rows, kv_width), kv_width)]
    outs += [still(low(width, qkv_width)), still(low(width, o_width))]
    kernel = functools.partial(qkv_kernel, len(fetched) + 1, q_width, kv_width)
    return gridded(kernel, half_rows // block, ins, outs, scalars=(side,))


def shares(q, k, visible):
    scores = contract_last(q, k) * (1.0 / math.sqrt(HEAD_SIZE))
    scores = jnp.where(visible, scores, -1e30)
    weights = jnp.exp(scores - jnp.max(scores, axis=-1, keepdims=True))
    weights = jnp.where(visible, weights, 0.0)
    return weights, jnp.sum(weights, axis=-1, keepdims=True)


def load_attention(q_ref, place_ref, start_ref, key_place_ref, kv_refs):
    q = q_ref[...]
    q = q.reshape(q.shape[0] * q.shape[1], q.shape[2])
    kv = jnp.concatenate([ref[...].reshape(q.shape[0], 2 * HEAD_SIZE) for ref in kv_refs], axis=0)
    key_place = key_place_ref[0]
    visible = (key_place <= place_ref[0]) & (key_place >= start_ref[0])
    return q, kv[:, :HEAD_SIZE], kv[:, HEAD_SIZE:], visible


def attend_kernel(groups, q_ref, place_ref, start_ref, key_place_ref, wo_ref, *refs):
    kv_refs, (out_ref, first_ref, second_ref) = refs[:-3], refs[-3:]
    q, k, v, visible = load_attention(q_ref, place_ref, start_ref, key_place_ref, kv_refs)
    mixed = []
    for g in range(groups):
        weights, totals = shares(q[:, g * HEAD_SIZE : (g + 1) * HEAD_SIZE], k, visible)
        mixed.append(dot(weights.astype(jnp.bfloat16), v) / totals)
    out = jnp.concatenate(mixed, axis=1).astype(jnp.bfloat16)
    out_ref[...] = out.reshape(out_ref.shape)
    branch = contract_last(out, wo_ref[...]).astype(jnp.bfloat16)
    half = first_ref.shape[0]
    first_ref[...] = branch[:half]
    second_ref[...] = branch[half:]


def attend_back_kernel(
    groups,
    here_ref,
    q_ref,
    mine_ref,
    other_ref,
    cos_ref,
    sin_ref,
    place_ref,
    start_ref,
    key_place_ref,
    wo_ref,
    *refs,
):
    kv_refs, (dq_ref, dkv_ref) = refs[:-2], refs[-2:]
    q, k, v, visible = load_attention(q_ref, place_ref, start_ref, key_place_ref, kv_refs)
    d_out = both(mine_ref, other_ref, wo_ref[...]).astype(jnp.bfloat16)
    scale = 1.0 / math.sqrt(HEAD_SIZE)
    d_q, d_k, d_v = [], 0.0, 0.0
    for g in range(groups):
        q_head = q[:, g * HEAD_SIZE : (g + 1) * HEAD_SIZE]
        d_head = d_out[:, g * HEAD_SIZE : (g + 1) * HEAD_SIZE]
        weights, totals = shares(q_head, k, visible)
        probs = weights / totals
        d_probs = contract_last(d_head, v)
        row_delta = jnp.sum(probs * d_probs, axis=-1, keepdims=True)
        d_scores = (probs * (d_probs - row_delta)).astype(jnp.bfloat16)
        d_q.append(dot(d_scores, k) * scale)
        d_k = d_k + contract_first(d_scores, q_head) * scale
        d_v = d_v + contract_first(probs.astype(jnp.bfloat16), d_head)
    d_q = jnp.concatenate(d_q, axis=1)
    cosine = cos_ref[...].reshape(q.shape[0], -1)
    sine = sin_ref[...].reshape(q.shape[0], -1)
    d_q = turned(d_q, side_by_side(cosine, q.shape[1]), -side_by_side(sine, q.shape[1]))
    dq_ref[...] = d_q.astype(jnp.bfloat16).reshape(dq_ref.shape)
    d_kv = jnp.concatenate([d_k, d_v], axis=1).astype(jnp.bfloat16)
    half, lanes, cycle = dkv_ref.shape[0], 2 * HEAD_SIZE, len(kv_refs)
    for j in range(cycle):
        for core_side in range(2):
            first = (2 * j + core_side) * half
            column = pl.multiple_of((core_side * cycle + (here_ref[0] ^ j)) * lanes, lanes)
            dkv_ref[:, pl.ds(column, lanes)] = d_kv[first : first + half]


def of_pack(array, half):
    return (array, (2, half, array.shape[-1]), lambda p: (0, p, 0))


def place_blocks(places):
    return [(array, (1,) + array.shape[1:], lambda p: (p, 0, 0)) for array in places]


def attend(q, places, wo, kvs, packs, groups):
    half = q.shape[1] // packs
    width = wo.shape[0]
    ins = [of_pack(q, half)] + place_blocks(places) + [still(wo)] + [of_pack(kv, half) for kv in kvs]
    outs = [of_pack(low(*q.shape), half)]
    outs += [(low(q.shape[1], width), (half, width), lambda p: (p, 0))] * 2
    return gridded(functools.partial(attend_kernel, groups), packs, ins, outs)


def attend_back(here, q, d_branch, cosine, sine, places, wo, kvs, packs, groups):
    half = q.shape[1] // packs
    cycle = len(kvs)
    ins = [of_pack(q, half)]
    ins += [(array, (half, array.shape[1]), lambda p: (p, 0)) for array in d_branch]
    ins += [of_pack(cosine, half), of_pack(sine, half)] + place_blocks(places) + [still(wo)]
    ins += [of_pack(kv, half) for kv in kvs]
    lanes = 2 * HEAD_SIZE
    outs = [of_pack(low(*q.shape), half)]
    outs.append((low(q.shape[1], 2 * cycle * lanes), (half, 2 * cycle * lanes), lambda p: (p, 0)))
    kernel = functools.partial(attend_back_kernel, groups)
    return gridded(kernel, packs, ins, outs, scalars=(here,))


def split_heads(
    hidden_in,
    out_cotangent,
    norm1_gain,
    q_weight,
    key_projection_weight,
    value_projection_weight,
    o_weight,
    norm2_gain,
    gate_weight,
    up_weight,
    down_weight,
    seq_lengths,
    span_order,
):
    packs = lax.axis_size("fsdp")
    cycle = lax.axis_size("ctx")
    pack = lax.axis_index("fsdp")
    core = lax.axis_index("tp")
    here = lax.axis_index("ctx")
    rows = hidden_in.shape[0]
    half = rows // 2
    tokens = packs * rows
    depth = q_weight.shape[0]
    width = depth * packs
    q_width = q_weight.shape[1] // packs
    k_width = key_projection_weight.shape[1] // packs
    ff_width = gate_weight.shape[1] // packs
    ff_half = ff_width // 2
    groups = q_width // k_width
    far = range(1, packs)
    steps = Steps(Line("ctx"))
    kept = {}


    def columns(weight, k, count, first=0, of=None):
        return lax.dynamic_slice_in_dim(weight, (pack ^ k) * (of or count) + first, count, 1)

    def to_pack(name, k, array):
        return ((name, k), array, "fsdp", pairs_by(k, packs))

    def send_all(name, arrays):
        return [to_pack(name, k, array) for k, array in zip(far, arrays)]

    def arrived(name):
        return [steps.take((name, k)) for k in far]

    def to_core(name, array):
        return [(name, array, "tp", pairs_by(1, 2))]

    def to_rows(name, first):
        kept[name], *others = fold(first, steps.take(name), packs)
        return send_all(name, others)

    def joined(name, own, others):
        kept[name] = join(own, others)
        return to_core(name, kept[name])

    def both_of(name):
        return kept[name], steps.take(name)

    index = jnp.stack([pack, core]).astype(jnp.int32)
    here_arg = here.astype(jnp.int32)[None]
    side_arg = here_arg & 1
    at_end = steps.line.at_end

    own_in, *in_moves = prepare(hidden_in, index, packs)
    own_cot, *cot_moves = prepare(out_cotangent, index, packs)

    side = here & 1
    weights = (q_weight, key_projection_weight, value_projection_weight, o_weight)
    widths = (q_width, k_width, k_width, q_width)

    def attention_piece(k, first, count):
        return jnp.concatenate(
            [
                lax.dynamic_slice(weight, (first, (pack ^ k) * each), (count, each))
                for weight, each in zip(weights, widths)
            ],
            axis=1,
        )

    meta = jnp.concatenate([span_order[0], seq_lengths[0]])
    order_len, meta_len = span_order.shape[1], meta.shape[0]
    metas = jnp.concatenate([(meta // 32).astype(jnp.bfloat16), (meta % 32).astype(jnp.bfloat16)])
    info = jnp.stack(
        [
            jnp.pad(jnp.concatenate([norm1_gain, metas]), (0, sum(widths) - depth - 2 * meta_len)),
            jnp.pad(norm2_gain, (0, sum(widths) - depth)),
        ]
    )
    info_rows = jnp.pad(info, ((0, 14), (0, 0)))
    row_half = depth // 2
    steps.step(
        [
            to_pack(
                "attention",
                k,
                jnp.concatenate([attention_piece(k, side * row_half, row_half), info_rows], axis=0),
            )
            for k in far
        ]
    )
    pieces = []

    def pass_rows():
        pieces.extend(arrived("attention"))
        rows_on = join_rows(pieces, row_half)
        return [("attention_rows", rows_on, "ctx", pairs_by(1, cycle))]

    steps.step(send_all("in", in_moves), late=pass_rows)
    infos = jnp.stack([info] + [piece[row_half : row_half + 2] for piece in pieces])
    all_gains = infos[:, :, :depth].astype(jnp.float32)
    gain_one = all_gains[:, 0].reshape(1, -1)
    gain_two = all_gains[:, 1].reshape(1, -1)
    metas = infos[:, 0, depth : depth + 2 * meta_len].astype(jnp.int32)
    metas = metas[:, :meta_len] * 32 + metas[:, meta_len:]
    orders, lengths = metas[:, :order_len], metas[:, order_len:]

    others = jnp.stack([here ^ j for j in range(cycle)])
    first = jnp.sum(
        jnp.where(
            others[None, :, None] == jnp.arange(order_len, dtype=jnp.int32)[None, None, :],
            orders[:, None, :],
            0,
        ),
        axis=2,
    )
    halves = jnp.stack([core, core ^ 1])[None, None, :]
    section = jnp.where(halves == 0, first[:, :, None], 2 * cycle - 1 - first[:, :, None])
    places = section[..., None] * half + jnp.arange(half, dtype=jnp.int32)
    places = places.reshape(packs, cycle * rows)
    starts = jnp.zeros_like(places)
    end = jnp.zeros((packs, 1), jnp.int32)
    for j in range(lengths.shape[1]):
        end = end + lengths[:, j : j + 1]
        starts = jnp.where(places >= end, end, starts)
    place_args = (places[:, :rows, None], starts[:, :rows, None], places[:, None, :])
    offsets = (places - starts)[:, :rows].reshape(packs, 2, half).transpose(1, 0, 2)
    cosine, sine = in_vmem(
        turns_kernel,
        [full(2, tokens // 2, 2 * HEAD_SIZE)] * 2,
        offsets.astype(jnp.float32).reshape(2, tokens // 2, 1),
    )


    def two_halves(weight, k):
        return jnp.concatenate(
            [
                columns(weight, k, ff_half, side * ff_half, ff_width),
                columns(weight, k, ff_half, (1 - side) * ff_half, ff_width),
            ],
            axis=1,
        )

    def fetch(ks):
        return [
            to_pack(
                "gate_up",
                k,
                jnp.concatenate(
                    [
                        columns(weight, k, ff_half, side * ff_half, ff_width)
                        for weight in (gate_weight, up_weight)
                    ],
                    axis=1,
                ),
            )
            for k in ks
        ]

    def to_neighbour(k):
        return [(("neighbour", k), fetched[k], "ctx", pairs_by(1, cycle))]

    fetched = {}
    own_piece = attention_piece(0, 0, depth)
    cosine, sine, own_piece, *place_args = steps.step(
        fetch([1, 2]), carry=(cosine, sine, own_piece, *place_args)
    )
    all_in = join(own_in, arrived("in"))
    all_in = (all_in, swap(all_in, "tp", 1))
    normed_mine, normed_other, q_rot, kv_own, wqkv, wo = project_qkv(
        side_arg,
        all_in,
        gain_one,
        cosine,
        sine,
        own_piece,
        pieces,
        steps.take("attention_rows"),
        q_width,
        2 * k_width,
    )
    normed_one = (normed_mine, normed_other)
    steps.step(
        [(("kv", j), kv_own, "ctx", pairs_by(j, cycle)) for j in range(1, cycle)] + fetch([3])
    )
    fetched[1], fetched[2] = steps.take(("gate_up", 1)), steps.take(("gate_up", 2))
    steps.step(send_all("cot", cot_moves) + to_neighbour(1))
    fetched[3] = steps.take(("gate_up", 3))
    kvs = [kv_own] + [steps.take(("kv", j)) for j in range(1, cycle)]
    attn, first, second = attend(q_rot, place_args, wo, kvs, packs, groups)
    attn_low = attn.reshape(tokens, q_width)
    steps.step(to_core("branch", second))
    steps.step(to_neighbour(2), late=lambda: to_rows("branch", first))
    kept["cot"] = join(own_cot, arrived("cot"))

    def middle_moves():
        kept["middle"], kept["normed"], *sends = in_vmem(
            functools.partial(middle_kernel, packs),
            [full(half, width)] + [low(half, width)] * packs,
            own_in,
            gain_two,
            kept["branch"],
            *arrived("branch"),
        )
        return send_all("two", sends)

    steps.step(to_neighbour(3) + to_core("cot", kept["cot"]), late=middle_moves)

    def wd_moves(ks):
        return [to_pack("down", k, two_halves(down_weight, k)) for k in ks]

    own_columns = [two_halves(weight, 0) for weight in (gate_weight, up_weight, down_weight)]
    own_gate, own_up, own_down = steps.step(
        wd_moves([1, 2]),
        late=lambda: joined("two", kept["normed"], arrived("two")),
        carry=own_columns,
    )
    all_cot = both_of("cot")
    neighbours = [steps.take(("neighbour", k)) for k in far]
    normed_two = (kept["two"], dict(steps.others)["two"])

    gate_val, up_val, hidden, wg, wu = gate_up(
        normed_two, own_gate, own_up, [fetched[k] for k in far], neighbours
    )
    d_wd = weight_grad([(*all_cot, hidden)], packs, side_arg)

    def back(name, grad, ks):
        return [to_pack(name, k, grad[k]) for k in ks]

    def entry(name, k, grad=None):
        return ((name, k), grad[0] if k == 0 else None)

    steps.step(back("wd", d_wd, [1, 2]), summed=entry("wd", 0, d_wd))
    steps.step(wd_moves([3]), summed=entry("wd", 1))
    steps.step(back("wd", d_wd, [3]), summed=entry("wd", 2))
    d_gate, d_up, wd = units_back(all_cot, [own_down] + arrived("down"), gate_val, up_val)
    first, second = rows_sum([d_gate, d_up], [wg, wu])
    steps.step(to_core("d_two", second), summed=entry("wd", 3))
    d_wg = weight_grad([(*normed_two, d_gate)], packs, side_arg)
    steps.step(back("wg", d_wg, [1, 2]), summed=entry("wg", 0, d_wg))
    d_wu = weight_grad([(*normed_two, d_up)], packs, side_arg)
    steps.step(
        summed=entry("wu", 0, d_wu), late=functools.partial(to_rows, "d_two", first)
    )

    def branch_back():
        kept["d_middle"], kept["d_gain_two"], kept["d_branch"], *sends = in_vmem(
            functools.partial(branch_back_kernel, packs),
            [full(half, width), full(1, width)] + [low(half, width)] * packs,
            kept["middle"],
            gain_two,
            own_cot,
            kept["d_two"],
            *arrived("d_two"),
        )
        return send_all("d_branch", sends)

    first, second = rows_sum([hidden], [wd])
    steps.step(summed=entry("wg", 1), late=branch_back, carry=(first, second))
    steps.step(
        back("wg", d_wg, [3]),
        summed=entry("wg", 2),
        late=lambda: joined("all_branch", kept["d_branch"], arrived("d_branch")),
    )
    d_branch = None

    def attention_back():
        return attend_back(
            here_arg, q_rot, d_branch, cosine, sine, place_args, wo, kvs, packs, groups
        )

    sums = steps.line.sums

    def settle_all(name):
        return settle(at_end, index, [sums[name, k] for k in range(packs)], ff_width)

    steps.step(back("wu", d_wu, [1, 2]), summed=entry("wg", 3))
    d_branch = both_of("all_branch")
    d_q, d_kv = attention_back()
    steps.step(back("wu", d_wu, [3]), summed=("d_kv", d_kv))
    down_grad = settle_all("wd")
    steps.step(to_core("ff", second), summed=entry("wu", 1))
    (down_grad,) = steps.step(
        summed=entry("wu", 2),
        late=functools.partial(to_rows, "ff", first),
        carry=(down_grad,),
    )
    steps.step(summed=entry("wu", 3))
    d_qkv = in_vmem(
        d_qkv_kernel,
        [low(tokens, q_width + 2 * k_width)],
        at_end,
        here_arg,
        *sums["d_kv"],
        d_q,
        cosine,
        sine,
        scalars=2,
    )[0]
    d_wqkvo = weight_grad([(*normed_one, d_qkv), (*d_branch, attn_low)], packs)
    first, second = rows_sum([d_qkv], [wqkv])
    result = in_vmem(
        result_kernel, [low(half, width)], kept["middle"], kept["ff"], *arrived("ff")
    )[0]
    steps.step(
        back("wqkvo", d_wqkvo, [1, 2]) + to_core("d_one", second) + to_core("result", result),
        summed=entry("wqkvo", 0, d_wqkvo),
    )
    steps.step(late=functools.partial(to_rows, "d_one", first), summed=entry("wqkvo", 1))

    def both_rows(own, other):
        return in_vmem(
            functools.partial(rows_back_kernel, packs),
            [low(rows, width)],
            index,
            own,
            other,
            scalars=1,
        )[0]

    out_hidden = both_rows(result, steps.take("result"))
    gate_grad = settle_all("wg")
    def gains_to_core():
        kept["in_grad"], d_gain_one = in_vmem(
            functools.partial(in_grad_kernel, packs),
            [low(half, width), full(1, width)],
            own_in,
            gain_one,
            kept["d_middle"],
            kept["d_one"],
            *arrived("d_one"),
        )
        kept["gains"] = jnp.concatenate([d_gain_one, kept["d_gain_two"]], axis=0)
        return to_core("gains", kept["gains"]) + to_core("in_grad", kept["in_grad"])

    def gains_to_packs():
        kept["gains"] = kept["gains"] + steps.take("gains")
        return [to_pack("gains", k, kept["gains"][:, k * depth : (k + 1) * depth]) for k in far]

    def gains_along():
        kept["gains"] = kept["gains"][:, :depth]
        for k in far:
            kept["gains"] = kept["gains"] + steps.take(("gains", k))
        return [(("gains", j), kept["gains"], "ctx", pairs_by(j, cycle)) for j in range(1, cycle)]

    out_hidden, gate_grad = steps.step(
        back("wqkvo", d_wqkvo, [3]),
        summed=entry("wqkvo", 2),
        late=gains_to_core,
        carry=(out_hidden, gate_grad),
    )
    up_grad = settle_all("wu")

    (up_grad,) = steps.step(summed=entry("wqkvo", 3), late=gains_to_packs, carry=(up_grad,))
    in_grad = both_rows(kept["in_grad"], steps.take("in_grad"))
    (in_grad,) = steps.step(late=gains_along, carry=(in_grad,))
    steps.step()
    steps.step()
    shares_of_gains = jnp.stack(
        [kept["gains"]] + [steps.take(("gains", j)) for j in range(1, cycle)]
    )
    gains = steps.token[0, 0]
    for place in range(cycle):
        gains = gains + lax.dynamic_index_in_dim(shares_of_gains, here ^ place, 0, keepdims=False)
    q_grad, k_grad, v_grad, o_grad = settle_attention(
        at_end, index, [sums["wqkvo", k] for k in range(packs)], q_width, 2 * k_width
    )
    return (
        out_hidden,
        in_grad,
        gains[0],
        q_grad,
        k_grad,
        v_grad,
        o_grad,
        gains[1],
        gate_grad,
        up_grad,
        down_grad,
    )


def gathered_weights(
    hidden_in,
    out_cotangent,
    norm1_gain,
    q_weight,
    key_projection_weight,
    value_projection_weight,
    o_weight,
    norm2_gain,
    gate_weight,
    up_weight,
    down_weight,
    seq_lengths,
    span_order,
):
    rows_here = hidden_in.shape[0]
    order_row = span_order[0]
    length_row = seq_lengths[0]
    kv_heads = key_projection_weight.shape[1] // HEAD_SIZE
    query_groups = QUERY_HEADS // KEY_VALUE_HEADS
    score_scale = 1.0 / math.sqrt(HEAD_SIZE)
    whole_rows = rows_here * lax.axis_size("ctx")
    local_rows = lax.axis_index("ctx") * rows_here + jnp.arange(rows_here, dtype=jnp.int32)
    q_place, q_segment, q_offset = stream_place(local_rows, order_row, length_row, rows_here)
    inputs = hidden_in.astype(jnp.float32)
    gain_one, wq_full, wk_full, wv_full, wo_full = (
        lax.all_gather(norm1_gain, "fsdp", axis=0, tiled=True),
        lax.all_gather(q_weight, "fsdp", axis=0, tiled=True),
        lax.all_gather(key_projection_weight, "fsdp", axis=0, tiled=True),
        lax.all_gather(value_projection_weight, "fsdp", axis=0, tiled=True),
        lax.all_gather(o_weight, "fsdp", axis=0, tiled=True),
    )
    gain_one = gain_one.astype(jnp.float32)
    first_normalized = normalize(inputs, gain_one)
    normed_low = first_normalized.astype(jnp.bfloat16)
    q_linear = jnp.dot(normed_low, wq_full, preferred_element_type=jnp.float32).reshape(
        rows_here, kv_heads * query_groups, HEAD_SIZE
    )
    k_linear = jnp.dot(normed_low, wk_full, preferred_element_type=jnp.float32).reshape(
        rows_here, kv_heads, HEAD_SIZE
    )
    q_rotated = (
        rotary_embedding(q_linear, q_offset)
        .astype(jnp.bfloat16)
        .reshape(rows_here, kv_heads, query_groups, HEAD_SIZE)
    )
    k_rotated = (
        rotary_embedding(k_linear, q_offset)
        .astype(jnp.bfloat16)
        .reshape(rows_here, kv_heads * HEAD_SIZE)
    )
    v_low = jnp.dot(normed_low, wv_full, preferred_element_type=jnp.float32).astype(jnp.bfloat16)

    def key_blocks(shard_rows):
        row_count = shard_rows.shape[0]
        key_total_width = math.gcd(row_count, 512)
        number = row_count // key_total_width
        k_place, k_segment, _ = stream_place(
            jnp.arange(row_count, dtype=jnp.int32), order_row, length_row, rows_here
        )
        return (
            key_total_width,
            number,
            k_place.reshape(number, key_total_width),
            k_segment.reshape(number, key_total_width),
        )

    def scores_of(key_block, place_block, segment_block):
        scores = (
            jnp.einsum("qkgd,skd->kgqs", q_rotated, key_block, preferred_element_type=jnp.float32)
            * score_scale
        )
        visible = (
            (q_place[:, None] >= place_block[None, :])
            & (q_segment[:, None] == segment_block[None, :])
        )[None, None]
        return (jnp.where(visible, scores, -1e30), visible)

    start_state = (
        jnp.full((kv_heads, query_groups, rows_here), -1e30, jnp.float32),
        jnp.zeros((kv_heads, query_groups, rows_here), jnp.float32),
        jnp.zeros((kv_heads, query_groups, rows_here, HEAD_SIZE), jnp.float32),
    )
    folded = start_state
    key_row_block = lax.all_gather(k_rotated, "ctx", axis=0, tiled=True)
    value_row_block = lax.all_gather(v_low, "ctx", axis=0, tiled=True)
    key_total_width, number, k_place, k_segment = key_blocks(key_row_block)

    def one_step(carried, pieces):
        running_max, totals, accumulated = carried
        key_block, value_block, place_block, segment_block = pieces
        scores, visible = scores_of(key_block, place_block, segment_block)
        new_max = jnp.maximum(running_max, jnp.max(scores, axis=-1))
        weights = jnp.where(visible, jnp.exp(scores - new_max[..., None]), 0.0)
        factor = jnp.exp(running_max - new_max)
        totals = totals * factor + jnp.sum(weights, axis=-1)
        accumulated = accumulated * factor[..., None] + jnp.einsum(
            "kgqs,skd->kgqd",
            weights.astype(jnp.bfloat16),
            value_block,
            preferred_element_type=jnp.float32,
        )
        return ((new_max, totals, accumulated), None)

    pieces = (
        key_row_block.reshape(number, key_total_width, kv_heads, HEAD_SIZE),
        value_row_block.reshape(number, key_total_width, kv_heads, HEAD_SIZE),
        k_place,
        k_segment,
    )
    folded, _ = lax.scan(one_step, folded, pieces)
    running_max, totals, accumulated = folded
    mixed_out = jnp.transpose(accumulated / totals[..., None], (2, 0, 1, 3))
    log_sum = running_max + jnp.log(totals)
    attn_low = mixed_out.reshape(rows_here, kv_heads * query_groups * HEAD_SIZE).astype(
        jnp.bfloat16
    )
    branch = lax.psum(contract_last(attn_low, wo_full).astype(jnp.bfloat16), "tp").astype(
        jnp.float32
    )
    middle = inputs + branch
    gain_two, wg_full, wu_full, wd_full = (
        lax.all_gather(norm2_gain, "fsdp", axis=0, tiled=True),
        lax.all_gather(gate_weight, "fsdp", axis=0, tiled=True),
        lax.all_gather(up_weight, "fsdp", axis=0, tiled=True),
        lax.all_gather(down_weight, "fsdp", axis=0, tiled=True),
    )
    gain_two = gain_two.astype(jnp.float32)
    normed_two = normalize(middle, gain_two)
    normed_two_low = normed_two.astype(jnp.bfloat16)
    gate_val = jnp.dot(normed_two_low, wg_full, preferred_element_type=jnp.float32)
    up_val = jnp.dot(normed_two_low, wu_full, preferred_element_type=jnp.float32)
    hidden = swiglu(gate_val, up_val).astype(jnp.bfloat16)
    ffn_out = lax.psum(contract_last(hidden, wd_full).astype(jnp.bfloat16), "tp").astype(
        jnp.float32
    )
    result = (middle + ffn_out).astype(jnp.bfloat16)
    grad_out = out_cotangent.astype(jnp.float32)
    d_wd = contract_first(out_cotangent, hidden)
    d_hidden = jnp.dot(out_cotangent, wd_full, preferred_element_type=jnp.float32)
    _, swiglu_back = jax.vjp(swiglu, gate_val, up_val)
    d_gate, d_up = swiglu_back(d_hidden)
    d_gate_low = d_gate.astype(jnp.bfloat16)
    d_up_low = d_up.astype(jnp.bfloat16)
    d_wg = contract_first(normed_two_low, d_gate_low)
    d_wu = contract_first(normed_two_low, d_up_low)
    d_normed_two = lax.psum(
        (contract_last(d_gate_low, wg_full) + contract_last(d_up_low, wu_full)).astype(
            jnp.bfloat16
        ),
        "tp",
    ).astype(jnp.float32)
    _, norm_two_back = jax.vjp(normalize, middle, gain_two)
    d_middle_norm, d_gain_two = norm_two_back(d_normed_two)
    d_middle = grad_out + d_middle_norm
    d_branch_low = d_middle.astype(jnp.bfloat16)
    d_wo = contract_first(d_branch_low, attn_low)
    d_attn = jnp.dot(d_branch_low, wo_full, preferred_element_type=jnp.float32).astype(jnp.bfloat16)
    d_attn_heads = d_attn.reshape(rows_here, kv_heads, query_groups, HEAD_SIZE)
    row_delta = jnp.einsum("qkgd,qkgd->kgq", d_attn_heads.astype(jnp.float32), mixed_out)
    back_state = (
        jnp.zeros((rows_here, kv_heads, query_groups, HEAD_SIZE), jnp.float32),
        jnp.zeros((whole_rows, kv_heads, HEAD_SIZE), jnp.float32),
        jnp.zeros((whole_rows, kv_heads, HEAD_SIZE), jnp.float32),
    )
    folded = back_state
    key_row_block = lax.all_gather(k_rotated, "ctx", axis=0, tiled=True)
    value_row_block = lax.all_gather(v_low, "ctx", axis=0, tiled=True)
    key_total_width, number, k_place, k_segment = key_blocks(key_row_block)

    def one_step(carried, pieces):
        d_query, d_keys, d_values = carried
        key_block, value_block, place_block, segment_block, step_index = pieces
        scores, visible = scores_of(key_block, place_block, segment_block)
        prob_rows = jnp.where(visible, jnp.exp(scores - log_sum[..., None]), 0.0)
        d_values_block = jnp.einsum(
            "kgqs,qkgd->skd",
            prob_rows.astype(jnp.bfloat16),
            d_attn_heads,
            preferred_element_type=jnp.float32,
        )
        d_probs = jnp.einsum(
            "qkgd,skd->kgqs", d_attn_heads, value_block, preferred_element_type=jnp.float32
        )
        d_scores = (prob_rows * (d_probs - row_delta[..., None])).astype(jnp.bfloat16)
        d_query = (
            d_query
            + jnp.einsum("kgqs,skd->qkgd", d_scores, key_block, preferred_element_type=jnp.float32)
            * score_scale
        )
        d_keys_block = (
            jnp.einsum("kgqs,qkgd->skd", d_scores, q_rotated, preferred_element_type=jnp.float32)
            * score_scale
        )
        row_first = step_index * key_total_width
        d_keys = lax.dynamic_update_slice_in_dim(
            d_keys,
            lax.dynamic_slice_in_dim(d_keys, row_first, key_total_width, 0) + d_keys_block,
            row_first,
            0,
        )
        d_values = lax.dynamic_update_slice_in_dim(
            d_values,
            lax.dynamic_slice_in_dim(d_values, row_first, key_total_width, 0) + d_values_block,
            row_first,
            0,
        )
        return ((d_query, d_keys, d_values), None)

    pieces = (
        key_row_block.reshape(number, key_total_width, kv_heads, HEAD_SIZE),
        value_row_block.reshape(number, key_total_width, kv_heads, HEAD_SIZE),
        k_place,
        k_segment,
        jnp.arange(number, dtype=jnp.int32),
    )
    folded, _ = lax.scan(one_step, folded, pieces)
    d_query, d_keys_all, d_values_all = folded
    d_key_own, d_value_own = (
        lax.psum_scatter(
            d_keys_all.astype(jnp.bfloat16), "ctx", scatter_dimension=0, tiled=True
        ).astype(jnp.float32),
        lax.psum_scatter(
            d_values_all.astype(jnp.bfloat16), "ctx", scatter_dimension=0, tiled=True
        ).astype(jnp.float32),
    )
    _, rope_q_back = jax.vjp(lambda rotated_in: rotary_embedding(rotated_in, q_offset), q_linear)
    _, rope_k_back = jax.vjp(lambda rotated_in: rotary_embedding(rotated_in, q_offset), k_linear)
    (d_q_linear,) = rope_q_back(d_query.reshape(rows_here, kv_heads * query_groups, HEAD_SIZE))
    (d_k_linear,) = rope_k_back(d_key_own)
    d_q_low = d_q_linear.reshape(rows_here, kv_heads * query_groups * HEAD_SIZE).astype(
        jnp.bfloat16
    )
    d_k_low = d_k_linear.reshape(rows_here, kv_heads * HEAD_SIZE).astype(jnp.bfloat16)
    d_v_low = d_value_own.reshape(rows_here, kv_heads * HEAD_SIZE).astype(jnp.bfloat16)
    d_wq = contract_first(normed_low, d_q_low)
    d_wk = contract_first(normed_low, d_k_low)
    d_wv = contract_first(normed_low, d_v_low)
    d_normed_one = lax.psum(
        (
            contract_last(d_q_low, wq_full)
            + contract_last(d_k_low, wk_full)
            + contract_last(d_v_low, wv_full)
        ).astype(jnp.bfloat16),
        "tp",
    ).astype(jnp.float32)
    _, norm_one_back = jax.vjp(normalize, inputs, gain_one)
    d_inputs_norm, d_gain_one = norm_one_back(d_normed_one)
    in_grad = (d_middle + d_inputs_norm).astype(jnp.bfloat16)
    weight_grads = (d_gain_one, d_wq, d_wk, d_wv, d_wo, d_gain_two, d_wg, d_wu, d_wd)
    shares = (
        lax.psum_scatter(weight_grads[0], ("fsdp", "ctx"), scatter_dimension=0, tiled=True),
        lax.psum_scatter(weight_grads[1], ("fsdp", "ctx"), scatter_dimension=0, tiled=True),
        lax.psum_scatter(weight_grads[2], ("fsdp", "ctx"), scatter_dimension=0, tiled=True),
        lax.psum_scatter(weight_grads[3], ("fsdp", "ctx"), scatter_dimension=0, tiled=True),
        lax.psum_scatter(weight_grads[4], ("fsdp", "ctx"), scatter_dimension=0, tiled=True),
        lax.psum_scatter(weight_grads[5], ("fsdp", "ctx"), scatter_dimension=0, tiled=True),
        lax.psum_scatter(weight_grads[6], ("fsdp", "ctx"), scatter_dimension=0, tiled=True),
        lax.psum_scatter(weight_grads[7], ("fsdp", "ctx"), scatter_dimension=0, tiled=True),
        lax.psum_scatter(weight_grads[8], ("fsdp", "ctx"), scatter_dimension=0, tiled=True),
    )
    owned_grads = (
        lax.all_gather(shares[0].astype(jnp.bfloat16), "ctx", axis=0, tiled=True).astype(
            jnp.float32
        ),
        lax.all_gather(shares[1].astype(jnp.bfloat16), "ctx", axis=0, tiled=True).astype(
            jnp.float32
        ),
        lax.all_gather(shares[2].astype(jnp.bfloat16), "ctx", axis=0, tiled=True).astype(
            jnp.float32
        ),
        lax.all_gather(shares[3].astype(jnp.bfloat16), "ctx", axis=0, tiled=True).astype(
            jnp.float32
        ),
        lax.all_gather(shares[4].astype(jnp.bfloat16), "ctx", axis=0, tiled=True).astype(
            jnp.float32
        ),
        lax.all_gather(shares[5].astype(jnp.bfloat16), "ctx", axis=0, tiled=True).astype(
            jnp.float32
        ),
        lax.all_gather(shares[6].astype(jnp.bfloat16), "ctx", axis=0, tiled=True).astype(
            jnp.float32
        ),
        lax.all_gather(shares[7].astype(jnp.bfloat16), "ctx", axis=0, tiled=True).astype(
            jnp.float32
        ),
        lax.all_gather(shares[8].astype(jnp.bfloat16), "ctx", axis=0, tiled=True).astype(
            jnp.float32
        ),
    )
    return (
        result,
        in_grad,
        owned_grads[0],
        owned_grads[1],
        owned_grads[2],
        owned_grads[3],
        owned_grads[4],
        owned_grads[5],
        owned_grads[6],
        owned_grads[7],
        owned_grads[8],
    )


def solution(mesh):
    placed = (
        P(("fsdp", "ctx"), None),
        P(("fsdp", "ctx"), None),
        P("fsdp"),
        P("fsdp", "tp"),
        P("fsdp", "tp"),
        P("fsdp", "tp"),
        P("fsdp", "tp"),
        P("fsdp"),
        P("fsdp", "tp"),
        P("fsdp", "tp"),
        P("fsdp", "tp"),
        P("fsdp", None),
        P("fsdp", None),
    )
    plane = mesh.shape["fsdp"] * mesh.shape["tp"]
    splits = mesh.shape["tp"] == 2 and KEY_VALUE_HEADS == plane and mesh.shape["ctx"] == 4
    return jax.shard_map(
        split_heads if splits else gathered_weights,
        mesh=mesh,
        in_specs=placed,
        out_specs=(
            P(("fsdp", "ctx"), None),
            P(("fsdp", "ctx"), None),
            P("fsdp"),
            P("fsdp", "tp"),
            P("fsdp", "tp"),
            P("fsdp", "tp"),
            P("fsdp", "tp"),
            P("fsdp"),
            P("fsdp", "tp"),
            P("fsdp", "tp"),
            P("fsdp", "tp"),
        ),
        check_vma=False,
    )
```

```python
import functools
import math

import jax
import jax.numpy as jnp
from jax import lax
from jax.experimental import pallas as pl
from jax.experimental.pallas import tpu as pltpu
from jax.sharding import PartitionSpec as P

QUERY_HEADS = 32
KEY_VALUE_HEADS = 8
HEAD_SIZE = 64


def stream_place(row_ids, order_row, length_row, tok_dev):
    cycle_size = order_row.shape[0]
    half_len = tok_dev // 2
    cycle_rank = row_ids // tok_dev
    within = row_ids % tok_dev
    first_section = jnp.sum(
        jnp.where(
            cycle_rank[:, None] == jnp.arange(cycle_size, dtype=jnp.int32)[None, :],
            order_row[None, :],
            0,
        ),
        axis=1,
        dtype=jnp.int32,
    )
    section = jnp.where(within >= half_len, 2 * cycle_size - 1 - first_section, first_section)
    places = section * half_len + within % half_len
    seq_ends = jnp.cumsum(length_row, dtype=jnp.int32)
    passed = places[:, None] >= seq_ends[None, :]
    segment = jnp.sum(passed.astype(jnp.int32), axis=1, dtype=jnp.int32)
    offset = places - jnp.sum(jnp.where(passed, length_row[None, :], 0), axis=1, dtype=jnp.int32)
    return (places, segment, offset)


def rotary_embedding(values, positions):
    half_len = values.shape[-1] // 2
    frequency = jnp.exp(
        -math.log(500000.0) * jnp.arange(half_len, dtype=jnp.float32) * 2.0 / values.shape[-1]
    )
    angles = positions.astype(jnp.float32)[:, None] * frequency[None, :]
    cosine = jnp.cos(angles)[:, None, :]
    sine = jnp.sin(angles)[:, None, :]
    lower_half = values[..., :half_len]
    upper_half = values[..., half_len:]
    return jnp.concatenate(
        [lower_half * cosine - upper_half * sine, upper_half * cosine + lower_half * sine], axis=-1
    )


def normalize(values, gain_vec):
    return values * lax.rsqrt(jnp.mean(values * values, axis=-1, keepdims=True) + 1e-05) * gain_vec


def swiglu(gate_val, up_val):
    return jax.nn.silu(gate_val) * up_val


def contract_last(left, right):
    return lax.dot_general(
        left, right, (((1,), (1,)), ((), ())), preferred_element_type=jnp.float32
    )


def contract_first(left, right):
    return lax.dot_general(
        left, right, (((0,), (0,)), ((), ())), preferred_element_type=jnp.float32
    )


VMEM_LIMIT = 30 * 1024 * 1024
MIDDLE_LIMIT = 20 * 1024 * 1024
SMALL_LIMIT = 12 * 1024 * 1024
SMALL = pl.CostEstimate(flops=1, bytes_accessed=1, transcendentals=0)


def pairs_by(distance, size):
    return [(i, i ^ distance) for i in range(size)]


def swap(array, axis, distance):
    return lax.ppermute(array, axis, pairs_by(distance, lax.axis_size(axis)))


class Line:
    def __init__(self, axis):
        index = lax.axis_index(axis)
        size = lax.axis_size(axis)
        self.axis = axis
        self.at_end = ((index == 0) | (index == size - 1)).astype(jnp.int32)[None]
        self.entered = self.halfway = self.leaving = None
        self.sums = {}

    def advance(self, got, entering):
        if self.leaving is not None:
            name, sent = self.leaving
            self.sums[name] = (got["ends"], sent)
        moves = []
        halfway = None
        if self.entered is not None:
            name, value = self.entered
            halfway = (name, add_low(value, got["ends"]))
            moves.append(("middle", halfway[1], self.axis, [(1, 2), (2, 1)]))
        leaving = None
        inwards, outwards = [(0, 1), (3, 2)], [(1, 0), (2, 3)]
        if self.halfway is not None:
            name, value = self.halfway
            if entering is None:
                sent, pairs = add_low(value, got["middle"]), outwards
            else:
                sent = either_way(self.at_end, entering[1], value, got["middle"])
                pairs = inwards + outwards
            leaving = (name, sent)
            moves.append(("ends", sent, self.axis, pairs))
        elif entering is not None:
            moves.append(("ends", entering[1], self.axis, inwards))
        self.entered, self.halfway, self.leaving = entering, halfway, leaving
        return moves


class Steps:
    def __init__(self, line):
        self.line = line
        self.got = {}
        self.on_line = []
        self.others = []
        self.token = jnp.zeros((8, 128), jnp.float32)

    def wait(self, flying, arrays):
        count = len(flying)
        held = lax.optimization_barrier(
            (self.token,) + tuple(value for _, value in flying) + tuple(arrays)
        )
        self.token = held[0]
        for (name, _), value in zip(flying, held[1:]):
            self.got[name] = value
        return list(held[1 + count :])

    def start(self, moves):
        return [(name, lax.ppermute(value, axis, pairs)) for name, value, axis, pairs in moves]

    def step(self, moves=(), summed=None, late=None, carry=(), hold=False):
        moves, carry = list(moves), list(carry)
        arrays = [move[1] for move in moves] + carry
        fresh = [summed[1]] if summed is not None and summed[1] is not None else []
        together = summed is not None and not fresh and summed[0] not in self.got
        if together or not self.on_line:
            held = self.wait(self.on_line + self.others, fresh + arrays)
            held_fresh, held = held[: len(fresh)], held[len(fresh) :]
        else:
            held_fresh = self.wait(self.on_line, fresh)
        entering = summed
        if summed is not None:
            entering = (summed[0], held_fresh[0] if fresh else self.take(summed[0]))
        along = self.line.advance(self.got, entering)
        if not together and self.on_line:
            self.on_line = self.start(along)
            held = self.wait([] if hold else self.others, arrays)
        else:
            self.on_line = self.start(along)
        moves = [
            (name, value, axis, pairs) for (name, _, axis, pairs), value in zip(moves, held)
        ]
        before = self.others if hold else []
        self.others = before + self.start(moves + (late() if late is not None else []))
        return held[len(moves) :]

    def take(self, name):
        return self.got.pop(name)


def in_vmem(kernel, out_shape, *args, scalars=0):
    specs = [pl.BlockSpec(memory_space=pltpu.SMEM)] * scalars
    specs += [pl.BlockSpec(memory_space=pltpu.VMEM)] * (len(args) - scalars)
    return pl.pallas_call(
        kernel,
        out_shape=out_shape,
        in_specs=specs,
        out_specs=[pl.BlockSpec(memory_space=pltpu.VMEM)] * len(out_shape),
        compiler_params=pltpu.CompilerParams(vmem_limit_bytes=SMALL_LIMIT),
        cost_estimate=SMALL,
    )(*args)


def low(*shape):
    return jax.ShapeDtypeStruct(shape, jnp.bfloat16)


def full(*shape):
    return jax.ShapeDtypeStruct(shape, jnp.float32)


def store_seen(ref, value, distance, count):
    width = value.shape[-1] // count
    for block in range(count):
        there = block ^ distance
        ref[: value.shape[0], block * width : (block + 1) * width] = value[
            :, there * width : (there + 1) * width
        ]


def prepare_kernel(count, index_ref, x_ref, own_ref, *sends):
    rows, width = own_ref.shape[0], own_ref.shape[1] // count
    first = pl.multiple_of(index_ref[1] * rows, rows)
    for block in range(count):
        column = pl.multiple_of((index_ref[0] ^ block) * width, width)
        own_ref[:, block * width : (block + 1) * width] = x_ref[
            pl.ds(first, rows), pl.ds(column, width)
        ]
    for k, send in enumerate(sends, 1):
        store_seen(send, own_ref[...], k, count)


def prepare(x, index, count):
    rows, width = x.shape[0] // 2, x.shape[1]
    return in_vmem(
        functools.partial(prepare_kernel, count), [low(rows, width)] * count, index, x, scalars=1
    )


def turns_kernel(offset_ref, cos_ref, sin_ref):
    lane = lax.broadcasted_iota(jnp.int32, cos_ref.shape, 2)
    place = lax.rem(lane, HEAD_SIZE // 2).astype(jnp.float32)
    frequency = jnp.exp(-math.log(500000.0) * place * 2.0 / HEAD_SIZE)
    angle = offset_ref[...] * frequency
    cos_ref[...] = jnp.cos(angle)
    sin_ref[...] = jnp.sin(angle)


def join_kernel(*refs):
    out_ref = refs[-1]
    rows = refs[0].shape[0]
    for i, ref in enumerate(refs[:-1]):
        out_ref[i * rows : (i + 1) * rows, :] = ref[:rows, :]


def join_rows(arrays, rows):
    def kernel(*refs):
        for i, ref in enumerate(refs[:-1]):
            refs[-1][i * rows : (i + 1) * rows, :] = ref[:rows, :]

    return in_vmem(kernel, [low(rows * len(arrays), arrays[0].shape[1])], *arrays)[0]


def join(own, others):
    rows, width = own.shape
    return in_vmem(join_kernel, [low(rows * (1 + len(others)), width)], own, *others)[0]


def fold_kernel(count, first_ref, came_ref, own_ref, *sends):
    rows = own_ref.shape[0]
    for k in range(count):
        here = slice(k * rows, (k + 1) * rows)
        total = first_ref[here, :].astype(jnp.float32) + came_ref[here, :].astype(jnp.float32)
        total = total.astype(jnp.bfloat16)
        if k == 0:
            own_ref[...] = total
        else:
            store_seen(sends[k - 1], total, k, count)


def fold(first, came, count):
    rows, width = first.shape[0] // count, first.shape[1]
    return in_vmem(
        functools.partial(fold_kernel, count), [low(rows, width)] * count, first, came
    )


def total_of(refs):
    total = refs[0][...].astype(jnp.float32)
    for ref in refs[1:]:
        total = total + ref[...].astype(jnp.float32)
    return total


def middle_kernel(count, in_ref, gain_ref, *refs):
    parts, (middle_ref, normed_ref, *sends) = refs[:count], refs[count:]
    middle = in_ref[...].astype(jnp.float32) + total_of(parts)
    middle_ref[...] = middle
    mean = jnp.mean(middle * middle, axis=-1, keepdims=True)
    normed = (middle * lax.rsqrt(mean + 1e-05) * gain_ref[...]).astype(jnp.bfloat16)
    normed_ref[...] = normed
    for k in range(1, count):
        store_seen(sends[k - 1], normed, k, count)


def norm_back(d_normed, x, gain):
    scale = lax.rsqrt(jnp.mean(x * x, axis=-1, keepdims=True) + 1e-05)
    unit = x * scale
    d_unit = d_normed * gain
    d_x = scale * (d_unit - unit * jnp.mean(d_unit * unit, axis=-1, keepdims=True))
    return d_x, jnp.sum(d_normed * unit, axis=0, keepdims=True)


def branch_back_kernel(count, middle_ref, gain_ref, cot_ref, *refs):
    parts, (d_middle_ref, d_gain_ref, branch_ref, *sends) = refs[:count], refs[count:]
    d_x, d_gain_ref[...] = norm_back(total_of(parts), middle_ref[...], gain_ref[...])
    d_middle = cot_ref[...].astype(jnp.float32) + d_x
    d_middle_ref[...] = d_middle
    branch = d_middle.astype(jnp.bfloat16)
    branch_ref[...] = branch
    for k in range(1, count):
        store_seen(sends[k - 1], branch, k, count)


def in_grad_kernel(count, in_ref, gain_ref, d_middle_ref, *refs):
    parts, (grad_ref, d_gain_ref) = refs[:count], refs[count:]
    x = in_ref[...].astype(jnp.float32)
    d_x, d_gain_ref[...] = norm_back(total_of(parts), x, gain_ref[...])
    grad_ref[...] = (d_middle_ref[...] + d_x).astype(jnp.bfloat16)


def gridded(kernel, steps, ins, outs, scalars=(), limit=None):
    return pl.pallas_call(
        kernel,
        grid=(steps,),
        in_specs=[pl.BlockSpec(memory_space=pltpu.SMEM)] * len(scalars)
        + [pl.BlockSpec(block, index) for _, block, index in ins],
        out_specs=[pl.BlockSpec(block, index) for _, block, index in outs],
        out_shape=[shape for shape, _, _ in outs],
        compiler_params=pltpu.CompilerParams(vmem_limit_bytes=limit or MIDDLE_LIMIT),
        cost_estimate=SMALL,
    )(*scalars, *[array for array, _, _ in ins])


def row_blocks(array, rows):
    return (array, (rows, array.shape[1]), lambda i: (i, 0))


def add_low(left, right):
    right = right[:, : left.shape[1]]
    return (left.astype(jnp.float32) + right.astype(jnp.float32)).astype(jnp.bfloat16)


def either_way(at_end, fresh, value, came):
    total = add_low(value, came)
    width = max(fresh.shape[1], value.shape[1])
    if fresh.shape[1] < width:
        fresh = jnp.pad(fresh, ((0, 0), (0, width - fresh.shape[1])))
    if total.shape[1] < width:
        total = jnp.pad(total, ((0, 0), (0, width - total.shape[1])))
    return jnp.where(at_end[0] == 1, fresh, total)


def settled(at_end, came_ref, sent_ref, columns):
    return jnp.where(at_end == 1, came_ref[:, columns], sent_ref[:, columns]).astype(jnp.float32)


def settle_kernel(count, at_end_ref, index_ref, *refs):
    out_ref = refs[-1]
    width = out_ref.shape[1] // count
    for k in range(count):
        column = pl.multiple_of((index_ref[0] ^ k) * width, width)
        out_ref[:, pl.ds(column, width)] = settled(
            at_end_ref[0], refs[2 * k], refs[2 * k + 1], slice(0, width)
        )


def settle(at_end, index, pairs, width):
    count = len(pairs)
    arrays = [array for pair in pairs for array in pair]
    depth = arrays[0].shape[0]
    rows = math.gcd(depth, 128)
    ins = [(array, (rows, width), lambda i: (i, 0)) for array in arrays]
    outs = [row_blocks(full(depth, width * count), rows)]
    kernel = functools.partial(settle_kernel, count)
    return gridded(kernel, depth // rows, ins, outs, scalars=(at_end, index))[0]


def settle_attention_kernel(count, q_width, kv_width, at_end_ref, index_ref, *refs):
    q_ref, k_ref, v_ref, o_ref = refs[-4:]
    o_width = o_ref.shape[1] // count
    o_first = q_width + kv_width
    kvs = []
    for k in range(count):
        came_ref, sent_ref = refs[2 * k], refs[2 * k + 1]
        column = pl.multiple_of((index_ref[0] ^ k) * q_width, q_width)
        q_ref[:, pl.ds(column, q_width)] = settled(
            at_end_ref[0], came_ref, sent_ref, slice(0, q_width)
        )
        column = pl.multiple_of((index_ref[0] ^ k) * o_width, o_width)
        o_ref[:, pl.ds(column, o_width)] = settled(
            at_end_ref[0], came_ref, sent_ref, slice(o_first, o_first + o_width)
        )
        kvs.append(settled(at_end_ref[0], came_ref, sent_ref, slice(q_width, o_first)))
    ordered = []
    for place in range(count):
        kv = kvs[0]
        for k in range(1, count):
            kv = jnp.where((index_ref[0] ^ k) == place, kvs[k], kv)
        ordered.append(kv)
    k_ref[...] = jnp.concatenate([kv[:, : kv_width // 2] for kv in ordered], axis=1)
    v_ref[...] = jnp.concatenate([kv[:, kv_width // 2 :] for kv in ordered], axis=1)


def settle_attention(at_end, index, pairs, q_width, kv_width):
    count = len(pairs)
    arrays = [array for pair in pairs for array in pair]
    depth = arrays[0].shape[0]
    width = min(array.shape[1] for array in arrays)
    o_width = width - q_width - kv_width
    rows = math.gcd(depth, 128)
    ins = [(array, (rows, width), lambda i: (i, 0)) for array in arrays]
    widths = (q_width, kv_width // 2, kv_width // 2, o_width)
    outs = [row_blocks(full(depth, each * count), rows) for each in widths]
    kernel = functools.partial(settle_attention_kernel, count, q_width, kv_width)
    return gridded(kernel, depth // rows, ins, outs, scalars=(at_end, index))


def d_qkv_kernel(at_end_ref, here_ref, came_ref, sent_ref, dq_ref, cos_ref, sin_ref, out_ref):
    lanes = 2 * HEAD_SIZE
    half, q_width = dq_ref.shape[1], dq_ref.shape[2]
    cycle = came_ref.shape[1] // lanes // 2
    for core_side in range(2):
        column = pl.multiple_of((core_side * cycle + here_ref[0]) * lanes, lanes)
        d_kv = settled(at_end_ref[0], came_ref, sent_ref, pl.ds(column, lanes))
        cosine, sine = of_keys(cos_ref[core_side], sin_ref[core_side])
        d_kv = turned(d_kv, cosine, -sine).astype(jnp.bfloat16)
        rows = slice(core_side * half, (core_side + 1) * half)
        out_ref[rows, :q_width] = dq_ref[core_side]
        out_ref[rows, q_width:] = d_kv


def rows_back_kernel(count, index_ref, own_ref, other_ref, out_ref):
    rows, width = own_ref.shape[0], own_ref.shape[1] // count
    for ref, core in ((own_ref, index_ref[1]), (other_ref, 1 - index_ref[1])):
        first = pl.multiple_of(core * rows, rows)
        for block in range(count):
            column = pl.multiple_of((index_ref[0] ^ block) * width, width)
            out_ref[pl.ds(first, rows), pl.ds(column, width)] = ref[
                :, block * width : (block + 1) * width
            ]


def result_kernel(middle_ref, *refs):
    refs[-1][...] = (middle_ref[...] + total_of(refs[:-1])).astype(jnp.bfloat16)


def still(array):
    zeros = (0,) * len(array.shape)
    return (array, array.shape, lambda i: zeros)


def dot(left, right):
    return jnp.dot(left, right, preferred_element_type=jnp.float32)


def both(mine_ref, other_ref, weight):
    return jnp.concatenate([dot(mine_ref[...], weight), dot(other_ref[...], weight)], axis=0)


def gate_up_kernel(count, here_steps, *refs):
    x_refs, refs = refs[:2], refs[2:]
    own, fetched, passed = refs[:2], refs[2 : 2 * count], refs[2 * count : 4 * count - 2]
    gate_ref, up_ref, hidden_ref, wg_ref, wu_ref = refs[4 * count - 2 :]
    here = pl.program_id(0) < here_steps
    lins = []
    for which, out_ref in ((0, wg_ref), (1, wu_ref)):
        pieces = [own[which][...]]
        for k in range(count - 1):
            pieces.append(
                jnp.where(here, fetched[2 * k + which][...], passed[2 * k + which][...])
            )
        weight = jnp.concatenate(pieces, axis=0)
        out_ref[...] = weight
        lins.append(both(*x_refs, weight))
    gate, up = lins
    gate_ref[...] = gate
    up_ref[...] = up
    hidden_ref[...] = (gate * jax.nn.sigmoid(gate) * up).astype(jnp.bfloat16)


def gate_up(x, own_gate, own_up, fetched, passed):
    tokens, depth = 2 * x[0].shape[0], own_gate.shape[0]
    width, units = x[0].shape[1], own_gate.shape[1]
    count = len(fetched) + 1
    block = math.gcd(units // 2, 256)
    steps, half = units // block, units // block // 2
    ins = [still(x[0]), still(x[1])]
    ins += [(w, (depth, block), lambda i: (0, i)) for w in (own_gate, own_up)]
    for arrays in (fetched, passed):
        for array in arrays:
            ins.append((array, (depth, block), lambda i: (0, lax.rem(i, half))))
            ins.append((array, (depth, block), lambda i: (0, half + lax.rem(i, half))))
    outs = [
        (full(tokens, units), (tokens, block), lambda i: (0, i)),
        (full(tokens, units), (tokens, block), lambda i: (0, i)),
        (low(tokens, units), (tokens, block), lambda i: (0, i)),
        (low(width, units), (width, block), lambda i: (0, i)),
        (low(width, units), (width, block), lambda i: (0, i)),
    ]
    kernel = functools.partial(gate_up_kernel, count, half)
    return gridded(kernel, steps, ins, outs, limit=VMEM_LIMIT)


def units_back_kernel(count, *refs):
    d_refs, refs = refs[:2], refs[2:]
    pieces, (gate_ref, up_ref, d_gate_ref, d_up_ref, wd_ref) = refs[:count], refs[count:]
    weight = jnp.concatenate([ref[...] for ref in pieces], axis=0)
    wd_ref[...] = weight
    d_hidden = both(*d_refs, weight)
    gate, up = gate_ref[...], up_ref[...]
    chance = jax.nn.sigmoid(gate)
    d_up_ref[...] = (d_hidden * (gate * chance)).astype(jnp.bfloat16)
    slope = chance + gate * chance * (1.0 - chance)
    d_gate_ref[...] = (d_hidden * up * slope).astype(jnp.bfloat16)


def units_back(d_out, pieces, gate, up):
    tokens, units = gate.shape
    depth, width = pieces[0].shape[0], d_out[0].shape[1]
    block = math.gcd(units, 256)

    def by_columns(array, rows):
        return (array, (rows, block), lambda i: (0, i))

    ins = [still(d_out[0]), still(d_out[1])] + [by_columns(piece, depth) for piece in pieces]
    ins += [by_columns(gate, tokens), by_columns(up, tokens)]
    outs = [by_columns(low(tokens, units), tokens)] * 2 + [by_columns(low(width, units), width)]
    kernel = functools.partial(units_back_kernel, len(pieces))
    return gridded(kernel, units // block, ins, outs, limit=VMEM_LIMIT)


def rows_sum_kernel(terms, *refs):
    first_ref, second_ref = refs[-2:]
    total = 0.0
    for left_ref, right_ref in zip(refs[:terms], refs[terms : 2 * terms]):
        total = total + contract_last(left_ref[...], right_ref[...])
    total = total.astype(jnp.bfloat16)
    half = first_ref.shape[0]
    first_ref[...] = total[:half]
    second_ref[...] = total[half:]


def rows_sum(lefts, rights):
    tokens, width = lefts[0].shape[0], rights[0].shape[0]
    block = math.gcd(width, 512)
    ins = [still(left) for left in lefts]
    ins += [(right, (block, right.shape[1]), lambda i: (i, 0)) for right in rights]
    outs = [(low(tokens // 2, width), (tokens // 2, block), lambda i: (0, i))] * 2
    return gridded(functools.partial(rows_sum_kernel, len(lefts)), width // block, ins, outs)


def weight_grad_kernel(count, terms, turn, *refs):
    if turn:
        side, refs = refs[0][0], refs[1:]
    outs = refs[3 * terms :]
    step = pl.program_id(0)
    first = 0
    for term in range(terms):
        mine_ref, other_ref, right_ref = refs[3 * term : 3 * term + 3]
        half = mine_ref.shape[0]
        grad = contract_first(mine_ref[...], right_ref[:half, :])
        grad = grad + contract_first(other_ref[...], right_ref[half:, :])
        grad = grad.astype(jnp.bfloat16)
        columns = grad.shape[1]
        for k in range(count):

            @pl.when(step == k)
            def _(k=k, first=first, grad=grad, columns=columns):
                if turn:
                    part = columns // 2
                    outs[k][:, pl.ds(pl.multiple_of(side * part, part), part)] = grad[:, :part]
                    outs[k][:, pl.ds(pl.multiple_of((1 - side) * part, part), part)] = grad[:, part:]
                else:
                    outs[k][:, first : first + columns] = grad

        first += columns


def weight_grad(terms, count, side=None):
    columns = sum(right.shape[1] for _, _, right in terms)
    depth = terms[0][0].shape[1] // count
    ins = []
    if side is not None:
        ins.append((side, None, None))
    for mine, other, right in terms:
        ins += [(left, (left.shape[0], depth), lambda i: (0, i)) for left in (mine, other)]
        ins.append(still(right))
    specs = [
        pl.BlockSpec(memory_space=pltpu.SMEM) if block is None else pl.BlockSpec(block, index)
        for _, block, index in ins
    ]
    return pl.pallas_call(
        functools.partial(weight_grad_kernel, count, len(terms), side is not None),
        grid=(count,),
        in_specs=specs,
        out_specs=[pl.BlockSpec((depth, columns), lambda i: (0, 0))] * count,
        out_shape=[low(depth, columns)] * count,
        compiler_params=pltpu.CompilerParams(vmem_limit_bytes=MIDDLE_LIMIT),
        cost_estimate=SMALL,
    )(*[array for array, _, _ in ins])


def turned(lin, cosine, sine):
    width = lin.shape[-1]
    quarter = HEAD_SIZE // 2
    lane = lax.broadcasted_iota(jnp.int32, lin.shape, lin.ndim - 1)
    first = lax.rem(lane, HEAD_SIZE) < quarter
    partner = jnp.where(
        first,
        -pltpu.roll(lin, width - quarter, lin.ndim - 1),
        pltpu.roll(lin, quarter, lin.ndim - 1),
    )
    return lin * cosine + partner * sine


def side_by_side(table, width):
    return jnp.concatenate([table] * (width // table.shape[-1]), axis=-1)


def of_keys(cosine, sine):
    keys = lax.broadcasted_iota(jnp.int32, cosine.shape, 1) < HEAD_SIZE
    return jnp.where(keys, cosine, 1.0), jnp.where(keys, sine, 0.0)


def qkv_kernel(count, q_width, kv_width, side_ref, *refs):
    x_refs, (gain_ref, cos_ref, sin_ref), refs = refs[:2], refs[2:5], refs[5:]
    own_ref, fetched, passed_ref, refs = refs[0], refs[1:count], refs[count], refs[count + 1 :]
    normed_refs, (q_ref, kv_ref, wqkv_ref, wo_ref) = refs[:2], refs[2:]
    qkv_width = q_width + kv_width
    depth = own_ref.shape[0]
    half = depth // 2

    @pl.when(pl.program_id(0) == 0)
    def _():
        wqkv_ref[:depth, :] = own_ref[:, :qkv_width]
        wo_ref[:depth, :] = own_ref[:, qkv_width:]
        for k in range(1, count):
            for which, piece in (
                (side_ref[0], fetched[k - 1][:half, :]),
                (1 - side_ref[0], passed_ref[(k - 1) * half : k * half, :]),
            ):
                first = pl.multiple_of(k * depth + which * half, half)
                wqkv_ref[pl.ds(first, half), :] = piece[:, :qkv_width]
                wo_ref[pl.ds(first, half), :] = piece[:, qkv_width:]

    for i in range(2):
        x = x_refs[i][...].astype(jnp.float32)
        mean = jnp.mean(x * x, axis=-1, keepdims=True)
        normed = (x * lax.rsqrt(mean + 1e-05) * gain_ref[...]).astype(jnp.bfloat16)
        normed_refs[i][...] = normed
        lin = dot(normed, wqkv_ref[...])
        cosine, sine = cos_ref[i], sin_ref[i]
        q = turned(lin[:, :q_width], side_by_side(cosine, q_width), side_by_side(sine, q_width))
        q_ref[i] = q.astype(jnp.bfloat16)
        kv = turned(lin[:, q_width:], *of_keys(cosine, sine))
        kv_ref[i] = kv.astype(jnp.bfloat16)


def project_qkv(side, x, gain, cosine, sine, own, fetched, passed, q_width, kv_width):
    half_rows, width = x[0].shape
    qkv_width = q_width + kv_width
    block = math.gcd(half_rows, 128)

    def rows_of(array, columns):
        return (array, (block, columns), lambda i: (i, 0))

    def of_both(array, columns):
        return (array, (2, block, columns), lambda i: (0, i, 0))

    lanes = cosine.shape[-1]
    ins = [rows_of(x[0], width), rows_of(x[1], width), still(gain)]
    ins += [of_both(cosine, lanes), of_both(sine, lanes)]
    ins += [still(array) for array in (own, *fetched, passed)]
    o_width = own.shape[1] - qkv_width
    outs = [rows_of(low(half_rows, width), width)] * 2
    outs += [of_both(low(2, half_rows, q_width), q_width), of_both(low(2, half_rows, kv_width), kv_width)]
    outs += [still(low(width, qkv_width)), still(low(width, o_width))]
    kernel = functools.partial(qkv_kernel, len(fetched) + 1, q_width, kv_width)
    return gridded(kernel, half_rows // block, ins, outs, scalars=(side,))


def shares(q, k, visible):
    scores = contract_last(q, k) * (1.0 / math.sqrt(HEAD_SIZE))
    scores = jnp.where(visible, scores, -1e30)
    weights = jnp.exp(scores - jnp.max(scores, axis=-1, keepdims=True))
    weights = jnp.where(visible, weights, 0.0)
    return weights, jnp.sum(weights, axis=-1, keepdims=True)


def load_attention(q_ref, place_ref, start_ref, key_place_ref, kv_refs):
    q = q_ref[...]
    q = q.reshape(q.shape[0] * q.shape[1], q.shape[2])
    kv = jnp.concatenate([ref[...].reshape(q.shape[0], 2 * HEAD_SIZE) for ref in kv_refs], axis=0)
    key_place = key_place_ref[0]
    visible = (key_place <= place_ref[0]) & (key_place >= start_ref[0])
    return q, kv[:, :HEAD_SIZE], kv[:, HEAD_SIZE:], visible


def attend_kernel(groups, q_ref, place_ref, start_ref, key_place_ref, wo_ref, *refs):
    kv_refs, (out_ref, first_ref, second_ref) = refs[:-3], refs[-3:]
    q, k, v, visible = load_attention(q_ref, place_ref, start_ref, key_place_ref, kv_refs)
    mixed = []
    for g in range(groups):
        weights, totals = shares(q[:, g * HEAD_SIZE : (g + 1) * HEAD_SIZE], k, visible)
        mixed.append(dot(weights.astype(jnp.bfloat16), v) / totals)
    out = jnp.concatenate(mixed, axis=1).astype(jnp.bfloat16)
    out_ref[...] = out.reshape(out_ref.shape)
    branch = contract_last(out, wo_ref[...]).astype(jnp.bfloat16)
    half = first_ref.shape[0]
    first_ref[...] = branch[:half]
    second_ref[...] = branch[half:]


def attend_back_kernel(
    groups,
    here_ref,
    q_ref,
    mine_ref,
    other_ref,
    cos_ref,
    sin_ref,
    place_ref,
    start_ref,
    key_place_ref,
    wo_ref,
    *refs,
):
    kv_refs, (dq_ref, dkv_ref) = refs[:-2], refs[-2:]
    q, k, v, visible = load_attention(q_ref, place_ref, start_ref, key_place_ref, kv_refs)
    d_out = both(mine_ref, other_ref, wo_ref[...]).astype(jnp.bfloat16)
    scale = 1.0 / math.sqrt(HEAD_SIZE)
    d_q, d_k, d_v = [], 0.0, 0.0
    for g in range(groups):
        q_head = q[:, g * HEAD_SIZE : (g + 1) * HEAD_SIZE]
        d_head = d_out[:, g * HEAD_SIZE : (g + 1) * HEAD_SIZE]
        weights, totals = shares(q_head, k, visible)
        probs = weights / totals
        d_probs = contract_last(d_head, v)
        row_delta = jnp.sum(probs * d_probs, axis=-1, keepdims=True)
        d_scores = (probs * (d_probs - row_delta)).astype(jnp.bfloat16)
        d_q.append(dot(d_scores, k) * scale)
        d_k = d_k + contract_first(d_scores, q_head) * scale
        d_v = d_v + contract_first(probs.astype(jnp.bfloat16), d_head)
    d_q = jnp.concatenate(d_q, axis=1)
    cosine = cos_ref[...].reshape(q.shape[0], -1)
    sine = sin_ref[...].reshape(q.shape[0], -1)
    d_q = turned(d_q, side_by_side(cosine, q.shape[1]), -side_by_side(sine, q.shape[1]))
    dq_ref[...] = d_q.astype(jnp.bfloat16).reshape(dq_ref.shape)
    d_kv = jnp.concatenate([d_k, d_v], axis=1).astype(jnp.bfloat16)
    half, lanes, cycle = dkv_ref.shape[0], 2 * HEAD_SIZE, len(kv_refs)
    for j in range(cycle):
        for core_side in range(2):
            first = (2 * j + core_side) * half
            column = pl.multiple_of((core_side * cycle + (here_ref[0] ^ j)) * lanes, lanes)
            dkv_ref[:, pl.ds(column, lanes)] = d_kv[first : first + half]


def of_pack(array, half):
    return (array, (2, half, array.shape[-1]), lambda p: (0, p, 0))


def place_blocks(places):
    return [(array, (1,) + array.shape[1:], lambda p: (p, 0, 0)) for array in places]


def attend(q, places, wo, kvs, packs, groups):
    half = q.shape[1] // packs
    width = wo.shape[0]
    ins = [of_pack(q, half)] + place_blocks(places) + [still(wo)] + [of_pack(kv, half) for kv in kvs]
    outs = [of_pack(low(*q.shape), half)]
    outs += [(low(q.shape[1], width), (half, width), lambda p: (p, 0))] * 2
    return gridded(functools.partial(attend_kernel, groups), packs, ins, outs)


def attend_back(here, q, d_branch, cosine, sine, places, wo, kvs, packs, groups):
    half = q.shape[1] // packs
    cycle = len(kvs)
    ins = [of_pack(q, half)]
    ins += [(array, (half, array.shape[1]), lambda p: (p, 0)) for array in d_branch]
    ins += [of_pack(cosine, half), of_pack(sine, half)] + place_blocks(places) + [still(wo)]
    ins += [of_pack(kv, half) for kv in kvs]
    lanes = 2 * HEAD_SIZE
    outs = [of_pack(low(*q.shape), half)]
    outs.append((low(q.shape[1], 2 * cycle * lanes), (half, 2 * cycle * lanes), lambda p: (p, 0)))
    kernel = functools.partial(attend_back_kernel, groups)
    return gridded(kernel, packs, ins, outs, scalars=(here,))


def split_heads(
    hidden_in,
    out_cotangent,
    norm1_gain,
    q_weight,
    key_projection_weight,
    value_projection_weight,
    o_weight,
    norm2_gain,
    gate_weight,
    up_weight,
    down_weight,
    seq_lengths,
    span_order,
):
    packs = lax.axis_size("fsdp")
    cycle = lax.axis_size("ctx")
    pack = lax.axis_index("fsdp")
    core = lax.axis_index("tp")
    here = lax.axis_index("ctx")
    rows = hidden_in.shape[0]
    half = rows // 2
    tokens = packs * rows
    depth = q_weight.shape[0]
    width = depth * packs
    q_width = q_weight.shape[1] // packs
    k_width = key_projection_weight.shape[1] // packs
    ff_width = gate_weight.shape[1] // packs
    ff_half = ff_width // 2
    groups = q_width // k_width
    far = range(1, packs)
    steps = Steps(Line("ctx"))
    kept = {}


    def columns(weight, k, count, first=0, of=None):
        return lax.dynamic_slice_in_dim(weight, (pack ^ k) * (of or count) + first, count, 1)

    def to_pack(name, k, array):
        return ((name, k), array, "fsdp", pairs_by(k, packs))

    def send_all(name, arrays):
        return [to_pack(name, k, array) for k, array in zip(far, arrays)]

    def arrived(name):
        return [steps.take((name, k)) for k in far]

    def to_core(name, array):
        return [(name, array, "tp", pairs_by(1, 2))]

    def to_rows(name, first):
        kept[name], *others = fold(first, steps.take(name), packs)
        return send_all(name, others)

    def joined(name, own, others):
        kept[name] = join(own, others)
        return to_core(name, kept[name])

    def unwaited(name):
        return dict(steps.others)[name]

    def both_of(name):
        return kept[name], steps.take(name)

    index = jnp.stack([pack, core]).astype(jnp.int32)
    here_arg = here.astype(jnp.int32)[None]
    side_arg = here_arg & 1
    at_end = steps.line.at_end

    own_in, *in_moves = prepare(hidden_in, index, packs)
    own_cot, *cot_moves = prepare(out_cotangent, index, packs)

    side = here & 1
    weights = (q_weight, key_projection_weight, value_projection_weight, o_weight)
    widths = (q_width, k_width, k_width, q_width)

    def attention_piece(k, first, count):
        return jnp.concatenate(
            [
                lax.dynamic_slice(weight, (first, (pack ^ k) * each), (count, each))
                for weight, each in zip(weights, widths)
            ],
            axis=1,
        )

    meta = jnp.concatenate([span_order[0], seq_lengths[0]])
    order_len, meta_len = span_order.shape[1], meta.shape[0]
    metas = jnp.concatenate([(meta // 32).astype(jnp.bfloat16), (meta % 32).astype(jnp.bfloat16)])
    info = jnp.stack(
        [
            jnp.pad(jnp.concatenate([norm1_gain, metas]), (0, sum(widths) - depth - 2 * meta_len)),
            jnp.pad(norm2_gain, (0, sum(widths) - depth)),
        ]
    )
    info_rows = jnp.pad(info, ((0, 14), (0, 0)))
    row_half = depth // 2
    steps.step(
        [
            to_pack(
                "attention",
                k,
                jnp.concatenate([attention_piece(k, side * row_half, row_half), info_rows], axis=0),
            )
            for k in far
        ]
    )
    pieces = []

    def pass_rows():
        pieces.extend(arrived("attention"))
        rows_on = join_rows(pieces, row_half)
        return [("attention_rows", rows_on, "ctx", pairs_by(1, cycle))]

    steps.step(send_all("in", in_moves), late=pass_rows)
    infos = jnp.stack([info] + [piece[row_half : row_half + 2] for piece in pieces])
    all_gains = infos[:, :, :depth].astype(jnp.float32)
    gain_one = all_gains[:, 0].reshape(1, -1)
    gain_two = all_gains[:, 1].reshape(1, -1)
    metas = infos[:, 0, depth : depth + 2 * meta_len].astype(jnp.int32)
    metas = metas[:, :meta_len] * 32 + metas[:, meta_len:]
    orders, lengths = metas[:, :order_len], metas[:, order_len:]

    others = jnp.stack([here ^ j for j in range(cycle)])
    first = jnp.sum(
        jnp.where(
            others[None, :, None] == jnp.arange(order_len, dtype=jnp.int32)[None, None, :],
            orders[:, None, :],
            0,
        ),
        axis=2,
    )
    halves = jnp.stack([core, core ^ 1])[None, None, :]
    section = jnp.where(halves == 0, first[:, :, None], 2 * cycle - 1 - first[:, :, None])
    places = section[..., None] * half + jnp.arange(half, dtype=jnp.int32)
    places = places.reshape(packs, cycle * rows)
    starts = jnp.zeros_like(places)
    end = jnp.zeros((packs, 1), jnp.int32)
    for j in range(lengths.shape[1]):
        end = end + lengths[:, j : j + 1]
        starts = jnp.where(places >= end, end, starts)
    place_args = (places[:, :rows, None], starts[:, :rows, None], places[:, None, :])
    offsets = (places - starts)[:, :rows].reshape(packs, 2, half).transpose(1, 0, 2)
    cosine, sine = in_vmem(
        turns_kernel,
        [full(2, tokens // 2, 2 * HEAD_SIZE)] * 2,
        offsets.astype(jnp.float32).reshape(2, tokens // 2, 1),
    )


    def two_halves(weight, k):
        return jnp.concatenate(
            [
                columns(weight, k, ff_half, side * ff_half, ff_width),
                columns(weight, k, ff_half, (1 - side) * ff_half, ff_width),
            ],
            axis=1,
        )

    def fetch(ks):
        return [
            to_pack(
                "gate_up",
                k,
                jnp.concatenate(
                    [
                        columns(weight, k, ff_half, side * ff_half, ff_width)
                        for weight in (gate_weight, up_weight)
                    ],
                    axis=1,
                ),
            )
            for k in ks
        ]

    def to_neighbour(k):
        return [(("neighbour", k), fetched[k], "ctx", pairs_by(1, cycle))]

    fetched = {}
    own_piece = attention_piece(0, 0, depth)
    cosine, sine, own_piece, *place_args = steps.step(
        fetch([1, 2]), carry=(cosine, sine, own_piece, *place_args)
    )
    all_in = join(own_in, arrived("in"))
    all_in = (all_in, swap(all_in, "tp", 1))
    normed_mine, normed_other, q_rot, kv_own, wqkv, wo = project_qkv(
        side_arg,
        all_in,
        gain_one,
        cosine,
        sine,
        own_piece,
        pieces,
        steps.take("attention_rows"),
        q_width,
        2 * k_width,
    )
    normed_one = (normed_mine, normed_other)
    steps.step(
        [(("kv", j), kv_own, "ctx", pairs_by(j, cycle)) for j in range(1, cycle)] + fetch([3])
    )
    fetched[1], fetched[2] = steps.take(("gate_up", 1)), steps.take(("gate_up", 2))
    steps.step(send_all("cot", cot_moves) + to_neighbour(1))
    fetched[3] = steps.take(("gate_up", 3))
    kvs = [kv_own] + [steps.take(("kv", j)) for j in range(1, cycle)]
    attn, first, second = attend(q_rot, place_args, wo, kvs, packs, groups)
    attn_low = attn.reshape(tokens, q_width)
    steps.step(to_core("branch", second))
    steps.step(to_neighbour(2), late=lambda: to_rows("branch", first))
    kept["cot"] = join(own_cot, arrived("cot"))

    def middle_moves():
        kept["middle"], kept["normed"], *sends = in_vmem(
            functools.partial(middle_kernel, packs),
            [full(half, width)] + [low(half, width)] * packs,
            own_in,
            gain_two,
            kept["branch"],
            *arrived("branch"),
        )
        return send_all("two", sends)

    steps.step(to_neighbour(3) + to_core("cot", kept["cot"]), late=middle_moves)

    def wd_moves(ks):
        return [to_pack("down", k, two_halves(down_weight, k)) for k in ks]

    own_columns = [two_halves(weight, 0) for weight in (gate_weight, up_weight, down_weight)]
    own_gate, own_up, own_down = steps.step(
        wd_moves([1, 2]),
        late=lambda: joined("two", kept["normed"], arrived("two")),
        carry=own_columns,
    )
    all_cot = both_of("cot")
    neighbours = [steps.take(("neighbour", k)) for k in far]
    normed_two = (kept["two"], unwaited("two"))

    gate_val, up_val, hidden, wg, wu = gate_up(
        normed_two, own_gate, own_up, [fetched[k] for k in far], neighbours
    )
    d_wd = weight_grad([(*all_cot, hidden)], packs, side_arg)

    def back(name, grad, ks):
        return [to_pack(name, k, grad[k]) for k in ks]

    def entry(name, k, grad=None):
        return ((name, k), grad[0] if k == 0 else None)

    steps.step(back("wd", d_wd, [1, 2]), summed=entry("wd", 0, d_wd))
    steps.step(wd_moves([3]), summed=entry("wd", 1))
    steps.step(back("wd", d_wd, [3]), summed=entry("wd", 2))
    d_gate, d_up, wd = units_back(all_cot, [own_down] + arrived("down"), gate_val, up_val)
    first, second = rows_sum([d_gate, d_up], [wg, wu])
    d_wg = weight_grad([(*normed_two, d_gate)], packs, side_arg)
    steps.step(to_core("d_two", second) + back("wg", d_wg, [1, 2]), summed=entry("wd", 3))
    d_wu = weight_grad([(*normed_two, d_up)], packs, side_arg)
    steps.step(
        summed=entry("wg", 0, d_wg), late=functools.partial(to_rows, "d_two", first)
    )

    def branch_back():
        kept["d_middle"], kept["d_gain_two"], kept["d_branch"], *sends = in_vmem(
            functools.partial(branch_back_kernel, packs),
            [full(half, width), full(1, width)] + [low(half, width)] * packs,
            kept["middle"],
            gain_two,
            own_cot,
            kept["d_two"],
            *arrived("d_two"),
        )
        return send_all("d_branch", sends)

    steps.step(summed=entry("wu", 0, d_wu), late=branch_back)
    ff_first, ff_second = rows_sum([hidden], [wd])
    steps.step(
        back("wg", d_wg, [3]),
        summed=entry("wg", 1),
        late=lambda: joined("all_branch", kept["d_branch"], arrived("d_branch")),
    )
    sums = steps.line.sums

    def settle_all(name):
        return settle(at_end, index, [sums[name, k] for k in range(packs)], ff_width)

    d_branch = (kept["all_branch"], unwaited("all_branch"))
    d_q, d_kv = attend_back(
        here_arg, q_rot, d_branch, cosine, sine, place_args, wo, kvs, packs, groups
    )
    d_q, d_kv = steps.step(back("wu", d_wu, [1, 2]), summed=entry("wg", 2), carry=(d_q, d_kv))
    steps.step(back("wu", d_wu, [3]), summed=("d_kv", d_kv))
    down_grad = settle_all("wd")
    steps.step(to_core("ff", ff_second), summed=entry("wg", 3))
    (down_grad,) = steps.step(
        summed=entry("wu", 1), late=functools.partial(to_rows, "ff", ff_first), carry=(down_grad,)
    )
    steps.step(summed=entry("wu", 2))
    result = in_vmem(
        result_kernel, [low(half, width)], kept["middle"], kept["ff"], *arrived("ff")
    )[0]
    d_qkv = in_vmem(
        d_qkv_kernel,
        [low(tokens, q_width + 2 * k_width)],
        at_end,
        here_arg,
        *sums["d_kv"],
        d_q,
        cosine,
        sine,
        scalars=2,
    )[0]
    d_wqkvo = weight_grad([(*normed_one, d_qkv), (*d_branch, attn_low)], packs)
    first, second = rows_sum([d_qkv], [wqkv])
    steps.step(
        back("wqkvo", d_wqkvo, [1, 2]) + to_core("d_one", second), summed=entry("wu", 3)
    )
    steps.step(
        summed=entry("wqkvo", 0, d_wqkvo), late=functools.partial(to_rows, "d_one", first)
    )

    def both_rows(own, other):
        return in_vmem(
            functools.partial(rows_back_kernel, packs),
            [low(rows, width)],
            index,
            own,
            other,
            scalars=1,
        )[0]

    gate_grad = settle_all("wg")
    def gains_to_core():
        kept["in_grad"], d_gain_one = in_vmem(
            functools.partial(in_grad_kernel, packs),
            [low(half, width), full(1, width)],
            own_in,
            gain_one,
            kept["d_middle"],
            kept["d_one"],
            *arrived("d_one"),
        )
        kept["gains"] = jnp.concatenate([d_gain_one, kept["d_gain_two"]], axis=0)
        return to_core("gains", kept["gains"]) + to_core("in_grad", kept["in_grad"])

    def gains_to_packs():
        kept["gains"] = kept["gains"] + steps.take("gains")
        return [to_pack("gains", k, kept["gains"][:, k * depth : (k + 1) * depth]) for k in far]

    def gains_along():
        kept["gains"] = kept["gains"][:, :depth]
        for k in far:
            kept["gains"] = kept["gains"] + steps.take(("gains", k))
        return [(("gains", j), kept["gains"], "ctx", pairs_by(j, cycle)) for j in range(1, cycle)]

    steps.step(back("wqkvo", d_wqkvo, [3]), summed=entry("wqkvo", 1), late=gains_to_core)
    (gate_grad,) = steps.step(
        summed=entry("wqkvo", 2), late=gains_to_packs, carry=(gate_grad,)
    )
    up_grad = settle_all("wu")
    in_grad = both_rows(kept["in_grad"], steps.take("in_grad"))
    in_grad, up_grad = steps.step(
        to_core("result", result), summed=entry("wqkvo", 3), carry=(in_grad, up_grad)
    )
    steps.step(late=gains_along)
    out_hidden = both_rows(result, steps.take("result"))
    (out_hidden,) = steps.step(carry=(out_hidden,))
    steps.step()
    shares_of_gains = jnp.stack(
        [kept["gains"]] + [steps.take(("gains", j)) for j in range(1, cycle)]
    )
    gains = steps.token[0, 0]
    for place in range(cycle):
        gains = gains + lax.dynamic_index_in_dim(shares_of_gains, here ^ place, 0, keepdims=False)
    q_grad, k_grad, v_grad, o_grad = settle_attention(
        at_end, index, [sums["wqkvo", k] for k in range(packs)], q_width, 2 * k_width
    )
    return (
        out_hidden,
        in_grad,
        gains[0],
        q_grad,
        k_grad,
        v_grad,
        o_grad,
        gains[1],
        gate_grad,
        up_grad,
        down_grad,
    )


def gathered_weights(
    hidden_in,
    out_cotangent,
    norm1_gain,
    q_weight,
    key_projection_weight,
    value_projection_weight,
    o_weight,
    norm2_gain,
    gate_weight,
    up_weight,
    down_weight,
    seq_lengths,
    span_order,
):
    rows_here = hidden_in.shape[0]
    order_row = span_order[0]
    length_row = seq_lengths[0]
    kv_heads = key_projection_weight.shape[1] // HEAD_SIZE
    query_groups = QUERY_HEADS // KEY_VALUE_HEADS
    score_scale = 1.0 / math.sqrt(HEAD_SIZE)
    whole_rows = rows_here * lax.axis_size("ctx")
    local_rows = lax.axis_index("ctx") * rows_here + jnp.arange(rows_here, dtype=jnp.int32)
    q_place, q_segment, q_offset = stream_place(local_rows, order_row, length_row, rows_here)
    inputs = hidden_in.astype(jnp.float32)
    gain_one, wq_full, wk_full, wv_full, wo_full = (
        lax.all_gather(norm1_gain, "fsdp", axis=0, tiled=True),
        lax.all_gather(q_weight, "fsdp", axis=0, tiled=True),
        lax.all_gather(key_projection_weight, "fsdp", axis=0, tiled=True),
        lax.all_gather(value_projection_weight, "fsdp", axis=0, tiled=True),
        lax.all_gather(o_weight, "fsdp", axis=0, tiled=True),
    )
    gain_one = gain_one.astype(jnp.float32)
    first_normalized = normalize(inputs, gain_one)
    normed_low = first_normalized.astype(jnp.bfloat16)
    q_linear = jnp.dot(normed_low, wq_full, preferred_element_type=jnp.float32).reshape(
        rows_here, kv_heads * query_groups, HEAD_SIZE
    )
    k_linear = jnp.dot(normed_low, wk_full, preferred_element_type=jnp.float32).reshape(
        rows_here, kv_heads, HEAD_SIZE
    )
    q_rotated = (
        rotary_embedding(q_linear, q_offset)
        .astype(jnp.bfloat16)
        .reshape(rows_here, kv_heads, query_groups, HEAD_SIZE)
    )
    k_rotated = (
        rotary_embedding(k_linear, q_offset)
        .astype(jnp.bfloat16)
        .reshape(rows_here, kv_heads * HEAD_SIZE)
    )
    v_low = jnp.dot(normed_low, wv_full, preferred_element_type=jnp.float32).astype(jnp.bfloat16)

    def key_blocks(shard_rows):
        row_count = shard_rows.shape[0]
        key_total_width = math.gcd(row_count, 512)
        number = row_count // key_total_width
        k_place, k_segment, _ = stream_place(
            jnp.arange(row_count, dtype=jnp.int32), order_row, length_row, rows_here
        )
        return (
            key_total_width,
            number,
            k_place.reshape(number, key_total_width),
            k_segment.reshape(number, key_total_width),
        )

    def scores_of(key_block, place_block, segment_block):
        scores = (
            jnp.einsum("qkgd,skd->kgqs", q_rotated, key_block, preferred_element_type=jnp.float32)
            * score_scale
        )
        visible = (
            (q_place[:, None] >= place_block[None, :])
            & (q_segment[:, None] == segment_block[None, :])
        )[None, None]
        return (jnp.where(visible, scores, -1e30), visible)

    start_state = (
        jnp.full((kv_heads, query_groups, rows_here), -1e30, jnp.float32),
        jnp.zeros((kv_heads, query_groups, rows_here), jnp.float32),
        jnp.zeros((kv_heads, query_groups, rows_here, HEAD_SIZE), jnp.float32),
    )
    folded = start_state
    key_row_block = lax.all_gather(k_rotated, "ctx", axis=0, tiled=True)
    value_row_block = lax.all_gather(v_low, "ctx", axis=0, tiled=True)
    key_total_width, number, k_place, k_segment = key_blocks(key_row_block)

    def one_step(carried, pieces):
        running_max, totals, accumulated = carried
        key_block, value_block, place_block, segment_block = pieces
        scores, visible = scores_of(key_block, place_block, segment_block)
        new_max = jnp.maximum(running_max, jnp.max(scores, axis=-1))
        weights = jnp.where(visible, jnp.exp(scores - new_max[..., None]), 0.0)
        factor = jnp.exp(running_max - new_max)
        totals = totals * factor + jnp.sum(weights, axis=-1)
        accumulated = accumulated * factor[..., None] + jnp.einsum(
            "kgqs,skd->kgqd",
            weights.astype(jnp.bfloat16),
            value_block,
            preferred_element_type=jnp.float32,
        )
        return ((new_max, totals, accumulated), None)

    pieces = (
        key_row_block.reshape(number, key_total_width, kv_heads, HEAD_SIZE),
        value_row_block.reshape(number, key_total_width, kv_heads, HEAD_SIZE),
        k_place,
        k_segment,
    )
    folded, _ = lax.scan(one_step, folded, pieces)
    running_max, totals, accumulated = folded
    mixed_out = jnp.transpose(accumulated / totals[..., None], (2, 0, 1, 3))
    log_sum = running_max + jnp.log(totals)
    attn_low = mixed_out.reshape(rows_here, kv_heads * query_groups * HEAD_SIZE).astype(
        jnp.bfloat16
    )
    branch = lax.psum(contract_last(attn_low, wo_full).astype(jnp.bfloat16), "tp").astype(
        jnp.float32
    )
    middle = inputs + branch
    gain_two, wg_full, wu_full, wd_full = (
        lax.all_gather(norm2_gain, "fsdp", axis=0, tiled=True),
        lax.all_gather(gate_weight, "fsdp", axis=0, tiled=True),
        lax.all_gather(up_weight, "fsdp", axis=0, tiled=True),
        lax.all_gather(down_weight, "fsdp", axis=0, tiled=True),
    )
    gain_two = gain_two.astype(jnp.float32)
    normed_two = normalize(middle, gain_two)
    normed_two_low = normed_two.astype(jnp.bfloat16)
    gate_val = jnp.dot(normed_two_low, wg_full, preferred_element_type=jnp.float32)
    up_val = jnp.dot(normed_two_low, wu_full, preferred_element_type=jnp.float32)
    hidden = swiglu(gate_val, up_val).astype(jnp.bfloat16)
    ffn_out = lax.psum(contract_last(hidden, wd_full).astype(jnp.bfloat16), "tp").astype(
        jnp.float32
    )
    result = (middle + ffn_out).astype(jnp.bfloat16)
    grad_out = out_cotangent.astype(jnp.float32)
    d_wd = contract_first(out_cotangent, hidden)
    d_hidden = jnp.dot(out_cotangent, wd_full, preferred_element_type=jnp.float32)
    _, swiglu_back = jax.vjp(swiglu, gate_val, up_val)
    d_gate, d_up = swiglu_back(d_hidden)
    d_gate_low = d_gate.astype(jnp.bfloat16)
    d_up_low = d_up.astype(jnp.bfloat16)
    d_wg = contract_first(normed_two_low, d_gate_low)
    d_wu = contract_first(normed_two_low, d_up_low)
    d_normed_two = lax.psum(
        (contract_last(d_gate_low, wg_full) + contract_last(d_up_low, wu_full)).astype(
            jnp.bfloat16
        ),
        "tp",
    ).astype(jnp.float32)
    _, norm_two_back = jax.vjp(normalize, middle, gain_two)
    d_middle_norm, d_gain_two = norm_two_back(d_normed_two)
    d_middle = grad_out + d_middle_norm
    d_branch_low = d_middle.astype(jnp.bfloat16)
    d_wo = contract_first(d_branch_low, attn_low)
    d_attn = jnp.dot(d_branch_low, wo_full, preferred_element_type=jnp.float32).astype(jnp.bfloat16)
    d_attn_heads = d_attn.reshape(rows_here, kv_heads, query_groups, HEAD_SIZE)
    row_delta = jnp.einsum("qkgd,qkgd->kgq", d_attn_heads.astype(jnp.float32), mixed_out)
    back_state = (
        jnp.zeros((rows_here, kv_heads, query_groups, HEAD_SIZE), jnp.float32),
        jnp.zeros((whole_rows, kv_heads, HEAD_SIZE), jnp.float32),
        jnp.zeros((whole_rows, kv_heads, HEAD_SIZE), jnp.float32),
    )
    folded = back_state
    key_row_block = lax.all_gather(k_rotated, "ctx", axis=0, tiled=True)
    value_row_block = lax.all_gather(v_low, "ctx", axis=0, tiled=True)
    key_total_width, number, k_place, k_segment = key_blocks(key_row_block)

    def one_step(carried, pieces):
        d_query, d_keys, d_values = carried
        key_block, value_block, place_block, segment_block, step_index = pieces
        scores, visible = scores_of(key_block, place_block, segment_block)
        prob_rows = jnp.where(visible, jnp.exp(scores - log_sum[..., None]), 0.0)
        d_values_block = jnp.einsum(
            "kgqs,qkgd->skd",
            prob_rows.astype(jnp.bfloat16),
            d_attn_heads,
            preferred_element_type=jnp.float32,
        )
        d_probs = jnp.einsum(
            "qkgd,skd->kgqs", d_attn_heads, value_block, preferred_element_type=jnp.float32
        )
        d_scores = (prob_rows * (d_probs - row_delta[..., None])).astype(jnp.bfloat16)
        d_query = (
            d_query
            + jnp.einsum("kgqs,skd->qkgd", d_scores, key_block, preferred_element_type=jnp.float32)
            * score_scale
        )
        d_keys_block = (
            jnp.einsum("kgqs,qkgd->skd", d_scores, q_rotated, preferred_element_type=jnp.float32)
            * score_scale
        )
        row_first = step_index * key_total_width
        d_keys = lax.dynamic_update_slice_in_dim(
            d_keys,
            lax.dynamic_slice_in_dim(d_keys, row_first, key_total_width, 0) + d_keys_block,
            row_first,
            0,
        )
        d_values = lax.dynamic_update_slice_in_dim(
            d_values,
            lax.dynamic_slice_in_dim(d_values, row_first, key_total_width, 0) + d_values_block,
            row_first,
            0,
        )
        return ((d_query, d_keys, d_values), None)

    pieces = (
        key_row_block.reshape(number, key_total_width, kv_heads, HEAD_SIZE),
        value_row_block.reshape(number, key_total_width, kv_heads, HEAD_SIZE),
        k_place,
        k_segment,
        jnp.arange(number, dtype=jnp.int32),
    )
    folded, _ = lax.scan(one_step, folded, pieces)
    d_query, d_keys_all, d_values_all = folded
    d_key_own, d_value_own = (
        lax.psum_scatter(
            d_keys_all.astype(jnp.bfloat16), "ctx", scatter_dimension=0, tiled=True
        ).astype(jnp.float32),
        lax.psum_scatter(
            d_values_all.astype(jnp.bfloat16), "ctx", scatter_dimension=0, tiled=True
        ).astype(jnp.float32),
    )
    _, rope_q_back = jax.vjp(lambda rotated_in: rotary_embedding(rotated_in, q_offset), q_linear)
    _, rope_k_back = jax.vjp(lambda rotated_in: rotary_embedding(rotated_in, q_offset), k_linear)
    (d_q_linear,) = rope_q_back(d_query.reshape(rows_here, kv_heads * query_groups, HEAD_SIZE))
    (d_k_linear,) = rope_k_back(d_key_own)
    d_q_low = d_q_linear.reshape(rows_here, kv_heads * query_groups * HEAD_SIZE).astype(
        jnp.bfloat16
    )
    d_k_low = d_k_linear.reshape(rows_here, kv_heads * HEAD_SIZE).astype(jnp.bfloat16)
    d_v_low = d_value_own.reshape(rows_here, kv_heads * HEAD_SIZE).astype(jnp.bfloat16)
    d_wq = contract_first(normed_low, d_q_low)
    d_wk = contract_first(normed_low, d_k_low)
    d_wv = contract_first(normed_low, d_v_low)
    d_normed_one = lax.psum(
        (
            contract_last(d_q_low, wq_full)
            + contract_last(d_k_low, wk_full)
            + contract_last(d_v_low, wv_full)
        ).astype(jnp.bfloat16),
        "tp",
    ).astype(jnp.float32)
    _, norm_one_back = jax.vjp(normalize, inputs, gain_one)
    d_inputs_norm, d_gain_one = norm_one_back(d_normed_one)
    in_grad = (d_middle + d_inputs_norm).astype(jnp.bfloat16)
    weight_grads = (d_gain_one, d_wq, d_wk, d_wv, d_wo, d_gain_two, d_wg, d_wu, d_wd)
    shares = (
        lax.psum_scatter(weight_grads[0], ("fsdp", "ctx"), scatter_dimension=0, tiled=True),
        lax.psum_scatter(weight_grads[1], ("fsdp", "ctx"), scatter_dimension=0, tiled=True),
        lax.psum_scatter(weight_grads[2], ("fsdp", "ctx"), scatter_dimension=0, tiled=True),
        lax.psum_scatter(weight_grads[3], ("fsdp", "ctx"), scatter_dimension=0, tiled=True),
        lax.psum_scatter(weight_grads[4], ("fsdp", "ctx"), scatter_dimension=0, tiled=True),
        lax.psum_scatter(weight_grads[5], ("fsdp", "ctx"), scatter_dimension=0, tiled=True),
        lax.psum_scatter(weight_grads[6], ("fsdp", "ctx"), scatter_dimension=0, tiled=True),
        lax.psum_scatter(weight_grads[7], ("fsdp", "ctx"), scatter_dimension=0, tiled=True),
        lax.psum_scatter(weight_grads[8], ("fsdp", "ctx"), scatter_dimension=0, tiled=True),
    )
    owned_grads = (
        lax.all_gather(shares[0].astype(jnp.bfloat16), "ctx", axis=0, tiled=True).astype(
            jnp.float32
        ),
        lax.all_gather(shares[1].astype(jnp.bfloat16), "ctx", axis=0, tiled=True).astype(
            jnp.float32
        ),
        lax.all_gather(shares[2].astype(jnp.bfloat16), "ctx", axis=0, tiled=True).astype(
            jnp.float32
        ),
        lax.all_gather(shares[3].astype(jnp.bfloat16), "ctx", axis=0, tiled=True).astype(
            jnp.float32
        ),
        lax.all_gather(shares[4].astype(jnp.bfloat16), "ctx", axis=0, tiled=True).astype(
            jnp.float32
        ),
        lax.all_gather(shares[5].astype(jnp.bfloat16), "ctx", axis=0, tiled=True).astype(
            jnp.float32
        ),
        lax.all_gather(shares[6].astype(jnp.bfloat16), "ctx", axis=0, tiled=True).astype(
            jnp.float32
        ),
        lax.all_gather(shares[7].astype(jnp.bfloat16), "ctx", axis=0, tiled=True).astype(
            jnp.float32
        ),
        lax.all_gather(shares[8].astype(jnp.bfloat16), "ctx", axis=0, tiled=True).astype(
            jnp.float32
        ),
    )
    return (
        result,
        in_grad,
        owned_grads[0],
        owned_grads[1],
        owned_grads[2],
        owned_grads[3],
        owned_grads[4],
        owned_grads[5],
        owned_grads[6],
        owned_grads[7],
        owned_grads[8],
    )


def solution(mesh):
    placed = (
        P(("fsdp", "ctx"), None),
        P(("fsdp", "ctx"), None),
        P("fsdp"),
        P("fsdp", "tp"),
        P("fsdp", "tp"),
        P("fsdp", "tp"),
        P("fsdp", "tp"),
        P("fsdp"),
        P("fsdp", "tp"),
        P("fsdp", "tp"),
        P("fsdp", "tp"),
        P("fsdp", None),
        P("fsdp", None),
    )
    plane = mesh.shape["fsdp"] * mesh.shape["tp"]
    splits = mesh.shape["tp"] == 2 and KEY_VALUE_HEADS == plane and mesh.shape["ctx"] == 4
    return jax.shard_map(
        split_heads if splits else gathered_weights,
        mesh=mesh,
        in_specs=placed,
        out_specs=(
            P(("fsdp", "ctx"), None),
            P(("fsdp", "ctx"), None),
            P("fsdp"),
            P("fsdp", "tp"),
            P("fsdp", "tp"),
            P("fsdp", "tp"),
            P("fsdp", "tp"),
            P("fsdp"),
            P("fsdp", "tp"),
            P("fsdp", "tp"),
            P("fsdp", "tp"),
        ),
        check_vma=False,
    )
```

```python
import functools
import math

import jax
import jax.numpy as jnp
from jax import lax
from jax.experimental import pallas as pl
from jax.experimental.pallas import tpu as pltpu
from jax.sharding import PartitionSpec as P

QUERY_HEADS = 32
KEY_VALUE_HEADS = 8
HEAD_SIZE = 64


def stream_place(row_ids, order_row, length_row, tok_dev):
    cycle_size = order_row.shape[0]
    half_len = tok_dev // 2
    cycle_rank = row_ids // tok_dev
    within = row_ids % tok_dev
    first_section = jnp.sum(
        jnp.where(
            cycle_rank[:, None] == jnp.arange(cycle_size, dtype=jnp.int32)[None, :],
            order_row[None, :],
            0,
        ),
        axis=1,
        dtype=jnp.int32,
    )
    section = jnp.where(within >= half_len, 2 * cycle_size - 1 - first_section, first_section)
    places = section * half_len + within % half_len
    seq_ends = jnp.cumsum(length_row, dtype=jnp.int32)
    passed = places[:, None] >= seq_ends[None, :]
    segment = jnp.sum(passed.astype(jnp.int32), axis=1, dtype=jnp.int32)
    offset = places - jnp.sum(jnp.where(passed, length_row[None, :], 0), axis=1, dtype=jnp.int32)
    return (places, segment, offset)


def rotary_embedding(values, positions):
    half_len = values.shape[-1] // 2
    frequency = jnp.exp(
        -math.log(500000.0) * jnp.arange(half_len, dtype=jnp.float32) * 2.0 / values.shape[-1]
    )
    angles = positions.astype(jnp.float32)[:, None] * frequency[None, :]
    cosine = jnp.cos(angles)[:, None, :]
    sine = jnp.sin(angles)[:, None, :]
    lower_half = values[..., :half_len]
    upper_half = values[..., half_len:]
    return jnp.concatenate(
        [lower_half * cosine - upper_half * sine, upper_half * cosine + lower_half * sine], axis=-1
    )


def normalize(values, gain_vec):
    return values * lax.rsqrt(jnp.mean(values * values, axis=-1, keepdims=True) + 1e-05) * gain_vec


def swiglu(gate_val, up_val):
    return jax.nn.silu(gate_val) * up_val


def contract_last(left, right):
    return lax.dot_general(
        left, right, (((1,), (1,)), ((), ())), preferred_element_type=jnp.float32
    )


def contract_first(left, right):
    return lax.dot_general(
        left, right, (((0,), (0,)), ((), ())), preferred_element_type=jnp.float32
    )


VMEM_LIMIT = 28 * 1024 * 1024
LARGE_LIMIT = 28 * 1024 * 1024
MIDDLE_LIMIT = 20 * 1024 * 1024
SMALL_LIMIT = 12 * 1024 * 1024
SMALL = pl.CostEstimate(flops=1, bytes_accessed=1, transcendentals=0)


def pairs_by(distance, size):
    return [(i, i ^ distance) for i in range(size)]


def swap(array, axis, distance):
    return lax.ppermute(array, axis, pairs_by(distance, lax.axis_size(axis)))


class Line:
    def __init__(self, axis):
        index = lax.axis_index(axis)
        size = lax.axis_size(axis)
        self.axis = axis
        self.at_end = ((index == 0) | (index == size - 1)).astype(jnp.int32)[None]
        self.entered = self.halfway = self.leaving = None
        self.sums = {}

    def advance(self, got, entering):
        if self.leaving is not None:
            name, sent = self.leaving
            self.sums[name] = (got["ends"], sent)
        moves = []
        halfway = None
        if self.entered is not None:
            name, value = self.entered
            halfway = (name, add_low(value, got["ends"]))
            moves.append(("middle", halfway[1], self.axis, [(1, 2), (2, 1)]))
        leaving = None
        inwards, outwards = [(0, 1), (3, 2)], [(1, 0), (2, 3)]
        if self.halfway is not None:
            name, value = self.halfway
            if entering is None:
                sent, pairs = add_low(value, got["middle"]), outwards
            else:
                sent = either_way(self.at_end, entering[1], value, got["middle"])
                pairs = inwards + outwards
            leaving = (name, sent)
            moves.append(("ends", sent, self.axis, pairs))
        elif entering is not None:
            moves.append(("ends", entering[1], self.axis, inwards))
        self.entered, self.halfway, self.leaving = entering, halfway, leaving
        return moves


class Steps:
    def __init__(self, line):
        self.line = line
        self.got = {}
        self.on_line = []
        self.others = []
        self.token = jnp.zeros((8, 128), jnp.float32)

    def wait(self, flying, arrays):
        count = len(flying)
        held = lax.optimization_barrier(
            (self.token,) + tuple(value for _, value in flying) + tuple(arrays)
        )
        self.token = held[0]
        for (name, _), value in zip(flying, held[1:]):
            self.got[name] = value
        return list(held[1 + count :])

    def start(self, moves):
        return [(name, lax.ppermute(value, axis, pairs)) for name, value, axis, pairs in moves]

    def step(self, moves=(), summed=None, late=None, carry=(), hold=False):
        moves, carry = list(moves), list(carry)
        arrays = [move[1] for move in moves] + carry
        fresh = [summed[1]] if summed is not None and summed[1] is not None else []
        together = summed is not None and not fresh and summed[0] not in self.got
        if together or not self.on_line:
            held = self.wait(self.on_line + self.others, fresh + arrays)
            held_fresh, held = held[: len(fresh)], held[len(fresh) :]
        else:
            held_fresh = self.wait(self.on_line, fresh)
        entering = summed
        if summed is not None:
            entering = (summed[0], held_fresh[0] if fresh else self.take(summed[0]))
        along = self.line.advance(self.got, entering)
        if not together and self.on_line:
            self.on_line = self.start(along)
            held = self.wait([] if hold else self.others, arrays)
        else:
            self.on_line = self.start(along)
        moves = [
            (name, value, axis, pairs) for (name, _, axis, pairs), value in zip(moves, held)
        ]
        before = self.others if hold else []
        self.others = before + self.start(moves + (late() if late is not None else []))
        return held[len(moves) :]

    def take(self, name):
        return self.got.pop(name)


def in_vmem(kernel, out_shape, *args, scalars=0):
    specs = [pl.BlockSpec(memory_space=pltpu.SMEM)] * scalars
    specs += [pl.BlockSpec(memory_space=pltpu.VMEM)] * (len(args) - scalars)
    return pl.pallas_call(
        kernel,
        out_shape=out_shape,
        in_specs=specs,
        out_specs=[pl.BlockSpec(memory_space=pltpu.VMEM)] * len(out_shape),
        compiler_params=pltpu.CompilerParams(vmem_limit_bytes=SMALL_LIMIT),
        cost_estimate=SMALL,
    )(*args)


def low(*shape):
    return jax.ShapeDtypeStruct(shape, jnp.bfloat16)


def full(*shape):
    return jax.ShapeDtypeStruct(shape, jnp.float32)


def store_seen(ref, value, distance, count):
    width = value.shape[-1] // count
    for block in range(count):
        there = block ^ distance
        ref[: value.shape[0], block * width : (block + 1) * width] = value[
            :, there * width : (there + 1) * width
        ]


def prepare_kernel(count, index_ref, x_ref, own_ref, *sends):
    rows, width = own_ref.shape[0], own_ref.shape[1] // count
    first = pl.multiple_of(index_ref[1] * rows, rows)
    for block in range(count):
        column = pl.multiple_of((index_ref[0] ^ block) * width, width)
        own_ref[:, block * width : (block + 1) * width] = x_ref[
            pl.ds(first, rows), pl.ds(column, width)
        ]
    for k, send in enumerate(sends, 1):
        store_seen(send, own_ref[...], k, count)


def prepare(x, index, count):
    rows, width = x.shape[0] // 2, x.shape[1]
    return in_vmem(
        functools.partial(prepare_kernel, count), [low(rows, width)] * count, index, x, scalars=1
    )


def turns_kernel(offset_ref, cos_ref, sin_ref):
    lane = lax.broadcasted_iota(jnp.int32, cos_ref.shape, 2)
    place = lax.rem(lane, HEAD_SIZE // 2).astype(jnp.float32)
    frequency = jnp.exp(-math.log(500000.0) * place * 2.0 / HEAD_SIZE)
    angle = offset_ref[...] * frequency
    cos_ref[...] = jnp.cos(angle)
    sin_ref[...] = jnp.sin(angle)


def join_kernel(*refs):
    out_ref = refs[-1]
    rows = refs[0].shape[0]
    for i, ref in enumerate(refs[:-1]):
        out_ref[i * rows : (i + 1) * rows, :] = ref[:rows, :]


def join_rows(arrays, rows):
    def kernel(*refs):
        for i, ref in enumerate(refs[:-1]):
            refs[-1][i * rows : (i + 1) * rows, :] = ref[:rows, :]

    return in_vmem(kernel, [low(rows * len(arrays), arrays[0].shape[1])], *arrays)[0]


def join(own, others):
    rows, width = own.shape
    return in_vmem(join_kernel, [low(rows * (1 + len(others)), width)], own, *others)[0]


def fold_kernel(count, first_ref, came_ref, own_ref, *sends):
    rows = own_ref.shape[0]
    for k in range(count):
        here = slice(k * rows, (k + 1) * rows)
        total = first_ref[here, :].astype(jnp.float32) + came_ref[here, :].astype(jnp.float32)
        total = total.astype(jnp.bfloat16)
        if k == 0:
            own_ref[...] = total
        else:
            store_seen(sends[k - 1], total, k, count)


def fold(first, came, count):
    rows, width = first.shape[0] // count, first.shape[1]
    return in_vmem(
        functools.partial(fold_kernel, count), [low(rows, width)] * count, first, came
    )


def total_of(refs):
    total = refs[0][...].astype(jnp.float32)
    for ref in refs[1:]:
        total = total + ref[...].astype(jnp.float32)
    return total


def middle_kernel(count, in_ref, gain_ref, *refs):
    parts, (middle_ref, normed_ref, *sends) = refs[:count], refs[count:]
    middle = in_ref[...].astype(jnp.float32) + total_of(parts)
    middle_ref[...] = middle
    mean = jnp.mean(middle * middle, axis=-1, keepdims=True)
    normed = (middle * lax.rsqrt(mean + 1e-05) * gain_ref[...]).astype(jnp.bfloat16)
    normed_ref[...] = normed
    for k in range(1, count):
        store_seen(sends[k - 1], normed, k, count)


def norm_back(d_normed, x, gain):
    scale = lax.rsqrt(jnp.mean(x * x, axis=-1, keepdims=True) + 1e-05)
    unit = x * scale
    d_unit = d_normed * gain
    d_x = scale * (d_unit - unit * jnp.mean(d_unit * unit, axis=-1, keepdims=True))
    return d_x, jnp.sum(d_normed * unit, axis=0, keepdims=True)


def branch_back_kernel(count, middle_ref, gain_ref, cot_ref, *refs):
    parts, (d_middle_ref, d_gain_ref, branch_ref, *sends) = refs[:count], refs[count:]
    d_x, d_gain_ref[...] = norm_back(total_of(parts), middle_ref[...], gain_ref[...])
    d_middle = cot_ref[...].astype(jnp.float32) + d_x
    d_middle_ref[...] = d_middle
    branch = d_middle.astype(jnp.bfloat16)
    branch_ref[...] = branch
    for k in range(1, count):
        store_seen(sends[k - 1], branch, k, count)


def in_grad_kernel(count, in_ref, gain_ref, d_middle_ref, *refs):
    parts, (grad_ref, d_gain_ref) = refs[:count], refs[count:]
    x = in_ref[...].astype(jnp.float32)
    d_x, d_gain_ref[...] = norm_back(total_of(parts), x, gain_ref[...])
    grad_ref[...] = (d_middle_ref[...] + d_x).astype(jnp.bfloat16)


def spec_of(array, block, index):
    if block == array.shape:
        return pl.BlockSpec(block, index, pipeline_mode=pl.Buffered(1))
    return pl.BlockSpec(block, index)


def gridded(kernel, steps, ins, outs, scalars=(), limit=None):
    return pl.pallas_call(
        kernel,
        grid=(steps,),
        in_specs=[pl.BlockSpec(memory_space=pltpu.SMEM)] * len(scalars)
        + [spec_of(array, block, index) for array, block, index in ins],
        out_specs=[pl.BlockSpec(block, index) for _, block, index in outs],
        out_shape=[shape for shape, _, _ in outs],
        compiler_params=pltpu.CompilerParams(vmem_limit_bytes=limit or MIDDLE_LIMIT),
        cost_estimate=SMALL,
    )(*scalars, *[array for array, _, _ in ins])


def row_blocks(array, rows):
    return (array, (rows, array.shape[1]), lambda i: (i, 0))


def add_low(left, right):
    right = right[:, : left.shape[1]]
    return (left.astype(jnp.float32) + right.astype(jnp.float32)).astype(jnp.bfloat16)


def either_way(at_end, fresh, value, came):
    total = add_low(value, came)
    width = max(fresh.shape[1], value.shape[1])
    if fresh.shape[1] < width:
        fresh = jnp.pad(fresh, ((0, 0), (0, width - fresh.shape[1])))
    if total.shape[1] < width:
        total = jnp.pad(total, ((0, 0), (0, width - total.shape[1])))
    return jnp.where(at_end[0] == 1, fresh, total)


def settled(at_end, came_ref, sent_ref, columns):
    return jnp.where(at_end == 1, came_ref[:, columns], sent_ref[:, columns]).astype(jnp.float32)


def settle_kernel(count, at_end_ref, index_ref, *refs):
    out_ref = refs[-1]
    width = out_ref.shape[1] // count
    for k in range(count):
        column = pl.multiple_of((index_ref[0] ^ k) * width, width)
        out_ref[:, pl.ds(column, width)] = settled(
            at_end_ref[0], refs[2 * k], refs[2 * k + 1], slice(0, width)
        )


def settle(at_end, index, pairs, width):
    count = len(pairs)
    arrays = [array for pair in pairs for array in pair]
    depth = arrays[0].shape[0]
    rows = math.gcd(depth, 128)
    ins = [(array, (rows, width), lambda i: (i, 0)) for array in arrays]
    outs = [row_blocks(full(depth, width * count), rows)]
    kernel = functools.partial(settle_kernel, count)
    return gridded(kernel, depth // rows, ins, outs, scalars=(at_end, index))[0]


def settle_attention_kernel(count, q_width, kv_width, at_end_ref, index_ref, *refs):
    q_ref, k_ref, v_ref, o_ref = refs[-4:]
    o_width = o_ref.shape[1] // count
    o_first = q_width + kv_width
    kvs = []
    for k in range(count):
        came_ref, sent_ref = refs[2 * k], refs[2 * k + 1]
        column = pl.multiple_of((index_ref[0] ^ k) * q_width, q_width)
        q_ref[:, pl.ds(column, q_width)] = settled(
            at_end_ref[0], came_ref, sent_ref, slice(0, q_width)
        )
        column = pl.multiple_of((index_ref[0] ^ k) * o_width, o_width)
        o_ref[:, pl.ds(column, o_width)] = settled(
            at_end_ref[0], came_ref, sent_ref, slice(o_first, o_first + o_width)
        )
        kvs.append(settled(at_end_ref[0], came_ref, sent_ref, slice(q_width, o_first)))
    ordered = []
    for place in range(count):
        kv = kvs[0]
        for k in range(1, count):
            kv = jnp.where((index_ref[0] ^ k) == place, kvs[k], kv)
        ordered.append(kv)
    k_ref[...] = jnp.concatenate([kv[:, : kv_width // 2] for kv in ordered], axis=1)
    v_ref[...] = jnp.concatenate([kv[:, kv_width // 2 :] for kv in ordered], axis=1)


def settle_attention(at_end, index, pairs, q_width, kv_width):
    count = len(pairs)
    arrays = [array for pair in pairs for array in pair]
    depth = arrays[0].shape[0]
    width = min(array.shape[1] for array in arrays)
    o_width = width - q_width - kv_width
    rows = math.gcd(depth, 128)
    ins = [(array, (rows, width), lambda i: (i, 0)) for array in arrays]
    widths = (q_width, kv_width // 2, kv_width // 2, o_width)
    outs = [row_blocks(full(depth, each * count), rows) for each in widths]
    kernel = functools.partial(settle_attention_kernel, count, q_width, kv_width)
    return gridded(kernel, depth // rows, ins, outs, scalars=(at_end, index))


def d_qkv_kernel(at_end_ref, here_ref, came_ref, sent_ref, dq_ref, cos_ref, sin_ref, out_ref):
    lanes = 2 * HEAD_SIZE
    half, q_width = dq_ref.shape[1], dq_ref.shape[2]
    cycle = came_ref.shape[1] // lanes // 2
    for core_side in range(2):
        column = pl.multiple_of((core_side * cycle + here_ref[0]) * lanes, lanes)
        d_kv = settled(at_end_ref[0], came_ref, sent_ref, pl.ds(column, lanes))
        cosine, sine = of_keys(cos_ref[core_side], sin_ref[core_side])
        d_kv = turned(d_kv, cosine, -sine).astype(jnp.bfloat16)
        rows = slice(core_side * half, (core_side + 1) * half)
        out_ref[rows, :q_width] = dq_ref[core_side]
        out_ref[rows, q_width:] = d_kv


def rows_back_kernel(count, index_ref, own_ref, other_ref, out_ref):
    rows, width = own_ref.shape[0], own_ref.shape[1] // count
    for ref, core in ((own_ref, index_ref[1]), (other_ref, 1 - index_ref[1])):
        first = pl.multiple_of(core * rows, rows)
        for block in range(count):
            column = pl.multiple_of((index_ref[0] ^ block) * width, width)
            out_ref[pl.ds(first, rows), pl.ds(column, width)] = ref[
                :, block * width : (block + 1) * width
            ]


def result_kernel(middle_ref, *refs):
    refs[-1][...] = (middle_ref[...] + total_of(refs[:-1])).astype(jnp.bfloat16)


def still(array):
    zeros = (0,) * len(array.shape)
    return (array, array.shape, lambda i: zeros)


def dot(left, right):
    return jnp.dot(left, right, preferred_element_type=jnp.float32)


def both(mine_ref, other_ref, weight):
    return jnp.concatenate([dot(mine_ref[...], weight), dot(other_ref[...], weight)], axis=0)


def chosen(here_steps, count, own, fetched, passed):
    here = pl.program_id(0) < here_steps
    weights = []
    for which in (0, 1):
        pieces = [own[which][...]]
        for k in range(count - 1):
            pieces.append(
                jnp.where(here, fetched[2 * k + which][...], passed[2 * k + which][...])
            )
        weights.append(jnp.concatenate(pieces, axis=0))
    return weights


def gate_up_kernel(count, here_steps, *refs):
    x_refs, refs = refs[:2], refs[2:]
    own, fetched, passed = refs[:2], refs[2 : 2 * count], refs[2 * count : 4 * count - 2]
    gate_ref, up_ref, hidden_ref = refs[4 * count - 2 :]
    weights = chosen(here_steps, count, own, fetched, passed)
    lin = both(*x_refs, jnp.concatenate(weights, axis=1))
    gate, up = lin[:, : lin.shape[1] // 2], lin[:, lin.shape[1] // 2 :]
    gate_ref[...] = gate.astype(jnp.bfloat16)
    up_ref[...] = up.astype(jnp.bfloat16)
    hidden_ref[...] = (gate * jax.nn.sigmoid(gate) * up).astype(jnp.bfloat16)


def columns_kernel(count, here_steps, *refs):
    own, fetched, passed = refs[:2], refs[2 : 2 * count], refs[2 * count : 4 * count - 2]
    wg_ref, wu_ref = refs[4 * count - 2 :]
    wg_ref[...], wu_ref[...] = chosen(here_steps, count, own, fetched, passed)


def column_blocks(own_gate, own_up, fetched, passed):
    depth, units = own_gate.shape
    block = math.gcd(units // 2, 256)
    steps, half = units // block, units // block // 2
    ins = [(w, (depth, block), lambda i: (0, i)) for w in (own_gate, own_up)]
    for arrays, step in (
        (fetched, lambda i: jnp.minimum(i, half - 1)),
        (passed, lambda i: jnp.maximum(i - half, 0)),
    ):
        for array in arrays:
            ins.append((array, (depth, block), lambda i, step=step: (0, step(i))))
            ins.append((array, (depth, block), lambda i, step=step: (0, half + step(i))))
    return ins, block, steps, half


def gate_up(x, *weights):
    tokens, units = 2 * x[0].shape[0], weights[0].shape[1]
    ins, block, steps, half = column_blocks(*weights)
    outs = [(low(tokens, units), (tokens, block), lambda i: (0, i))] * 3
    kernel = functools.partial(gate_up_kernel, len(weights[2]) + 1, half)
    return gridded(kernel, steps, [still(x[0]), still(x[1])] + ins, outs, limit=VMEM_LIMIT)


def whole_columns(*weights):
    depth, units = weights[0].shape
    ins, block, steps, half = column_blocks(*weights)
    count = len(weights[2]) + 1
    outs = [(low(count * depth, units), (count * depth, block), lambda i: (0, i))] * 2
    return gridded(functools.partial(columns_kernel, count, half), steps, ins, outs)


def units_back_kernel(count, *refs):
    d_refs, refs = refs[:2], refs[2:]
    pieces, (gate_ref, up_ref, d_gate_ref, d_up_ref) = refs[:count], refs[count:]
    weight = jnp.concatenate([ref[...] for ref in pieces], axis=0)
    d_hidden = both(*d_refs, weight)
    gate, up = gate_ref[...].astype(jnp.float32), up_ref[...].astype(jnp.float32)
    chance = jax.nn.sigmoid(gate)
    d_up_ref[...] = (d_hidden * (gate * chance)).astype(jnp.bfloat16)
    slope = chance + gate * chance * (1.0 - chance)
    d_gate_ref[...] = (d_hidden * up * slope).astype(jnp.bfloat16)


def units_back(d_out, pieces, gate, up):
    tokens, units = gate.shape
    depth = pieces[0].shape[0]
    block = math.gcd(units, 512)

    def by_columns(array, rows):
        return (array, (rows, block), lambda i: (0, i))

    ins = [still(d_out[0]), still(d_out[1])] + [by_columns(piece, depth) for piece in pieces]
    ins += [by_columns(gate, tokens), by_columns(up, tokens)]
    outs = [by_columns(low(tokens, units), tokens)] * 2
    kernel = functools.partial(units_back_kernel, len(pieces))
    return gridded(kernel, units // block, ins, outs, limit=LARGE_LIMIT)


def rows_sum_kernel(terms, *refs):
    first_ref, second_ref = refs[-2:]
    total = 0.0
    for left_ref, right_ref in zip(refs[:terms], refs[terms : 2 * terms]):
        total = total + contract_last(left_ref[...], right_ref[...])
    total = total.astype(jnp.bfloat16)
    half = first_ref.shape[0]
    first_ref[...] = total[:half]
    second_ref[...] = total[half:]


def rows_sum(lefts, rights):
    tokens, width = lefts[0].shape[0], rights[0].shape[0]
    block = math.gcd(width, 512)
    ins = [still(left) for left in lefts]
    ins += [(right, (block, right.shape[1]), lambda i: (i, 0)) for right in rights]
    outs = [(low(tokens // 2, width), (tokens // 2, block), lambda i: (0, i))] * 2
    return gridded(functools.partial(rows_sum_kernel, len(lefts)), width // block, ins, outs)


def weight_grad_kernel(count, terms, turn, *refs):
    if turn:
        side, refs = refs[0][0], refs[1:]
    outs = refs[3 * terms :]
    step = pl.program_id(0)
    first = 0
    for term in range(terms):
        mine_ref, other_ref, right_ref = refs[3 * term : 3 * term + 3]
        half = mine_ref.shape[0]
        grad = contract_first(mine_ref[...], right_ref[:half, :])
        grad = grad + contract_first(other_ref[...], right_ref[half:, :])
        grad = grad.astype(jnp.bfloat16)
        columns = grad.shape[1]
        for k in range(count):

            @pl.when(step == k)
            def _(k=k, first=first, grad=grad, columns=columns):
                if turn:
                    part = columns // 2
                    outs[k][:, pl.ds(pl.multiple_of(side * part, part), part)] = grad[:, :part]
                    outs[k][:, pl.ds(pl.multiple_of((1 - side) * part, part), part)] = grad[:, part:]
                else:
                    outs[k][:, first : first + columns] = grad

        first += columns


def weight_grad(terms, count, side=None):
    columns = sum(right.shape[1] for _, _, right in terms)
    depth = terms[0][0].shape[1] // count
    ins = []
    if side is not None:
        ins.append((side, None, None))
    for mine, other, right in terms:
        ins += [(left, (left.shape[0], depth), lambda i: (0, i)) for left in (mine, other)]
        ins.append(still(right))
    specs = [
        pl.BlockSpec(memory_space=pltpu.SMEM) if block is None else pl.BlockSpec(block, index)
        for _, block, index in ins
    ]
    return pl.pallas_call(
        functools.partial(weight_grad_kernel, count, len(terms), side is not None),
        grid=(count,),
        in_specs=specs,
        out_specs=[pl.BlockSpec((depth, columns), lambda i: (0, 0))] * count,
        out_shape=[low(depth, columns)] * count,
        compiler_params=pltpu.CompilerParams(vmem_limit_bytes=MIDDLE_LIMIT),
        cost_estimate=SMALL,
    )(*[array for array, _, _ in ins])


def turned(lin, cosine, sine):
    width = lin.shape[-1]
    quarter = HEAD_SIZE // 2
    lane = lax.broadcasted_iota(jnp.int32, lin.shape, lin.ndim - 1)
    first = lax.rem(lane, HEAD_SIZE) < quarter
    partner = jnp.where(
        first,
        -pltpu.roll(lin, width - quarter, lin.ndim - 1),
        pltpu.roll(lin, quarter, lin.ndim - 1),
    )
    return lin * cosine + partner * sine


def side_by_side(table, width):
    return jnp.concatenate([table] * (width // table.shape[-1]), axis=-1)


def of_keys(cosine, sine):
    keys = lax.broadcasted_iota(jnp.int32, cosine.shape, 1) < HEAD_SIZE
    return jnp.where(keys, cosine, 1.0), jnp.where(keys, sine, 0.0)


def qkv_kernel(count, q_width, kv_width, side_ref, *refs):
    x_refs, (gain_ref, cos_ref, sin_ref), refs = refs[:2], refs[2:5], refs[5:]
    own_ref, fetched, passed_ref, refs = refs[0], refs[1:count], refs[count], refs[count + 1 :]
    normed_refs, (q_ref, kv_ref, wqkv_ref, wo_ref) = refs[:2], refs[2:]
    qkv_width = q_width + kv_width
    depth = own_ref.shape[0]
    half = depth // 2

    @pl.when(pl.program_id(0) == 0)
    def _():
        wqkv_ref[:depth, :] = own_ref[:, :qkv_width]
        wo_ref[:depth, :] = own_ref[:, qkv_width:]
        for k in range(1, count):
            for which, piece in (
                (side_ref[0], fetched[k - 1][:half, :]),
                (1 - side_ref[0], passed_ref[(k - 1) * half : k * half, :]),
            ):
                first = pl.multiple_of(k * depth + which * half, half)
                wqkv_ref[pl.ds(first, half), :] = piece[:, :qkv_width]
                wo_ref[pl.ds(first, half), :] = piece[:, qkv_width:]

    for i in range(2):
        x = x_refs[i][...].astype(jnp.float32)
        mean = jnp.mean(x * x, axis=-1, keepdims=True)
        normed = (x * lax.rsqrt(mean + 1e-05) * gain_ref[...]).astype(jnp.bfloat16)
        normed_refs[i][...] = normed
        lin = dot(normed, wqkv_ref[...])
        cosine, sine = cos_ref[i], sin_ref[i]
        q = turned(lin[:, :q_width], side_by_side(cosine, q_width), side_by_side(sine, q_width))
        q_ref[i] = q.astype(jnp.bfloat16)
        kv = turned(lin[:, q_width:], *of_keys(cosine, sine))
        kv_ref[i] = kv.astype(jnp.bfloat16)


def project_qkv(side, x, gain, cosine, sine, own, fetched, passed, q_width, kv_width):
    half_rows, width = x[0].shape
    qkv_width = q_width + kv_width
    block = math.gcd(half_rows, 128)

    def rows_of(array, columns):
        return (array, (block, columns), lambda i: (i, 0))

    def of_both(array, columns):
        return (array, (2, block, columns), lambda i: (0, i, 0))

    lanes = cosine.shape[-1]
    ins = [rows_of(x[0], width), rows_of(x[1], width), still(gain)]
    ins += [of_both(cosine, lanes), of_both(sine, lanes)]
    ins += [still(array) for array in (own, *fetched, passed)]
    o_width = own.shape[1] - qkv_width
    outs = [rows_of(low(half_rows, width), width)] * 2
    outs += [of_both(low(2, half_rows, q_width), q_width), of_both(low(2, half_rows, kv_width), kv_width)]
    outs += [still(low(width, qkv_width)), still(low(width, o_width))]
    kernel = functools.partial(qkv_kernel, len(fetched) + 1, q_width, kv_width)
    return gridded(kernel, half_rows // block, ins, outs, scalars=(side,))


def shares(q, k, visible):
    scores = jnp.where(visible, contract_last(q, k), -1e30)
    weights = jnp.exp(scores - jnp.max(scores, axis=-1, keepdims=True))
    return weights, 1.0 / jnp.sum(weights, axis=-1, keepdims=True)


def load_attention(q_ref, place_ref, start_ref, key_place_ref, kv_refs):
    q = q_ref[...]
    q = q.reshape(q.shape[0] * q.shape[1], q.shape[2])
    kv = jnp.concatenate([ref[...].reshape(q.shape[0], 2 * HEAD_SIZE) for ref in kv_refs], axis=0)
    q = q * jnp.bfloat16(1.0 / math.sqrt(HEAD_SIZE))
    key_place = key_place_ref[0]
    visible = (key_place <= place_ref[0]) & (key_place >= start_ref[0])
    return q, kv[:, :HEAD_SIZE], kv[:, HEAD_SIZE:], visible


def attend_kernel(groups, q_ref, place_ref, start_ref, key_place_ref, wo_ref, *refs):
    kv_refs, (out_ref, first_ref, second_ref) = refs[:-3], refs[-3:]
    q, k, v, visible = load_attention(q_ref, place_ref, start_ref, key_place_ref, kv_refs)
    mixed = []
    for g in range(groups):
        weights, parts = shares(q[:, g * HEAD_SIZE : (g + 1) * HEAD_SIZE], k, visible)
        mixed.append(dot(weights.astype(jnp.bfloat16), v) * parts)
    out = jnp.concatenate(mixed, axis=1).astype(jnp.bfloat16)
    out_ref[...] = out.reshape(out_ref.shape)
    branch = contract_last(out, wo_ref[...]).astype(jnp.bfloat16)
    half = first_ref.shape[0]
    first_ref[...] = branch[:half]
    second_ref[...] = branch[half:]


def attend_back_kernel(
    groups,
    here_ref,
    q_ref,
    mine_ref,
    other_ref,
    cos_ref,
    sin_ref,
    place_ref,
    start_ref,
    key_place_ref,
    wo_ref,
    *refs,
):
    kv_refs, (dq_ref, dkv_ref) = refs[:-2], refs[-2:]
    q, k, v, visible = load_attention(q_ref, place_ref, start_ref, key_place_ref, kv_refs)
    d_out = both(mine_ref, other_ref, wo_ref[...]).astype(jnp.bfloat16)
    scale = 1.0 / math.sqrt(HEAD_SIZE)
    d_q, d_k, d_v = [], 0.0, 0.0
    for g in range(groups):
        q_head = q[:, g * HEAD_SIZE : (g + 1) * HEAD_SIZE]
        d_head = d_out[:, g * HEAD_SIZE : (g + 1) * HEAD_SIZE]
        weights, parts = shares(q_head, k, visible)
        probs = weights * parts
        d_probs = contract_last(d_head, v)
        row_delta = jnp.sum(probs * d_probs, axis=-1, keepdims=True)
        d_scores = (probs * (d_probs - row_delta)).astype(jnp.bfloat16)
        d_q.append(dot(d_scores, k) * scale)
        d_k = d_k + contract_first(d_scores, q_head)
        d_v = d_v + contract_first(probs.astype(jnp.bfloat16), d_head)
    d_q = jnp.concatenate(d_q, axis=1)
    cosine = cos_ref[...].reshape(q.shape[0], -1)
    sine = sin_ref[...].reshape(q.shape[0], -1)
    d_q = turned(d_q, side_by_side(cosine, q.shape[1]), -side_by_side(sine, q.shape[1]))
    dq_ref[...] = d_q.astype(jnp.bfloat16).reshape(dq_ref.shape)
    d_kv = jnp.concatenate([d_k, d_v], axis=1).astype(jnp.bfloat16)
    half, lanes, cycle = dkv_ref.shape[0], 2 * HEAD_SIZE, len(kv_refs)
    for j in range(cycle):
        for core_side in range(2):
            first = (2 * j + core_side) * half
            column = pl.multiple_of((core_side * cycle + (here_ref[0] ^ j)) * lanes, lanes)
            dkv_ref[:, pl.ds(column, lanes)] = d_kv[first : first + half]


def of_pack(array, half):
    return (array, (2, half, array.shape[-1]), lambda p: (0, p, 0))


def place_blocks(places):
    return [(array, (1,) + array.shape[1:], lambda p: (p, 0, 0)) for array in places]


def attend(q, places, wo, kvs, packs, groups):
    half = q.shape[1] // packs
    width = wo.shape[0]
    ins = [of_pack(q, half)] + place_blocks(places) + [still(wo)] + [of_pack(kv, half) for kv in kvs]
    outs = [of_pack(low(*q.shape), half)]
    outs += [(low(q.shape[1], width), (half, width), lambda p: (p, 0))] * 2
    return gridded(functools.partial(attend_kernel, groups), packs, ins, outs)


def attend_back(here, q, d_branch, cosine, sine, places, wo, kvs, packs, groups):
    half = q.shape[1] // packs
    cycle = len(kvs)
    ins = [of_pack(q, half)]
    ins += [(array, (half, array.shape[1]), lambda p: (p, 0)) for array in d_branch]
    ins += [of_pack(cosine, half), of_pack(sine, half)] + place_blocks(places) + [still(wo)]
    ins += [of_pack(kv, half) for kv in kvs]
    lanes = 2 * HEAD_SIZE
    outs = [of_pack(low(*q.shape), half)]
    outs.append((low(q.shape[1], 2 * cycle * lanes), (half, 2 * cycle * lanes), lambda p: (p, 0)))
    kernel = functools.partial(attend_back_kernel, groups)
    return gridded(kernel, packs, ins, outs, scalars=(here,))


def split_heads(
    hidden_in,
    out_cotangent,
    norm1_gain,
    q_weight,
    key_projection_weight,
    value_projection_weight,
    o_weight,
    norm2_gain,
    gate_weight,
    up_weight,
    down_weight,
    seq_lengths,
    span_order,
):
    packs = lax.axis_size("fsdp")
    cycle = lax.axis_size("ctx")
    pack = lax.axis_index("fsdp")
    core = lax.axis_index("tp")
    here = lax.axis_index("ctx")
    rows = hidden_in.shape[0]
    half = rows // 2
    tokens = packs * rows
    depth = q_weight.shape[0]
    width = depth * packs
    q_width = q_weight.shape[1] // packs
    k_width = key_projection_weight.shape[1] // packs
    ff_width = gate_weight.shape[1] // packs
    ff_half = ff_width // 2
    groups = q_width // k_width
    far = range(1, packs)
    steps = Steps(Line("ctx"))
    kept = {}


    def columns(weight, k, count, first=0, of=None):
        return lax.dynamic_slice_in_dim(weight, (pack ^ k) * (of or count) + first, count, 1)

    def to_pack(name, k, array):
        return ((name, k), array, "fsdp", pairs_by(k, packs))

    def send_all(name, arrays):
        return [to_pack(name, k, array) for k, array in zip(far, arrays)]

    def arrived(name):
        return [steps.take((name, k)) for k in far]

    def to_core(name, array):
        return [(name, array, "tp", pairs_by(1, 2))]

    def to_rows(name, first):
        kept[name], *others = fold(first, steps.take(name), packs)
        return send_all(name, others)

    def joined(name, own, others):
        kept[name] = join(own, others)
        return to_core(name, kept[name])

    def unwaited(name):
        return dict(steps.others)[name]

    def both_of(name):
        return kept[name], steps.take(name)

    index = jnp.stack([pack, core]).astype(jnp.int32)
    here_arg = here.astype(jnp.int32)[None]
    side_arg = here_arg & 1
    at_end = steps.line.at_end

    own_in, *in_moves = prepare(hidden_in, index, packs)
    own_cot, *cot_moves = prepare(out_cotangent, index, packs)

    side = here & 1
    weights = (q_weight, key_projection_weight, value_projection_weight, o_weight)
    widths = (q_width, k_width, k_width, q_width)

    def attention_piece(k, first, count):
        return jnp.concatenate(
            [
                lax.dynamic_slice(weight, (first, (pack ^ k) * each), (count, each))
                for weight, each in zip(weights, widths)
            ],
            axis=1,
        )

    meta = jnp.concatenate([span_order[0], seq_lengths[0]])
    order_len, meta_len = span_order.shape[1], meta.shape[0]
    metas = jnp.concatenate([(meta // 32).astype(jnp.bfloat16), (meta % 32).astype(jnp.bfloat16)])
    info = jnp.stack(
        [
            jnp.pad(jnp.concatenate([norm1_gain, metas]), (0, sum(widths) - depth - 2 * meta_len)),
            jnp.pad(norm2_gain, (0, sum(widths) - depth)),
        ]
    )
    info_rows = jnp.pad(info, ((0, 14), (0, 0)))
    row_half = depth // 2
    steps.step(
        [
            to_pack(
                "attention",
                k,
                jnp.concatenate([attention_piece(k, side * row_half, row_half), info_rows], axis=0),
            )
            for k in far
        ]
    )
    pieces = []

    def pass_rows():
        pieces.extend(arrived("attention"))
        rows_on = join_rows(pieces, row_half)
        return [("attention_rows", rows_on, "ctx", pairs_by(1, cycle))]

    steps.step(send_all("in", in_moves), late=pass_rows)
    infos = jnp.stack([info] + [piece[row_half : row_half + 2] for piece in pieces])
    all_gains = infos[:, :, :depth].astype(jnp.float32)
    gain_one = all_gains[:, 0].reshape(1, -1)
    gain_two = all_gains[:, 1].reshape(1, -1)
    metas = infos[:, 0, depth : depth + 2 * meta_len].astype(jnp.int32)
    metas = metas[:, :meta_len] * 32 + metas[:, meta_len:]
    orders, lengths = metas[:, :order_len], metas[:, order_len:]

    others = jnp.stack([here ^ j for j in range(cycle)])
    first = jnp.sum(
        jnp.where(
            others[None, :, None] == jnp.arange(order_len, dtype=jnp.int32)[None, None, :],
            orders[:, None, :],
            0,
        ),
        axis=2,
    )
    halves = jnp.stack([core, core ^ 1])[None, None, :]
    section = jnp.where(halves == 0, first[:, :, None], 2 * cycle - 1 - first[:, :, None])
    places = section[..., None] * half + jnp.arange(half, dtype=jnp.int32)
    places = places.reshape(packs, cycle * rows)
    starts = jnp.zeros_like(places)
    end = jnp.zeros((packs, 1), jnp.int32)
    for j in range(lengths.shape[1]):
        end = end + lengths[:, j : j + 1]
        starts = jnp.where(places >= end, end, starts)
    place_args = (places[:, :rows, None], starts[:, :rows, None], places[:, None, :])
    offsets = (places - starts)[:, :rows].reshape(packs, 2, half).transpose(1, 0, 2)
    cosine, sine = in_vmem(
        turns_kernel,
        [full(2, tokens // 2, 2 * HEAD_SIZE)] * 2,
        offsets.astype(jnp.float32).reshape(2, tokens // 2, 1),
    )


    def two_halves(weight, k):
        return jnp.concatenate(
            [
                columns(weight, k, ff_half, side * ff_half, ff_width),
                columns(weight, k, ff_half, (1 - side) * ff_half, ff_width),
            ],
            axis=1,
        )

    def fetch(ks):
        return [
            to_pack(
                "gate_up",
                k,
                jnp.concatenate(
                    [
                        columns(weight, k, ff_half, side * ff_half, ff_width)
                        for weight in (gate_weight, up_weight)
                    ],
                    axis=1,
                ),
            )
            for k in ks
        ]

    def to_neighbour(k):
        return [(("neighbour", k), fetched[k], "ctx", pairs_by(1, cycle))]

    fetched = {}
    own_piece = attention_piece(0, 0, depth)
    cosine, sine, own_piece, *place_args = steps.step(
        fetch([1, 2]), carry=(cosine, sine, own_piece, *place_args)
    )
    all_in = join(own_in, arrived("in"))
    all_in = (all_in, swap(all_in, "tp", 1))
    normed_mine, normed_other, q_rot, kv_own, wqkv, wo = project_qkv(
        side_arg,
        all_in,
        gain_one,
        cosine,
        sine,
        own_piece,
        pieces,
        steps.take("attention_rows"),
        q_width,
        2 * k_width,
    )
    normed_one = (normed_mine, normed_other)
    steps.step(
        [(("kv", j), kv_own, "ctx", pairs_by(j, cycle)) for j in range(1, cycle)] + fetch([3])
    )
    fetched[1], fetched[2] = steps.take(("gate_up", 1)), steps.take(("gate_up", 2))
    steps.step(send_all("cot", cot_moves) + to_neighbour(1))
    fetched[3] = steps.take(("gate_up", 3))
    kvs = [kv_own] + [steps.take(("kv", j)) for j in range(1, cycle)]
    attn, first, second = attend(q_rot, place_args, wo, kvs, packs, groups)
    attn_low = attn.reshape(tokens, q_width)
    steps.step(to_core("branch", second))
    steps.step(to_neighbour(2), late=lambda: to_rows("branch", first))
    kept["cot"] = join(own_cot, arrived("cot"))

    def middle_moves():
        kept["middle"], kept["normed"], *sends = in_vmem(
            functools.partial(middle_kernel, packs),
            [full(half, width)] + [low(half, width)] * packs,
            own_in,
            gain_two,
            kept["branch"],
            *arrived("branch"),
        )
        return send_all("two", sends)

    steps.step(to_neighbour(3) + to_core("cot", kept["cot"]), late=middle_moves)

    def wd_moves(ks):
        return [to_pack("down", k, two_halves(down_weight, k)) for k in ks]

    own_columns = [two_halves(weight, 0) for weight in (gate_weight, up_weight, down_weight)]
    own_gate, own_up, own_down = steps.step(
        wd_moves([1, 2]),
        late=lambda: joined("two", kept["normed"], arrived("two")),
        carry=own_columns,
    )
    all_cot = both_of("cot")
    neighbours = [steps.take(("neighbour", k)) for k in far]
    normed_two = (kept["two"], unwaited("two"))

    unit_weights = (own_gate, own_up, [fetched[k] for k in far], neighbours)
    gate_val, up_val, hidden = gate_up(normed_two, *unit_weights)
    d_wd = weight_grad([(*all_cot, hidden)], packs, side_arg)

    def back(name, grad, ks):
        return [to_pack(name, k, grad[k]) for k in ks]

    def entry(name, k, grad=None):
        return ((name, k), grad[0] if k == 0 else None)

    steps.step(back("wd", d_wd, [1, 2]), summed=entry("wd", 0, d_wd))
    wg, wu = whole_columns(*unit_weights)
    wg, wu = steps.step(wd_moves([3]), summed=entry("wd", 1), carry=(wg, wu))
    steps.step(back("wd", d_wd, [3]), summed=entry("wd", 2))
    wd_pieces = [own_down] + arrived("down")
    d_gate, d_up = units_back(all_cot, wd_pieces, gate_val, up_val)
    first, second = rows_sum([d_gate, d_up], [wg, wu])
    d_wg = weight_grad([(*normed_two, d_gate)], packs, side_arg)
    steps.step(to_core("d_two", second) + back("wg", d_wg, [1, 2]), summed=entry("wd", 3))
    d_wu = weight_grad([(*normed_two, d_up)], packs, side_arg)
    steps.step(
        summed=entry("wg", 0, d_wg), late=functools.partial(to_rows, "d_two", first)
    )

    def branch_back():
        kept["d_middle"], kept["d_gain_two"], kept["d_branch"], *sends = in_vmem(
            functools.partial(branch_back_kernel, packs),
            [full(half, width), full(1, width)] + [low(half, width)] * packs,
            kept["middle"],
            gain_two,
            own_cot,
            kept["d_two"],
            *arrived("d_two"),
        )
        return send_all("d_branch", sends)

    steps.step(summed=entry("wu", 0, d_wu), late=branch_back)
    ff_first, ff_second = rows_sum([hidden], [join(wd_pieces[0], wd_pieces[1:])])
    steps.step(
        back("wg", d_wg, [3]),
        summed=entry("wg", 1),
        late=lambda: joined("all_branch", kept["d_branch"], arrived("d_branch")),
    )
    sums = steps.line.sums

    def settle_all(name):
        return settle(at_end, index, [sums[name, k] for k in range(packs)], ff_width)

    d_branch = (kept["all_branch"], unwaited("all_branch"))
    d_q, d_kv = attend_back(
        here_arg, q_rot, d_branch, cosine, sine, place_args, wo, kvs, packs, groups
    )
    d_q, d_kv = steps.step(back("wu", d_wu, [1, 2]), summed=entry("wg", 2), carry=(d_q, d_kv))
    steps.step(back("wu", d_wu, [3]), summed=("d_kv", d_kv))
    down_grad = settle_all("wd")
    steps.step(to_core("ff", ff_second), summed=entry("wg", 3))
    (down_grad,) = steps.step(
        summed=entry("wu", 1), late=functools.partial(to_rows, "ff", ff_first), carry=(down_grad,)
    )
    steps.step(summed=entry("wu", 2))
    result = in_vmem(
        result_kernel, [low(half, width)], kept["middle"], kept["ff"], *arrived("ff")
    )[0]
    d_qkv = in_vmem(
        d_qkv_kernel,
        [low(tokens, q_width + 2 * k_width)],
        at_end,
        here_arg,
        *sums["d_kv"],
        d_q,
        cosine,
        sine,
        scalars=2,
    )[0]
    d_wqkvo = weight_grad([(*normed_one, d_qkv), (*d_branch, attn_low)], packs)
    first, second = rows_sum([d_qkv], [wqkv])
    steps.step(
        back("wqkvo", d_wqkvo, [1, 2]) + to_core("d_one", second), summed=entry("wu", 3)
    )
    steps.step(
        summed=entry("wqkvo", 0, d_wqkvo), late=functools.partial(to_rows, "d_one", first)
    )

    def both_rows(own, other):
        return in_vmem(
            functools.partial(rows_back_kernel, packs),
            [low(rows, width)],
            index,
            own,
            other,
            scalars=1,
        )[0]

    gate_grad = settle_all("wg")
    def gains_to_core():
        kept["in_grad"], d_gain_one = in_vmem(
            functools.partial(in_grad_kernel, packs),
            [low(half, width), full(1, width)],
            own_in,
            gain_one,
            kept["d_middle"],
            kept["d_one"],
            *arrived("d_one"),
        )
        kept["gains"] = jnp.concatenate([d_gain_one, kept["d_gain_two"]], axis=0)
        return to_core("gains", kept["gains"]) + to_core("in_grad", kept["in_grad"])

    def gains_to_packs():
        kept["gains"] = kept["gains"] + steps.take("gains")
        return [to_pack("gains", k, kept["gains"][:, k * depth : (k + 1) * depth]) for k in far]

    def gains_along():
        kept["gains"] = kept["gains"][:, :depth]
        for k in far:
            kept["gains"] = kept["gains"] + steps.take(("gains", k))
        return [(("gains", j), kept["gains"], "ctx", pairs_by(j, cycle)) for j in range(1, cycle)]

    steps.step(back("wqkvo", d_wqkvo, [3]), summed=entry("wqkvo", 1), late=gains_to_core)
    (gate_grad,) = steps.step(
        summed=entry("wqkvo", 2), late=gains_to_packs, carry=(gate_grad,)
    )
    up_grad = settle_all("wu")
    in_grad = both_rows(kept["in_grad"], steps.take("in_grad"))
    in_grad, up_grad = steps.step(
        to_core("result", result), summed=entry("wqkvo", 3), carry=(in_grad, up_grad)
    )
    steps.step(late=gains_along)
    out_hidden = both_rows(result, steps.take("result"))
    (out_hidden,) = steps.step(carry=(out_hidden,))
    steps.step()
    shares_of_gains = jnp.stack(
        [kept["gains"]] + [steps.take(("gains", j)) for j in range(1, cycle)]
    )
    gains = steps.token[0, 0]
    for place in range(cycle):
        gains = gains + lax.dynamic_index_in_dim(shares_of_gains, here ^ place, 0, keepdims=False)
    q_grad, k_grad, v_grad, o_grad = settle_attention(
        at_end, index, [sums["wqkvo", k] for k in range(packs)], q_width, 2 * k_width
    )
    return (
        out_hidden,
        in_grad,
        gains[0],
        q_grad,
        k_grad,
        v_grad,
        o_grad,
        gains[1],
        gate_grad,
        up_grad,
        down_grad,
    )


def gathered_weights(
    hidden_in,
    out_cotangent,
    norm1_gain,
    q_weight,
    key_projection_weight,
    value_projection_weight,
    o_weight,
    norm2_gain,
    gate_weight,
    up_weight,
    down_weight,
    seq_lengths,
    span_order,
):
    rows_here = hidden_in.shape[0]
    order_row = span_order[0]
    length_row = seq_lengths[0]
    kv_heads = key_projection_weight.shape[1] // HEAD_SIZE
    query_groups = QUERY_HEADS // KEY_VALUE_HEADS
    score_scale = 1.0 / math.sqrt(HEAD_SIZE)
    whole_rows = rows_here * lax.axis_size("ctx")
    local_rows = lax.axis_index("ctx") * rows_here + jnp.arange(rows_here, dtype=jnp.int32)
    q_place, q_segment, q_offset = stream_place(local_rows, order_row, length_row, rows_here)
    inputs = hidden_in.astype(jnp.float32)
    gain_one, wq_full, wk_full, wv_full, wo_full = (
        lax.all_gather(norm1_gain, "fsdp", axis=0, tiled=True),
        lax.all_gather(q_weight, "fsdp", axis=0, tiled=True),
        lax.all_gather(key_projection_weight, "fsdp", axis=0, tiled=True),
        lax.all_gather(value_projection_weight, "fsdp", axis=0, tiled=True),
        lax.all_gather(o_weight, "fsdp", axis=0, tiled=True),
    )
    gain_one = gain_one.astype(jnp.float32)
    first_normalized = normalize(inputs, gain_one)
    normed_low = first_normalized.astype(jnp.bfloat16)
    q_linear = jnp.dot(normed_low, wq_full, preferred_element_type=jnp.float32).reshape(
        rows_here, kv_heads * query_groups, HEAD_SIZE
    )
    k_linear = jnp.dot(normed_low, wk_full, preferred_element_type=jnp.float32).reshape(
        rows_here, kv_heads, HEAD_SIZE
    )
    q_rotated = (
        rotary_embedding(q_linear, q_offset)
        .astype(jnp.bfloat16)
        .reshape(rows_here, kv_heads, query_groups, HEAD_SIZE)
    )
    k_rotated = (
        rotary_embedding(k_linear, q_offset)
        .astype(jnp.bfloat16)
        .reshape(rows_here, kv_heads * HEAD_SIZE)
    )
    v_low = jnp.dot(normed_low, wv_full, preferred_element_type=jnp.float32).astype(jnp.bfloat16)

    def key_blocks(shard_rows):
        row_count = shard_rows.shape[0]
        key_total_width = math.gcd(row_count, 512)
        number = row_count // key_total_width
        k_place, k_segment, _ = stream_place(
            jnp.arange(row_count, dtype=jnp.int32), order_row, length_row, rows_here
        )
        return (
            key_total_width,
            number,
            k_place.reshape(number, key_total_width),
            k_segment.reshape(number, key_total_width),
        )

    def scores_of(key_block, place_block, segment_block):
        scores = (
            jnp.einsum("qkgd,skd->kgqs", q_rotated, key_block, preferred_element_type=jnp.float32)
            * score_scale
        )
        visible = (
            (q_place[:, None] >= place_block[None, :])
            & (q_segment[:, None] == segment_block[None, :])
        )[None, None]
        return (jnp.where(visible, scores, -1e30), visible)

    start_state = (
        jnp.full((kv_heads, query_groups, rows_here), -1e30, jnp.float32),
        jnp.zeros((kv_heads, query_groups, rows_here), jnp.float32),
        jnp.zeros((kv_heads, query_groups, rows_here, HEAD_SIZE), jnp.float32),
    )
    folded = start_state
    key_row_block = lax.all_gather(k_rotated, "ctx", axis=0, tiled=True)
    value_row_block = lax.all_gather(v_low, "ctx", axis=0, tiled=True)
    key_total_width, number, k_place, k_segment = key_blocks(key_row_block)

    def one_step(carried, pieces):
        running_max, totals, accumulated = carried
        key_block, value_block, place_block, segment_block = pieces
        scores, visible = scores_of(key_block, place_block, segment_block)
        new_max = jnp.maximum(running_max, jnp.max(scores, axis=-1))
        weights = jnp.where(visible, jnp.exp(scores - new_max[..., None]), 0.0)
        factor = jnp.exp(running_max - new_max)
        totals = totals * factor + jnp.sum(weights, axis=-1)
        accumulated = accumulated * factor[..., None] + jnp.einsum(
            "kgqs,skd->kgqd",
            weights.astype(jnp.bfloat16),
            value_block,
            preferred_element_type=jnp.float32,
        )
        return ((new_max, totals, accumulated), None)

    pieces = (
        key_row_block.reshape(number, key_total_width, kv_heads, HEAD_SIZE),
        value_row_block.reshape(number, key_total_width, kv_heads, HEAD_SIZE),
        k_place,
        k_segment,
    )
    folded, _ = lax.scan(one_step, folded, pieces)
    running_max, totals, accumulated = folded
    mixed_out = jnp.transpose(accumulated / totals[..., None], (2, 0, 1, 3))
    log_sum = running_max + jnp.log(totals)
    attn_low = mixed_out.reshape(rows_here, kv_heads * query_groups * HEAD_SIZE).astype(
        jnp.bfloat16
    )
    branch = lax.psum(contract_last(attn_low, wo_full).astype(jnp.bfloat16), "tp").astype(
        jnp.float32
    )
    middle = inputs + branch
    gain_two, wg_full, wu_full, wd_full = (
        lax.all_gather(norm2_gain, "fsdp", axis=0, tiled=True),
        lax.all_gather(gate_weight, "fsdp", axis=0, tiled=True),
        lax.all_gather(up_weight, "fsdp", axis=0, tiled=True),
        lax.all_gather(down_weight, "fsdp", axis=0, tiled=True),
    )
    gain_two = gain_two.astype(jnp.float32)
    normed_two = normalize(middle, gain_two)
    normed_two_low = normed_two.astype(jnp.bfloat16)
    gate_val = jnp.dot(normed_two_low, wg_full, preferred_element_type=jnp.float32)
    up_val = jnp.dot(normed_two_low, wu_full, preferred_element_type=jnp.float32)
    hidden = swiglu(gate_val, up_val).astype(jnp.bfloat16)
    ffn_out = lax.psum(contract_last(hidden, wd_full).astype(jnp.bfloat16), "tp").astype(
        jnp.float32
    )
    result = (middle + ffn_out).astype(jnp.bfloat16)
    grad_out = out_cotangent.astype(jnp.float32)
    d_wd = contract_first(out_cotangent, hidden)
    d_hidden = jnp.dot(out_cotangent, wd_full, preferred_element_type=jnp.float32)
    _, swiglu_back = jax.vjp(swiglu, gate_val, up_val)
    d_gate, d_up = swiglu_back(d_hidden)
    d_gate_low = d_gate.astype(jnp.bfloat16)
    d_up_low = d_up.astype(jnp.bfloat16)
    d_wg = contract_first(normed_two_low, d_gate_low)
    d_wu = contract_first(normed_two_low, d_up_low)
    d_normed_two = lax.psum(
        (contract_last(d_gate_low, wg_full) + contract_last(d_up_low, wu_full)).astype(
            jnp.bfloat16
        ),
        "tp",
    ).astype(jnp.float32)
    _, norm_two_back = jax.vjp(normalize, middle, gain_two)
    d_middle_norm, d_gain_two = norm_two_back(d_normed_two)
    d_middle = grad_out + d_middle_norm
    d_branch_low = d_middle.astype(jnp.bfloat16)
    d_wo = contract_first(d_branch_low, attn_low)
    d_attn = jnp.dot(d_branch_low, wo_full, preferred_element_type=jnp.float32).astype(jnp.bfloat16)
    d_attn_heads = d_attn.reshape(rows_here, kv_heads, query_groups, HEAD_SIZE)
    row_delta = jnp.einsum("qkgd,qkgd->kgq", d_attn_heads.astype(jnp.float32), mixed_out)
    back_state = (
        jnp.zeros((rows_here, kv_heads, query_groups, HEAD_SIZE), jnp.float32),
        jnp.zeros((whole_rows, kv_heads, HEAD_SIZE), jnp.float32),
        jnp.zeros((whole_rows, kv_heads, HEAD_SIZE), jnp.float32),
    )
    folded = back_state
    key_row_block = lax.all_gather(k_rotated, "ctx", axis=0, tiled=True)
    value_row_block = lax.all_gather(v_low, "ctx", axis=0, tiled=True)
    key_total_width, number, k_place, k_segment = key_blocks(key_row_block)

    def one_step(carried, pieces):
        d_query, d_keys, d_values = carried
        key_block, value_block, place_block, segment_block, step_index = pieces
        scores, visible = scores_of(key_block, place_block, segment_block)
        prob_rows = jnp.where(visible, jnp.exp(scores - log_sum[..., None]), 0.0)
        d_values_block = jnp.einsum(
            "kgqs,qkgd->skd",
            prob_rows.astype(jnp.bfloat16),
            d_attn_heads,
            preferred_element_type=jnp.float32,
        )
        d_probs = jnp.einsum(
            "qkgd,skd->kgqs", d_attn_heads, value_block, preferred_element_type=jnp.float32
        )
        d_scores = (prob_rows * (d_probs - row_delta[..., None])).astype(jnp.bfloat16)
        d_query = (
            d_query
            + jnp.einsum("kgqs,skd->qkgd", d_scores, key_block, preferred_element_type=jnp.float32)
            * score_scale
        )
        d_keys_block = (
            jnp.einsum("kgqs,qkgd->skd", d_scores, q_rotated, preferred_element_type=jnp.float32)
            * score_scale
        )
        row_first = step_index * key_total_width
        d_keys = lax.dynamic_update_slice_in_dim(
            d_keys,
            lax.dynamic_slice_in_dim(d_keys, row_first, key_total_width, 0) + d_keys_block,
            row_first,
            0,
        )
        d_values = lax.dynamic_update_slice_in_dim(
            d_values,
            lax.dynamic_slice_in_dim(d_values, row_first, key_total_width, 0) + d_values_block,
            row_first,
            0,
        )
        return ((d_query, d_keys, d_values), None)

    pieces = (
        key_row_block.reshape(number, key_total_width, kv_heads, HEAD_SIZE),
        value_row_block.reshape(number, key_total_width, kv_heads, HEAD_SIZE),
        k_place,
        k_segment,
        jnp.arange(number, dtype=jnp.int32),
    )
    folded, _ = lax.scan(one_step, folded, pieces)
    d_query, d_keys_all, d_values_all = folded
    d_key_own, d_value_own = (
        lax.psum_scatter(
            d_keys_all.astype(jnp.bfloat16), "ctx", scatter_dimension=0, tiled=True
        ).astype(jnp.float32),
        lax.psum_scatter(
            d_values_all.astype(jnp.bfloat16), "ctx", scatter_dimension=0, tiled=True
        ).astype(jnp.float32),
    )
    _, rope_q_back = jax.vjp(lambda rotated_in: rotary_embedding(rotated_in, q_offset), q_linear)
    _, rope_k_back = jax.vjp(lambda rotated_in: rotary_embedding(rotated_in, q_offset), k_linear)
    (d_q_linear,) = rope_q_back(d_query.reshape(rows_here, kv_heads * query_groups, HEAD_SIZE))
    (d_k_linear,) = rope_k_back(d_key_own)
    d_q_low = d_q_linear.reshape(rows_here, kv_heads * query_groups * HEAD_SIZE).astype(
        jnp.bfloat16
    )
    d_k_low = d_k_linear.reshape(rows_here, kv_heads * HEAD_SIZE).astype(jnp.bfloat16)
    d_v_low = d_value_own.reshape(rows_here, kv_heads * HEAD_SIZE).astype(jnp.bfloat16)
    d_wq = contract_first(normed_low, d_q_low)
    d_wk = contract_first(normed_low, d_k_low)
    d_wv = contract_first(normed_low, d_v_low)
    d_normed_one = lax.psum(
        (
            contract_last(d_q_low, wq_full)
            + contract_last(d_k_low, wk_full)
            + contract_last(d_v_low, wv_full)
        ).astype(jnp.bfloat16),
        "tp",
    ).astype(jnp.float32)
    _, norm_one_back = jax.vjp(normalize, inputs, gain_one)
    d_inputs_norm, d_gain_one = norm_one_back(d_normed_one)
    in_grad = (d_middle + d_inputs_norm).astype(jnp.bfloat16)
    weight_grads = (d_gain_one, d_wq, d_wk, d_wv, d_wo, d_gain_two, d_wg, d_wu, d_wd)
    shares = (
        lax.psum_scatter(weight_grads[0], ("fsdp", "ctx"), scatter_dimension=0, tiled=True),
        lax.psum_scatter(weight_grads[1], ("fsdp", "ctx"), scatter_dimension=0, tiled=True),
        lax.psum_scatter(weight_grads[2], ("fsdp", "ctx"), scatter_dimension=0, tiled=True),
        lax.psum_scatter(weight_grads[3], ("fsdp", "ctx"), scatter_dimension=0, tiled=True),
        lax.psum_scatter(weight_grads[4], ("fsdp", "ctx"), scatter_dimension=0, tiled=True),
        lax.psum_scatter(weight_grads[5], ("fsdp", "ctx"), scatter_dimension=0, tiled=True),
        lax.psum_scatter(weight_grads[6], ("fsdp", "ctx"), scatter_dimension=0, tiled=True),
        lax.psum_scatter(weight_grads[7], ("fsdp", "ctx"), scatter_dimension=0, tiled=True),
        lax.psum_scatter(weight_grads[8], ("fsdp", "ctx"), scatter_dimension=0, tiled=True),
    )
    owned_grads = (
        lax.all_gather(shares[0].astype(jnp.bfloat16), "ctx", axis=0, tiled=True).astype(
            jnp.float32
        ),
        lax.all_gather(shares[1].astype(jnp.bfloat16), "ctx", axis=0, tiled=True).astype(
            jnp.float32
        ),
        lax.all_gather(shares[2].astype(jnp.bfloat16), "ctx", axis=0, tiled=True).astype(
            jnp.float32
        ),
        lax.all_gather(shares[3].astype(jnp.bfloat16), "ctx", axis=0, tiled=True).astype(
            jnp.float32
        ),
        lax.all_gather(shares[4].astype(jnp.bfloat16), "ctx", axis=0, tiled=True).astype(
            jnp.float32
        ),
        lax.all_gather(shares[5].astype(jnp.bfloat16), "ctx", axis=0, tiled=True).astype(
            jnp.float32
        ),
        lax.all_gather(shares[6].astype(jnp.bfloat16), "ctx", axis=0, tiled=True).astype(
            jnp.float32
        ),
        lax.all_gather(shares[7].astype(jnp.bfloat16), "ctx", axis=0, tiled=True).astype(
            jnp.float32
        ),
        lax.all_gather(shares[8].astype(jnp.bfloat16), "ctx", axis=0, tiled=True).astype(
            jnp.float32
        ),
    )
    return (
        result,
        in_grad,
        owned_grads[0],
        owned_grads[1],
        owned_grads[2],
        owned_grads[3],
        owned_grads[4],
        owned_grads[5],
        owned_grads[6],
        owned_grads[7],
        owned_grads[8],
    )


def solution(mesh):
    placed = (
        P(("fsdp", "ctx"), None),
        P(("fsdp", "ctx"), None),
        P("fsdp"),
        P("fsdp", "tp"),
        P("fsdp", "tp"),
        P("fsdp", "tp"),
        P("fsdp", "tp"),
        P("fsdp"),
        P("fsdp", "tp"),
        P("fsdp", "tp"),
        P("fsdp", "tp"),
        P("fsdp", None),
        P("fsdp", None),
    )
    plane = mesh.shape["fsdp"] * mesh.shape["tp"]
    splits = mesh.shape["tp"] == 2 and KEY_VALUE_HEADS == plane and mesh.shape["ctx"] == 4
    return jax.shard_map(
        split_heads if splits else gathered_weights,
        mesh=mesh,
        in_specs=placed,
        out_specs=(
            P(("fsdp", "ctx"), None),
            P(("fsdp", "ctx"), None),
            P("fsdp"),
            P("fsdp", "tp"),
            P("fsdp", "tp"),
            P("fsdp", "tp"),
            P("fsdp", "tp"),
            P("fsdp"),
            P("fsdp", "tp"),
            P("fsdp", "tp"),
            P("fsdp", "tp"),
        ),
        check_vma=False,
    )
```

```python
import functools
import math

import jax
import jax.numpy as jnp
from jax import lax
from jax.experimental import pallas as pl
from jax.experimental.pallas import tpu as pltpu
from jax.sharding import PartitionSpec as P

QUERY_HEADS = 32
KEY_VALUE_HEADS = 8
HEAD_SIZE = 64


def stream_place(row_ids, order_row, length_row, tok_dev):
    cycle_size = order_row.shape[0]
    half_len = tok_dev // 2
    cycle_rank = row_ids // tok_dev
    within = row_ids % tok_dev
    first_section = jnp.sum(
        jnp.where(
            cycle_rank[:, None] == jnp.arange(cycle_size, dtype=jnp.int32)[None, :],
            order_row[None, :],
            0,
        ),
        axis=1,
        dtype=jnp.int32,
    )
    section = jnp.where(within >= half_len, 2 * cycle_size - 1 - first_section, first_section)
    places = section * half_len + within % half_len
    seq_ends = jnp.cumsum(length_row, dtype=jnp.int32)
    passed = places[:, None] >= seq_ends[None, :]
    segment = jnp.sum(passed.astype(jnp.int32), axis=1, dtype=jnp.int32)
    offset = places - jnp.sum(jnp.where(passed, length_row[None, :], 0), axis=1, dtype=jnp.int32)
    return (places, segment, offset)


def rotary_embedding(values, positions):
    half_len = values.shape[-1] // 2
    frequency = jnp.exp(
        -math.log(500000.0) * jnp.arange(half_len, dtype=jnp.float32) * 2.0 / values.shape[-1]
    )
    angles = positions.astype(jnp.float32)[:, None] * frequency[None, :]
    cosine = jnp.cos(angles)[:, None, :]
    sine = jnp.sin(angles)[:, None, :]
    lower_half = values[..., :half_len]
    upper_half = values[..., half_len:]
    return jnp.concatenate(
        [lower_half * cosine - upper_half * sine, upper_half * cosine + lower_half * sine], axis=-1
    )


def normalize(values, gain_vec):
    return values * lax.rsqrt(jnp.mean(values * values, axis=-1, keepdims=True) + 1e-05) * gain_vec


def swiglu(gate_val, up_val):
    return jax.nn.silu(gate_val) * up_val


def contract_last(left, right):
    return lax.dot_general(
        left, right, (((1,), (1,)), ((), ())), preferred_element_type=jnp.float32
    )


def contract_first(left, right):
    return lax.dot_general(
        left, right, (((0,), (0,)), ((), ())), preferred_element_type=jnp.float32
    )


VMEM_LIMIT = 28 * 1024 * 1024
LARGE_LIMIT = 28 * 1024 * 1024
MIDDLE_LIMIT = 20 * 1024 * 1024
SMALL_LIMIT = 12 * 1024 * 1024
SMALL = pl.CostEstimate(flops=1, bytes_accessed=1, transcendentals=0)
LARGE = pl.CostEstimate(flops=12_000_000_000, bytes_accessed=1, transcendentals=0)


def pairs_by(distance, size):
    return [(i, i ^ distance) for i in range(size)]


def swap(array, axis, distance):
    return lax.ppermute(array, axis, pairs_by(distance, lax.axis_size(axis)))


class Line:
    def __init__(self, axis):
        index = lax.axis_index(axis)
        size = lax.axis_size(axis)
        self.axis = axis
        self.at_end = ((index == 0) | (index == size - 1)).astype(jnp.int32)[None]
        self.entered = self.halfway = self.leaving = None
        self.sums = {}

    def advance(self, got, entering):
        if self.leaving is not None:
            name, sent = self.leaving
            self.sums[name] = (got["ends"], sent)
        moves = []
        halfway = None
        if self.entered is not None:
            name, value = self.entered
            halfway = (name, add_low(value, got["ends"]))
            moves.append(("middle", halfway[1], self.axis, [(1, 2), (2, 1)]))
        leaving = None
        inwards, outwards = [(0, 1), (3, 2)], [(1, 0), (2, 3)]
        if self.halfway is not None:
            name, value = self.halfway
            if entering is None:
                sent, pairs = add_low(value, got["middle"]), outwards
            else:
                sent = either_way(self.at_end, entering[1], value, got["middle"])
                pairs = inwards + outwards
            leaving = (name, sent)
            moves.append(("ends", sent, self.axis, pairs))
        elif entering is not None and halfway is not None:
            sent = jnp.where(self.at_end[0] == 1, entering[1], halfway[1])
            moves.append(("ends", sent, self.axis, inwards + outwards))
        elif entering is not None:
            moves.append(("ends", entering[1], self.axis, inwards))
        self.entered, self.halfway, self.leaving = entering, halfway, leaving
        return moves


class Steps:
    def __init__(self, line):
        self.line = line
        self.got = {}
        self.on_line = []
        self.others = []
        self.token = jnp.zeros((8, 128), jnp.float32)

    def wait(self, flying, arrays):
        count = len(flying)
        held = lax.optimization_barrier(
            (self.token,) + tuple(value for _, value in flying) + tuple(arrays)
        )
        self.token = held[0]
        for (name, _), value in zip(flying, held[1:]):
            self.got[name] = value
        return list(held[1 + count :])

    def start(self, moves):
        return [(name, lax.ppermute(value, axis, pairs)) for name, value, axis, pairs in moves]

    def step(self, moves=(), summed=None, late=None, carry=(), first=()):
        moves, carry, first = list(moves), list(carry), list(first)
        arrays = [move[1] for move in moves] + carry
        fresh = [summed[1]] if summed is not None and summed[1] is not None else []
        together = summed is not None and not fresh and summed[0] not in self.got
        together = together or not self.on_line
        flying = self.on_line + (self.others if together else [])
        held = self.wait(flying, fresh + first + (arrays if together else []))
        held_fresh, held = held[: len(fresh)], held[len(fresh) :]
        held_first, held = held[: len(first)], held[len(first) :]
        entering = summed
        if summed is not None:
            entering = (summed[0], held_fresh[0] if fresh else self.take(summed[0]))
        self.on_line = self.start(self.line.advance(self.got, entering))
        if not together:
            held = self.wait(self.others, arrays)
        moves = [
            (name, value, axis, pairs) for (name, _, axis, pairs), value in zip(moves, held)
        ]
        self.others = self.start(moves + (late() if late is not None else []))
        return held[len(moves) :] + held_first

    def take(self, name):
        return self.got.pop(name)


def in_vmem(kernel, out_shape, *args, scalars=0):
    specs = [pl.BlockSpec(memory_space=pltpu.SMEM)] * scalars
    specs += [pl.BlockSpec(memory_space=pltpu.VMEM)] * (len(args) - scalars)
    return pl.pallas_call(
        kernel,
        out_shape=out_shape,
        in_specs=specs,
        out_specs=[pl.BlockSpec(memory_space=pltpu.VMEM)] * len(out_shape),
        compiler_params=pltpu.CompilerParams(vmem_limit_bytes=SMALL_LIMIT),
        cost_estimate=SMALL,
    )(*args)


def low(*shape):
    return jax.ShapeDtypeStruct(shape, jnp.bfloat16)


def full(*shape):
    return jax.ShapeDtypeStruct(shape, jnp.float32)


def store_seen(ref, value, distance, count):
    width = value.shape[-1] // count
    for block in range(count):
        there = block ^ distance
        ref[: value.shape[0], block * width : (block + 1) * width] = value[
            :, there * width : (there + 1) * width
        ]


def prepare_kernel(count, index_ref, x_ref, own_ref, *sends):
    rows, width = own_ref.shape[0], own_ref.shape[1] // count
    first = pl.multiple_of(index_ref[1] * rows, rows)
    for block in range(count):
        column = pl.multiple_of((index_ref[0] ^ block) * width, width)
        own_ref[:, block * width : (block + 1) * width] = x_ref[
            pl.ds(first, rows), pl.ds(column, width)
        ]
    for k, send in enumerate(sends, 1):
        store_seen(send, own_ref[...], k, count)


def prepare(x, index, count):
    rows, width = x.shape[0] // 2, x.shape[1]
    return in_vmem(
        functools.partial(prepare_kernel, count), [low(rows, width)] * count, index, x, scalars=1
    )


def turns_kernel(offset_ref, cos_ref, sin_ref):
    lane = lax.broadcasted_iota(jnp.int32, cos_ref.shape, 2)
    place = lax.rem(lane, HEAD_SIZE // 2).astype(jnp.float32)
    frequency = jnp.exp(-math.log(500000.0) * place * 2.0 / HEAD_SIZE)
    angle = offset_ref[...] * frequency
    cos_ref[...] = jnp.cos(angle)
    sin_ref[...] = jnp.sin(angle)


def join_kernel(*refs):
    out_ref = refs[-1]
    rows = refs[0].shape[0]
    for i, ref in enumerate(refs[:-1]):
        out_ref[i * rows : (i + 1) * rows, :] = ref[:rows, :]


def join_rows(arrays, rows):
    def kernel(*refs):
        for i, ref in enumerate(refs[:-1]):
            refs[-1][i * rows : (i + 1) * rows, :] = ref[:rows, :]

    return in_vmem(kernel, [low(rows * len(arrays), arrays[0].shape[1])], *arrays)[0]


def join(own, others):
    rows, width = own.shape
    return in_vmem(join_kernel, [low(rows * (1 + len(others)), width)], own, *others)[0]


def fold_kernel(count, first_ref, came_ref, own_ref, *sends):
    rows = own_ref.shape[0]
    for k in range(count):
        here = slice(k * rows, (k + 1) * rows)
        total = first_ref[here, :].astype(jnp.float32) + came_ref[here, :].astype(jnp.float32)
        total = total.astype(jnp.bfloat16)
        if k == 0:
            own_ref[...] = total
        else:
            store_seen(sends[k - 1], total, k, count)


def fold(first, came, count):
    rows, width = first.shape[0] // count, first.shape[1]
    return in_vmem(
        functools.partial(fold_kernel, count), [low(rows, width)] * count, first, came
    )


def total_of(refs):
    total = refs[0][...].astype(jnp.float32)
    for ref in refs[1:]:
        total = total + ref[...].astype(jnp.float32)
    return total


def middle_kernel(count, in_ref, gain_ref, *refs):
    parts, (middle_ref, normed_ref, *sends) = refs[:count], refs[count:]
    middle = in_ref[...].astype(jnp.float32) + total_of(parts)
    middle_ref[...] = middle
    mean = jnp.mean(middle * middle, axis=-1, keepdims=True)
    normed = (middle * lax.rsqrt(mean + 1e-05) * gain_ref[...]).astype(jnp.bfloat16)
    normed_ref[...] = normed
    for k in range(1, count):
        store_seen(sends[k - 1], normed, k, count)


def norm_back(d_normed, x, gain):
    scale = lax.rsqrt(jnp.mean(x * x, axis=-1, keepdims=True) + 1e-05)
    unit = x * scale
    d_unit = d_normed * gain
    d_x = scale * (d_unit - unit * jnp.mean(d_unit * unit, axis=-1, keepdims=True))
    return d_x, jnp.sum(d_normed * unit, axis=0, keepdims=True)


def branch_back_kernel(count, middle_ref, gain_ref, cot_ref, *refs):
    parts, (d_middle_ref, d_gain_ref, branch_ref, *sends) = refs[:count], refs[count:]
    d_x, d_gain_ref[...] = norm_back(total_of(parts), middle_ref[...], gain_ref[...])
    d_middle = cot_ref[...].astype(jnp.float32) + d_x
    d_middle_ref[...] = d_middle
    branch = d_middle.astype(jnp.bfloat16)
    branch_ref[...] = branch
    for k in range(1, count):
        store_seen(sends[k - 1], branch, k, count)


def in_grad_kernel(count, in_ref, gain_ref, d_middle_ref, *refs):
    parts, (grad_ref, d_gain_ref) = refs[:count], refs[count:]
    x = in_ref[...].astype(jnp.float32)
    d_x, d_gain_ref[...] = norm_back(total_of(parts), x, gain_ref[...])
    grad_ref[...] = (d_middle_ref[...] + d_x).astype(jnp.bfloat16)


def spec_of(array, block, index):
    if block == array.shape:
        return pl.BlockSpec(block, index, pipeline_mode=pl.Buffered(1))
    return pl.BlockSpec(block, index)


def gridded(kernel, steps, ins, outs, scalars=(), limit=None, cost=SMALL):
    return pl.pallas_call(
        kernel,
        grid=(steps,),
        in_specs=[pl.BlockSpec(memory_space=pltpu.SMEM)] * len(scalars)
        + [spec_of(array, block, index) for array, block, index in ins],
        out_specs=[pl.BlockSpec(block, index) for _, block, index in outs],
        out_shape=[shape for shape, _, _ in outs],
        compiler_params=pltpu.CompilerParams(vmem_limit_bytes=limit or MIDDLE_LIMIT),
        cost_estimate=cost,
    )(*scalars, *[array for array, _, _ in ins])


def row_blocks(array, rows):
    return (array, (rows, array.shape[1]), lambda i: (i, 0))


def add_low(left, right):
    right = right[:, : left.shape[1]]
    return (left.astype(jnp.float32) + right.astype(jnp.float32)).astype(jnp.bfloat16)


def either_way(at_end, fresh, value, came):
    total = add_low(value, came)
    width = max(fresh.shape[1], value.shape[1])
    if fresh.shape[1] < width:
        fresh = jnp.pad(fresh, ((0, 0), (0, width - fresh.shape[1])))
    if total.shape[1] < width:
        total = jnp.pad(total, ((0, 0), (0, width - total.shape[1])))
    return jnp.where(at_end[0] == 1, fresh, total)


def settled(at_end, came_ref, sent_ref, columns):
    return jnp.where(at_end == 1, came_ref[:, columns], sent_ref[:, columns]).astype(jnp.float32)


def settle_kernel(count, at_end_ref, index_ref, *refs):
    out_ref = refs[-1]
    width = out_ref.shape[1] // count
    for k in range(count):
        column = pl.multiple_of((index_ref[0] ^ k) * width, width)
        out_ref[:, pl.ds(column, width)] = settled(
            at_end_ref[0], refs[2 * k], refs[2 * k + 1], slice(0, width)
        )


def settle(at_end, index, pairs, width, cost=SMALL):
    count = len(pairs)
    arrays = [array for pair in pairs for array in pair]
    depth = arrays[0].shape[0]
    rows = math.gcd(depth, 128)
    ins = [(array, (rows, width), lambda i: (i, 0)) for array in arrays]
    outs = [row_blocks(full(depth, width * count), rows)]
    kernel = functools.partial(settle_kernel, count)
    return gridded(kernel, depth // rows, ins, outs, scalars=(at_end, index), cost=cost)[0]


def settle_attention_kernel(count, q_width, kv_width, at_end_ref, index_ref, *refs):
    q_ref, k_ref, v_ref, o_ref = refs[-4:]
    o_width = o_ref.shape[1] // count
    o_first = q_width + kv_width
    kvs = []
    for k in range(count):
        came_ref, sent_ref = refs[2 * k], refs[2 * k + 1]
        column = pl.multiple_of((index_ref[0] ^ k) * q_width, q_width)
        q_ref[:, pl.ds(column, q_width)] = settled(
            at_end_ref[0], came_ref, sent_ref, slice(0, q_width)
        )
        column = pl.multiple_of((index_ref[0] ^ k) * o_width, o_width)
        o_ref[:, pl.ds(column, o_width)] = settled(
            at_end_ref[0], came_ref, sent_ref, slice(o_first, o_first + o_width)
        )
        kvs.append(settled(at_end_ref[0], came_ref, sent_ref, slice(q_width, o_first)))
    ordered = []
    for place in range(count):
        kv = kvs[0]
        for k in range(1, count):
            kv = jnp.where((index_ref[0] ^ k) == place, kvs[k], kv)
        ordered.append(kv)
    k_ref[...] = jnp.concatenate([kv[:, : kv_width // 2] for kv in ordered], axis=1)
    v_ref[...] = jnp.concatenate([kv[:, kv_width // 2 :] for kv in ordered], axis=1)


def settle_attention(at_end, index, pairs, q_width, kv_width):
    count = len(pairs)
    arrays = [array for pair in pairs for array in pair]
    depth = arrays[0].shape[0]
    width = min(array.shape[1] for array in arrays)
    o_width = width - q_width - kv_width
    rows = math.gcd(depth, 128)
    ins = [(array, (rows, width), lambda i: (i, 0)) for array in arrays]
    widths = (q_width, kv_width // 2, kv_width // 2, o_width)
    outs = [row_blocks(full(depth, each * count), rows) for each in widths]
    kernel = functools.partial(settle_attention_kernel, count, q_width, kv_width)
    return gridded(kernel, depth // rows, ins, outs, scalars=(at_end, index))


def d_qkv_kernel(at_end_ref, here_ref, came_ref, sent_ref, dq_ref, cos_ref, sin_ref, out_ref):
    lanes = 2 * HEAD_SIZE
    half, q_width = dq_ref.shape[1], dq_ref.shape[2]
    cycle = came_ref.shape[1] // lanes // 2
    for core_side in range(2):
        column = pl.multiple_of((core_side * cycle + here_ref[0]) * lanes, lanes)
        d_kv = settled(at_end_ref[0], came_ref, sent_ref, pl.ds(column, lanes))
        cosine, sine = of_keys(cos_ref[core_side], sin_ref[core_side])
        d_kv = turned(d_kv, cosine, -sine).astype(jnp.bfloat16)
        rows = slice(core_side * half, (core_side + 1) * half)
        out_ref[rows, :q_width] = dq_ref[core_side]
        out_ref[rows, q_width:] = d_kv


def rows_back_kernel(count, index_ref, own_ref, other_ref, out_ref):
    rows, width = own_ref.shape[0], own_ref.shape[1] // count
    for ref, core in ((own_ref, index_ref[1]), (other_ref, 1 - index_ref[1])):
        first = pl.multiple_of(core * rows, rows)
        for block in range(count):
            column = pl.multiple_of((index_ref[0] ^ block) * width, width)
            out_ref[pl.ds(first, rows), pl.ds(column, width)] = ref[
                :, block * width : (block + 1) * width
            ]


def result_kernel(middle_ref, *refs):
    refs[-1][...] = (middle_ref[...] + total_of(refs[:-1])).astype(jnp.bfloat16)


def still(array):
    zeros = (0,) * len(array.shape)
    return (array, array.shape, lambda i: zeros)


def dot(left, right):
    return jnp.dot(left, right, preferred_element_type=jnp.float32)


def both(mine_ref, other_ref, weight):
    return jnp.concatenate([dot(mine_ref[...], weight), dot(other_ref[...], weight)], axis=0)


def chosen(here_steps, count, own, fetched, passed):
    here = pl.program_id(0) < here_steps
    weights = []
    for which in (0, 1):
        pieces = [own[which][...]]
        for k in range(count - 1):
            pieces.append(
                jnp.where(here, fetched[2 * k + which][...], passed[2 * k + which][...])
            )
        weights.append(jnp.concatenate(pieces, axis=0))
    return weights


def gate_up_kernel(count, here_steps, *refs):
    x_refs, refs = refs[:2], refs[2:]
    own, fetched, passed = refs[:2], refs[2 : 2 * count], refs[2 * count : 4 * count - 2]
    gate_ref, up_ref, hidden_ref = refs[4 * count - 2 :]
    weights = chosen(here_steps, count, own, fetched, passed)
    lin = both(*x_refs, jnp.concatenate(weights, axis=1))
    gate, up = lin[:, : lin.shape[1] // 2], lin[:, lin.shape[1] // 2 :]
    gate_ref[...] = gate.astype(jnp.bfloat16)
    up_ref[...] = up.astype(jnp.bfloat16)
    hidden_ref[...] = (gate * jax.nn.sigmoid(gate) * up).astype(jnp.bfloat16)


def columns_kernel(count, here_steps, *refs):
    own, fetched, passed = refs[:2], refs[2 : 2 * count], refs[2 * count : 4 * count - 2]
    wg_ref, wu_ref = refs[4 * count - 2 :]
    wg_ref[...], wu_ref[...] = chosen(here_steps, count, own, fetched, passed)


def column_blocks(own_gate, own_up, fetched, passed):
    depth, units = own_gate.shape
    block = math.gcd(units // 2, 256)
    steps, half = units // block, units // block // 2
    ins = [(w, (depth, block), lambda i: (0, i)) for w in (own_gate, own_up)]
    for arrays, step in (
        (fetched, lambda i: jnp.minimum(i, half - 1)),
        (passed, lambda i: jnp.maximum(i - half, 0)),
    ):
        for array in arrays:
            ins.append((array, (depth, block), lambda i, step=step: (0, step(i))))
            ins.append((array, (depth, block), lambda i, step=step: (0, half + step(i))))
    return ins, block, steps, half


def gate_up(x, *weights):
    tokens, units = 2 * x[0].shape[0], weights[0].shape[1]
    ins, block, steps, half = column_blocks(*weights)
    outs = [(low(tokens, units), (tokens, block), lambda i: (0, i))] * 3
    kernel = functools.partial(gate_up_kernel, len(weights[2]) + 1, half)
    return gridded(kernel, steps, [still(x[0]), still(x[1])] + ins, outs, limit=VMEM_LIMIT)


def whole_columns(*weights):
    depth, units = weights[0].shape
    ins, block, steps, half = column_blocks(*weights)
    count = len(weights[2]) + 1
    outs = [(low(count * depth, units), (count * depth, block), lambda i: (0, i))] * 2
    return gridded(functools.partial(columns_kernel, count, half), steps, ins, outs)


def units_back_kernel(count, *refs):
    d_refs, refs = refs[:2], refs[2:]
    pieces, (gate_ref, up_ref, d_gate_ref, d_up_ref) = refs[:count], refs[count:]
    weight = jnp.concatenate([ref[...] for ref in pieces], axis=0)
    d_hidden = both(*d_refs, weight)
    gate, up = gate_ref[...].astype(jnp.float32), up_ref[...].astype(jnp.float32)
    chance = jax.nn.sigmoid(gate)
    d_up_ref[...] = (d_hidden * (gate * chance)).astype(jnp.bfloat16)
    slope = chance + gate * chance * (1.0 - chance)
    d_gate_ref[...] = (d_hidden * up * slope).astype(jnp.bfloat16)


def units_back(d_out, pieces, gate, up):
    tokens, units = gate.shape
    depth = pieces[0].shape[0]
    block = math.gcd(units, 512)

    def by_columns(array, rows):
        return (array, (rows, block), lambda i: (0, i))

    ins = [still(d_out[0]), still(d_out[1])] + [by_columns(piece, depth) for piece in pieces]
    ins += [by_columns(gate, tokens), by_columns(up, tokens)]
    outs = [by_columns(low(tokens, units), tokens)] * 2
    kernel = functools.partial(units_back_kernel, len(pieces))
    return gridded(kernel, units // block, ins, outs, limit=LARGE_LIMIT)


def rows_sum_kernel(terms, *refs):
    first_ref, second_ref = refs[-2:]
    total = 0.0
    for left_ref, right_ref in zip(refs[:terms], refs[terms : 2 * terms]):
        total = total + contract_last(left_ref[...], right_ref[...])
    total = total.astype(jnp.bfloat16)
    half = first_ref.shape[0]
    first_ref[...] = total[:half]
    second_ref[...] = total[half:]


def rows_sum(lefts, rights, cost=SMALL):
    tokens, width = lefts[0].shape[0], rights[0].shape[0]
    block = math.gcd(width, 512)
    ins = [still(left) for left in lefts]
    ins += [(right, (block, right.shape[1]), lambda i: (i, 0)) for right in rights]
    outs = [(low(tokens // 2, width), (tokens // 2, block), lambda i: (0, i))] * 2
    kernel = functools.partial(rows_sum_kernel, len(lefts))
    return gridded(kernel, width // block, ins, outs, cost=cost)


def half_rows_kernel(terms, *refs):
    total = 0.0
    for left_ref, right_ref in zip(refs[:terms], refs[terms : 2 * terms]):
        total = total + contract_last(left_ref[...], right_ref[...])
    refs[-1][...] = total.astype(jnp.bfloat16)


def half_rows(lefts, rights, which):
    half, width = lefts[0].shape[0] // 2, rights[0].shape[0]
    block = math.gcd(width, 512)
    ins = [(left, (half, left.shape[1]), lambda i: (which, 0)) for left in lefts]
    ins += [(right, (block, right.shape[1]), lambda i: (i, 0)) for right in rights]
    outs = [(low(half, width), (half, block), lambda i: (0, i))]
    kernel = functools.partial(half_rows_kernel, len(lefts))
    return gridded(kernel, width // block, ins, outs)[0]


def weight_grad_kernel(count, terms, turn, *refs):
    if turn:
        side, refs = refs[0][0], refs[1:]
    outs = refs[3 * terms :]
    step = pl.program_id(0)
    first = 0
    for term in range(terms):
        mine_ref, other_ref, right_ref = refs[3 * term : 3 * term + 3]
        half = mine_ref.shape[0]
        grad = contract_first(mine_ref[...], right_ref[:half, :])
        grad = grad + contract_first(other_ref[...], right_ref[half:, :])
        grad = grad.astype(jnp.bfloat16)
        columns = grad.shape[1]
        for k in range(count):

            @pl.when(step == k)
            def _(k=k, first=first, grad=grad, columns=columns):
                if turn:
                    part = columns // 2
                    outs[k][:, pl.ds(pl.multiple_of(side * part, part), part)] = grad[:, :part]
                    outs[k][:, pl.ds(pl.multiple_of((1 - side) * part, part), part)] = grad[:, part:]
                else:
                    outs[k][:, first : first + columns] = grad

        first += columns


def weight_grad(terms, count, side=None, packs=None):
    columns = sum(right.shape[1] for _, _, right in terms)
    depth = terms[0][0].shape[1] // count
    packs = range(count) if packs is None else packs
    first, apart = packs[0], packs[1] - packs[0]
    ins = []
    if side is not None:
        ins.append((side, None, None))
    for mine, other, right in terms:
        for left in (mine, other):
            ins.append((left, (left.shape[0], depth), lambda i: (0, first + apart * i)))
        ins.append(still(right))
    specs = [
        pl.BlockSpec(memory_space=pltpu.SMEM) if block is None else pl.BlockSpec(block, index)
        for _, block, index in ins
    ]
    return pl.pallas_call(
        functools.partial(weight_grad_kernel, len(packs), len(terms), side is not None),
        grid=(len(packs),),
        in_specs=specs,
        out_specs=[pl.BlockSpec((depth, columns), lambda i: (0, 0))] * len(packs),
        out_shape=[low(depth, columns)] * len(packs),
        compiler_params=pltpu.CompilerParams(vmem_limit_bytes=MIDDLE_LIMIT),
        cost_estimate=SMALL,
    )(*[array for array, _, _ in ins])


def turned(lin, cosine, sine):
    width = lin.shape[-1]
    quarter = HEAD_SIZE // 2
    lane = lax.broadcasted_iota(jnp.int32, lin.shape, lin.ndim - 1)
    first = lax.rem(lane, HEAD_SIZE) < quarter
    partner = jnp.where(
        first,
        -pltpu.roll(lin, width - quarter, lin.ndim - 1),
        pltpu.roll(lin, quarter, lin.ndim - 1),
    )
    return lin * cosine + partner * sine


def side_by_side(table, width):
    return jnp.concatenate([table] * (width // table.shape[-1]), axis=-1)


def of_keys(cosine, sine):
    keys = lax.broadcasted_iota(jnp.int32, cosine.shape, 1) < HEAD_SIZE
    return jnp.where(keys, cosine, 1.0), jnp.where(keys, sine, 0.0)


def qkv_kernel(count, q_width, kv_width, side_ref, *refs):
    x_refs, (gain_ref, cos_ref, sin_ref), refs = refs[:2], refs[2:5], refs[5:]
    own_ref, fetched, passed_ref, refs = refs[0], refs[1:count], refs[count], refs[count + 1 :]
    normed_refs, (q_ref, kv_ref, wqkv_ref, wo_ref) = refs[:2], refs[2:]
    qkv_width = q_width + kv_width
    depth = own_ref.shape[0]
    half = depth // 2

    @pl.when(pl.program_id(0) == 0)
    def _():
        wqkv_ref[:depth, :] = own_ref[:, :qkv_width]
        wo_ref[:depth, :] = own_ref[:, qkv_width:]
        for k in range(1, count):
            for which, piece in (
                (side_ref[0], fetched[k - 1][:half, :]),
                (1 - side_ref[0], passed_ref[(k - 1) * half : k * half, :]),
            ):
                first = pl.multiple_of(k * depth + which * half, half)
                wqkv_ref[pl.ds(first, half), :] = piece[:, :qkv_width]
                wo_ref[pl.ds(first, half), :] = piece[:, qkv_width:]

    for i in range(2):
        x = x_refs[i][...].astype(jnp.float32)
        mean = jnp.mean(x * x, axis=-1, keepdims=True)
        normed = (x * lax.rsqrt(mean + 1e-05) * gain_ref[...]).astype(jnp.bfloat16)
        normed_refs[i][...] = normed
        lin = dot(normed, wqkv_ref[...])
        cosine, sine = cos_ref[i], sin_ref[i]
        q = turned(lin[:, :q_width], side_by_side(cosine, q_width), side_by_side(sine, q_width))
        q_ref[i] = q.astype(jnp.bfloat16)
        kv = turned(lin[:, q_width:], *of_keys(cosine, sine))
        kv_ref[i] = kv.astype(jnp.bfloat16)


def project_qkv(side, x, gain, cosine, sine, own, fetched, passed, q_width, kv_width):
    half_rows, width = x[0].shape
    qkv_width = q_width + kv_width
    block = math.gcd(half_rows, 128)

    def rows_of(array, columns):
        return (array, (block, columns), lambda i: (i, 0))

    def of_both(array, columns):
        return (array, (2, block, columns), lambda i: (0, i, 0))

    lanes = cosine.shape[-1]
    ins = [rows_of(x[0], width), rows_of(x[1], width), still(gain)]
    ins += [of_both(cosine, lanes), of_both(sine, lanes)]
    ins += [still(array) for array in (own, *fetched, passed)]
    o_width = own.shape[1] - qkv_width
    outs = [rows_of(low(half_rows, width), width)] * 2
    outs += [of_both(low(2, half_rows, q_width), q_width), of_both(low(2, half_rows, kv_width), kv_width)]
    outs += [still(low(width, qkv_width)), still(low(width, o_width))]
    kernel = functools.partial(qkv_kernel, len(fetched) + 1, q_width, kv_width)
    return gridded(kernel, half_rows // block, ins, outs, scalars=(side,))


def shares(q, k, visible):
    scores = jnp.where(visible, contract_last(q, k), -1e30)
    weights = jnp.exp(scores - jnp.max(scores, axis=-1, keepdims=True))
    return weights, 1.0 / jnp.sum(weights, axis=-1, keepdims=True)


def load_attention(q_ref, place_ref, start_ref, key_place_ref, kv_refs):
    q = q_ref[...]
    q = q.reshape(q.shape[0] * q.shape[1], q.shape[2])
    kv = jnp.concatenate([ref[...].reshape(q.shape[0], 2 * HEAD_SIZE) for ref in kv_refs], axis=0)
    q = q * jnp.bfloat16(1.0 / math.sqrt(HEAD_SIZE))
    key_place = key_place_ref[0]
    visible = (key_place <= place_ref[0]) & (key_place >= start_ref[0])
    return q, kv[:, :HEAD_SIZE], kv[:, HEAD_SIZE:], visible


def attend_kernel(groups, q_ref, place_ref, start_ref, key_place_ref, wo_ref, *refs):
    kv_refs, (out_ref, first_ref, second_ref) = refs[:-3], refs[-3:]
    q, k, v, visible = load_attention(q_ref, place_ref, start_ref, key_place_ref, kv_refs)
    mixed = []
    for g in range(groups):
        weights, parts = shares(q[:, g * HEAD_SIZE : (g + 1) * HEAD_SIZE], k, visible)
        mixed.append(dot(weights.astype(jnp.bfloat16), v) * parts)
    out = jnp.concatenate(mixed, axis=1).astype(jnp.bfloat16)
    out_ref[...] = out.reshape(out_ref.shape)
    branch = contract_last(out, wo_ref[...]).astype(jnp.bfloat16)
    half = first_ref.shape[0]
    first_ref[...] = branch[:half]
    second_ref[...] = branch[half:]


def attend_back_kernel(
    groups,
    here_ref,
    q_ref,
    mine_ref,
    other_ref,
    cos_ref,
    sin_ref,
    place_ref,
    start_ref,
    key_place_ref,
    wo_ref,
    *refs,
):
    kv_refs, (dq_ref, dkv_ref) = refs[:-2], refs[-2:]
    q, k, v, visible = load_attention(q_ref, place_ref, start_ref, key_place_ref, kv_refs)
    d_out = both(mine_ref, other_ref, wo_ref[...]).astype(jnp.bfloat16)
    scale = 1.0 / math.sqrt(HEAD_SIZE)
    d_q, d_k, d_v = [], 0.0, 0.0
    for g in range(groups):
        q_head = q[:, g * HEAD_SIZE : (g + 1) * HEAD_SIZE]
        d_head = d_out[:, g * HEAD_SIZE : (g + 1) * HEAD_SIZE]
        weights, parts = shares(q_head, k, visible)
        probs = weights * parts
        d_probs = contract_last(d_head, v)
        row_delta = jnp.sum(probs * d_probs, axis=-1, keepdims=True)
        d_scores = (probs * (d_probs - row_delta)).astype(jnp.bfloat16)
        d_q.append(dot(d_scores, k) * scale)
        d_k = d_k + contract_first(d_scores, q_head)
        d_v = d_v + contract_first(probs.astype(jnp.bfloat16), d_head)
    d_q = jnp.concatenate(d_q, axis=1)
    cosine = cos_ref[...].reshape(q.shape[0], -1)
    sine = sin_ref[...].reshape(q.shape[0], -1)
    d_q = turned(d_q, side_by_side(cosine, q.shape[1]), -side_by_side(sine, q.shape[1]))
    dq_ref[...] = d_q.astype(jnp.bfloat16).reshape(dq_ref.shape)
    d_kv = jnp.concatenate([d_k, d_v], axis=1).astype(jnp.bfloat16)
    half, lanes, cycle = dkv_ref.shape[0], 2 * HEAD_SIZE, len(kv_refs)
    for j in range(cycle):
        for core_side in range(2):
            first = (2 * j + core_side) * half
            column = pl.multiple_of((core_side * cycle + (here_ref[0] ^ j)) * lanes, lanes)
            dkv_ref[:, pl.ds(column, lanes)] = d_kv[first : first + half]


def of_pack(array, half):
    return (array, (2, half, array.shape[-1]), lambda p: (0, p, 0))


def place_blocks(places):
    return [(array, (1,) + array.shape[1:], lambda p: (p, 0, 0)) for array in places]


def attend(q, places, wo, kvs, packs, groups):
    half = q.shape[1] // packs
    width = wo.shape[0]
    ins = [of_pack(q, half)] + place_blocks(places) + [still(wo)] + [of_pack(kv, half) for kv in kvs]
    outs = [of_pack(low(*q.shape), half)]
    outs += [(low(q.shape[1], width), (half, width), lambda p: (p, 0))] * 2
    return gridded(functools.partial(attend_kernel, groups), packs, ins, outs)


def attend_back(here, q, d_branch, cosine, sine, places, wo, kvs, packs, groups):
    half = q.shape[1] // packs
    cycle = len(kvs)
    ins = [of_pack(q, half)]
    ins += [(array, (half, array.shape[1]), lambda p: (p, 0)) for array in d_branch]
    ins += [of_pack(cosine, half), of_pack(sine, half)] + place_blocks(places) + [still(wo)]
    ins += [of_pack(kv, half) for kv in kvs]
    lanes = 2 * HEAD_SIZE
    outs = [of_pack(low(*q.shape), half)]
    outs.append((low(q.shape[1], 2 * cycle * lanes), (half, 2 * cycle * lanes), lambda p: (p, 0)))
    kernel = functools.partial(attend_back_kernel, groups)
    return gridded(kernel, packs, ins, outs, scalars=(here,))


def split_heads(
    hidden_in,
    out_cotangent,
    norm1_gain,
    q_weight,
    key_projection_weight,
    value_projection_weight,
    o_weight,
    norm2_gain,
    gate_weight,
    up_weight,
    down_weight,
    seq_lengths,
    span_order,
):
    packs = lax.axis_size("fsdp")
    cycle = lax.axis_size("ctx")
    pack = lax.axis_index("fsdp")
    core = lax.axis_index("tp")
    here = lax.axis_index("ctx")
    rows = hidden_in.shape[0]
    half = rows // 2
    tokens = packs * rows
    depth = q_weight.shape[0]
    width = depth * packs
    q_width = q_weight.shape[1] // packs
    k_width = key_projection_weight.shape[1] // packs
    ff_width = gate_weight.shape[1] // packs
    ff_half = ff_width // 2
    groups = q_width // k_width
    far = range(1, packs)
    steps = Steps(Line("ctx"))
    kept = {}


    def columns(weight, k, count, first=0, of=None):
        return lax.dynamic_slice_in_dim(weight, (pack ^ k) * (of or count) + first, count, 1)

    def to_pack(name, k, array):
        return ((name, k), array, "fsdp", pairs_by(k, packs))

    def send_all(name, arrays):
        return [to_pack(name, k, array) for k, array in zip(far, arrays)]

    def arrived(name):
        return [steps.take((name, k)) for k in far]

    def to_core(name, array):
        return [(name, array, "tp", pairs_by(1, 2))]

    def to_rows(name, first):
        kept[name], *others = fold(first, steps.take(name), packs)
        return send_all(name, others)

    def joined(name, own, others):
        kept[name] = join(own, others)
        return to_core(name, kept[name])

    def unwaited(name):
        return dict(steps.others)[name]

    def both_of(name):
        return kept[name], steps.take(name)

    index = jnp.stack([pack, core]).astype(jnp.int32)
    here_arg = here.astype(jnp.int32)[None]
    side_arg = here_arg & 1
    at_end = steps.line.at_end

    own_in, *in_moves = prepare(hidden_in, index, packs)
    own_cot, *cot_moves = prepare(out_cotangent, index, packs)

    side = here & 1
    weights = (q_weight, key_projection_weight, value_projection_weight, o_weight)
    widths = (q_width, k_width, k_width, q_width)

    def attention_piece(k, first, count):
        return jnp.concatenate(
            [
                lax.dynamic_slice(weight, (first, (pack ^ k) * each), (count, each))
                for weight, each in zip(weights, widths)
            ],
            axis=1,
        )

    meta = jnp.concatenate([span_order[0], seq_lengths[0]])
    order_len, meta_len = span_order.shape[1], meta.shape[0]
    metas = jnp.concatenate([(meta // 32).astype(jnp.bfloat16), (meta % 32).astype(jnp.bfloat16)])
    info = jnp.stack(
        [
            jnp.pad(jnp.concatenate([norm1_gain, metas]), (0, sum(widths) - depth - 2 * meta_len)),
            jnp.pad(norm2_gain, (0, sum(widths) - depth)),
        ]
    )
    info_rows = jnp.pad(info, ((0, 14), (0, 0)))
    row_half = depth // 2
    steps.step(
        [
            to_pack(
                "attention",
                k,
                jnp.concatenate([attention_piece(k, side * row_half, row_half), info_rows], axis=0),
            )
            for k in far
        ]
    )
    pieces = []

    def pass_rows():
        pieces.extend(arrived("attention"))
        rows_on = join_rows(pieces, row_half)
        return [("attention_rows", rows_on, "ctx", pairs_by(1, cycle))]

    steps.step(send_all("in", in_moves), late=pass_rows)
    infos = jnp.stack([info] + [piece[row_half : row_half + 2] for piece in pieces])
    all_gains = infos[:, :, :depth].astype(jnp.float32)
    gain_one = all_gains[:, 0].reshape(1, -1)
    gain_two = all_gains[:, 1].reshape(1, -1)
    metas = infos[:, 0, depth : depth + 2 * meta_len].astype(jnp.int32)
    metas = metas[:, :meta_len] * 32 + metas[:, meta_len:]
    orders, lengths = metas[:, :order_len], metas[:, order_len:]

    others = jnp.stack([here ^ j for j in range(cycle)])
    first = jnp.sum(
        jnp.where(
            others[None, :, None] == jnp.arange(order_len, dtype=jnp.int32)[None, None, :],
            orders[:, None, :],
            0,
        ),
        axis=2,
    )
    halves = jnp.stack([core, core ^ 1])[None, None, :]
    section = jnp.where(halves == 0, first[:, :, None], 2 * cycle - 1 - first[:, :, None])
    places = section[..., None] * half + jnp.arange(half, dtype=jnp.int32)
    places = places.reshape(packs, cycle * rows)
    starts = jnp.zeros_like(places)
    end = jnp.zeros((packs, 1), jnp.int32)
    for j in range(lengths.shape[1]):
        end = end + lengths[:, j : j + 1]
        starts = jnp.where(places >= end, end, starts)
    place_args = (places[:, :rows, None], starts[:, :rows, None], places[:, None, :])
    offsets = (places - starts)[:, :rows].reshape(packs, 2, half).transpose(1, 0, 2)
    cosine, sine = in_vmem(
        turns_kernel,
        [full(2, tokens // 2, 2 * HEAD_SIZE)] * 2,
        offsets.astype(jnp.float32).reshape(2, tokens // 2, 1),
    )


    def two_halves(weight, k):
        return jnp.concatenate(
            [
                columns(weight, k, ff_half, side * ff_half, ff_width),
                columns(weight, k, ff_half, (1 - side) * ff_half, ff_width),
            ],
            axis=1,
        )

    def fetch(ks):
        return [
            to_pack(
                "gate_up",
                k,
                jnp.concatenate(
                    [
                        columns(weight, k, ff_half, side * ff_half, ff_width)
                        for weight in (gate_weight, up_weight)
                    ],
                    axis=1,
                ),
            )
            for k in ks
        ]

    def to_neighbour(k):
        return [(("neighbour", k), fetched[k], "ctx", pairs_by(1, cycle))]

    fetched = {}
    own_piece = attention_piece(0, 0, depth)
    cosine, sine, own_piece, *place_args = steps.step(
        fetch([1, 2]), carry=(cosine, sine, own_piece, *place_args)
    )
    all_in = join(own_in, arrived("in"))
    all_in = (all_in, swap(all_in, "tp", 1))
    normed_mine, normed_other, q_rot, kv_own, wqkv, wo = project_qkv(
        side_arg,
        all_in,
        gain_one,
        cosine,
        sine,
        own_piece,
        pieces,
        steps.take("attention_rows"),
        q_width,
        2 * k_width,
    )
    normed_one = (normed_mine, normed_other)
    steps.step(
        [(("kv", j), kv_own, "ctx", pairs_by(j, cycle)) for j in range(1, cycle)] + fetch([3])
    )
    fetched[1], fetched[2] = steps.take(("gate_up", 1)), steps.take(("gate_up", 2))
    steps.step(send_all("cot", cot_moves) + to_neighbour(1))
    fetched[3] = steps.take(("gate_up", 3))
    kvs = [kv_own] + [steps.take(("kv", j)) for j in range(1, cycle)]
    attn, first, second = attend(q_rot, place_args, wo, kvs, packs, groups)
    attn_low = attn.reshape(tokens, q_width)
    steps.step(to_core("branch", second))
    steps.step(to_neighbour(2), late=lambda: to_rows("branch", first))
    kept["cot"] = join(own_cot, arrived("cot"))

    def middle_moves():
        kept["middle"], kept["normed"], *sends = in_vmem(
            functools.partial(middle_kernel, packs),
            [full(half, width)] + [low(half, width)] * packs,
            own_in,
            gain_two,
            kept["branch"],
            *arrived("branch"),
        )
        return send_all("two", sends)

    steps.step(to_neighbour(3) + to_core("cot", kept["cot"]), late=middle_moves)

    def wd_moves(ks):
        return [to_pack("down", k, two_halves(down_weight, k)) for k in ks]

    own_columns = [two_halves(weight, 0) for weight in (gate_weight, up_weight, down_weight)]
    own_gate, own_up, own_down = steps.step(
        wd_moves([1, 2]),
        late=lambda: joined("two", kept["normed"], arrived("two")),
        carry=own_columns,
    )
    all_cot = both_of("cot")
    neighbours = [steps.take(("neighbour", k)) for k in far]
    normed_two = (kept["two"], unwaited("two"))

    unit_weights = (own_gate, own_up, [fetched[k] for k in far], neighbours)
    gate_val, up_val, hidden = gate_up(normed_two, *unit_weights)
    d_wd = weight_grad([(*all_cot, hidden)], packs, side_arg)

    def back(name, grad, ks):
        return [to_pack(name, k, grad[k]) for k in ks]

    def entry(name, k, grad=None):
        return ((name, k), grad[0] if k == 0 else None)

    steps.step(back("wd", d_wd, [1, 2]), summed=entry("wd", 0, d_wd))
    wg, wu = whole_columns(*unit_weights)
    wg, wu = steps.step(wd_moves([3]), summed=entry("wd", 1), carry=(wg, wu))
    steps.step(back("wd", d_wd, [3]), summed=entry("wd", 2))
    wd_pieces = [own_down] + arrived("down")
    d_gate, d_up = units_back(all_cot, wd_pieces, gate_val, up_val)
    second = half_rows([d_gate, d_up], [wg, wu], 1)
    d_wg = dict(zip((1, 2), weight_grad([(*normed_two, d_gate)], packs, side_arg, (1, 2))))
    steps.step(to_core("d_two", second) + back("wg", d_wg, [1, 2]), summed=entry("wd", 3))
    first = half_rows([d_gate, d_up], [wg, wu], 0)
    d_wg.update(zip((0, 3), weight_grad([(*normed_two, d_gate)], packs, side_arg, (0, 3))))
    d_wu = weight_grad([(*normed_two, d_up)], packs, side_arg)
    steps.step(
        summed=entry("wg", 0, d_wg), late=functools.partial(to_rows, "d_two", first)
    )

    def branch_back():
        kept["d_middle"], kept["d_gain_two"], kept["d_branch"], *sends = in_vmem(
            functools.partial(branch_back_kernel, packs),
            [full(half, width), full(1, width)] + [low(half, width)] * packs,
            kept["middle"],
            gain_two,
            own_cot,
            kept["d_two"],
            *arrived("d_two"),
        )
        return send_all("d_branch", sends)

    steps.step(summed=entry("wu", 0, d_wu), late=branch_back)
    ff_first, ff_second = rows_sum([hidden], [join(wd_pieces[0], wd_pieces[1:])], LARGE)
    ff_first, ff_second = steps.step(
        back("wg", d_wg, [3]),
        summed=entry("wg", 1),
        late=lambda: joined("all_branch", kept["d_branch"], arrived("d_branch")),
        first=(ff_first, ff_second),
    )
    sums = steps.line.sums

    def settle_all(name, cost=SMALL):
        return settle(at_end, index, [sums[name, k] for k in range(packs)], ff_width, cost)

    d_branch = (kept["all_branch"], unwaited("all_branch"))
    d_q, d_kv = attend_back(
        here_arg, q_rot, d_branch, cosine, sine, place_args, wo, kvs, packs, groups
    )
    down_grad = settle_all("wd", LARGE)
    d_q, d_kv, down_grad = steps.step(
        back("wu", d_wu, [1, 2]), summed=entry("wg", 2), carry=(d_q, d_kv), first=(down_grad,)
    )
    steps.step(back("wu", d_wu, [3]) + to_core("ff", ff_second), summed=("d_kv", d_kv))
    steps.step(summed=entry("wg", 3), late=functools.partial(to_rows, "ff", ff_first))
    steps.step(summed=entry("wu", 1))
    steps.step(summed=entry("wu", 2))
    result = in_vmem(
        result_kernel, [low(half, width)], kept["middle"], kept["ff"], *arrived("ff")
    )[0]
    d_qkv = in_vmem(
        d_qkv_kernel,
        [low(tokens, q_width + 2 * k_width)],
        at_end,
        here_arg,
        *sums["d_kv"],
        d_q,
        cosine,
        sine,
        scalars=2,
    )[0]
    d_wqkvo = weight_grad([(*normed_one, d_qkv), (*d_branch, attn_low)], packs)
    first, second = rows_sum([d_qkv], [wqkv])
    steps.step(
        back("wqkvo", d_wqkvo, [1, 2]) + to_core("d_one", second), summed=entry("wu", 3)
    )
    steps.step(
        summed=entry("wqkvo", 0, d_wqkvo), late=functools.partial(to_rows, "d_one", first)
    )

    def both_rows(own, other):
        return in_vmem(
            functools.partial(rows_back_kernel, packs),
            [low(rows, width)],
            index,
            own,
            other,
            scalars=1,
        )[0]

    gate_grad = settle_all("wg", LARGE)
    def gains_to_core():
        kept["in_grad"], d_gain_one = in_vmem(
            functools.partial(in_grad_kernel, packs),
            [low(half, width), full(1, width)],
            own_in,
            gain_one,
            kept["d_middle"],
            kept["d_one"],
            *arrived("d_one"),
        )
        kept["gains"] = jnp.concatenate([d_gain_one, kept["d_gain_two"]], axis=0)
        return to_core("gains", kept["gains"]) + to_core("in_grad", kept["in_grad"])

    def gains_to_packs():
        kept["gains"] = kept["gains"] + steps.take("gains")
        return [to_pack("gains", k, kept["gains"][:, k * depth : (k + 1) * depth]) for k in far]

    def gains_along():
        kept["gains"] = kept["gains"][:, :depth]
        for k in far:
            kept["gains"] = kept["gains"] + steps.take(("gains", k))
        return [(("gains", j), kept["gains"], "ctx", pairs_by(j, cycle)) for j in range(1, cycle)]

    steps.step(back("wqkvo", d_wqkvo, [3]), summed=entry("wqkvo", 1), late=gains_to_core)
    (gate_grad,) = steps.step(
        summed=entry("wqkvo", 2), late=gains_to_packs, first=(gate_grad,)
    )
    up_grad = settle_all("wu")
    in_grad = both_rows(kept["in_grad"], steps.take("in_grad"))
    in_grad, up_grad = steps.step(
        to_core("result", result), summed=entry("wqkvo", 3), carry=(in_grad, up_grad)
    )
    steps.step(late=gains_along)
    out_hidden = both_rows(result, steps.take("result"))
    (out_hidden,) = steps.step(carry=(out_hidden,))
    steps.step()
    shares_of_gains = jnp.stack(
        [kept["gains"]] + [steps.take(("gains", j)) for j in range(1, cycle)]
    )
    gains = steps.token[0, 0]
    for place in range(cycle):
        gains = gains + lax.dynamic_index_in_dim(shares_of_gains, here ^ place, 0, keepdims=False)
    q_grad, k_grad, v_grad, o_grad = settle_attention(
        at_end, index, [sums["wqkvo", k] for k in range(packs)], q_width, 2 * k_width
    )
    return (
        out_hidden,
        in_grad,
        gains[0],
        q_grad,
        k_grad,
        v_grad,
        o_grad,
        gains[1],
        gate_grad,
        up_grad,
        down_grad,
    )


def gathered_weights(
    hidden_in,
    out_cotangent,
    norm1_gain,
    q_weight,
    key_projection_weight,
    value_projection_weight,
    o_weight,
    norm2_gain,
    gate_weight,
    up_weight,
    down_weight,
    seq_lengths,
    span_order,
):
    rows_here = hidden_in.shape[0]
    order_row = span_order[0]
    length_row = seq_lengths[0]
    kv_heads = key_projection_weight.shape[1] // HEAD_SIZE
    query_groups = QUERY_HEADS // KEY_VALUE_HEADS
    score_scale = 1.0 / math.sqrt(HEAD_SIZE)
    whole_rows = rows_here * lax.axis_size("ctx")
    local_rows = lax.axis_index("ctx") * rows_here + jnp.arange(rows_here, dtype=jnp.int32)
    q_place, q_segment, q_offset = stream_place(local_rows, order_row, length_row, rows_here)
    inputs = hidden_in.astype(jnp.float32)
    gain_one, wq_full, wk_full, wv_full, wo_full = (
        lax.all_gather(norm1_gain, "fsdp", axis=0, tiled=True),
        lax.all_gather(q_weight, "fsdp", axis=0, tiled=True),
        lax.all_gather(key_projection_weight, "fsdp", axis=0, tiled=True),
        lax.all_gather(value_projection_weight, "fsdp", axis=0, tiled=True),
        lax.all_gather(o_weight, "fsdp", axis=0, tiled=True),
    )
    gain_one = gain_one.astype(jnp.float32)
    first_normalized = normalize(inputs, gain_one)
    normed_low = first_normalized.astype(jnp.bfloat16)
    q_linear = jnp.dot(normed_low, wq_full, preferred_element_type=jnp.float32).reshape(
        rows_here, kv_heads * query_groups, HEAD_SIZE
    )
    k_linear = jnp.dot(normed_low, wk_full, preferred_element_type=jnp.float32).reshape(
        rows_here, kv_heads, HEAD_SIZE
    )
    q_rotated = (
        rotary_embedding(q_linear, q_offset)
        .astype(jnp.bfloat16)
        .reshape(rows_here, kv_heads, query_groups, HEAD_SIZE)
    )
    k_rotated = (
        rotary_embedding(k_linear, q_offset)
        .astype(jnp.bfloat16)
        .reshape(rows_here, kv_heads * HEAD_SIZE)
    )
    v_low = jnp.dot(normed_low, wv_full, preferred_element_type=jnp.float32).astype(jnp.bfloat16)

    def key_blocks(shard_rows):
        row_count = shard_rows.shape[0]
        key_total_width = math.gcd(row_count, 512)
        number = row_count // key_total_width
        k_place, k_segment, _ = stream_place(
            jnp.arange(row_count, dtype=jnp.int32), order_row, length_row, rows_here
        )
        return (
            key_total_width,
            number,
            k_place.reshape(number, key_total_width),
            k_segment.reshape(number, key_total_width),
        )

    def scores_of(key_block, place_block, segment_block):
        scores = (
            jnp.einsum("qkgd,skd->kgqs", q_rotated, key_block, preferred_element_type=jnp.float32)
            * score_scale
        )
        visible = (
            (q_place[:, None] >= place_block[None, :])
            & (q_segment[:, None] == segment_block[None, :])
        )[None, None]
        return (jnp.where(visible, scores, -1e30), visible)

    start_state = (
        jnp.full((kv_heads, query_groups, rows_here), -1e30, jnp.float32),
        jnp.zeros((kv_heads, query_groups, rows_here), jnp.float32),
        jnp.zeros((kv_heads, query_groups, rows_here, HEAD_SIZE), jnp.float32),
    )
    folded = start_state
    key_row_block = lax.all_gather(k_rotated, "ctx", axis=0, tiled=True)
    value_row_block = lax.all_gather(v_low, "ctx", axis=0, tiled=True)
    key_total_width, number, k_place, k_segment = key_blocks(key_row_block)

    def one_step(carried, pieces):
        running_max, totals, accumulated = carried
        key_block, value_block, place_block, segment_block = pieces
        scores, visible = scores_of(key_block, place_block, segment_block)
        new_max = jnp.maximum(running_max, jnp.max(scores, axis=-1))
        weights = jnp.where(visible, jnp.exp(scores - new_max[..., None]), 0.0)
        factor = jnp.exp(running_max - new_max)
        totals = totals * factor + jnp.sum(weights, axis=-1)
        accumulated = accumulated * factor[..., None] + jnp.einsum(
            "kgqs,skd->kgqd",
            weights.astype(jnp.bfloat16),
            value_block,
            preferred_element_type=jnp.float32,
        )
        return ((new_max, totals, accumulated), None)

    pieces = (
        key_row_block.reshape(number, key_total_width, kv_heads, HEAD_SIZE),
        value_row_block.reshape(number, key_total_width, kv_heads, HEAD_SIZE),
        k_place,
        k_segment,
    )
    folded, _ = lax.scan(one_step, folded, pieces)
    running_max, totals, accumulated = folded
    mixed_out = jnp.transpose(accumulated / totals[..., None], (2, 0, 1, 3))
    log_sum = running_max + jnp.log(totals)
    attn_low = mixed_out.reshape(rows_here, kv_heads * query_groups * HEAD_SIZE).astype(
        jnp.bfloat16
    )
    branch = lax.psum(contract_last(attn_low, wo_full).astype(jnp.bfloat16), "tp").astype(
        jnp.float32
    )
    middle = inputs + branch
    gain_two, wg_full, wu_full, wd_full = (
        lax.all_gather(norm2_gain, "fsdp", axis=0, tiled=True),
        lax.all_gather(gate_weight, "fsdp", axis=0, tiled=True),
        lax.all_gather(up_weight, "fsdp", axis=0, tiled=True),
        lax.all_gather(down_weight, "fsdp", axis=0, tiled=True),
    )
    gain_two = gain_two.astype(jnp.float32)
    normed_two = normalize(middle, gain_two)
    normed_two_low = normed_two.astype(jnp.bfloat16)
    gate_val = jnp.dot(normed_two_low, wg_full, preferred_element_type=jnp.float32)
    up_val = jnp.dot(normed_two_low, wu_full, preferred_element_type=jnp.float32)
    hidden = swiglu(gate_val, up_val).astype(jnp.bfloat16)
    ffn_out = lax.psum(contract_last(hidden, wd_full).astype(jnp.bfloat16), "tp").astype(
        jnp.float32
    )
    result = (middle + ffn_out).astype(jnp.bfloat16)
    grad_out = out_cotangent.astype(jnp.float32)
    d_wd = contract_first(out_cotangent, hidden)
    d_hidden = jnp.dot(out_cotangent, wd_full, preferred_element_type=jnp.float32)
    _, swiglu_back = jax.vjp(swiglu, gate_val, up_val)
    d_gate, d_up = swiglu_back(d_hidden)
    d_gate_low = d_gate.astype(jnp.bfloat16)
    d_up_low = d_up.astype(jnp.bfloat16)
    d_wg = contract_first(normed_two_low, d_gate_low)
    d_wu = contract_first(normed_two_low, d_up_low)
    d_normed_two = lax.psum(
        (contract_last(d_gate_low, wg_full) + contract_last(d_up_low, wu_full)).astype(
            jnp.bfloat16
        ),
        "tp",
    ).astype(jnp.float32)
    _, norm_two_back = jax.vjp(normalize, middle, gain_two)
    d_middle_norm, d_gain_two = norm_two_back(d_normed_two)
    d_middle = grad_out + d_middle_norm
    d_branch_low = d_middle.astype(jnp.bfloat16)
    d_wo = contract_first(d_branch_low, attn_low)
    d_attn = jnp.dot(d_branch_low, wo_full, preferred_element_type=jnp.float32).astype(jnp.bfloat16)
    d_attn_heads = d_attn.reshape(rows_here, kv_heads, query_groups, HEAD_SIZE)
    row_delta = jnp.einsum("qkgd,qkgd->kgq", d_attn_heads.astype(jnp.float32), mixed_out)
    back_state = (
        jnp.zeros((rows_here, kv_heads, query_groups, HEAD_SIZE), jnp.float32),
        jnp.zeros((whole_rows, kv_heads, HEAD_SIZE), jnp.float32),
        jnp.zeros((whole_rows, kv_heads, HEAD_SIZE), jnp.float32),
    )
    folded = back_state
    key_row_block = lax.all_gather(k_rotated, "ctx", axis=0, tiled=True)
    value_row_block = lax.all_gather(v_low, "ctx", axis=0, tiled=True)
    key_total_width, number, k_place, k_segment = key_blocks(key_row_block)

    def one_step(carried, pieces):
        d_query, d_keys, d_values = carried
        key_block, value_block, place_block, segment_block, step_index = pieces
        scores, visible = scores_of(key_block, place_block, segment_block)
        prob_rows = jnp.where(visible, jnp.exp(scores - log_sum[..., None]), 0.0)
        d_values_block = jnp.einsum(
            "kgqs,qkgd->skd",
            prob_rows.astype(jnp.bfloat16),
            d_attn_heads,
            preferred_element_type=jnp.float32,
        )
        d_probs = jnp.einsum(
            "qkgd,skd->kgqs", d_attn_heads, value_block, preferred_element_type=jnp.float32
        )
        d_scores = (prob_rows * (d_probs - row_delta[..., None])).astype(jnp.bfloat16)
        d_query = (
            d_query
            + jnp.einsum("kgqs,skd->qkgd", d_scores, key_block, preferred_element_type=jnp.float32)
            * score_scale
        )
        d_keys_block = (
            jnp.einsum("kgqs,qkgd->skd", d_scores, q_rotated, preferred_element_type=jnp.float32)
            * score_scale
        )
        row_first = step_index * key_total_width
        d_keys = lax.dynamic_update_slice_in_dim(
            d_keys,
            lax.dynamic_slice_in_dim(d_keys, row_first, key_total_width, 0) + d_keys_block,
            row_first,
            0,
        )
        d_values = lax.dynamic_update_slice_in_dim(
            d_values,
            lax.dynamic_slice_in_dim(d_values, row_first, key_total_width, 0) + d_values_block,
            row_first,
            0,
        )
        return ((d_query, d_keys, d_values), None)

    pieces = (
        key_row_block.reshape(number, key_total_width, kv_heads, HEAD_SIZE),
        value_row_block.reshape(number, key_total_width, kv_heads, HEAD_SIZE),
        k_place,
        k_segment,
        jnp.arange(number, dtype=jnp.int32),
    )
    folded, _ = lax.scan(one_step, folded, pieces)
    d_query, d_keys_all, d_values_all = folded
    d_key_own, d_value_own = (
        lax.psum_scatter(
            d_keys_all.astype(jnp.bfloat16), "ctx", scatter_dimension=0, tiled=True
        ).astype(jnp.float32),
        lax.psum_scatter(
            d_values_all.astype(jnp.bfloat16), "ctx", scatter_dimension=0, tiled=True
        ).astype(jnp.float32),
    )
    _, rope_q_back = jax.vjp(lambda rotated_in: rotary_embedding(rotated_in, q_offset), q_linear)
    _, rope_k_back = jax.vjp(lambda rotated_in: rotary_embedding(rotated_in, q_offset), k_linear)
    (d_q_linear,) = rope_q_back(d_query.reshape(rows_here, kv_heads * query_groups, HEAD_SIZE))
    (d_k_linear,) = rope_k_back(d_key_own)
    d_q_low = d_q_linear.reshape(rows_here, kv_heads * query_groups * HEAD_SIZE).astype(
        jnp.bfloat16
    )
    d_k_low = d_k_linear.reshape(rows_here, kv_heads * HEAD_SIZE).astype(jnp.bfloat16)
    d_v_low = d_value_own.reshape(rows_here, kv_heads * HEAD_SIZE).astype(jnp.bfloat16)
    d_wq = contract_first(normed_low, d_q_low)
    d_wk = contract_first(normed_low, d_k_low)
    d_wv = contract_first(normed_low, d_v_low)
    d_normed_one = lax.psum(
        (
            contract_last(d_q_low, wq_full)
            + contract_last(d_k_low, wk_full)
            + contract_last(d_v_low, wv_full)
        ).astype(jnp.bfloat16),
        "tp",
    ).astype(jnp.float32)
    _, norm_one_back = jax.vjp(normalize, inputs, gain_one)
    d_inputs_norm, d_gain_one = norm_one_back(d_normed_one)
    in_grad = (d_middle + d_inputs_norm).astype(jnp.bfloat16)
    weight_grads = (d_gain_one, d_wq, d_wk, d_wv, d_wo, d_gain_two, d_wg, d_wu, d_wd)
    shares = (
        lax.psum_scatter(weight_grads[0], ("fsdp", "ctx"), scatter_dimension=0, tiled=True),
        lax.psum_scatter(weight_grads[1], ("fsdp", "ctx"), scatter_dimension=0, tiled=True),
        lax.psum_scatter(weight_grads[2], ("fsdp", "ctx"), scatter_dimension=0, tiled=True),
        lax.psum_scatter(weight_grads[3], ("fsdp", "ctx"), scatter_dimension=0, tiled=True),
        lax.psum_scatter(weight_grads[4], ("fsdp", "ctx"), scatter_dimension=0, tiled=True),
        lax.psum_scatter(weight_grads[5], ("fsdp", "ctx"), scatter_dimension=0, tiled=True),
        lax.psum_scatter(weight_grads[6], ("fsdp", "ctx"), scatter_dimension=0, tiled=True),
        lax.psum_scatter(weight_grads[7], ("fsdp", "ctx"), scatter_dimension=0, tiled=True),
        lax.psum_scatter(weight_grads[8], ("fsdp", "ctx"), scatter_dimension=0, tiled=True),
    )
    owned_grads = (
        lax.all_gather(shares[0].astype(jnp.bfloat16), "ctx", axis=0, tiled=True).astype(
            jnp.float32
        ),
        lax.all_gather(shares[1].astype(jnp.bfloat16), "ctx", axis=0, tiled=True).astype(
            jnp.float32
        ),
        lax.all_gather(shares[2].astype(jnp.bfloat16), "ctx", axis=0, tiled=True).astype(
            jnp.float32
        ),
        lax.all_gather(shares[3].astype(jnp.bfloat16), "ctx", axis=0, tiled=True).astype(
            jnp.float32
        ),
        lax.all_gather(shares[4].astype(jnp.bfloat16), "ctx", axis=0, tiled=True).astype(
            jnp.float32
        ),
        lax.all_gather(shares[5].astype(jnp.bfloat16), "ctx", axis=0, tiled=True).astype(
            jnp.float32
        ),
        lax.all_gather(shares[6].astype(jnp.bfloat16), "ctx", axis=0, tiled=True).astype(
            jnp.float32
        ),
        lax.all_gather(shares[7].astype(jnp.bfloat16), "ctx", axis=0, tiled=True).astype(
            jnp.float32
        ),
        lax.all_gather(shares[8].astype(jnp.bfloat16), "ctx", axis=0, tiled=True).astype(
            jnp.float32
        ),
    )
    return (
        result,
        in_grad,
        owned_grads[0],
        owned_grads[1],
        owned_grads[2],
        owned_grads[3],
        owned_grads[4],
        owned_grads[5],
        owned_grads[6],
        owned_grads[7],
        owned_grads[8],
    )


def solution(mesh):
    placed = (
        P(("fsdp", "ctx"), None),
        P(("fsdp", "ctx"), None),
        P("fsdp"),
        P("fsdp", "tp"),
        P("fsdp", "tp"),
        P("fsdp", "tp"),
        P("fsdp", "tp"),
        P("fsdp"),
        P("fsdp", "tp"),
        P("fsdp", "tp"),
        P("fsdp", "tp"),
        P("fsdp", None),
        P("fsdp", None),
    )
    plane = mesh.shape["fsdp"] * mesh.shape["tp"]
    splits = mesh.shape["tp"] == 2 and KEY_VALUE_HEADS == plane and mesh.shape["ctx"] == 4
    return jax.shard_map(
        split_heads if splits else gathered_weights,
        mesh=mesh,
        in_specs=placed,
        out_specs=(
            P(("fsdp", "ctx"), None),
            P(("fsdp", "ctx"), None),
            P("fsdp"),
            P("fsdp", "tp"),
            P("fsdp", "tp"),
            P("fsdp", "tp"),
            P("fsdp", "tp"),
            P("fsdp"),
            P("fsdp", "tp"),
            P("fsdp", "tp"),
            P("fsdp", "tp"),
        ),
        check_vma=False,
    )
```

```python
import functools
import math

import jax
import jax.numpy as jnp
from jax import lax
from jax.experimental import pallas as pl
from jax.experimental.pallas import tpu as pltpu
from jax.sharding import PartitionSpec as P

QUERY_HEADS = 32
KEY_VALUE_HEADS = 8
HEAD_SIZE = 64


def stream_place(row_ids, order_row, length_row, tok_dev):
    cycle_size = order_row.shape[0]
    half_len = tok_dev // 2
    cycle_rank = row_ids // tok_dev
    within = row_ids % tok_dev
    first_section = jnp.sum(
        jnp.where(
            cycle_rank[:, None] == jnp.arange(cycle_size, dtype=jnp.int32)[None, :],
            order_row[None, :],
            0,
        ),
        axis=1,
        dtype=jnp.int32,
    )
    section = jnp.where(within >= half_len, 2 * cycle_size - 1 - first_section, first_section)
    places = section * half_len + within % half_len
    seq_ends = jnp.cumsum(length_row, dtype=jnp.int32)
    passed = places[:, None] >= seq_ends[None, :]
    segment = jnp.sum(passed.astype(jnp.int32), axis=1, dtype=jnp.int32)
    offset = places - jnp.sum(jnp.where(passed, length_row[None, :], 0), axis=1, dtype=jnp.int32)
    return (places, segment, offset)


def rotary_embedding(values, positions):
    half_len = values.shape[-1] // 2
    frequency = jnp.exp(
        -math.log(500000.0) * jnp.arange(half_len, dtype=jnp.float32) * 2.0 / values.shape[-1]
    )
    angles = positions.astype(jnp.float32)[:, None] * frequency[None, :]
    cosine = jnp.cos(angles)[:, None, :]
    sine = jnp.sin(angles)[:, None, :]
    lower_half = values[..., :half_len]
    upper_half = values[..., half_len:]
    return jnp.concatenate(
        [lower_half * cosine - upper_half * sine, upper_half * cosine + lower_half * sine], axis=-1
    )


def normalize(values, gain_vec):
    return values * lax.rsqrt(jnp.mean(values * values, axis=-1, keepdims=True) + 1e-05) * gain_vec


def swiglu(gate_val, up_val):
    return jax.nn.silu(gate_val) * up_val


def contract_last(left, right):
    return lax.dot_general(
        left, right, (((1,), (1,)), ((), ())), preferred_element_type=jnp.float32
    )


def contract_first(left, right):
    return lax.dot_general(
        left, right, (((0,), (0,)), ((), ())), preferred_element_type=jnp.float32
    )


VMEM_LIMIT = 28 * 1024 * 1024
LARGE_LIMIT = 28 * 1024 * 1024
MIDDLE_LIMIT = 20 * 1024 * 1024
SMALL_LIMIT = 12 * 1024 * 1024
SMALL = pl.CostEstimate(flops=1, bytes_accessed=1, transcendentals=0)
LARGE = pl.CostEstimate(flops=12_000_000_000, bytes_accessed=1, transcendentals=0)


def pairs_by(distance, size):
    return [(i, i ^ distance) for i in range(size)]


def swap(array, axis, distance):
    return lax.ppermute(array, axis, pairs_by(distance, lax.axis_size(axis)))


class Line:
    def __init__(self, axis):
        index = lax.axis_index(axis)
        size = lax.axis_size(axis)
        self.axis = axis
        self.at_end = ((index == 0) | (index == size - 1)).astype(jnp.int32)[None]
        self.entered = self.halfway = self.leaving = None
        self.sums = {}

    def advance(self, got, entering):
        if self.leaving is not None:
            name, sent = self.leaving
            self.sums[name] = (got["ends"], sent)
        moves = []
        halfway = None
        if self.entered is not None:
            name, value = self.entered
            halfway = (name, add_low(value, got["ends"]))
            moves.append(("middle", halfway[1], self.axis, [(1, 2), (2, 1)]))
        leaving = None
        inwards, outwards = [(0, 1), (3, 2)], [(1, 0), (2, 3)]
        if self.halfway is not None:
            name, value = self.halfway
            if entering is None:
                sent, pairs = add_low(value, got["middle"]), outwards
            else:
                sent = either_way(self.at_end, entering[1], value, got["middle"])
                pairs = inwards + outwards
            leaving = (name, sent)
            moves.append(("ends", sent, self.axis, pairs))
        elif entering is not None and halfway is not None:
            sent = jnp.where(self.at_end[0] == 1, entering[1], halfway[1])
            moves.append(("ends", sent, self.axis, inwards + outwards))
        elif entering is not None:
            moves.append(("ends", entering[1], self.axis, inwards))
        self.entered, self.halfway, self.leaving = entering, halfway, leaving
        return moves


class Steps:
    def __init__(self, line):
        self.line = line
        self.got = {}
        self.on_line = []
        self.others = []
        self.token = jnp.zeros((8, 128), jnp.float32)

    def wait(self, flying, arrays):
        count = len(flying)
        held = lax.optimization_barrier(
            (self.token,) + tuple(value for _, value in flying) + tuple(arrays)
        )
        self.token = held[0]
        for (name, _), value in zip(flying, held[1:]):
            self.got[name] = value
        return list(held[1 + count :])

    def start(self, moves):
        return [(name, lax.ppermute(value, axis, pairs)) for name, value, axis, pairs in moves]

    def step(self, moves=(), summed=None, late=None, carry=(), first=()):
        moves, carry, first = list(moves), list(carry), list(first)
        arrays = [move[1] for move in moves] + carry
        fresh = [summed[1]] if summed is not None and summed[1] is not None else []
        together = summed is not None and not fresh and summed[0] not in self.got
        together = together or not self.on_line
        flying = self.on_line + (self.others if together else [])
        held = self.wait(flying, fresh + first + (arrays if together else []))
        held_fresh, held = held[: len(fresh)], held[len(fresh) :]
        held_first, held = held[: len(first)], held[len(first) :]
        entering = summed
        if summed is not None:
            entering = (summed[0], held_fresh[0] if fresh else self.take(summed[0]))
        self.on_line = self.start(self.line.advance(self.got, entering))
        if not together:
            held = self.wait(self.others, arrays)
        moves = [
            (name, value, axis, pairs) for (name, _, axis, pairs), value in zip(moves, held)
        ]
        self.others = self.start(moves + (late() if late is not None else []))
        return held[len(moves) :] + held_first

    def take(self, name):
        return self.got.pop(name)


def in_vmem(kernel, out_shape, *args, scalars=0):
    specs = [pl.BlockSpec(memory_space=pltpu.SMEM)] * scalars
    specs += [pl.BlockSpec(memory_space=pltpu.VMEM)] * (len(args) - scalars)
    return pl.pallas_call(
        kernel,
        out_shape=out_shape,
        in_specs=specs,
        out_specs=[pl.BlockSpec(memory_space=pltpu.VMEM)] * len(out_shape),
        compiler_params=pltpu.CompilerParams(vmem_limit_bytes=SMALL_LIMIT),
        cost_estimate=SMALL,
    )(*args)


def low(*shape):
    return jax.ShapeDtypeStruct(shape, jnp.bfloat16)


def full(*shape):
    return jax.ShapeDtypeStruct(shape, jnp.float32)


def store_seen(ref, value, distance, count):
    width = value.shape[-1] // count
    for block in range(count):
        there = block ^ distance
        ref[: value.shape[0], block * width : (block + 1) * width] = value[
            :, there * width : (there + 1) * width
        ]


def prepare_kernel(count, index_ref, x_ref, own_ref, *sends):
    rows, width = own_ref.shape[0], own_ref.shape[1] // count
    first = pl.multiple_of(index_ref[1] * rows, rows)
    for block in range(count):
        column = pl.multiple_of((index_ref[0] ^ block) * width, width)
        own_ref[:, block * width : (block + 1) * width] = x_ref[
            pl.ds(first, rows), pl.ds(column, width)
        ]
    for k, send in enumerate(sends, 1):
        store_seen(send, own_ref[...], k, count)


def prepare(x, index, count):
    rows, width = x.shape[0] // 2, x.shape[1]
    return in_vmem(
        functools.partial(prepare_kernel, count), [low(rows, width)] * count, index, x, scalars=1
    )


def turns_kernel(offset_ref, cos_ref, sin_ref):
    lane = lax.broadcasted_iota(jnp.int32, cos_ref.shape, 2)
    place = lax.rem(lane, HEAD_SIZE // 2).astype(jnp.float32)
    frequency = jnp.exp(-math.log(500000.0) * place * 2.0 / HEAD_SIZE)
    angle = offset_ref[...] * frequency
    cos_ref[...] = jnp.cos(angle)
    sin_ref[...] = jnp.sin(angle)


def join_kernel(*refs):
    out_ref = refs[-1]
    rows = refs[0].shape[0]
    for i, ref in enumerate(refs[:-1]):
        out_ref[i * rows : (i + 1) * rows, :] = ref[:rows, :]


def join_rows(arrays, rows):
    def kernel(*refs):
        for i, ref in enumerate(refs[:-1]):
            refs[-1][i * rows : (i + 1) * rows, :] = ref[:rows, :]

    return in_vmem(kernel, [low(rows * len(arrays), arrays[0].shape[1])], *arrays)[0]


def join(own, others):
    rows, width = own.shape
    return in_vmem(join_kernel, [low(rows * (1 + len(others)), width)], own, *others)[0]


def fold_kernel(count, first_ref, came_ref, own_ref, *sends):
    rows = own_ref.shape[0]
    for k in range(count):
        here = slice(k * rows, (k + 1) * rows)
        total = first_ref[here, :].astype(jnp.float32) + came_ref[here, :].astype(jnp.float32)
        total = total.astype(jnp.bfloat16)
        if k == 0:
            own_ref[...] = total
        else:
            store_seen(sends[k - 1], total, k, count)


def fold(first, came, count):
    rows, width = first.shape[0] // count, first.shape[1]
    return in_vmem(
        functools.partial(fold_kernel, count), [low(rows, width)] * count, first, came
    )


def total_of(refs):
    total = refs[0][...].astype(jnp.float32)
    for ref in refs[1:]:
        total = total + ref[...].astype(jnp.float32)
    return total


def middle_kernel(count, in_ref, gain_ref, *refs):
    parts, (middle_ref, normed_ref, *sends) = refs[:count], refs[count:]
    middle = in_ref[...].astype(jnp.float32) + total_of(parts)
    middle_ref[...] = middle
    mean = jnp.mean(middle * middle, axis=-1, keepdims=True)
    normed = (middle * lax.rsqrt(mean + 1e-05) * gain_ref[...]).astype(jnp.bfloat16)
    normed_ref[...] = normed
    for k in range(1, count):
        store_seen(sends[k - 1], normed, k, count)


def norm_back(d_normed, x, gain):
    scale = lax.rsqrt(jnp.mean(x * x, axis=-1, keepdims=True) + 1e-05)
    unit = x * scale
    d_unit = d_normed * gain
    d_x = scale * (d_unit - unit * jnp.mean(d_unit * unit, axis=-1, keepdims=True))
    return d_x, jnp.sum(d_normed * unit, axis=0, keepdims=True)


def branch_back_kernel(count, middle_ref, gain_ref, cot_ref, *refs):
    parts, (d_middle_ref, d_gain_ref, branch_ref, *sends) = refs[:count], refs[count:]
    d_x, d_gain_ref[...] = norm_back(total_of(parts), middle_ref[...], gain_ref[...])
    d_middle = cot_ref[...].astype(jnp.float32) + d_x
    d_middle_ref[...] = d_middle
    branch = d_middle.astype(jnp.bfloat16)
    branch_ref[...] = branch
    for k in range(1, count):
        store_seen(sends[k - 1], branch, k, count)


def in_grad_kernel(count, in_ref, gain_ref, d_middle_ref, *refs):
    parts, (grad_ref, d_gain_ref) = refs[:count], refs[count:]
    x = in_ref[...].astype(jnp.float32)
    d_x, d_gain_ref[...] = norm_back(total_of(parts), x, gain_ref[...])
    grad_ref[...] = (d_middle_ref[...] + d_x).astype(jnp.bfloat16)


def spec_of(array, block, index):
    if block == array.shape:
        return pl.BlockSpec(block, index, pipeline_mode=pl.Buffered(1))
    return pl.BlockSpec(block, index)


def gridded(kernel, steps, ins, outs, scalars=(), limit=None, cost=SMALL):
    return pl.pallas_call(
        kernel,
        grid=(steps,),
        in_specs=[pl.BlockSpec(memory_space=pltpu.SMEM)] * len(scalars)
        + [spec_of(array, block, index) for array, block, index in ins],
        out_specs=[pl.BlockSpec(block, index) for _, block, index in outs],
        out_shape=[shape for shape, _, _ in outs],
        compiler_params=pltpu.CompilerParams(vmem_limit_bytes=limit or MIDDLE_LIMIT),
        cost_estimate=cost,
    )(*scalars, *[array for array, _, _ in ins])


def row_blocks(array, rows):
    return (array, (rows, array.shape[1]), lambda i: (i, 0))


def add_low(left, right):
    right = right[:, : left.shape[1]]
    return (left.astype(jnp.float32) + right.astype(jnp.float32)).astype(jnp.bfloat16)


def either_way(at_end, fresh, value, came):
    total = add_low(value, came)
    width = max(fresh.shape[1], value.shape[1])
    if fresh.shape[1] < width:
        fresh = jnp.pad(fresh, ((0, 0), (0, width - fresh.shape[1])))
    if total.shape[1] < width:
        total = jnp.pad(total, ((0, 0), (0, width - total.shape[1])))
    return jnp.where(at_end[0] == 1, fresh, total)


def settled(at_end, came_ref, sent_ref, columns):
    return jnp.where(at_end == 1, came_ref[:, columns], sent_ref[:, columns]).astype(jnp.float32)


def settle_kernel(count, at_end_ref, index_ref, *refs):
    out_ref = refs[-1]
    width = out_ref.shape[1] // count
    for k in range(count):
        column = pl.multiple_of((index_ref[0] ^ k) * width, width)
        out_ref[:, pl.ds(column, width)] = settled(
            at_end_ref[0], refs[2 * k], refs[2 * k + 1], slice(0, width)
        )


def settle(at_end, index, pairs, width, cost=SMALL):
    count = len(pairs)
    arrays = [array for pair in pairs for array in pair]
    depth = arrays[0].shape[0]
    rows = math.gcd(depth, 128)
    ins = [(array, (rows, width), lambda i: (i, 0)) for array in arrays]
    outs = [row_blocks(full(depth, width * count), rows)]
    kernel = functools.partial(settle_kernel, count)
    return gridded(kernel, depth // rows, ins, outs, scalars=(at_end, index), cost=cost)[0]


def settle_attention_kernel(count, q_width, kv_width, at_end_ref, index_ref, *refs):
    q_ref, k_ref, v_ref, o_ref = refs[-4:]
    o_width = o_ref.shape[1] // count
    o_first = q_width + kv_width
    kvs = []
    for k in range(count):
        came_ref, sent_ref = refs[2 * k], refs[2 * k + 1]
        column = pl.multiple_of((index_ref[0] ^ k) * q_width, q_width)
        q_ref[:, pl.ds(column, q_width)] = settled(
            at_end_ref[0], came_ref, sent_ref, slice(0, q_width)
        )
        column = pl.multiple_of((index_ref[0] ^ k) * o_width, o_width)
        o_ref[:, pl.ds(column, o_width)] = settled(
            at_end_ref[0], came_ref, sent_ref, slice(o_first, o_first + o_width)
        )
        kvs.append(settled(at_end_ref[0], came_ref, sent_ref, slice(q_width, o_first)))
    ordered = []
    for place in range(count):
        kv = kvs[0]
        for k in range(1, count):
            kv = jnp.where((index_ref[0] ^ k) == place, kvs[k], kv)
        ordered.append(kv)
    k_ref[...] = jnp.concatenate([kv[:, : kv_width // 2] for kv in ordered], axis=1)
    v_ref[...] = jnp.concatenate([kv[:, kv_width // 2 :] for kv in ordered], axis=1)


def settle_attention(at_end, index, pairs, q_width, kv_width):
    count = len(pairs)
    arrays = [array for pair in pairs for array in pair]
    depth = arrays[0].shape[0]
    width = min(array.shape[1] for array in arrays)
    o_width = width - q_width - kv_width
    rows = math.gcd(depth, 128)
    ins = [(array, (rows, width), lambda i: (i, 0)) for array in arrays]
    widths = (q_width, kv_width // 2, kv_width // 2, o_width)
    outs = [row_blocks(full(depth, each * count), rows) for each in widths]
    kernel = functools.partial(settle_attention_kernel, count, q_width, kv_width)
    return gridded(kernel, depth // rows, ins, outs, scalars=(at_end, index))


def d_qkv_kernel(at_end_ref, here_ref, came_ref, sent_ref, dq_ref, cos_ref, sin_ref, out_ref):
    lanes = 2 * HEAD_SIZE
    half, q_width = dq_ref.shape[1], dq_ref.shape[2]
    cycle = came_ref.shape[1] // lanes // 2
    for core_side in range(2):
        column = pl.multiple_of((core_side * cycle + here_ref[0]) * lanes, lanes)
        d_kv = settled(at_end_ref[0], came_ref, sent_ref, pl.ds(column, lanes))
        cosine, sine = of_keys(cos_ref[core_side], sin_ref[core_side])
        d_kv = turned(d_kv, cosine, -sine).astype(jnp.bfloat16)
        rows = slice(core_side * half, (core_side + 1) * half)
        out_ref[rows, :q_width] = dq_ref[core_side]
        out_ref[rows, q_width:] = d_kv


def rows_back_kernel(count, index_ref, own_ref, other_ref, out_ref):
    rows, width = own_ref.shape[0], own_ref.shape[1] // count
    for ref, core in ((own_ref, index_ref[1]), (other_ref, 1 - index_ref[1])):
        first = pl.multiple_of(core * rows, rows)
        for block in range(count):
            column = pl.multiple_of((index_ref[0] ^ block) * width, width)
            out_ref[pl.ds(first, rows), pl.ds(column, width)] = ref[
                :, block * width : (block + 1) * width
            ]


def result_kernel(middle_ref, *refs):
    refs[-1][...] = (middle_ref[...] + total_of(refs[:-1])).astype(jnp.bfloat16)


def still(array):
    zeros = (0,) * len(array.shape)
    return (array, array.shape, lambda i: zeros)


def dot(left, right):
    return jnp.dot(left, right, preferred_element_type=jnp.float32)


def both(mine_ref, other_ref, weight):
    return jnp.concatenate([dot(mine_ref[...], weight), dot(other_ref[...], weight)], axis=0)


def chosen(here_steps, count, own, fetched, passed):
    here = pl.program_id(0) < here_steps
    weights = []
    for which in (0, 1):
        pieces = [own[which][...]]
        for k in range(count - 1):
            pieces.append(
                jnp.where(here, fetched[2 * k + which][...], passed[2 * k + which][...])
            )
        weights.append(jnp.concatenate(pieces, axis=0))
    return weights


def gate_up_kernel(count, here_steps, *refs):
    x_refs, refs = refs[:2], refs[2:]
    own, fetched, passed = refs[:2], refs[2 : 2 * count], refs[2 * count : 4 * count - 2]
    gate_ref, up_ref, hidden_ref = refs[4 * count - 2 :]
    weights = chosen(here_steps, count, own, fetched, passed)
    lin = both(*x_refs, jnp.concatenate(weights, axis=1))
    gate, up = lin[:, : lin.shape[1] // 2], lin[:, lin.shape[1] // 2 :]
    gate_ref[...] = gate.astype(jnp.bfloat16)
    up_ref[...] = up.astype(jnp.bfloat16)
    hidden_ref[...] = (gate * jax.nn.sigmoid(gate) * up).astype(jnp.bfloat16)


def columns_kernel(count, here_steps, *refs):
    own, fetched, passed = refs[:2], refs[2 : 2 * count], refs[2 * count : 4 * count - 2]
    wg_ref, wu_ref = refs[4 * count - 2 :]
    wg_ref[...], wu_ref[...] = chosen(here_steps, count, own, fetched, passed)


def column_blocks(own_gate, own_up, fetched, passed):
    depth, units = own_gate.shape
    block = math.gcd(units // 2, 256)
    steps, half = units // block, units // block // 2
    ins = [(w, (depth, block), lambda i: (0, i)) for w in (own_gate, own_up)]
    for arrays, step in (
        (fetched, lambda i: jnp.minimum(i, half - 1)),
        (passed, lambda i: jnp.maximum(i - half, 0)),
    ):
        for array in arrays:
            ins.append((array, (depth, block), lambda i, step=step: (0, step(i))))
            ins.append((array, (depth, block), lambda i, step=step: (0, half + step(i))))
    return ins, block, steps, half


def gate_up(x, *weights):
    tokens, units = 2 * x[0].shape[0], weights[0].shape[1]
    ins, block, steps, half = column_blocks(*weights)
    outs = [(low(tokens, units), (tokens, block), lambda i: (0, i))] * 3
    kernel = functools.partial(gate_up_kernel, len(weights[2]) + 1, half)
    return gridded(kernel, steps, [still(x[0]), still(x[1])] + ins, outs, limit=VMEM_LIMIT)


def whole_columns(*weights):
    depth, units = weights[0].shape
    ins, block, steps, half = column_blocks(*weights)
    count = len(weights[2]) + 1
    outs = [(low(count * depth, units), (count * depth, block), lambda i: (0, i))] * 2
    return gridded(functools.partial(columns_kernel, count, half), steps, ins, outs)


def units_back_kernel(count, *refs):
    d_refs, refs = refs[:2], refs[2:]
    pieces, (gate_ref, up_ref, d_gate_ref, d_up_ref) = refs[:count], refs[count:]
    weight = jnp.concatenate([ref[...] for ref in pieces], axis=0)
    d_hidden = both(*d_refs, weight)
    gate, up = gate_ref[...].astype(jnp.float32), up_ref[...].astype(jnp.float32)
    chance = jax.nn.sigmoid(gate)
    d_up_ref[...] = (d_hidden * (gate * chance)).astype(jnp.bfloat16)
    slope = chance + gate * chance * (1.0 - chance)
    d_gate_ref[...] = (d_hidden * up * slope).astype(jnp.bfloat16)


def units_back(d_out, pieces, gate, up):
    tokens, units = gate.shape
    depth = pieces[0].shape[0]
    block = math.gcd(units, 512)

    def by_columns(array, rows):
        return (array, (rows, block), lambda i: (0, i))

    ins = [still(d_out[0]), still(d_out[1])] + [by_columns(piece, depth) for piece in pieces]
    ins += [by_columns(gate, tokens), by_columns(up, tokens)]
    outs = [by_columns(low(tokens, units), tokens)] * 2
    kernel = functools.partial(units_back_kernel, len(pieces))
    return gridded(kernel, units // block, ins, outs, limit=LARGE_LIMIT)


def rows_sum_kernel(terms, *refs):
    first_ref, second_ref = refs[-2:]
    total = 0.0
    for left_ref, right_ref in zip(refs[:terms], refs[terms : 2 * terms]):
        total = total + contract_last(left_ref[...], right_ref[...])
    total = total.astype(jnp.bfloat16)
    half = first_ref.shape[0]
    first_ref[...] = total[:half]
    second_ref[...] = total[half:]


def rows_sum(lefts, rights, cost=SMALL):
    tokens, width = lefts[0].shape[0], rights[0].shape[0]
    block = math.gcd(width, 512)
    ins = [still(left) for left in lefts]
    ins += [(right, (block, right.shape[1]), lambda i: (i, 0)) for right in rights]
    outs = [(low(tokens // 2, width), (tokens // 2, block), lambda i: (0, i))] * 2
    kernel = functools.partial(rows_sum_kernel, len(lefts))
    return gridded(kernel, width // block, ins, outs, cost=cost)


def half_rows_kernel(terms, *refs):
    total = 0.0
    for left_ref, right_ref in zip(refs[:terms], refs[terms : 2 * terms]):
        total = total + contract_last(left_ref[...], right_ref[...])
    refs[-1][...] = total.astype(jnp.bfloat16)


def half_rows(lefts, rights, which, cost=SMALL):
    half, width = lefts[0].shape[0] // 2, rights[0].shape[0]
    block = math.gcd(width, 512)
    ins = [(left, (half, left.shape[1]), lambda i: (which, 0)) for left in lefts]
    ins += [(right, (block, right.shape[1]), lambda i: (i, 0)) for right in rights]
    outs = [(low(half, width), (half, block), lambda i: (0, i))]
    kernel = functools.partial(half_rows_kernel, len(lefts))
    return gridded(kernel, width // block, ins, outs, cost=cost)[0]


def weight_grad_kernel(count, terms, turn, *refs):
    if turn:
        side, refs = refs[0][0], refs[1:]
    outs = refs[3 * terms :]
    step = pl.program_id(0)
    first = 0
    for term in range(terms):
        mine_ref, other_ref, right_ref = refs[3 * term : 3 * term + 3]
        half = mine_ref.shape[0]
        grad = contract_first(mine_ref[...], right_ref[:half, :])
        grad = grad + contract_first(other_ref[...], right_ref[half:, :])
        grad = grad.astype(jnp.bfloat16)
        columns = grad.shape[1]
        for k in range(count):

            @pl.when(step == k)
            def _(k=k, first=first, grad=grad, columns=columns):
                if turn:
                    part = columns // 2
                    outs[k][:, pl.ds(pl.multiple_of(side * part, part), part)] = grad[:, :part]
                    outs[k][:, pl.ds(pl.multiple_of((1 - side) * part, part), part)] = grad[:, part:]
                else:
                    outs[k][:, first : first + columns] = grad

        first += columns


def weight_grad(terms, count, side=None, packs=None):
    columns = sum(right.shape[1] for _, _, right in terms)
    depth = terms[0][0].shape[1] // count
    packs = range(count) if packs is None else packs
    first, apart = packs[0], packs[-1] - packs[0]
    apart = apart // max(len(packs) - 1, 1)
    ins = []
    if side is not None:
        ins.append((side, None, None))
    for mine, other, right in terms:
        for left in (mine, other):
            ins.append((left, (left.shape[0], depth), lambda i: (0, first + apart * i)))
        ins.append(still(right))
    specs = [
        pl.BlockSpec(memory_space=pltpu.SMEM) if block is None else pl.BlockSpec(block, index)
        for _, block, index in ins
    ]
    return pl.pallas_call(
        functools.partial(weight_grad_kernel, len(packs), len(terms), side is not None),
        grid=(len(packs),),
        in_specs=specs,
        out_specs=[pl.BlockSpec((depth, columns), lambda i: (0, 0))] * len(packs),
        out_shape=[low(depth, columns)] * len(packs),
        compiler_params=pltpu.CompilerParams(vmem_limit_bytes=MIDDLE_LIMIT),
        cost_estimate=SMALL,
    )(*[array for array, _, _ in ins])


def turned(lin, cosine, sine):
    width = lin.shape[-1]
    quarter = HEAD_SIZE // 2
    lane = lax.broadcasted_iota(jnp.int32, lin.shape, lin.ndim - 1)
    first = lax.rem(lane, HEAD_SIZE) < quarter
    partner = jnp.where(
        first,
        -pltpu.roll(lin, width - quarter, lin.ndim - 1),
        pltpu.roll(lin, quarter, lin.ndim - 1),
    )
    return lin * cosine + partner * sine


def side_by_side(table, width):
    return jnp.concatenate([table] * (width // table.shape[-1]), axis=-1)


def of_keys(cosine, sine):
    keys = lax.broadcasted_iota(jnp.int32, cosine.shape, 1) < HEAD_SIZE
    return jnp.where(keys, cosine, 1.0), jnp.where(keys, sine, 0.0)


def qkv_kernel(count, q_width, kv_width, side_ref, *refs):
    x_refs, (gain_ref, cos_ref, sin_ref), refs = refs[:2], refs[2:5], refs[5:]
    own_ref, fetched, passed_ref, refs = refs[0], refs[1:count], refs[count], refs[count + 1 :]
    normed_refs, (q_ref, kv_ref, wqkv_ref, wo_ref) = refs[:2], refs[2:]
    qkv_width = q_width + kv_width
    depth = own_ref.shape[0]
    half = depth // 2

    @pl.when(pl.program_id(0) == 0)
    def _():
        wqkv_ref[:depth, :] = own_ref[:, :qkv_width]
        wo_ref[:depth, :] = own_ref[:, qkv_width:]
        for k in range(1, count):
            for which, piece in (
                (side_ref[0], fetched[k - 1][:half, :]),
                (1 - side_ref[0], passed_ref[(k - 1) * half : k * half, :]),
            ):
                first = pl.multiple_of(k * depth + which * half, half)
                wqkv_ref[pl.ds(first, half), :] = piece[:, :qkv_width]
                wo_ref[pl.ds(first, half), :] = piece[:, qkv_width:]

    for i in range(2):
        x = x_refs[i][...].astype(jnp.float32)
        mean = jnp.mean(x * x, axis=-1, keepdims=True)
        normed = (x * lax.rsqrt(mean + 1e-05) * gain_ref[...]).astype(jnp.bfloat16)
        normed_refs[i][...] = normed
        lin = dot(normed, wqkv_ref[...])
        cosine, sine = cos_ref[i], sin_ref[i]
        q = turned(lin[:, :q_width], side_by_side(cosine, q_width), side_by_side(sine, q_width))
        q_ref[i] = q.astype(jnp.bfloat16)
        kv = turned(lin[:, q_width:], *of_keys(cosine, sine))
        kv_ref[i] = kv.astype(jnp.bfloat16)


def project_qkv(side, x, gain, cosine, sine, own, fetched, passed, q_width, kv_width):
    half_rows, width = x[0].shape
    qkv_width = q_width + kv_width
    block = math.gcd(half_rows, 128)

    def rows_of(array, columns):
        return (array, (block, columns), lambda i: (i, 0))

    def of_both(array, columns):
        return (array, (2, block, columns), lambda i: (0, i, 0))

    lanes = cosine.shape[-1]
    ins = [rows_of(x[0], width), rows_of(x[1], width), still(gain)]
    ins += [of_both(cosine, lanes), of_both(sine, lanes)]
    ins += [still(array) for array in (own, *fetched, passed)]
    o_width = own.shape[1] - qkv_width
    outs = [rows_of(low(half_rows, width), width)] * 2
    outs += [of_both(low(2, half_rows, q_width), q_width), of_both(low(2, half_rows, kv_width), kv_width)]
    outs += [still(low(width, qkv_width)), still(low(width, o_width))]
    kernel = functools.partial(qkv_kernel, len(fetched) + 1, q_width, kv_width)
    return gridded(kernel, half_rows // block, ins, outs, scalars=(side,))


def shares(q, k, visible):
    scores = jnp.where(visible, contract_last(q, k), -1e30)
    weights = jnp.exp(scores - jnp.max(scores, axis=-1, keepdims=True))
    return weights, 1.0 / jnp.sum(weights, axis=-1, keepdims=True)


def load_attention(q_ref, place_ref, start_ref, key_place_ref, kv_refs):
    q = q_ref[...]
    q = q.reshape(q.shape[0] * q.shape[1], q.shape[2])
    kv = jnp.concatenate([ref[...].reshape(q.shape[0], 2 * HEAD_SIZE) for ref in kv_refs], axis=0)
    q = q * jnp.bfloat16(1.0 / math.sqrt(HEAD_SIZE))
    key_place = key_place_ref[0]
    visible = (key_place <= place_ref[0]) & (key_place >= start_ref[0])
    return q, kv[:, :HEAD_SIZE], kv[:, HEAD_SIZE:], visible


def attend_kernel(groups, q_ref, place_ref, start_ref, key_place_ref, wo_ref, *refs):
    kv_refs, (out_ref, first_ref, second_ref) = refs[:-3], refs[-3:]
    q, k, v, visible = load_attention(q_ref, place_ref, start_ref, key_place_ref, kv_refs)
    mixed = []
    for g in range(groups):
        weights, parts = shares(q[:, g * HEAD_SIZE : (g + 1) * HEAD_SIZE], k, visible)
        mixed.append(dot(weights.astype(jnp.bfloat16), v) * parts)
    out = jnp.concatenate(mixed, axis=1).astype(jnp.bfloat16)
    out_ref[...] = out.reshape(out_ref.shape)
    branch = contract_last(out, wo_ref[...]).astype(jnp.bfloat16)
    half = first_ref.shape[0]
    first_ref[...] = branch[:half]
    second_ref[...] = branch[half:]


def attend_back_kernel(
    groups,
    here_ref,
    q_ref,
    mine_ref,
    other_ref,
    cos_ref,
    sin_ref,
    place_ref,
    start_ref,
    key_place_ref,
    wo_ref,
    *refs,
):
    kv_refs, (dq_ref, dkv_ref) = refs[:-2], refs[-2:]
    q, k, v, visible = load_attention(q_ref, place_ref, start_ref, key_place_ref, kv_refs)
    d_out = both(mine_ref, other_ref, wo_ref[...]).astype(jnp.bfloat16)
    scale = 1.0 / math.sqrt(HEAD_SIZE)
    d_q, d_k, d_v = [], 0.0, 0.0
    for g in range(groups):
        q_head = q[:, g * HEAD_SIZE : (g + 1) * HEAD_SIZE]
        d_head = d_out[:, g * HEAD_SIZE : (g + 1) * HEAD_SIZE]
        weights, parts = shares(q_head, k, visible)
        probs = weights * parts
        d_probs = contract_last(d_head, v)
        row_delta = jnp.sum(probs * d_probs, axis=-1, keepdims=True)
        d_scores = (probs * (d_probs - row_delta)).astype(jnp.bfloat16)
        d_q.append(dot(d_scores, k) * scale)
        d_k = d_k + contract_first(q_head, d_scores)
        d_v = d_v + contract_first(d_head, probs.astype(jnp.bfloat16))
    d_q = jnp.concatenate(d_q, axis=1)
    cosine = cos_ref[...].reshape(q.shape[0], -1)
    sine = sin_ref[...].reshape(q.shape[0], -1)
    d_q = turned(d_q, side_by_side(cosine, q.shape[1]), -side_by_side(sine, q.shape[1]))
    dq_ref[...] = d_q.astype(jnp.bfloat16).reshape(dq_ref.shape)
    d_kv = jnp.concatenate([d_k, d_v], axis=0).T.astype(jnp.bfloat16)
    half, lanes, cycle = dkv_ref.shape[0], 2 * HEAD_SIZE, len(kv_refs)
    for j in range(cycle):
        for core_side in range(2):
            first = (2 * j + core_side) * half
            column = pl.multiple_of((core_side * cycle + (here_ref[0] ^ j)) * lanes, lanes)
            dkv_ref[:, pl.ds(column, lanes)] = d_kv[first : first + half]


def of_pack(array, half):
    return (array, (2, half, array.shape[-1]), lambda p: (0, p, 0))


def place_blocks(places):
    return [(array, (1,) + array.shape[1:], lambda p: (p, 0, 0)) for array in places]


def attend(q, places, wo, kvs, packs, groups):
    half = q.shape[1] // packs
    width = wo.shape[0]
    ins = [of_pack(q, half)] + place_blocks(places) + [still(wo)] + [of_pack(kv, half) for kv in kvs]
    outs = [of_pack(low(*q.shape), half)]
    outs += [(low(q.shape[1], width), (half, width), lambda p: (p, 0))] * 2
    return gridded(functools.partial(attend_kernel, groups), packs, ins, outs)


def attend_back(here, q, d_branch, cosine, sine, places, wo, kvs, packs, groups):
    half = q.shape[1] // packs
    cycle = len(kvs)
    ins = [of_pack(q, half)]
    ins += [(array, (half, array.shape[1]), lambda p: (p, 0)) for array in d_branch]
    ins += [of_pack(cosine, half), of_pack(sine, half)] + place_blocks(places) + [still(wo)]
    ins += [of_pack(kv, half) for kv in kvs]
    lanes = 2 * HEAD_SIZE
    outs = [of_pack(low(*q.shape), half)]
    outs.append((low(q.shape[1], 2 * cycle * lanes), (half, 2 * cycle * lanes), lambda p: (p, 0)))
    kernel = functools.partial(attend_back_kernel, groups)
    return gridded(kernel, packs, ins, outs, scalars=(here,))


def split_heads(
    hidden_in,
    out_cotangent,
    norm1_gain,
    q_weight,
    key_projection_weight,
    value_projection_weight,
    o_weight,
    norm2_gain,
    gate_weight,
    up_weight,
    down_weight,
    seq_lengths,
    span_order,
):
    packs = lax.axis_size("fsdp")
    cycle = lax.axis_size("ctx")
    pack = lax.axis_index("fsdp")
    core = lax.axis_index("tp")
    here = lax.axis_index("ctx")
    rows = hidden_in.shape[0]
    half = rows // 2
    tokens = packs * rows
    depth = q_weight.shape[0]
    width = depth * packs
    q_width = q_weight.shape[1] // packs
    k_width = key_projection_weight.shape[1] // packs
    ff_width = gate_weight.shape[1] // packs
    ff_half = ff_width // 2
    groups = q_width // k_width
    far = range(1, packs)
    steps = Steps(Line("ctx"))
    kept = {}


    def columns(weight, k, count, first=0, of=None):
        return lax.dynamic_slice_in_dim(weight, (pack ^ k) * (of or count) + first, count, 1)

    def to_pack(name, k, array):
        return ((name, k), array, "fsdp", pairs_by(k, packs))

    def send_all(name, arrays):
        return [to_pack(name, k, array) for k, array in zip(far, arrays)]

    def arrived(name):
        return [steps.take((name, k)) for k in far]

    def to_core(name, array):
        return [(name, array, "tp", pairs_by(1, 2))]

    def to_rows(name, first):
        kept[name], *others = fold(first, steps.take(name), packs)
        return send_all(name, others)

    def joined(name, own, others):
        kept[name] = join(own, others)
        return to_core(name, kept[name])

    def unwaited(name):
        return dict(steps.others)[name]

    def both_of(name):
        return kept[name], steps.take(name)

    index = jnp.stack([pack, core]).astype(jnp.int32)
    here_arg = here.astype(jnp.int32)[None]
    side_arg = here_arg & 1
    at_end = steps.line.at_end

    own_in, *in_moves = prepare(hidden_in, index, packs)
    own_cot, *cot_moves = prepare(out_cotangent, index, packs)

    side = here & 1
    weights = (q_weight, key_projection_weight, value_projection_weight, o_weight)
    widths = (q_width, k_width, k_width, q_width)

    def attention_piece(k, first, count):
        return jnp.concatenate(
            [
                lax.dynamic_slice(weight, (first, (pack ^ k) * each), (count, each))
                for weight, each in zip(weights, widths)
            ],
            axis=1,
        )

    meta = jnp.concatenate([span_order[0], seq_lengths[0]])
    order_len, meta_len = span_order.shape[1], meta.shape[0]
    metas = jnp.concatenate([(meta // 32).astype(jnp.bfloat16), (meta % 32).astype(jnp.bfloat16)])
    info = jnp.stack(
        [
            jnp.pad(jnp.concatenate([norm1_gain, metas]), (0, sum(widths) - depth - 2 * meta_len)),
            jnp.pad(norm2_gain, (0, sum(widths) - depth)),
        ]
    )
    info_rows = jnp.pad(info, ((0, 14), (0, 0)))
    row_half = depth // 2
    steps.step(
        [
            to_pack(
                "attention",
                k,
                jnp.concatenate([attention_piece(k, side * row_half, row_half), info_rows], axis=0),
            )
            for k in far
        ]
    )
    pieces = []

    def pass_rows():
        pieces.extend(arrived("attention"))
        rows_on = join_rows(pieces, row_half)
        return [("attention_rows", rows_on, "ctx", pairs_by(1, cycle))]

    steps.step(send_all("in", in_moves), late=pass_rows)
    infos = jnp.stack([info] + [piece[row_half : row_half + 2] for piece in pieces])
    all_gains = infos[:, :, :depth].astype(jnp.float32)
    gain_one = all_gains[:, 0].reshape(1, -1)
    gain_two = all_gains[:, 1].reshape(1, -1)
    metas = infos[:, 0, depth : depth + 2 * meta_len].astype(jnp.int32)
    metas = metas[:, :meta_len] * 32 + metas[:, meta_len:]
    orders, lengths = metas[:, :order_len], metas[:, order_len:]

    others = jnp.stack([here ^ j for j in range(cycle)])
    first = jnp.sum(
        jnp.where(
            others[None, :, None] == jnp.arange(order_len, dtype=jnp.int32)[None, None, :],
            orders[:, None, :],
            0,
        ),
        axis=2,
    )
    halves = jnp.stack([core, core ^ 1])[None, None, :]
    section = jnp.where(halves == 0, first[:, :, None], 2 * cycle - 1 - first[:, :, None])
    places = section[..., None] * half + jnp.arange(half, dtype=jnp.int32)
    places = places.reshape(packs, cycle * rows)
    starts = jnp.zeros_like(places)
    end = jnp.zeros((packs, 1), jnp.int32)
    for j in range(lengths.shape[1]):
        end = end + lengths[:, j : j + 1]
        starts = jnp.where(places >= end, end, starts)
    place_args = (places[:, :rows, None], starts[:, :rows, None], places[:, None, :])
    offsets = (places - starts)[:, :rows].reshape(packs, 2, half).transpose(1, 0, 2)
    cosine, sine = in_vmem(
        turns_kernel,
        [full(2, tokens // 2, 2 * HEAD_SIZE)] * 2,
        offsets.astype(jnp.float32).reshape(2, tokens // 2, 1),
    )


    def two_halves(weight, k):
        return jnp.concatenate(
            [
                columns(weight, k, ff_half, side * ff_half, ff_width),
                columns(weight, k, ff_half, (1 - side) * ff_half, ff_width),
            ],
            axis=1,
        )

    def fetch(ks):
        return [
            to_pack(
                "gate_up",
                k,
                jnp.concatenate(
                    [
                        columns(weight, k, ff_half, side * ff_half, ff_width)
                        for weight in (gate_weight, up_weight)
                    ],
                    axis=1,
                ),
            )
            for k in ks
        ]

    def to_neighbour(k):
        return [(("neighbour", k), fetched[k], "ctx", pairs_by(1, cycle))]

    fetched = {}
    own_piece = attention_piece(0, 0, depth)
    cosine, sine, own_piece, *place_args = steps.step(
        fetch([1, 2]), carry=(cosine, sine, own_piece, *place_args)
    )
    all_in = join(own_in, arrived("in"))
    all_in = (all_in, swap(all_in, "tp", 1))
    normed_mine, normed_other, q_rot, kv_own, wqkv, wo = project_qkv(
        side_arg,
        all_in,
        gain_one,
        cosine,
        sine,
        own_piece,
        pieces,
        steps.take("attention_rows"),
        q_width,
        2 * k_width,
    )
    normed_one = (normed_mine, normed_other)
    steps.step(
        [(("kv", j), kv_own, "ctx", pairs_by(j, cycle)) for j in range(1, cycle)] + fetch([3])
    )
    fetched[1], fetched[2] = steps.take(("gate_up", 1)), steps.take(("gate_up", 2))
    steps.step(send_all("cot", cot_moves) + to_neighbour(1))
    fetched[3] = steps.take(("gate_up", 3))
    kvs = [kv_own] + [steps.take(("kv", j)) for j in range(1, cycle)]
    attn, first, second = attend(q_rot, place_args, wo, kvs, packs, groups)
    attn_low = attn.reshape(tokens, q_width)
    steps.step(to_core("branch", second))
    steps.step(to_neighbour(2), late=lambda: to_rows("branch", first))
    kept["cot"] = join(own_cot, arrived("cot"))

    def middle_moves():
        kept["middle"], kept["normed"], *sends = in_vmem(
            functools.partial(middle_kernel, packs),
            [full(half, width)] + [low(half, width)] * packs,
            own_in,
            gain_two,
            kept["branch"],
            *arrived("branch"),
        )
        return send_all("two", sends)

    steps.step(to_neighbour(3) + to_core("cot", kept["cot"]), late=middle_moves)

    def wd_moves(ks):
        return [to_pack("down", k, two_halves(down_weight, k)) for k in ks]

    own_columns = [two_halves(weight, 0) for weight in (gate_weight, up_weight, down_weight)]
    own_gate, own_up, own_down = steps.step(
        wd_moves([1, 2]),
        late=lambda: joined("two", kept["normed"], arrived("two")),
        carry=own_columns,
    )
    all_cot = both_of("cot")
    neighbours = [steps.take(("neighbour", k)) for k in far]
    normed_two = (kept["two"], unwaited("two"))

    unit_weights = (own_gate, own_up, [fetched[k] for k in far], neighbours)
    gate_val, up_val, hidden = gate_up(normed_two, *unit_weights)
    d_wd = weight_grad([(*all_cot, hidden)], packs, side_arg)

    def back(name, grad, ks):
        return [to_pack(name, k, grad[k]) for k in ks]

    def entry(name, k, grad=None):
        return ((name, k), grad[0] if k == 0 else None)

    steps.step(back("wd", d_wd, [1, 2]), summed=entry("wd", 0, d_wd))
    wg, wu = whole_columns(*unit_weights)
    wg, wu = steps.step(wd_moves([3]), summed=entry("wd", 1), carry=(wg, wu))
    steps.step(back("wd", d_wd, [3]), summed=entry("wd", 2))
    wd_pieces = [own_down] + arrived("down")
    d_gate, d_up = units_back(all_cot, wd_pieces, gate_val, up_val)
    second = half_rows([d_gate, d_up], [wg, wu], 1)
    d_wg = dict(zip((0, 1, 2), weight_grad([(*normed_two, d_gate)], packs, side_arg, (0, 1, 2))))
    steps.step(to_core("d_two", second) + back("wg", d_wg, [1, 2]), summed=entry("wg", 0, d_wg))
    first = half_rows([d_gate, d_up], [wg, wu], 0)
    (d_wg[3],) = weight_grad([(*normed_two, d_gate)], packs, side_arg, (3,))
    d_wu = weight_grad([(*normed_two, d_up)], packs, side_arg)
    steps.step(summed=entry("wd", 3), late=functools.partial(to_rows, "d_two", first))

    def branch_back():
        kept["d_middle"], kept["d_gain_two"], kept["d_branch"], *sends = in_vmem(
            functools.partial(branch_back_kernel, packs),
            [full(half, width), full(1, width)] + [low(half, width)] * packs,
            kept["middle"],
            gain_two,
            own_cot,
            kept["d_two"],
            *arrived("d_two"),
        )
        return send_all("d_branch", sends)

    steps.step(summed=entry("wu", 0, d_wu), late=branch_back)
    wd = join(wd_pieces[0], wd_pieces[1:])
    ff_second = half_rows([hidden], [wd], 1, LARGE)
    (ff_second,) = steps.step(
        back("wg", d_wg, [3]),
        summed=entry("wg", 1),
        late=lambda: joined("all_branch", kept["d_branch"], arrived("d_branch")),
        first=(ff_second,),
    )
    sums = steps.line.sums

    def settle_all(name, cost=SMALL):
        return settle(at_end, index, [sums[name, k] for k in range(packs)], ff_width, cost)

    d_branch = (kept["all_branch"], unwaited("all_branch"))
    d_q, d_kv = attend_back(
        here_arg, q_rot, d_branch, cosine, sine, place_args, wo, kvs, packs, groups
    )
    ff_first = half_rows([hidden], [wd], 0, LARGE)
    d_q, d_kv, ff_first = steps.step(
        back("wu", d_wu, [1, 2]), summed=entry("wg", 2), carry=(d_q, d_kv), first=(ff_first,)
    )
    steps.step(back("wu", d_wu, [3]) + to_core("ff", ff_second), summed=("d_kv", d_kv))
    steps.step(summed=entry("wg", 3), late=functools.partial(to_rows, "ff", ff_first))
    steps.step(summed=entry("wu", 1))
    down_grad = settle_all("wd", LARGE)
    (down_grad,) = steps.step(summed=entry("wu", 2), first=(down_grad,))
    result = in_vmem(
        result_kernel, [low(half, width)], kept["middle"], kept["ff"], *arrived("ff")
    )[0]
    d_qkv = in_vmem(
        d_qkv_kernel,
        [low(tokens, q_width + 2 * k_width)],
        at_end,
        here_arg,
        *sums["d_kv"],
        d_q,
        cosine,
        sine,
        scalars=2,
    )[0]
    d_wqkvo = weight_grad([(*normed_one, d_qkv), (*d_branch, attn_low)], packs)
    first, second = rows_sum([d_qkv], [wqkv])
    steps.step(
        back("wqkvo", d_wqkvo, [1, 2]) + to_core("d_one", second), summed=entry("wu", 3)
    )
    steps.step(
        summed=entry("wqkvo", 0, d_wqkvo), late=functools.partial(to_rows, "d_one", first)
    )

    def both_rows(own, other):
        return in_vmem(
            functools.partial(rows_back_kernel, packs),
            [low(rows, width)],
            index,
            own,
            other,
            scalars=1,
        )[0]

    gate_grad = settle_all("wg", LARGE)
    def gains_to_core():
        kept["in_grad"], d_gain_one = in_vmem(
            functools.partial(in_grad_kernel, packs),
            [low(half, width), full(1, width)],
            own_in,
            gain_one,
            kept["d_middle"],
            kept["d_one"],
            *arrived("d_one"),
        )
        kept["gains"] = jnp.concatenate([d_gain_one, kept["d_gain_two"]], axis=0)
        return to_core("gains", kept["gains"]) + to_core("in_grad", kept["in_grad"])

    def gains_to_packs():
        kept["gains"] = kept["gains"] + steps.take("gains")
        return [to_pack("gains", k, kept["gains"][:, k * depth : (k + 1) * depth]) for k in far]

    def gains_along():
        kept["gains"] = kept["gains"][:, :depth]
        for k in far:
            kept["gains"] = kept["gains"] + steps.take(("gains", k))
        return [(("gains", j), kept["gains"], "ctx", pairs_by(j, cycle)) for j in range(1, cycle)]

    steps.step(back("wqkvo", d_wqkvo, [3]), summed=entry("wqkvo", 1), late=gains_to_core)
    (gate_grad,) = steps.step(
        summed=entry("wqkvo", 2), late=gains_to_packs, first=(gate_grad,)
    )
    up_grad = settle_all("wu")
    in_grad = both_rows(kept["in_grad"], steps.take("in_grad"))
    in_grad, up_grad = steps.step(
        to_core("result", result), summed=entry("wqkvo", 3), carry=(in_grad, up_grad)
    )
    steps.step(late=gains_along)
    out_hidden = both_rows(result, steps.take("result"))
    (out_hidden,) = steps.step(carry=(out_hidden,))
    steps.step()
    shares_of_gains = jnp.stack(
        [kept["gains"]] + [steps.take(("gains", j)) for j in range(1, cycle)]
    )
    gains = steps.token[0, 0]
    for place in range(cycle):
        gains = gains + lax.dynamic_index_in_dim(shares_of_gains, here ^ place, 0, keepdims=False)
    q_grad, k_grad, v_grad, o_grad = settle_attention(
        at_end, index, [sums["wqkvo", k] for k in range(packs)], q_width, 2 * k_width
    )
    return (
        out_hidden,
        in_grad,
        gains[0],
        q_grad,
        k_grad,
        v_grad,
        o_grad,
        gains[1],
        gate_grad,
        up_grad,
        down_grad,
    )


def gathered_weights(
    hidden_in,
    out_cotangent,
    norm1_gain,
    q_weight,
    key_projection_weight,
    value_projection_weight,
    o_weight,
    norm2_gain,
    gate_weight,
    up_weight,
    down_weight,
    seq_lengths,
    span_order,
):
    rows_here = hidden_in.shape[0]
    order_row = span_order[0]
    length_row = seq_lengths[0]
    kv_heads = key_projection_weight.shape[1] // HEAD_SIZE
    query_groups = QUERY_HEADS // KEY_VALUE_HEADS
    score_scale = 1.0 / math.sqrt(HEAD_SIZE)
    whole_rows = rows_here * lax.axis_size("ctx")
    local_rows = lax.axis_index("ctx") * rows_here + jnp.arange(rows_here, dtype=jnp.int32)
    q_place, q_segment, q_offset = stream_place(local_rows, order_row, length_row, rows_here)
    inputs = hidden_in.astype(jnp.float32)
    gain_one, wq_full, wk_full, wv_full, wo_full = (
        lax.all_gather(norm1_gain, "fsdp", axis=0, tiled=True),
        lax.all_gather(q_weight, "fsdp", axis=0, tiled=True),
        lax.all_gather(key_projection_weight, "fsdp", axis=0, tiled=True),
        lax.all_gather(value_projection_weight, "fsdp", axis=0, tiled=True),
        lax.all_gather(o_weight, "fsdp", axis=0, tiled=True),
    )
    gain_one = gain_one.astype(jnp.float32)
    first_normalized = normalize(inputs, gain_one)
    normed_low = first_normalized.astype(jnp.bfloat16)
    q_linear = jnp.dot(normed_low, wq_full, preferred_element_type=jnp.float32).reshape(
        rows_here, kv_heads * query_groups, HEAD_SIZE
    )
    k_linear = jnp.dot(normed_low, wk_full, preferred_element_type=jnp.float32).reshape(
        rows_here, kv_heads, HEAD_SIZE
    )
    q_rotated = (
        rotary_embedding(q_linear, q_offset)
        .astype(jnp.bfloat16)
        .reshape(rows_here, kv_heads, query_groups, HEAD_SIZE)
    )
    k_rotated = (
        rotary_embedding(k_linear, q_offset)
        .astype(jnp.bfloat16)
        .reshape(rows_here, kv_heads * HEAD_SIZE)
    )
    v_low = jnp.dot(normed_low, wv_full, preferred_element_type=jnp.float32).astype(jnp.bfloat16)

    def key_blocks(shard_rows):
        row_count = shard_rows.shape[0]
        key_total_width = math.gcd(row_count, 512)
        number = row_count // key_total_width
        k_place, k_segment, _ = stream_place(
            jnp.arange(row_count, dtype=jnp.int32), order_row, length_row, rows_here
        )
        return (
            key_total_width,
            number,
            k_place.reshape(number, key_total_width),
            k_segment.reshape(number, key_total_width),
        )

    def scores_of(key_block, place_block, segment_block):
        scores = (
            jnp.einsum("qkgd,skd->kgqs", q_rotated, key_block, preferred_element_type=jnp.float32)
            * score_scale
        )
        visible = (
            (q_place[:, None] >= place_block[None, :])
            & (q_segment[:, None] == segment_block[None, :])
        )[None, None]
        return (jnp.where(visible, scores, -1e30), visible)

    start_state = (
        jnp.full((kv_heads, query_groups, rows_here), -1e30, jnp.float32),
        jnp.zeros((kv_heads, query_groups, rows_here), jnp.float32),
        jnp.zeros((kv_heads, query_groups, rows_here, HEAD_SIZE), jnp.float32),
    )
    folded = start_state
    key_row_block = lax.all_gather(k_rotated, "ctx", axis=0, tiled=True)
    value_row_block = lax.all_gather(v_low, "ctx", axis=0, tiled=True)
    key_total_width, number, k_place, k_segment = key_blocks(key_row_block)

    def one_step(carried, pieces):
        running_max, totals, accumulated = carried
        key_block, value_block, place_block, segment_block = pieces
        scores, visible = scores_of(key_block, place_block, segment_block)
        new_max = jnp.maximum(running_max, jnp.max(scores, axis=-1))
        weights = jnp.where(visible, jnp.exp(scores - new_max[..., None]), 0.0)
        factor = jnp.exp(running_max - new_max)
        totals = totals * factor + jnp.sum(weights, axis=-1)
        accumulated = accumulated * factor[..., None] + jnp.einsum(
            "kgqs,skd->kgqd",
            weights.astype(jnp.bfloat16),
            value_block,
            preferred_element_type=jnp.float32,
        )
        return ((new_max, totals, accumulated), None)

    pieces = (
        key_row_block.reshape(number, key_total_width, kv_heads, HEAD_SIZE),
        value_row_block.reshape(number, key_total_width, kv_heads, HEAD_SIZE),
        k_place,
        k_segment,
    )
    folded, _ = lax.scan(one_step, folded, pieces)
    running_max, totals, accumulated = folded
    mixed_out = jnp.transpose(accumulated / totals[..., None], (2, 0, 1, 3))
    log_sum = running_max + jnp.log(totals)
    attn_low = mixed_out.reshape(rows_here, kv_heads * query_groups * HEAD_SIZE).astype(
        jnp.bfloat16
    )
    branch = lax.psum(contract_last(attn_low, wo_full).astype(jnp.bfloat16), "tp").astype(
        jnp.float32
    )
    middle = inputs + branch
    gain_two, wg_full, wu_full, wd_full = (
        lax.all_gather(norm2_gain, "fsdp", axis=0, tiled=True),
        lax.all_gather(gate_weight, "fsdp", axis=0, tiled=True),
        lax.all_gather(up_weight, "fsdp", axis=0, tiled=True),
        lax.all_gather(down_weight, "fsdp", axis=0, tiled=True),
    )
    gain_two = gain_two.astype(jnp.float32)
    normed_two = normalize(middle, gain_two)
    normed_two_low = normed_two.astype(jnp.bfloat16)
    gate_val = jnp.dot(normed_two_low, wg_full, preferred_element_type=jnp.float32)
    up_val = jnp.dot(normed_two_low, wu_full, preferred_element_type=jnp.float32)
    hidden = swiglu(gate_val, up_val).astype(jnp.bfloat16)
    ffn_out = lax.psum(contract_last(hidden, wd_full).astype(jnp.bfloat16), "tp").astype(
        jnp.float32
    )
    result = (middle + ffn_out).astype(jnp.bfloat16)
    grad_out = out_cotangent.astype(jnp.float32)
    d_wd = contract_first(out_cotangent, hidden)
    d_hidden = jnp.dot(out_cotangent, wd_full, preferred_element_type=jnp.float32)
    _, swiglu_back = jax.vjp(swiglu, gate_val, up_val)
    d_gate, d_up = swiglu_back(d_hidden)
    d_gate_low = d_gate.astype(jnp.bfloat16)
    d_up_low = d_up.astype(jnp.bfloat16)
    d_wg = contract_first(normed_two_low, d_gate_low)
    d_wu = contract_first(normed_two_low, d_up_low)
    d_normed_two = lax.psum(
        (contract_last(d_gate_low, wg_full) + contract_last(d_up_low, wu_full)).astype(
            jnp.bfloat16
        ),
        "tp",
    ).astype(jnp.float32)
    _, norm_two_back = jax.vjp(normalize, middle, gain_two)
    d_middle_norm, d_gain_two = norm_two_back(d_normed_two)
    d_middle = grad_out + d_middle_norm
    d_branch_low = d_middle.astype(jnp.bfloat16)
    d_wo = contract_first(d_branch_low, attn_low)
    d_attn = jnp.dot(d_branch_low, wo_full, preferred_element_type=jnp.float32).astype(jnp.bfloat16)
    d_attn_heads = d_attn.reshape(rows_here, kv_heads, query_groups, HEAD_SIZE)
    row_delta = jnp.einsum("qkgd,qkgd->kgq", d_attn_heads.astype(jnp.float32), mixed_out)
    back_state = (
        jnp.zeros((rows_here, kv_heads, query_groups, HEAD_SIZE), jnp.float32),
        jnp.zeros((whole_rows, kv_heads, HEAD_SIZE), jnp.float32),
        jnp.zeros((whole_rows, kv_heads, HEAD_SIZE), jnp.float32),
    )
    folded = back_state
    key_row_block = lax.all_gather(k_rotated, "ctx", axis=0, tiled=True)
    value_row_block = lax.all_gather(v_low, "ctx", axis=0, tiled=True)
    key_total_width, number, k_place, k_segment = key_blocks(key_row_block)

    def one_step(carried, pieces):
        d_query, d_keys, d_values = carried
        key_block, value_block, place_block, segment_block, step_index = pieces
        scores, visible = scores_of(key_block, place_block, segment_block)
        prob_rows = jnp.where(visible, jnp.exp(scores - log_sum[..., None]), 0.0)
        d_values_block = jnp.einsum(
            "kgqs,qkgd->skd",
            prob_rows.astype(jnp.bfloat16),
            d_attn_heads,
            preferred_element_type=jnp.float32,
        )
        d_probs = jnp.einsum(
            "qkgd,skd->kgqs", d_attn_heads, value_block, preferred_element_type=jnp.float32
        )
        d_scores = (prob_rows * (d_probs - row_delta[..., None])).astype(jnp.bfloat16)
        d_query = (
            d_query
            + jnp.einsum("kgqs,skd->qkgd", d_scores, key_block, preferred_element_type=jnp.float32)
            * score_scale
        )
        d_keys_block = (
            jnp.einsum("kgqs,qkgd->skd", d_scores, q_rotated, preferred_element_type=jnp.float32)
            * score_scale
        )
        row_first = step_index * key_total_width
        d_keys = lax.dynamic_update_slice_in_dim(
            d_keys,
            lax.dynamic_slice_in_dim(d_keys, row_first, key_total_width, 0) + d_keys_block,
            row_first,
            0,
        )
        d_values = lax.dynamic_update_slice_in_dim(
            d_values,
            lax.dynamic_slice_in_dim(d_values, row_first, key_total_width, 0) + d_values_block,
            row_first,
            0,
        )
        return ((d_query, d_keys, d_values), None)

    pieces = (
        key_row_block.reshape(number, key_total_width, kv_heads, HEAD_SIZE),
        value_row_block.reshape(number, key_total_width, kv_heads, HEAD_SIZE),
        k_place,
        k_segment,
        jnp.arange(number, dtype=jnp.int32),
    )
    folded, _ = lax.scan(one_step, folded, pieces)
    d_query, d_keys_all, d_values_all = folded
    d_key_own, d_value_own = (
        lax.psum_scatter(
            d_keys_all.astype(jnp.bfloat16), "ctx", scatter_dimension=0, tiled=True
        ).astype(jnp.float32),
        lax.psum_scatter(
            d_values_all.astype(jnp.bfloat16), "ctx", scatter_dimension=0, tiled=True
        ).astype(jnp.float32),
    )
    _, rope_q_back = jax.vjp(lambda rotated_in: rotary_embedding(rotated_in, q_offset), q_linear)
    _, rope_k_back = jax.vjp(lambda rotated_in: rotary_embedding(rotated_in, q_offset), k_linear)
    (d_q_linear,) = rope_q_back(d_query.reshape(rows_here, kv_heads * query_groups, HEAD_SIZE))
    (d_k_linear,) = rope_k_back(d_key_own)
    d_q_low = d_q_linear.reshape(rows_here, kv_heads * query_groups * HEAD_SIZE).astype(
        jnp.bfloat16
    )
    d_k_low = d_k_linear.reshape(rows_here, kv_heads * HEAD_SIZE).astype(jnp.bfloat16)
    d_v_low = d_value_own.reshape(rows_here, kv_heads * HEAD_SIZE).astype(jnp.bfloat16)
    d_wq = contract_first(normed_low, d_q_low)
    d_wk = contract_first(normed_low, d_k_low)
    d_wv = contract_first(normed_low, d_v_low)
    d_normed_one = lax.psum(
        (
            contract_last(d_q_low, wq_full)
            + contract_last(d_k_low, wk_full)
            + contract_last(d_v_low, wv_full)
        ).astype(jnp.bfloat16),
        "tp",
    ).astype(jnp.float32)
    _, norm_one_back = jax.vjp(normalize, inputs, gain_one)
    d_inputs_norm, d_gain_one = norm_one_back(d_normed_one)
    in_grad = (d_middle + d_inputs_norm).astype(jnp.bfloat16)
    weight_grads = (d_gain_one, d_wq, d_wk, d_wv, d_wo, d_gain_two, d_wg, d_wu, d_wd)
    shares = (
        lax.psum_scatter(weight_grads[0], ("fsdp", "ctx"), scatter_dimension=0, tiled=True),
        lax.psum_scatter(weight_grads[1], ("fsdp", "ctx"), scatter_dimension=0, tiled=True),
        lax.psum_scatter(weight_grads[2], ("fsdp", "ctx"), scatter_dimension=0, tiled=True),
        lax.psum_scatter(weight_grads[3], ("fsdp", "ctx"), scatter_dimension=0, tiled=True),
        lax.psum_scatter(weight_grads[4], ("fsdp", "ctx"), scatter_dimension=0, tiled=True),
        lax.psum_scatter(weight_grads[5], ("fsdp", "ctx"), scatter_dimension=0, tiled=True),
        lax.psum_scatter(weight_grads[6], ("fsdp", "ctx"), scatter_dimension=0, tiled=True),
        lax.psum_scatter(weight_grads[7], ("fsdp", "ctx"), scatter_dimension=0, tiled=True),
        lax.psum_scatter(weight_grads[8], ("fsdp", "ctx"), scatter_dimension=0, tiled=True),
    )
    owned_grads = (
        lax.all_gather(shares[0].astype(jnp.bfloat16), "ctx", axis=0, tiled=True).astype(
            jnp.float32
        ),
        lax.all_gather(shares[1].astype(jnp.bfloat16), "ctx", axis=0, tiled=True).astype(
            jnp.float32
        ),
        lax.all_gather(shares[2].astype(jnp.bfloat16), "ctx", axis=0, tiled=True).astype(
            jnp.float32
        ),
        lax.all_gather(shares[3].astype(jnp.bfloat16), "ctx", axis=0, tiled=True).astype(
            jnp.float32
        ),
        lax.all_gather(shares[4].astype(jnp.bfloat16), "ctx", axis=0, tiled=True).astype(
            jnp.float32
        ),
        lax.all_gather(shares[5].astype(jnp.bfloat16), "ctx", axis=0, tiled=True).astype(
            jnp.float32
        ),
        lax.all_gather(shares[6].astype(jnp.bfloat16), "ctx", axis=0, tiled=True).astype(
            jnp.float32
        ),
        lax.all_gather(shares[7].astype(jnp.bfloat16), "ctx", axis=0, tiled=True).astype(
            jnp.float32
        ),
        lax.all_gather(shares[8].astype(jnp.bfloat16), "ctx", axis=0, tiled=True).astype(
            jnp.float32
        ),
    )
    return (
        result,
        in_grad,
        owned_grads[0],
        owned_grads[1],
        owned_grads[2],
        owned_grads[3],
        owned_grads[4],
        owned_grads[5],
        owned_grads[6],
        owned_grads[7],
        owned_grads[8],
    )


def solution(mesh):
    placed = (
        P(("fsdp", "ctx"), None),
        P(("fsdp", "ctx"), None),
        P("fsdp"),
        P("fsdp", "tp"),
        P("fsdp", "tp"),
        P("fsdp", "tp"),
        P("fsdp", "tp"),
        P("fsdp"),
        P("fsdp", "tp"),
        P("fsdp", "tp"),
        P("fsdp", "tp"),
        P("fsdp", None),
        P("fsdp", None),
    )
    plane = mesh.shape["fsdp"] * mesh.shape["tp"]
    splits = mesh.shape["tp"] == 2 and KEY_VALUE_HEADS == plane and mesh.shape["ctx"] == 4
    return jax.shard_map(
        split_heads if splits else gathered_weights,
        mesh=mesh,
        in_specs=placed,
        out_specs=(
            P(("fsdp", "ctx"), None),
            P(("fsdp", "ctx"), None),
            P("fsdp"),
            P("fsdp", "tp"),
            P("fsdp", "tp"),
            P("fsdp", "tp"),
            P("fsdp", "tp"),
            P("fsdp"),
            P("fsdp", "tp"),
            P("fsdp", "tp"),
            P("fsdp", "tp"),
        ),
        check_vma=False,
    )
```

```python
import functools
import math

import jax
import jax.numpy as jnp
from jax import lax
from jax.experimental import pallas as pl
from jax.experimental.pallas import tpu as pltpu
from jax.sharding import PartitionSpec as P

QUERY_HEADS = 32
KEY_VALUE_HEADS = 8
HEAD_SIZE = 64


def stream_place(row_ids, order_row, length_row, tok_dev):
    cycle_size = order_row.shape[0]
    half_len = tok_dev // 2
    cycle_rank = row_ids // tok_dev
    within = row_ids % tok_dev
    first_section = jnp.sum(
        jnp.where(
            cycle_rank[:, None] == jnp.arange(cycle_size, dtype=jnp.int32)[None, :],
            order_row[None, :],
            0,
        ),
        axis=1,
        dtype=jnp.int32,
    )
    section = jnp.where(within >= half_len, 2 * cycle_size - 1 - first_section, first_section)
    places = section * half_len + within % half_len
    seq_ends = jnp.cumsum(length_row, dtype=jnp.int32)
    passed = places[:, None] >= seq_ends[None, :]
    segment = jnp.sum(passed.astype(jnp.int32), axis=1, dtype=jnp.int32)
    offset = places - jnp.sum(jnp.where(passed, length_row[None, :], 0), axis=1, dtype=jnp.int32)
    return (places, segment, offset)


def rotary_embedding(values, positions):
    half_len = values.shape[-1] // 2
    frequency = jnp.exp(
        -math.log(500000.0) * jnp.arange(half_len, dtype=jnp.float32) * 2.0 / values.shape[-1]
    )
    angles = positions.astype(jnp.float32)[:, None] * frequency[None, :]
    cosine = jnp.cos(angles)[:, None, :]
    sine = jnp.sin(angles)[:, None, :]
    lower_half = values[..., :half_len]
    upper_half = values[..., half_len:]
    return jnp.concatenate(
        [lower_half * cosine - upper_half * sine, upper_half * cosine + lower_half * sine], axis=-1
    )


def normalize(values, gain_vec):
    return values * lax.rsqrt(jnp.mean(values * values, axis=-1, keepdims=True) + 1e-05) * gain_vec


def swiglu(gate_val, up_val):
    return jax.nn.silu(gate_val) * up_val


def contract_last(left, right):
    return lax.dot_general(
        left, right, (((1,), (1,)), ((), ())), preferred_element_type=jnp.float32
    )


def contract_first(left, right):
    return lax.dot_general(
        left, right, (((0,), (0,)), ((), ())), preferred_element_type=jnp.float32
    )


VMEM_LIMIT = 22 * 1024 * 1024
LARGE_LIMIT = 22 * 1024 * 1024
MIDDLE_LIMIT = 16 * 1024 * 1024
SMALL_LIMIT = 12 * 1024 * 1024
SMALL = pl.CostEstimate(flops=1, bytes_accessed=1, transcendentals=0)
LARGE = pl.CostEstimate(flops=12_000_000_000, bytes_accessed=1, transcendentals=0)


def pairs_by(distance, size):
    return [(i, i ^ distance) for i in range(size)]


def swap(array, axis, distance):
    return lax.ppermute(array, axis, pairs_by(distance, lax.axis_size(axis)))


class Line:
    def __init__(self, axis):
        index = lax.axis_index(axis)
        size = lax.axis_size(axis)
        self.axis = axis
        self.at_end = ((index == 0) | (index == size - 1)).astype(jnp.int32)[None]
        self.entered = self.halfway = self.leaving = None
        self.sums = {}

    def advance(self, got, entering):
        if self.leaving is not None:
            name, sent = self.leaving
            self.sums[name] = (got["ends"], sent)
        moves = []
        halfway = None
        together = None
        if self.leaving is None and self.halfway is not None:
            name, value = self.entered
            together, summed = both_ways(
                self.at_end, entering[1], self.halfway[1], got["middle"], value, got["ends"]
            )
            halfway = (name, summed)
            moves.append(("middle", summed, self.axis, [(1, 2), (2, 1)]))
        elif self.entered is not None:
            name, value = self.entered
            halfway = (name, add_low(value, got["ends"]))
            moves.append(("middle", halfway[1], self.axis, [(1, 2), (2, 1)]))
        leaving = None
        inwards, outwards = [(0, 1), (3, 2)], [(1, 0), (2, 3)]
        if self.halfway is not None:
            name, value = self.halfway
            if entering is None:
                sent, pairs = add_low(value, got["middle"]), outwards
            else:
                sent, pairs = together, inwards + outwards
                if together is None:
                    sent = either_way(self.at_end, entering[1], value, got["middle"])
            leaving = (name, sent)
            moves.append(("ends", sent, self.axis, pairs))
        elif entering is not None and halfway is not None:
            sent = jnp.where(self.at_end[0] == 1, entering[1], halfway[1])
            moves.append(("ends", sent, self.axis, inwards + outwards))
        elif entering is not None:
            moves.append(("ends", entering[1], self.axis, inwards))
        self.entered, self.halfway, self.leaving = entering, halfway, leaving
        return moves


class Steps:
    def __init__(self, line):
        self.line = line
        self.got = {}
        self.on_line = []
        self.others = []
        self.token = jnp.zeros((8, 128), jnp.float32)

    def wait(self, flying, arrays):
        count = len(flying)
        held = lax.optimization_barrier(
            (self.token,) + tuple(value for _, value in flying) + tuple(arrays)
        )
        self.token = held[0]
        for (name, _), value in zip(flying, held[1:]):
            self.got[name] = value
        return list(held[1 + count :])

    def start(self, moves):
        return [(name, lax.ppermute(value, axis, pairs)) for name, value, axis, pairs in moves]

    def step(self, moves=(), summed=None, late=None, carry=(), first=()):
        moves, carry, first = list(moves), list(carry), list(first)
        arrays = [move[1] for move in moves] + carry
        fresh = [summed[1]] if summed is not None and summed[1] is not None else []
        together = summed is not None and not fresh and summed[0] not in self.got
        together = together or not self.on_line
        flying = self.on_line + (self.others if together else [])
        held = self.wait(flying, fresh + first + (arrays if together else []))
        held_fresh, held = held[: len(fresh)], held[len(fresh) :]
        held_first, held = held[: len(first)], held[len(first) :]
        entering = summed
        if summed is not None:
            entering = (summed[0], held_fresh[0] if fresh else self.take(summed[0]))
        self.on_line = self.start(self.line.advance(self.got, entering))
        if not together:
            held = self.wait(self.others, arrays)
        moves = [
            (name, value, axis, pairs) for (name, _, axis, pairs), value in zip(moves, held)
        ]
        self.others = self.start(moves + (late() if late is not None else []))
        return held[len(moves) :] + held_first

    def take(self, name):
        return self.got.pop(name)


def in_vmem(kernel, out_shape, *args, scalars=0):
    specs = [pl.BlockSpec(memory_space=pltpu.SMEM)] * scalars
    specs += [pl.BlockSpec(memory_space=pltpu.VMEM)] * (len(args) - scalars)
    return pl.pallas_call(
        kernel,
        out_shape=out_shape,
        in_specs=specs,
        out_specs=[pl.BlockSpec(memory_space=pltpu.VMEM)] * len(out_shape),
        compiler_params=pltpu.CompilerParams(vmem_limit_bytes=SMALL_LIMIT),
        cost_estimate=SMALL,
    )(*args)


def low(*shape):
    return jax.ShapeDtypeStruct(shape, jnp.bfloat16)


def full(*shape):
    return jax.ShapeDtypeStruct(shape, jnp.float32)


def store_seen(ref, value, distance, count):
    width = value.shape[-1] // count
    for block in range(count):
        there = block ^ distance
        ref[: value.shape[0], block * width : (block + 1) * width] = value[
            :, there * width : (there + 1) * width
        ]


def prepare_kernel(count, index_ref, x_ref, own_ref, *sends):
    rows, width = own_ref.shape[0], own_ref.shape[1] // count
    first = pl.multiple_of(index_ref[1] * rows, rows)
    for block in range(count):
        column = pl.multiple_of((index_ref[0] ^ block) * width, width)
        own_ref[:, block * width : (block + 1) * width] = x_ref[
            pl.ds(first, rows), pl.ds(column, width)
        ]
    for k, send in enumerate(sends, 1):
        store_seen(send, own_ref[...], k, count)


def prepare(x, index, count):
    rows, width = x.shape[0] // 2, x.shape[1]
    return in_vmem(
        functools.partial(prepare_kernel, count), [low(rows, width)] * count, index, x, scalars=1
    )


def turns_kernel(offset_ref, cos_ref, sin_ref):
    lane = lax.broadcasted_iota(jnp.int32, cos_ref.shape, 2)
    place = lax.rem(lane, HEAD_SIZE // 2).astype(jnp.float32)
    frequency = jnp.exp(-math.log(500000.0) * place * 2.0 / HEAD_SIZE)
    angle = offset_ref[...] * frequency
    cos_ref[...] = jnp.cos(angle)
    sin_ref[...] = jnp.sin(angle)


def join_kernel(*refs):
    out_ref = refs[-1]
    rows = refs[0].shape[0]
    for i, ref in enumerate(refs[:-1]):
        out_ref[i * rows : (i + 1) * rows, :] = ref[:rows, :]


def join_rows(arrays, rows):
    def kernel(*refs):
        for i, ref in enumerate(refs[:-1]):
            refs[-1][i * rows : (i + 1) * rows, :] = ref[:rows, :]

    return in_vmem(kernel, [low(rows * len(arrays), arrays[0].shape[1])], *arrays)[0]


def join(own, others):
    rows, width = own.shape
    return in_vmem(join_kernel, [low(rows * (1 + len(others)), width)], own, *others)[0]


def fold_kernel(count, first_ref, came_ref, own_ref, *sends):
    rows = own_ref.shape[0]
    for k in range(count):
        here = slice(k * rows, (k + 1) * rows)
        total = first_ref[here, :].astype(jnp.float32) + came_ref[here, :].astype(jnp.float32)
        total = total.astype(jnp.bfloat16)
        if k == 0:
            own_ref[...] = total
        else:
            store_seen(sends[k - 1], total, k, count)


def fold(first, came, count):
    rows, width = first.shape[0] // count, first.shape[1]
    return in_vmem(
        functools.partial(fold_kernel, count), [low(rows, width)] * count, first, came
    )


def total_of(refs):
    total = refs[0][...].astype(jnp.float32)
    for ref in refs[1:]:
        total = total + ref[...].astype(jnp.float32)
    return total


def middle_kernel(count, in_ref, gain_ref, *refs):
    parts, (middle_ref, normed_ref, *sends) = refs[:count], refs[count:]
    middle = in_ref[...].astype(jnp.float32) + total_of(parts)
    middle_ref[...] = middle
    mean = jnp.mean(middle * middle, axis=-1, keepdims=True)
    normed = (middle * lax.rsqrt(mean + 1e-05) * gain_ref[...]).astype(jnp.bfloat16)
    normed_ref[...] = normed
    for k in range(1, count):
        store_seen(sends[k - 1], normed, k, count)


def norm_back(d_normed, x, gain):
    scale = lax.rsqrt(jnp.mean(x * x, axis=-1, keepdims=True) + 1e-05)
    unit = x * scale
    d_unit = d_normed * gain
    d_x = scale * (d_unit - unit * jnp.mean(d_unit * unit, axis=-1, keepdims=True))
    return d_x, jnp.sum(d_normed * unit, axis=0, keepdims=True)


def branch_back_kernel(count, middle_ref, gain_ref, cot_ref, *refs):
    parts, (d_middle_ref, d_gain_ref, branch_ref, *sends) = refs[:count], refs[count:]
    d_x, d_gain_ref[...] = norm_back(total_of(parts), middle_ref[...], gain_ref[...])
    d_middle = cot_ref[...].astype(jnp.float32) + d_x
    d_middle_ref[...] = d_middle
    branch = d_middle.astype(jnp.bfloat16)
    branch_ref[...] = branch
    for k in range(1, count):
        store_seen(sends[k - 1], branch, k, count)


def in_grad_kernel(count, in_ref, gain_ref, d_middle_ref, *refs):
    parts, (grad_ref, d_gain_ref) = refs[:count], refs[count:]
    x = in_ref[...].astype(jnp.float32)
    d_x, d_gain_ref[...] = norm_back(total_of(parts), x, gain_ref[...])
    grad_ref[...] = (d_middle_ref[...] + d_x).astype(jnp.bfloat16)


def spec_of(array, block, index):
    if block == array.shape:
        return pl.BlockSpec(block, index, pipeline_mode=pl.Buffered(1))
    return pl.BlockSpec(block, index)


def gridded(kernel, steps, ins, outs, scalars=(), limit=None, cost=SMALL):
    return pl.pallas_call(
        kernel,
        grid=(steps,),
        in_specs=[pl.BlockSpec(memory_space=pltpu.SMEM)] * len(scalars)
        + [spec_of(array, block, index) for array, block, index in ins],
        out_specs=[pl.BlockSpec(block, index) for _, block, index in outs],
        out_shape=[shape for shape, _, _ in outs],
        compiler_params=pltpu.CompilerParams(vmem_limit_bytes=limit or MIDDLE_LIMIT),
        cost_estimate=cost,
    )(*scalars, *[array for array, _, _ in ins])


def row_blocks(array, rows):
    return (array, (rows, array.shape[1]), lambda i: (i, 0))


def add_low(left, right):
    right = right[:, : left.shape[1]]
    return (left.astype(jnp.float32) + right.astype(jnp.float32)).astype(jnp.bfloat16)


def either_way(at_end, fresh, value, came):
    total = add_low(value, came)
    width = max(fresh.shape[1], value.shape[1])
    if fresh.shape[1] < width:
        fresh = jnp.pad(fresh, ((0, 0), (0, width - fresh.shape[1])))
    if total.shape[1] < width:
        total = jnp.pad(total, ((0, 0), (0, width - total.shape[1])))
    return jnp.where(at_end[0] == 1, fresh, total)


def both_ways_kernel(at_end_ref, fresh_ref, half_ref, across_ref, value_ref, came_ref, sent_ref, sum_ref):
    def add(left_ref, right_ref):
        total = left_ref[...].astype(jnp.float32) + right_ref[...].astype(jnp.float32)
        return total.astype(jnp.bfloat16)

    sum_ref[...] = add(value_ref, came_ref)
    sent_ref[...] = jnp.where(at_end_ref[0] == 1, fresh_ref[...], add(half_ref, across_ref))


def both_ways(at_end, *arrays):
    rows = math.gcd(arrays[0].shape[0], 256)
    ins = [row_blocks(array, rows) for array in arrays]
    outs = [row_blocks(low(*arrays[0].shape), rows)] * 2
    return gridded(both_ways_kernel, arrays[0].shape[0] // rows, ins, outs, scalars=(at_end,))


def settled(at_end, came_ref, sent_ref, columns):
    return jnp.where(at_end == 1, came_ref[:, columns], sent_ref[:, columns]).astype(jnp.float32)


def settle_kernel(count, at_end_ref, index_ref, *refs):
    out_ref = refs[-1]
    width = out_ref.shape[1] // count
    for k in range(count):
        column = pl.multiple_of((index_ref[0] ^ k) * width, width)
        out_ref[:, pl.ds(column, width)] = settled(
            at_end_ref[0], refs[2 * k], refs[2 * k + 1], slice(0, width)
        )


def settle(at_end, index, pairs, width, cost=SMALL):
    count = len(pairs)
    arrays = [array for pair in pairs for array in pair]
    depth = arrays[0].shape[0]
    rows = math.gcd(depth, 128)
    ins = [(array, (rows, width), lambda i: (i, 0)) for array in arrays]
    outs = [row_blocks(full(depth, width * count), rows)]
    kernel = functools.partial(settle_kernel, count)
    return gridded(kernel, depth // rows, ins, outs, scalars=(at_end, index), cost=cost)[0]


def settle_attention_kernel(count, q_width, kv_width, at_end_ref, index_ref, *refs):
    q_ref, k_ref, v_ref, o_ref = refs[-4:]
    o_width = o_ref.shape[1] // count
    o_first = q_width + kv_width
    kvs = []
    for k in range(count):
        came_ref, sent_ref = refs[2 * k], refs[2 * k + 1]
        column = pl.multiple_of((index_ref[0] ^ k) * q_width, q_width)
        q_ref[:, pl.ds(column, q_width)] = settled(
            at_end_ref[0], came_ref, sent_ref, slice(0, q_width)
        )
        column = pl.multiple_of((index_ref[0] ^ k) * o_width, o_width)
        o_ref[:, pl.ds(column, o_width)] = settled(
            at_end_ref[0], came_ref, sent_ref, slice(o_first, o_first + o_width)
        )
        kvs.append(settled(at_end_ref[0], came_ref, sent_ref, slice(q_width, o_first)))
    ordered = []
    for place in range(count):
        kv = kvs[0]
        for k in range(1, count):
            kv = jnp.where((index_ref[0] ^ k) == place, kvs[k], kv)
        ordered.append(kv)
    k_ref[...] = jnp.concatenate([kv[:, : kv_width // 2] for kv in ordered], axis=1)
    v_ref[...] = jnp.concatenate([kv[:, kv_width // 2 :] for kv in ordered], axis=1)


def settle_attention(at_end, index, pairs, q_width, kv_width):
    count = len(pairs)
    arrays = [array for pair in pairs for array in pair]
    depth = arrays[0].shape[0]
    width = min(array.shape[1] for array in arrays)
    o_width = width - q_width - kv_width
    rows = math.gcd(depth, 256)
    ins = [(array, (rows, width), lambda i: (i, 0)) for array in arrays]
    widths = (q_width, kv_width // 2, kv_width // 2, o_width)
    outs = [row_blocks(full(depth, each * count), rows) for each in widths]
    kernel = functools.partial(settle_attention_kernel, count, q_width, kv_width)
    return gridded(kernel, depth // rows, ins, outs, scalars=(at_end, index))


def d_qkv_kernel(at_end_ref, here_ref, came_ref, sent_ref, dq_ref, cos_ref, sin_ref, out_ref):
    lanes = 2 * HEAD_SIZE
    half, q_width = dq_ref.shape[1], dq_ref.shape[2]
    cycle = came_ref.shape[1] // lanes // 2
    for core_side in range(2):
        column = pl.multiple_of((core_side * cycle + here_ref[0]) * lanes, lanes)
        d_kv = settled(at_end_ref[0], came_ref, sent_ref, pl.ds(column, lanes))
        cosine, sine = of_keys(cos_ref[core_side], sin_ref[core_side])
        d_kv = turned(d_kv, cosine, -sine).astype(jnp.bfloat16)
        rows = slice(core_side * half, (core_side + 1) * half)
        out_ref[rows, :q_width] = dq_ref[core_side]
        out_ref[rows, q_width:] = d_kv


def rows_back_kernel(count, index_ref, own_ref, other_ref, out_ref):
    rows, width = own_ref.shape[0], own_ref.shape[1] // count
    for ref, core in ((own_ref, index_ref[1]), (other_ref, 1 - index_ref[1])):
        first = pl.multiple_of(core * rows, rows)
        for block in range(count):
            column = pl.multiple_of((index_ref[0] ^ block) * width, width)
            out_ref[pl.ds(first, rows), pl.ds(column, width)] = ref[
                :, block * width : (block + 1) * width
            ]


def result_kernel(middle_ref, *refs):
    refs[-1][...] = (middle_ref[...] + total_of(refs[:-1])).astype(jnp.bfloat16)


def still(array):
    zeros = (0,) * len(array.shape)
    return (array, array.shape, lambda i: zeros)


def dot(left, right):
    return jnp.dot(left, right, preferred_element_type=jnp.float32)


def both(mine_ref, other_ref, weight):
    return jnp.concatenate([dot(mine_ref[...], weight), dot(other_ref[...], weight)], axis=0)


def chosen(here_steps, count, own, fetched, passed):
    here = pl.program_id(0) < here_steps
    weights = []
    for which in (0, 1):
        pieces = [own[which][...]]
        for k in range(count - 1):
            pieces.append(
                jnp.where(here, fetched[2 * k + which][...], passed[2 * k + which][...])
            )
        weights.append(jnp.concatenate(pieces, axis=0))
    return weights


def gate_up_kernel(count, here_steps, *refs):
    x_refs, refs = refs[:2], refs[2:]
    own, fetched, passed = refs[:2], refs[2 : 2 * count], refs[2 * count : 4 * count - 2]
    gate_ref, up_ref, hidden_ref = refs[4 * count - 2 :]
    weights = chosen(here_steps, count, own, fetched, passed)
    lin = both(*x_refs, jnp.concatenate(weights, axis=1))
    gate, up = lin[:, : lin.shape[1] // 2], lin[:, lin.shape[1] // 2 :]
    gate_ref[...] = gate.astype(jnp.bfloat16)
    up_ref[...] = up.astype(jnp.bfloat16)
    hidden_ref[...] = (gate * jax.nn.sigmoid(gate) * up).astype(jnp.bfloat16)


def columns_kernel(count, here_steps, *refs):
    own, fetched, passed = refs[:2], refs[2 : 2 * count], refs[2 * count : 4 * count - 2]
    wg_ref, wu_ref = refs[4 * count - 2 :]
    wg_ref[...], wu_ref[...] = chosen(here_steps, count, own, fetched, passed)


def column_blocks(own_gate, own_up, fetched, passed):
    depth, units = own_gate.shape
    block = math.gcd(units // 2, 256)
    steps, half = units // block, units // block // 2
    ins = [(w, (depth, block), lambda i: (0, i)) for w in (own_gate, own_up)]
    for arrays, step in (
        (fetched, lambda i: jnp.minimum(i, half - 1)),
        (passed, lambda i: jnp.maximum(i - half, 0)),
    ):
        for array in arrays:
            ins.append((array, (depth, block), lambda i, step=step: (0, step(i))))
            ins.append((array, (depth, block), lambda i, step=step: (0, half + step(i))))
    return ins, block, steps, half


def gate_up(x, *weights):
    tokens, units = 2 * x[0].shape[0], weights[0].shape[1]
    ins, block, steps, half = column_blocks(*weights)
    outs = [(low(tokens, units), (tokens, block), lambda i: (0, i))] * 3
    kernel = functools.partial(gate_up_kernel, len(weights[2]) + 1, half)
    return gridded(kernel, steps, [still(x[0]), still(x[1])] + ins, outs, limit=VMEM_LIMIT)


def whole_columns(*weights):
    depth, units = weights[0].shape
    ins, block, steps, half = column_blocks(*weights)
    count = len(weights[2]) + 1
    outs = [(low(count * depth, units), (count * depth, block), lambda i: (0, i))] * 2
    return gridded(functools.partial(columns_kernel, count, half), steps, ins, outs)


def units_back_kernel(count, *refs):
    d_refs, refs = refs[:2], refs[2:]
    pieces, (gate_ref, up_ref, d_gate_ref, d_up_ref) = refs[:count], refs[count:]
    weight = jnp.concatenate([ref[...] for ref in pieces], axis=0)
    d_hidden = both(*d_refs, weight)
    gate, up = gate_ref[...].astype(jnp.float32), up_ref[...].astype(jnp.float32)
    chance = jax.nn.sigmoid(gate)
    d_up_ref[...] = (d_hidden * (gate * chance)).astype(jnp.bfloat16)
    slope = chance + gate * chance * (1.0 - chance)
    d_gate_ref[...] = (d_hidden * up * slope).astype(jnp.bfloat16)


def units_back(d_out, pieces, gate, up):
    tokens, units = gate.shape
    depth = pieces[0].shape[0]
    block = math.gcd(units, 512)

    def by_columns(array, rows):
        return (array, (rows, block), lambda i: (0, i))

    ins = [still(d_out[0]), still(d_out[1])] + [by_columns(piece, depth) for piece in pieces]
    ins += [by_columns(gate, tokens), by_columns(up, tokens)]
    outs = [by_columns(low(tokens, units), tokens)] * 2
    kernel = functools.partial(units_back_kernel, len(pieces))
    return gridded(kernel, units // block, ins, outs, limit=LARGE_LIMIT)


def rows_sum_kernel(terms, *refs):
    first_ref, second_ref = refs[-2:]
    total = 0.0
    for left_ref, right_ref in zip(refs[:terms], refs[terms : 2 * terms]):
        total = total + contract_last(left_ref[...], right_ref[...])
    total = total.astype(jnp.bfloat16)
    half = first_ref.shape[0]
    first_ref[...] = total[:half]
    second_ref[...] = total[half:]


def rows_sum(lefts, rights, cost=SMALL):
    tokens, width = lefts[0].shape[0], rights[0].shape[0]
    block = math.gcd(width, 512)
    ins = [still(left) for left in lefts]
    ins += [(right, (block, right.shape[1]), lambda i: (i, 0)) for right in rights]
    outs = [(low(tokens // 2, width), (tokens // 2, block), lambda i: (0, i))] * 2
    kernel = functools.partial(rows_sum_kernel, len(lefts))
    return gridded(kernel, width // block, ins, outs, cost=cost)


def half_rows_kernel(terms, *refs):
    total = 0.0
    for left_ref, right_ref in zip(refs[:terms], refs[terms : 2 * terms]):
        total = total + contract_last(left_ref[...], right_ref[...])
    refs[-1][...] = total.astype(jnp.bfloat16)


def half_rows(lefts, rights, which, cost=SMALL):
    half, width = lefts[0].shape[0] // 2, rights[0].shape[0]
    block = math.gcd(width, 512)
    ins = [(left, (half, left.shape[1]), lambda i: (which, 0)) for left in lefts]
    ins += [(right, (block, right.shape[1]), lambda i: (i, 0)) for right in rights]
    outs = [(low(half, width), (half, block), lambda i: (0, i))]
    kernel = functools.partial(half_rows_kernel, len(lefts))
    return gridded(kernel, width // block, ins, outs, cost=cost)[0]


def weight_grad_kernel(count, terms, turn, *refs):
    if turn:
        side, refs = refs[0][0], refs[1:]
    outs = refs[3 * terms :]
    step = pl.program_id(0)
    first = 0
    for term in range(terms):
        mine_ref, other_ref, right_ref = refs[3 * term : 3 * term + 3]
        half = mine_ref.shape[0]
        grad = contract_first(mine_ref[...], right_ref[:half, :])
        grad = grad + contract_first(other_ref[...], right_ref[half:, :])
        grad = grad.astype(jnp.bfloat16)
        columns = grad.shape[1]
        for k in range(count):

            @pl.when(step == k)
            def _(k=k, first=first, grad=grad, columns=columns):
                if turn:
                    part = columns // 2
                    outs[k][:, pl.ds(pl.multiple_of(side * part, part), part)] = grad[:, :part]
                    outs[k][:, pl.ds(pl.multiple_of((1 - side) * part, part), part)] = grad[:, part:]
                else:
                    outs[k][:, first : first + columns] = grad

        first += columns


def weight_grad(terms, count, side=None, packs=None):
    columns = sum(right.shape[1] for _, _, right in terms)
    depth = terms[0][0].shape[1] // count
    packs = range(count) if packs is None else packs
    first, apart = packs[0], packs[-1] - packs[0]
    apart = apart // max(len(packs) - 1, 1)
    ins = []
    if side is not None:
        ins.append((side, None, None))
    for mine, other, right in terms:
        for left in (mine, other):
            ins.append((left, (left.shape[0], depth), lambda i: (0, first + apart * i)))
        ins.append(still(right))
    specs = [
        pl.BlockSpec(memory_space=pltpu.SMEM) if block is None else pl.BlockSpec(block, index)
        for _, block, index in ins
    ]
    return pl.pallas_call(
        functools.partial(weight_grad_kernel, len(packs), len(terms), side is not None),
        grid=(len(packs),),
        in_specs=specs,
        out_specs=[pl.BlockSpec((depth, columns), lambda i: (0, 0))] * len(packs),
        out_shape=[low(depth, columns)] * len(packs),
        compiler_params=pltpu.CompilerParams(vmem_limit_bytes=MIDDLE_LIMIT),
        cost_estimate=SMALL,
    )(*[array for array, _, _ in ins])


def turned(lin, cosine, sine):
    width = lin.shape[-1]
    quarter = HEAD_SIZE // 2
    lane = lax.broadcasted_iota(jnp.int32, lin.shape, lin.ndim - 1)
    first = lax.rem(lane, HEAD_SIZE) < quarter
    partner = jnp.where(
        first,
        -pltpu.roll(lin, width - quarter, lin.ndim - 1),
        pltpu.roll(lin, quarter, lin.ndim - 1),
    )
    return lin * cosine + partner * sine


def side_by_side(table, width):
    return jnp.concatenate([table] * (width // table.shape[-1]), axis=-1)


def of_keys(cosine, sine):
    keys = lax.broadcasted_iota(jnp.int32, cosine.shape, 1) < HEAD_SIZE
    return jnp.where(keys, cosine, 1.0), jnp.where(keys, sine, 0.0)


def qkv_kernel(count, q_width, kv_width, side_ref, *refs):
    x_refs, (gain_ref, cos_ref, sin_ref), refs = refs[:2], refs[2:5], refs[5:]
    own_ref, fetched, passed_ref, refs = refs[0], refs[1:count], refs[count], refs[count + 1 :]
    normed_refs, (q_ref, kv_ref, wqkv_ref, wo_ref) = refs[:2], refs[2:]
    qkv_width = q_width + kv_width
    depth = own_ref.shape[0]
    half = depth // 2

    @pl.when(pl.program_id(0) == 0)
    def _():
        wqkv_ref[:depth, :] = own_ref[:, :qkv_width]
        wo_ref[:depth, :] = own_ref[:, qkv_width:]
        for k in range(1, count):
            for which, piece in (
                (side_ref[0], fetched[k - 1][:half, :]),
                (1 - side_ref[0], passed_ref[(k - 1) * half : k * half, :]),
            ):
                first = pl.multiple_of(k * depth + which * half, half)
                wqkv_ref[pl.ds(first, half), :] = piece[:, :qkv_width]
                wo_ref[pl.ds(first, half), :] = piece[:, qkv_width:]

    for i in range(2):
        x = x_refs[i][...].astype(jnp.float32)
        mean = jnp.mean(x * x, axis=-1, keepdims=True)
        normed = (x * lax.rsqrt(mean + 1e-05) * gain_ref[...]).astype(jnp.bfloat16)
        normed_refs[i][...] = normed
        lin = dot(normed, wqkv_ref[...])
        cosine, sine = cos_ref[i], sin_ref[i]
        q = turned(lin[:, :q_width], side_by_side(cosine, q_width), side_by_side(sine, q_width))
        q_ref[i] = q.astype(jnp.bfloat16)
        kv = turned(lin[:, q_width:], *of_keys(cosine, sine))
        kv_ref[i] = kv.astype(jnp.bfloat16)


def project_qkv(side, x, gain, cosine, sine, own, fetched, passed, q_width, kv_width):
    half_rows, width = x[0].shape
    qkv_width = q_width + kv_width
    block = math.gcd(half_rows, 128)

    def rows_of(array, columns):
        return (array, (block, columns), lambda i: (i, 0))

    def of_both(array, columns):
        return (array, (2, block, columns), lambda i: (0, i, 0))

    lanes = cosine.shape[-1]
    ins = [rows_of(x[0], width), rows_of(x[1], width), still(gain)]
    ins += [of_both(cosine, lanes), of_both(sine, lanes)]
    ins += [still(array) for array in (own, *fetched, passed)]
    o_width = own.shape[1] - qkv_width
    outs = [rows_of(low(half_rows, width), width)] * 2
    outs += [of_both(low(2, half_rows, q_width), q_width), of_both(low(2, half_rows, kv_width), kv_width)]
    outs += [still(low(width, qkv_width)), still(low(width, o_width))]
    kernel = functools.partial(qkv_kernel, len(fetched) + 1, q_width, kv_width)
    return gridded(kernel, half_rows // block, ins, outs, scalars=(side,))


def shares(q, k, visible):
    scores = jnp.where(visible, contract_last(q, k), -1e30)
    weights = jnp.exp(scores - jnp.max(scores, axis=-1, keepdims=True))
    return weights, 1.0 / jnp.sum(weights, axis=-1, keepdims=True)


def load_attention(q_ref, place_ref, start_ref, key_place_ref, kv_refs):
    q = q_ref[...]
    q = q.reshape(q.shape[0] * q.shape[1], q.shape[2])
    kv = jnp.concatenate([ref[...].reshape(q.shape[0], 2 * HEAD_SIZE) for ref in kv_refs], axis=0)
    q = q * jnp.bfloat16(1.0 / math.sqrt(HEAD_SIZE))
    key_place = key_place_ref[0]
    visible = (key_place <= place_ref[0]) & (key_place >= start_ref[0])
    return q, kv[:, :HEAD_SIZE], kv[:, HEAD_SIZE:], visible


def attend_kernel(groups, q_ref, place_ref, start_ref, key_place_ref, wo_ref, *refs):
    kv_refs, (out_ref, first_ref, second_ref) = refs[:-3], refs[-3:]
    q, k, v, visible = load_attention(q_ref, place_ref, start_ref, key_place_ref, kv_refs)
    mixed = []
    for g in range(groups):
        weights, parts = shares(q[:, g * HEAD_SIZE : (g + 1) * HEAD_SIZE], k, visible)
        mixed.append(dot(weights.astype(jnp.bfloat16), v) * parts)
    out = jnp.concatenate(mixed, axis=1).astype(jnp.bfloat16)
    out_ref[...] = out.reshape(out_ref.shape)
    branch = contract_last(out, wo_ref[...]).astype(jnp.bfloat16)
    half = first_ref.shape[0]
    first_ref[...] = branch[:half]
    second_ref[...] = branch[half:]


def attend_back_kernel(
    groups,
    here_ref,
    q_ref,
    mine_ref,
    other_ref,
    cos_ref,
    sin_ref,
    place_ref,
    start_ref,
    key_place_ref,
    wo_ref,
    *refs,
):
    kv_refs, (dq_ref, dkv_ref) = refs[:-2], refs[-2:]
    q, k, v, visible = load_attention(q_ref, place_ref, start_ref, key_place_ref, kv_refs)
    d_out = both(mine_ref, other_ref, wo_ref[...]).astype(jnp.bfloat16)
    scale = 1.0 / math.sqrt(HEAD_SIZE)
    d_q, d_k, d_v = [], 0.0, 0.0
    for g in range(groups):
        q_head = q[:, g * HEAD_SIZE : (g + 1) * HEAD_SIZE]
        d_head = d_out[:, g * HEAD_SIZE : (g + 1) * HEAD_SIZE]
        weights, parts = shares(q_head, k, visible)
        probs = weights * parts
        d_probs = contract_last(d_head, v)
        row_delta = jnp.sum(probs * d_probs, axis=-1, keepdims=True)
        d_scores = (probs * (d_probs - row_delta)).astype(jnp.bfloat16)
        d_q.append(dot(d_scores, k) * scale)
        d_k = d_k + contract_first(q_head, d_scores)
        d_v = d_v + contract_first(d_head, probs.astype(jnp.bfloat16))
    d_q = jnp.concatenate(d_q, axis=1)
    cosine = cos_ref[...].reshape(q.shape[0], -1)
    sine = sin_ref[...].reshape(q.shape[0], -1)
    d_q = turned(d_q, side_by_side(cosine, q.shape[1]), -side_by_side(sine, q.shape[1]))
    dq_ref[...] = d_q.astype(jnp.bfloat16).reshape(dq_ref.shape)
    d_kv = jnp.concatenate([d_k, d_v], axis=0).T.astype(jnp.bfloat16)
    half, lanes, cycle = dkv_ref.shape[0], 2 * HEAD_SIZE, len(kv_refs)
    for j in range(cycle):
        for core_side in range(2):
            first = (2 * j + core_side) * half
            column = pl.multiple_of((core_side * cycle + (here_ref[0] ^ j)) * lanes, lanes)
            dkv_ref[:, pl.ds(column, lanes)] = d_kv[first : first + half]


def of_pack(array, half):
    return (array, (2, half, array.shape[-1]), lambda p: (0, p, 0))


def place_blocks(places):
    return [(array, (1,) + array.shape[1:], lambda p: (p, 0, 0)) for array in places]


def attend(q, places, wo, kvs, packs, groups):
    half = q.shape[1] // packs
    width = wo.shape[0]
    ins = [of_pack(q, half)] + place_blocks(places) + [still(wo)] + [of_pack(kv, half) for kv in kvs]
    outs = [of_pack(low(*q.shape), half)]
    outs += [(low(q.shape[1], width), (half, width), lambda p: (p, 0))] * 2
    return gridded(functools.partial(attend_kernel, groups), packs, ins, outs)


def attend_back(here, q, d_branch, cosine, sine, places, wo, kvs, packs, groups):
    half = q.shape[1] // packs
    cycle = len(kvs)
    ins = [of_pack(q, half)]
    ins += [(array, (half, array.shape[1]), lambda p: (p, 0)) for array in d_branch]
    ins += [of_pack(cosine, half), of_pack(sine, half)] + place_blocks(places) + [still(wo)]
    ins += [of_pack(kv, half) for kv in kvs]
    lanes = 2 * HEAD_SIZE
    outs = [of_pack(low(*q.shape), half)]
    outs.append((low(q.shape[1], 2 * cycle * lanes), (half, 2 * cycle * lanes), lambda p: (p, 0)))
    kernel = functools.partial(attend_back_kernel, groups)
    return gridded(kernel, packs, ins, outs, scalars=(here,))


def split_heads(
    hidden_in,
    out_cotangent,
    norm1_gain,
    q_weight,
    key_projection_weight,
    value_projection_weight,
    o_weight,
    norm2_gain,
    gate_weight,
    up_weight,
    down_weight,
    seq_lengths,
    span_order,
):
    packs = lax.axis_size("fsdp")
    cycle = lax.axis_size("ctx")
    pack = lax.axis_index("fsdp")
    core = lax.axis_index("tp")
    here = lax.axis_index("ctx")
    rows = hidden_in.shape[0]
    half = rows // 2
    tokens = packs * rows
    depth = q_weight.shape[0]
    width = depth * packs
    q_width = q_weight.shape[1] // packs
    k_width = key_projection_weight.shape[1] // packs
    ff_width = gate_weight.shape[1] // packs
    ff_half = ff_width // 2
    groups = q_width // k_width
    far = range(1, packs)
    steps = Steps(Line("ctx"))
    kept = {}


    def columns(weight, k, count, first=0, of=None):
        return lax.dynamic_slice_in_dim(weight, (pack ^ k) * (of or count) + first, count, 1)

    def to_pack(name, k, array):
        return ((name, k), array, "fsdp", pairs_by(k, packs))

    def send_all(name, arrays):
        return [to_pack(name, k, array) for k, array in zip(far, arrays)]

    def arrived(name):
        return [steps.take((name, k)) for k in far]

    def to_core(name, array):
        return [(name, array, "tp", pairs_by(1, 2))]

    def to_rows(name, first):
        kept[name], *others = fold(first, steps.take(name), packs)
        return send_all(name, others)

    def joined(name, own, others):
        kept[name] = join(own, others)
        return to_core(name, kept[name])

    def unwaited(name):
        return dict(steps.others)[name]

    def both_of(name):
        return kept[name], steps.take(name)

    index = jnp.stack([pack, core]).astype(jnp.int32)
    here_arg = here.astype(jnp.int32)[None]
    side_arg = here_arg & 1
    at_end = steps.line.at_end

    own_in, *in_moves = prepare(hidden_in, index, packs)
    own_cot, *cot_moves = prepare(out_cotangent, index, packs)

    side = here & 1
    weights = (q_weight, key_projection_weight, value_projection_weight, o_weight)
    widths = (q_width, k_width, k_width, q_width)

    def attention_piece(k, first, count):
        return jnp.concatenate(
            [
                lax.dynamic_slice(weight, (first, (pack ^ k) * each), (count, each))
                for weight, each in zip(weights, widths)
            ],
            axis=1,
        )

    meta = jnp.concatenate([span_order[0], seq_lengths[0]])
    order_len, meta_len = span_order.shape[1], meta.shape[0]
    metas = jnp.concatenate([(meta // 32).astype(jnp.bfloat16), (meta % 32).astype(jnp.bfloat16)])
    info = jnp.stack(
        [
            jnp.pad(jnp.concatenate([norm1_gain, metas]), (0, sum(widths) - depth - 2 * meta_len)),
            jnp.pad(norm2_gain, (0, sum(widths) - depth)),
        ]
    )
    info_rows = jnp.pad(info, ((0, 14), (0, 0)))
    row_half = depth // 2
    steps.step(
        [
            to_pack(
                "attention",
                k,
                jnp.concatenate([attention_piece(k, side * row_half, row_half), info_rows], axis=0),
            )
            for k in far
        ]
    )
    pieces = []

    def pass_rows():
        pieces.extend(arrived("attention"))
        rows_on = join_rows(pieces, row_half)
        return [("attention_rows", rows_on, "ctx", pairs_by(1, cycle))]

    steps.step(send_all("in", in_moves), late=pass_rows)
    infos = jnp.stack([info] + [piece[row_half : row_half + 2] for piece in pieces])
    all_gains = infos[:, :, :depth].astype(jnp.float32)
    gain_one = all_gains[:, 0].reshape(1, -1)
    gain_two = all_gains[:, 1].reshape(1, -1)
    metas = infos[:, 0, depth : depth + 2 * meta_len].astype(jnp.int32)
    metas = metas[:, :meta_len] * 32 + metas[:, meta_len:]
    orders, lengths = metas[:, :order_len], metas[:, order_len:]

    others = jnp.stack([here ^ j for j in range(cycle)])
    first = jnp.sum(
        jnp.where(
            others[None, :, None] == jnp.arange(order_len, dtype=jnp.int32)[None, None, :],
            orders[:, None, :],
            0,
        ),
        axis=2,
    )
    halves = jnp.stack([core, core ^ 1])[None, None, :]
    section = jnp.where(halves == 0, first[:, :, None], 2 * cycle - 1 - first[:, :, None])
    places = section[..., None] * half + jnp.arange(half, dtype=jnp.int32)
    places = places.reshape(packs, cycle * rows)
    starts = jnp.zeros_like(places)
    end = jnp.zeros((packs, 1), jnp.int32)
    for j in range(lengths.shape[1]):
        end = end + lengths[:, j : j + 1]
        starts = jnp.where(places >= end, end, starts)
    place_args = (places[:, :rows, None], starts[:, :rows, None], places[:, None, :])
    offsets = (places - starts)[:, :rows].reshape(packs, 2, half).transpose(1, 0, 2)
    cosine, sine = in_vmem(
        turns_kernel,
        [full(2, tokens // 2, 2 * HEAD_SIZE)] * 2,
        offsets.astype(jnp.float32).reshape(2, tokens // 2, 1),
    )


    def two_halves(weight, k):
        return jnp.concatenate(
            [
                columns(weight, k, ff_half, side * ff_half, ff_width),
                columns(weight, k, ff_half, (1 - side) * ff_half, ff_width),
            ],
            axis=1,
        )

    def fetch(ks):
        return [
            to_pack(
                "gate_up",
                k,
                jnp.concatenate(
                    [
                        columns(weight, k, ff_half, side * ff_half, ff_width)
                        for weight in (gate_weight, up_weight)
                    ],
                    axis=1,
                ),
            )
            for k in ks
        ]

    def to_neighbour(k):
        return [(("neighbour", k), fetched[k], "ctx", pairs_by(1, cycle))]

    fetched = {}
    own_piece = attention_piece(0, 0, depth)
    cosine, sine, own_piece, *place_args = steps.step(
        fetch([1, 2]), carry=(cosine, sine, own_piece, *place_args)
    )
    all_in = join(own_in, arrived("in"))
    all_in = (all_in, swap(all_in, "tp", 1))
    normed_mine, normed_other, q_rot, kv_own, wqkv, wo = project_qkv(
        side_arg,
        all_in,
        gain_one,
        cosine,
        sine,
        own_piece,
        pieces,
        steps.take("attention_rows"),
        q_width,
        2 * k_width,
    )
    normed_one = (normed_mine, normed_other)
    steps.step(
        [(("kv", j), kv_own, "ctx", pairs_by(j, cycle)) for j in range(1, cycle)] + fetch([3])
    )
    fetched[1], fetched[2] = steps.take(("gate_up", 1)), steps.take(("gate_up", 2))
    steps.step(send_all("cot", cot_moves) + to_neighbour(1))
    fetched[3] = steps.take(("gate_up", 3))
    kvs = [kv_own] + [steps.take(("kv", j)) for j in range(1, cycle)]
    attn, first, second = attend(q_rot, place_args, wo, kvs, packs, groups)
    attn_low = attn.reshape(tokens, q_width)
    steps.step(to_core("branch", second))
    steps.step(to_neighbour(2), late=lambda: to_rows("branch", first))
    kept["cot"] = join(own_cot, arrived("cot"))

    def middle_moves():
        kept["middle"], kept["normed"], *sends = in_vmem(
            functools.partial(middle_kernel, packs),
            [full(half, width)] + [low(half, width)] * packs,
            own_in,
            gain_two,
            kept["branch"],
            *arrived("branch"),
        )
        return send_all("two", sends)

    steps.step(to_neighbour(3) + to_core("cot", kept["cot"]), late=middle_moves)

    def wd_moves(ks):
        return [to_pack("down", k, two_halves(down_weight, k)) for k in ks]

    own_columns = [two_halves(weight, 0) for weight in (gate_weight, up_weight, down_weight)]
    own_gate, own_up, own_down = steps.step(
        wd_moves([1, 2]),
        late=lambda: joined("two", kept["normed"], arrived("two")),
        carry=own_columns,
    )
    all_cot = both_of("cot")
    neighbours = [steps.take(("neighbour", k)) for k in far]
    normed_two = (kept["two"], unwaited("two"))

    unit_weights = (own_gate, own_up, [fetched[k] for k in far], neighbours)
    gate_val, up_val, hidden = gate_up(normed_two, *unit_weights)
    d_wd = weight_grad([(*all_cot, hidden)], packs, side_arg)

    def back(name, grad, ks):
        return [to_pack(name, k, grad[k]) for k in ks]

    def entry(name, k, grad=None):
        return ((name, k), grad[0] if k == 0 else None)

    steps.step(back("wd", d_wd, [1, 2]), summed=entry("wd", 0, d_wd))
    wg, wu = whole_columns(*unit_weights)
    wg, wu = steps.step(wd_moves([3]), summed=entry("wd", 1), carry=(wg, wu))
    steps.step(back("wd", d_wd, [3]), summed=entry("wd", 2))
    wd_pieces = [own_down] + arrived("down")
    d_gate, d_up = units_back(all_cot, wd_pieces, gate_val, up_val)
    second = half_rows([d_gate, d_up], [wg, wu], 1)
    d_wg = dict(zip((0, 1, 2), weight_grad([(*normed_two, d_gate)], packs, side_arg, (0, 1, 2))))
    steps.step(to_core("d_two", second) + back("wg", d_wg, [1, 2]), summed=entry("wg", 0, d_wg))
    first = half_rows([d_gate, d_up], [wg, wu], 0)
    (d_wg[3],) = weight_grad([(*normed_two, d_gate)], packs, side_arg, (3,))
    d_wu = weight_grad([(*normed_two, d_up)], packs, side_arg)
    steps.step(summed=entry("wd", 3), late=functools.partial(to_rows, "d_two", first))

    def branch_back():
        kept["d_middle"], kept["d_gain_two"], kept["d_branch"], *sends = in_vmem(
            functools.partial(branch_back_kernel, packs),
            [full(half, width), full(1, width)] + [low(half, width)] * packs,
            kept["middle"],
            gain_two,
            own_cot,
            kept["d_two"],
            *arrived("d_two"),
        )
        return send_all("d_branch", sends)

    steps.step(summed=entry("wu", 0, d_wu), late=branch_back)
    wd = join(wd_pieces[0], wd_pieces[1:])
    ff_second = half_rows([hidden], [wd], 1, LARGE)
    (ff_second,) = steps.step(
        back("wg", d_wg, [3]),
        summed=entry("wg", 1),
        late=lambda: joined("all_branch", kept["d_branch"], arrived("d_branch")),
        first=(ff_second,),
    )
    sums = steps.line.sums

    def settle_all(name, cost=SMALL):
        return settle(at_end, index, [sums[name, k] for k in range(packs)], ff_width, cost)

    d_branch = (kept["all_branch"], unwaited("all_branch"))
    d_q, d_kv = attend_back(
        here_arg, q_rot, d_branch, cosine, sine, place_args, wo, kvs, packs, groups
    )
    ff_first = half_rows([hidden], [wd], 0, LARGE)
    d_q, d_kv, ff_first = steps.step(
        back("wu", d_wu, [1, 2]), summed=entry("wg", 2), carry=(d_q, d_kv), first=(ff_first,)
    )
    steps.step(back("wu", d_wu, [3]) + to_core("ff", ff_second), summed=("d_kv", d_kv))
    steps.step(summed=entry("wg", 3), late=functools.partial(to_rows, "ff", ff_first))
    steps.step(summed=entry("wu", 1))
    down_grad = settle_all("wd", LARGE)
    (down_grad,) = steps.step(summed=entry("wu", 2), first=(down_grad,))
    result = in_vmem(
        result_kernel, [low(half, width)], kept["middle"], kept["ff"], *arrived("ff")
    )[0]
    d_qkv = in_vmem(
        d_qkv_kernel,
        [low(tokens, q_width + 2 * k_width)],
        at_end,
        here_arg,
        *sums["d_kv"],
        d_q,
        cosine,
        sine,
        scalars=2,
    )[0]
    d_wqkvo = weight_grad([(*normed_one, d_qkv), (*d_branch, attn_low)], packs)
    first, second = rows_sum([d_qkv], [wqkv])
    steps.step(
        back("wqkvo", d_wqkvo, [1, 2]) + to_core("d_one", second), summed=entry("wu", 3)
    )
    steps.step(
        summed=entry("wqkvo", 0, d_wqkvo), late=functools.partial(to_rows, "d_one", first)
    )

    def both_rows(own, other):
        return in_vmem(
            functools.partial(rows_back_kernel, packs),
            [low(rows, width)],
            index,
            own,
            other,
            scalars=1,
        )[0]

    gate_grad = settle_all("wg", LARGE)
    def gains_to_core():
        kept["in_grad"], d_gain_one = in_vmem(
            functools.partial(in_grad_kernel, packs),
            [low(half, width), full(1, width)],
            own_in,
            gain_one,
            kept["d_middle"],
            kept["d_one"],
            *arrived("d_one"),
        )
        kept["gains"] = jnp.concatenate([d_gain_one, kept["d_gain_two"]], axis=0)
        return to_core("gains", kept["gains"]) + to_core("in_grad", kept["in_grad"])

    def gains_to_packs():
        kept["gains"] = kept["gains"] + steps.take("gains")
        return [to_pack("gains", k, kept["gains"][:, k * depth : (k + 1) * depth]) for k in far]

    def gains_along():
        kept["gains"] = kept["gains"][:, :depth]
        for k in far:
            kept["gains"] = kept["gains"] + steps.take(("gains", k))
        return [(("gains", j), kept["gains"], "ctx", pairs_by(j, cycle)) for j in range(1, cycle)]

    steps.step(back("wqkvo", d_wqkvo, [3]), summed=entry("wqkvo", 1), late=gains_to_core)
    (gate_grad,) = steps.step(
        summed=entry("wqkvo", 2), late=gains_to_packs, first=(gate_grad,)
    )
    up_grad = settle_all("wu")
    in_grad = both_rows(kept["in_grad"], steps.take("in_grad"))
    in_grad, up_grad = steps.step(
        to_core("result", result), summed=entry("wqkvo", 3), carry=(in_grad, up_grad)
    )
    steps.step(late=gains_along)
    out_hidden = both_rows(result, steps.take("result"))
    (out_hidden,) = steps.step(carry=(out_hidden,))
    steps.step()
    shares_of_gains = jnp.stack(
        [kept["gains"]] + [steps.take(("gains", j)) for j in range(1, cycle)]
    )
    gains = steps.token[0, 0]
    for place in range(cycle):
        gains = gains + lax.dynamic_index_in_dim(shares_of_gains, here ^ place, 0, keepdims=False)
    q_grad, k_grad, v_grad, o_grad = settle_attention(
        at_end, index, [sums["wqkvo", k] for k in range(packs)], q_width, 2 * k_width
    )
    return (
        out_hidden,
        in_grad,
        gains[0],
        q_grad,
        k_grad,
        v_grad,
        o_grad,
        gains[1],
        gate_grad,
        up_grad,
        down_grad,
    )


def gathered_weights(
    hidden_in,
    out_cotangent,
    norm1_gain,
    q_weight,
    key_projection_weight,
    value_projection_weight,
    o_weight,
    norm2_gain,
    gate_weight,
    up_weight,
    down_weight,
    seq_lengths,
    span_order,
):
    rows_here = hidden_in.shape[0]
    order_row = span_order[0]
    length_row = seq_lengths[0]
    kv_heads = key_projection_weight.shape[1] // HEAD_SIZE
    query_groups = QUERY_HEADS // KEY_VALUE_HEADS
    score_scale = 1.0 / math.sqrt(HEAD_SIZE)
    whole_rows = rows_here * lax.axis_size("ctx")
    local_rows = lax.axis_index("ctx") * rows_here + jnp.arange(rows_here, dtype=jnp.int32)
    q_place, q_segment, q_offset = stream_place(local_rows, order_row, length_row, rows_here)
    inputs = hidden_in.astype(jnp.float32)
    gain_one, wq_full, wk_full, wv_full, wo_full = (
        lax.all_gather(norm1_gain, "fsdp", axis=0, tiled=True),
        lax.all_gather(q_weight, "fsdp", axis=0, tiled=True),
        lax.all_gather(key_projection_weight, "fsdp", axis=0, tiled=True),
        lax.all_gather(value_projection_weight, "fsdp", axis=0, tiled=True),
        lax.all_gather(o_weight, "fsdp", axis=0, tiled=True),
    )
    gain_one = gain_one.astype(jnp.float32)
    first_normalized = normalize(inputs, gain_one)
    normed_low = first_normalized.astype(jnp.bfloat16)
    q_linear = jnp.dot(normed_low, wq_full, preferred_element_type=jnp.float32).reshape(
        rows_here, kv_heads * query_groups, HEAD_SIZE
    )
    k_linear = jnp.dot(normed_low, wk_full, preferred_element_type=jnp.float32).reshape(
        rows_here, kv_heads, HEAD_SIZE
    )
    q_rotated = (
        rotary_embedding(q_linear, q_offset)
        .astype(jnp.bfloat16)
        .reshape(rows_here, kv_heads, query_groups, HEAD_SIZE)
    )
    k_rotated = (
        rotary_embedding(k_linear, q_offset)
        .astype(jnp.bfloat16)
        .reshape(rows_here, kv_heads * HEAD_SIZE)
    )
    v_low = jnp.dot(normed_low, wv_full, preferred_element_type=jnp.float32).astype(jnp.bfloat16)

    def key_blocks(shard_rows):
        row_count = shard_rows.shape[0]
        key_total_width = math.gcd(row_count, 512)
        number = row_count // key_total_width
        k_place, k_segment, _ = stream_place(
            jnp.arange(row_count, dtype=jnp.int32), order_row, length_row, rows_here
        )
        return (
            key_total_width,
            number,
            k_place.reshape(number, key_total_width),
            k_segment.reshape(number, key_total_width),
        )

    def scores_of(key_block, place_block, segment_block):
        scores = (
            jnp.einsum("qkgd,skd->kgqs", q_rotated, key_block, preferred_element_type=jnp.float32)
            * score_scale
        )
        visible = (
            (q_place[:, None] >= place_block[None, :])
            & (q_segment[:, None] == segment_block[None, :])
        )[None, None]
        return (jnp.where(visible, scores, -1e30), visible)

    start_state = (
        jnp.full((kv_heads, query_groups, rows_here), -1e30, jnp.float32),
        jnp.zeros((kv_heads, query_groups, rows_here), jnp.float32),
        jnp.zeros((kv_heads, query_groups, rows_here, HEAD_SIZE), jnp.float32),
    )
    folded = start_state
    key_row_block = lax.all_gather(k_rotated, "ctx", axis=0, tiled=True)
    value_row_block = lax.all_gather(v_low, "ctx", axis=0, tiled=True)
    key_total_width, number, k_place, k_segment = key_blocks(key_row_block)

    def one_step(carried, pieces):
        running_max, totals, accumulated = carried
        key_block, value_block, place_block, segment_block = pieces
        scores, visible = scores_of(key_block, place_block, segment_block)
        new_max = jnp.maximum(running_max, jnp.max(scores, axis=-1))
        weights = jnp.where(visible, jnp.exp(scores - new_max[..., None]), 0.0)
        factor = jnp.exp(running_max - new_max)
        totals = totals * factor + jnp.sum(weights, axis=-1)
        accumulated = accumulated * factor[..., None] + jnp.einsum(
            "kgqs,skd->kgqd",
            weights.astype(jnp.bfloat16),
            value_block,
            preferred_element_type=jnp.float32,
        )
        return ((new_max, totals, accumulated), None)

    pieces = (
        key_row_block.reshape(number, key_total_width, kv_heads, HEAD_SIZE),
        value_row_block.reshape(number, key_total_width, kv_heads, HEAD_SIZE),
        k_place,
        k_segment,
    )
    folded, _ = lax.scan(one_step, folded, pieces)
    running_max, totals, accumulated = folded
    mixed_out = jnp.transpose(accumulated / totals[..., None], (2, 0, 1, 3))
    log_sum = running_max + jnp.log(totals)
    attn_low = mixed_out.reshape(rows_here, kv_heads * query_groups * HEAD_SIZE).astype(
        jnp.bfloat16
    )
    branch = lax.psum(contract_last(attn_low, wo_full).astype(jnp.bfloat16), "tp").astype(
        jnp.float32
    )
    middle = inputs + branch
    gain_two, wg_full, wu_full, wd_full = (
        lax.all_gather(norm2_gain, "fsdp", axis=0, tiled=True),
        lax.all_gather(gate_weight, "fsdp", axis=0, tiled=True),
        lax.all_gather(up_weight, "fsdp", axis=0, tiled=True),
        lax.all_gather(down_weight, "fsdp", axis=0, tiled=True),
    )
    gain_two = gain_two.astype(jnp.float32)
    normed_two = normalize(middle, gain_two)
    normed_two_low = normed_two.astype(jnp.bfloat16)
    gate_val = jnp.dot(normed_two_low, wg_full, preferred_element_type=jnp.float32)
    up_val = jnp.dot(normed_two_low, wu_full, preferred_element_type=jnp.float32)
    hidden = swiglu(gate_val, up_val).astype(jnp.bfloat16)
    ffn_out = lax.psum(contract_last(hidden, wd_full).astype(jnp.bfloat16), "tp").astype(
        jnp.float32
    )
    result = (middle + ffn_out).astype(jnp.bfloat16)
    grad_out = out_cotangent.astype(jnp.float32)
    d_wd = contract_first(out_cotangent, hidden)
    d_hidden = jnp.dot(out_cotangent, wd_full, preferred_element_type=jnp.float32)
    _, swiglu_back = jax.vjp(swiglu, gate_val, up_val)
    d_gate, d_up = swiglu_back(d_hidden)
    d_gate_low = d_gate.astype(jnp.bfloat16)
    d_up_low = d_up.astype(jnp.bfloat16)
    d_wg = contract_first(normed_two_low, d_gate_low)
    d_wu = contract_first(normed_two_low, d_up_low)
    d_normed_two = lax.psum(
        (contract_last(d_gate_low, wg_full) + contract_last(d_up_low, wu_full)).astype(
            jnp.bfloat16
        ),
        "tp",
    ).astype(jnp.float32)
    _, norm_two_back = jax.vjp(normalize, middle, gain_two)
    d_middle_norm, d_gain_two = norm_two_back(d_normed_two)
    d_middle = grad_out + d_middle_norm
    d_branch_low = d_middle.astype(jnp.bfloat16)
    d_wo = contract_first(d_branch_low, attn_low)
    d_attn = jnp.dot(d_branch_low, wo_full, preferred_element_type=jnp.float32).astype(jnp.bfloat16)
    d_attn_heads = d_attn.reshape(rows_here, kv_heads, query_groups, HEAD_SIZE)
    row_delta = jnp.einsum("qkgd,qkgd->kgq", d_attn_heads.astype(jnp.float32), mixed_out)
    back_state = (
        jnp.zeros((rows_here, kv_heads, query_groups, HEAD_SIZE), jnp.float32),
        jnp.zeros((whole_rows, kv_heads, HEAD_SIZE), jnp.float32),
        jnp.zeros((whole_rows, kv_heads, HEAD_SIZE), jnp.float32),
    )
    folded = back_state
    key_row_block = lax.all_gather(k_rotated, "ctx", axis=0, tiled=True)
    value_row_block = lax.all_gather(v_low, "ctx", axis=0, tiled=True)
    key_total_width, number, k_place, k_segment = key_blocks(key_row_block)

    def one_step(carried, pieces):
        d_query, d_keys, d_values = carried
        key_block, value_block, place_block, segment_block, step_index = pieces
        scores, visible = scores_of(key_block, place_block, segment_block)
        prob_rows = jnp.where(visible, jnp.exp(scores - log_sum[..., None]), 0.0)
        d_values_block = jnp.einsum(
            "kgqs,qkgd->skd",
            prob_rows.astype(jnp.bfloat16),
            d_attn_heads,
            preferred_element_type=jnp.float32,
        )
        d_probs = jnp.einsum(
            "qkgd,skd->kgqs", d_attn_heads, value_block, preferred_element_type=jnp.float32
        )
        d_scores = (prob_rows * (d_probs - row_delta[..., None])).astype(jnp.bfloat16)
        d_query = (
            d_query
            + jnp.einsum("kgqs,skd->qkgd", d_scores, key_block, preferred_element_type=jnp.float32)
            * score_scale
        )
        d_keys_block = (
            jnp.einsum("kgqs,qkgd->skd", d_scores, q_rotated, preferred_element_type=jnp.float32)
            * score_scale
        )
        row_first = step_index * key_total_width
        d_keys = lax.dynamic_update_slice_in_dim(
            d_keys,
            lax.dynamic_slice_in_dim(d_keys, row_first, key_total_width, 0) + d_keys_block,
            row_first,
            0,
        )
        d_values = lax.dynamic_update_slice_in_dim(
            d_values,
            lax.dynamic_slice_in_dim(d_values, row_first, key_total_width, 0) + d_values_block,
            row_first,
            0,
        )
        return ((d_query, d_keys, d_values), None)

    pieces = (
        key_row_block.reshape(number, key_total_width, kv_heads, HEAD_SIZE),
        value_row_block.reshape(number, key_total_width, kv_heads, HEAD_SIZE),
        k_place,
        k_segment,
        jnp.arange(number, dtype=jnp.int32),
    )
    folded, _ = lax.scan(one_step, folded, pieces)
    d_query, d_keys_all, d_values_all = folded
    d_key_own, d_value_own = (
        lax.psum_scatter(
            d_keys_all.astype(jnp.bfloat16), "ctx", scatter_dimension=0, tiled=True
        ).astype(jnp.float32),
        lax.psum_scatter(
            d_values_all.astype(jnp.bfloat16), "ctx", scatter_dimension=0, tiled=True
        ).astype(jnp.float32),
    )
    _, rope_q_back = jax.vjp(lambda rotated_in: rotary_embedding(rotated_in, q_offset), q_linear)
    _, rope_k_back = jax.vjp(lambda rotated_in: rotary_embedding(rotated_in, q_offset), k_linear)
    (d_q_linear,) = rope_q_back(d_query.reshape(rows_here, kv_heads * query_groups, HEAD_SIZE))
    (d_k_linear,) = rope_k_back(d_key_own)
    d_q_low = d_q_linear.reshape(rows_here, kv_heads * query_groups * HEAD_SIZE).astype(
        jnp.bfloat16
    )
    d_k_low = d_k_linear.reshape(rows_here, kv_heads * HEAD_SIZE).astype(jnp.bfloat16)
    d_v_low = d_value_own.reshape(rows_here, kv_heads * HEAD_SIZE).astype(jnp.bfloat16)
    d_wq = contract_first(normed_low, d_q_low)
    d_wk = contract_first(normed_low, d_k_low)
    d_wv = contract_first(normed_low, d_v_low)
    d_normed_one = lax.psum(
        (
            contract_last(d_q_low, wq_full)
            + contract_last(d_k_low, wk_full)
            + contract_last(d_v_low, wv_full)
        ).astype(jnp.bfloat16),
        "tp",
    ).astype(jnp.float32)
    _, norm_one_back = jax.vjp(normalize, inputs, gain_one)
    d_inputs_norm, d_gain_one = norm_one_back(d_normed_one)
    in_grad = (d_middle + d_inputs_norm).astype(jnp.bfloat16)
    weight_grads = (d_gain_one, d_wq, d_wk, d_wv, d_wo, d_gain_two, d_wg, d_wu, d_wd)
    shares = (
        lax.psum_scatter(weight_grads[0], ("fsdp", "ctx"), scatter_dimension=0, tiled=True),
        lax.psum_scatter(weight_grads[1], ("fsdp", "ctx"), scatter_dimension=0, tiled=True),
        lax.psum_scatter(weight_grads[2], ("fsdp", "ctx"), scatter_dimension=0, tiled=True),
        lax.psum_scatter(weight_grads[3], ("fsdp", "ctx"), scatter_dimension=0, tiled=True),
        lax.psum_scatter(weight_grads[4], ("fsdp", "ctx"), scatter_dimension=0, tiled=True),
        lax.psum_scatter(weight_grads[5], ("fsdp", "ctx"), scatter_dimension=0, tiled=True),
        lax.psum_scatter(weight_grads[6], ("fsdp", "ctx"), scatter_dimension=0, tiled=True),
        lax.psum_scatter(weight_grads[7], ("fsdp", "ctx"), scatter_dimension=0, tiled=True),
        lax.psum_scatter(weight_grads[8], ("fsdp", "ctx"), scatter_dimension=0, tiled=True),
    )
    owned_grads = (
        lax.all_gather(shares[0].astype(jnp.bfloat16), "ctx", axis=0, tiled=True).astype(
            jnp.float32
        ),
        lax.all_gather(shares[1].astype(jnp.bfloat16), "ctx", axis=0, tiled=True).astype(
            jnp.float32
        ),
        lax.all_gather(shares[2].astype(jnp.bfloat16), "ctx", axis=0, tiled=True).astype(
            jnp.float32
        ),
        lax.all_gather(shares[3].astype(jnp.bfloat16), "ctx", axis=0, tiled=True).astype(
            jnp.float32
        ),
        lax.all_gather(shares[4].astype(jnp.bfloat16), "ctx", axis=0, tiled=True).astype(
            jnp.float32
        ),
        lax.all_gather(shares[5].astype(jnp.bfloat16), "ctx", axis=0, tiled=True).astype(
            jnp.float32
        ),
        lax.all_gather(shares[6].astype(jnp.bfloat16), "ctx", axis=0, tiled=True).astype(
            jnp.float32
        ),
        lax.all_gather(shares[7].astype(jnp.bfloat16), "ctx", axis=0, tiled=True).astype(
            jnp.float32
        ),
        lax.all_gather(shares[8].astype(jnp.bfloat16), "ctx", axis=0, tiled=True).astype(
            jnp.float32
        ),
    )
    return (
        result,
        in_grad,
        owned_grads[0],
        owned_grads[1],
        owned_grads[2],
        owned_grads[3],
        owned_grads[4],
        owned_grads[5],
        owned_grads[6],
        owned_grads[7],
        owned_grads[8],
    )


def solution(mesh):
    placed = (
        P(("fsdp", "ctx"), None),
        P(("fsdp", "ctx"), None),
        P("fsdp"),
        P("fsdp", "tp"),
        P("fsdp", "tp"),
        P("fsdp", "tp"),
        P("fsdp", "tp"),
        P("fsdp"),
        P("fsdp", "tp"),
        P("fsdp", "tp"),
        P("fsdp", "tp"),
        P("fsdp", None),
        P("fsdp", None),
    )
    plane = mesh.shape["fsdp"] * mesh.shape["tp"]
    splits = mesh.shape["tp"] == 2 and KEY_VALUE_HEADS == plane and mesh.shape["ctx"] == 4
    return jax.shard_map(
        split_heads if splits else gathered_weights,
        mesh=mesh,
        in_specs=placed,
        out_specs=(
            P(("fsdp", "ctx"), None),
            P(("fsdp", "ctx"), None),
            P("fsdp"),
            P("fsdp", "tp"),
            P("fsdp", "tp"),
            P("fsdp", "tp"),
            P("fsdp", "tp"),
            P("fsdp"),
            P("fsdp", "tp"),
            P("fsdp", "tp"),
            P("fsdp", "tp"),
        ),
        check_vma=False,
    )
```
